32 devices in a mesh: wide: 8 (over z, x), narrow: 4 (over y, core).
Axes of the slice: x: 2, y: 2, z: 4, core: 2. Of those that a mesh axis runs over, the one named last changes fastest.
Arguments:
- inputs: float32 [8192, 768], P(('wide', 'narrow')), may hold values from -6 to 6
- history: bfloat16 [4, 8192, 768], P(None, ('wide', 'narrow')), may hold values from -6 to 6
- lengths: int32 [32], P(('wide', 'narrow')), may hold values from 192 to 256, as said below
- cotangent: float32 [8192, 768], P(('wide', 'narrow')), may hold values from -1536 to 1536
- w_qkv: bfloat16 [2, 768, 2304], P(None, ('wide', 'narrow')), may hold values from -0.21875 to 0.21875
- w_out: bfloat16 [2, 768, 768], P(None, ('wide', 'narrow')), may hold values from -1.75 to 1.75
- w_up: bfloat16 [2, 768, 3072], P(None, ('wide', 'narrow')), may hold values from -0.21875 to 0.21875
- w_down: bfloat16 [2, 3072, 768], P(None, ('wide', 'narrow')), may hold values from -0.109375 to 0.109375
- gains: bfloat16 [2, 2, 768], P(None, None, ('wide', 'narrow')), may hold values from 0.5 to 1.5
- alpha_first: float32 [5], replicated, may hold values from -0.6 to 0.8
- alpha_second: float32 [6], replicated, may hold values from -0.6 to 1.2
Outputs:
- blended: float32 [8192, 768], P(('wide', 'narrow'))
- stored: float32 [2, 8192, 768], P(None, ('wide', 'narrow'))
- grad_inputs: float32 [8192, 768], P(('wide', 'narrow'))
- grad_history: float32 [4, 8192, 768], P(None, ('wide', 'narrow'))
- grad_w_qkv: float32 [2, 768, 2304], P(None, ('wide', 'narrow'))
- grad_w_out: float32 [2, 768, 768], P(None, ('wide', 'narrow'))
- grad_w_up: float32 [2, 768, 3072], P(None, ('wide', 'narrow'))
- grad_w_down: float32 [2, 3072, 768], P(None, ('wide', 'narrow'))
- grad_gains: float32 [2, 2, 768], P(None, None, ('wide', 'narrow'))
- grad_alpha_first: float32 [5], replicated
- grad_alpha_second: float32 [6], replicated
The draws below stay inside these ranges and needn't reach their ends.
Inputs may be any that keep to these rules, and one draw needn't show every extreme that they name: `lengths`: real tokens of each sequence; one sequence has exactly 256 and another exactly 192.
All inputs are finite; a program needn't handle non-finite values.
Results may differ from the reference program's by a relative error of at most 0.034.
Values may be sent and summed in bfloat16 or wider, within the bound.
A program may use at most 256 MiB of HBM per device.

```python
import math
import jax
import jax.numpy as jnp
from jax import lax

D = 768
HEADS = 12
FF = 3072
SEQ = 256
HIST = 4
LEN_MIN = 192
BATCH = 32
TOKENS = 8192


def draw_lengths(key, part):
    places = jnp.arange(BATCH, dtype=jnp.int32)
    spread_range = SEQ - LEN_MIN
    base = LEN_MIN + spread_range * places // BATCH
    jitter = jax.random.randint(key, (BATCH,), 0, spread_range // 4 + 1)
    counts = jnp.minimum(base + jitter, SEQ)
    counts = counts.at[BATCH - 1].set(SEQ)
    counts = counts.at[0].set(LEN_MIN)
    return counts.astype(jnp.int32)


def signed_weights(key, count, low_end, high_end):
    mag_key, sign_key = jax.random.split(key)
    magnitude = jax.random.uniform(mag_key, (count,), jnp.float32, low_end, high_end)
    signs = (2 * jax.random.randint(sign_key, (count,), 0, 2) - 1).astype(jnp.float32)
    return magnitude * signs


def draw_alpha_first(key, part):
    key = jax.random.fold_in(key, 11)
    past_key, last_key = jax.random.split(key)
    past_part = signed_weights(past_key, HIST, 0.15, 0.6)
    last_part = jax.random.uniform(last_key, (1,), jnp.float32, 0.4, 0.8)
    return jnp.concatenate([past_part, last_part]).astype(jnp.float32)


def draw_alpha_second(key, part):
    key = jax.random.fold_in(key, 12)
    past_key, middle_key, last_key = jax.random.split(key, 3)
    past_part = signed_weights(past_key, HIST, 0.15, 0.6)
    middle_part = signed_weights(middle_key, 1, 0.2, 0.6)
    last_part = jax.random.uniform(last_key, (1,), jnp.float32, 0.8, 1.2)
    return jnp.concatenate([past_part, middle_part, last_part]).astype(jnp.float32)


def shard_levels(own_key, shape, cuts, low, largest):
    def one(position, parts):
        heights = jax.random.uniform(jax.random.fold_in(jax.random.fold_in(own_key, 6), position), (parts,), jnp.float32, low / len(cuts), largest / len(cuts))
        return jnp.repeat(jnp.exp(heights), shape[position] // parts).reshape((-1,) + (1,) * (len(shape) - position - 1))

    level = one(*cuts[0])
    for cut in cuts[1:]:
        level = level * one(*cut)
    return level


def noise(key, dims, scale, bound, pieces=(), kind=jnp.bfloat16):
    values = jax.random.normal(key, dims, jnp.float32) * scale
    if len(pieces) > 0:
        values = shard_levels(key, dims, pieces, -0.22, 0.18) * values
    return jnp.clip(values, min=-bound, max=bound).astype(kind)


def setup_inputs(seed: int = 0) -> dict:
    streams_of = jax.random.split(jax.random.key(seed), 12)
    return {
        "inputs": noise(streams_of[0], (TOKENS, D), 1.0, 6.0, ((0, 32),), jnp.float32),
        "history": noise(streams_of[1], (HIST, TOKENS, D), 1.0, 6.0, ((1, 32),)),
        "lengths": draw_lengths(jax.random.fold_in(streams_of[11], 71), 0),
        "cotangent": noise(streams_of[3], (TOKENS, D), (TOKENS // 32), 1536.0, ((0, 32),), jnp.float32),
        "w_qkv": noise(streams_of[4], (2, D, 3 * D), D ** -0.5, 0.21875, ((1, 32),)),
        "w_out": noise(streams_of[5], (2, D, D), (max(D // 64, 8)) ** -0.5, 1.75, ((1, 32),)),
        "w_up": noise(streams_of[6], (2, D, FF), D ** -0.5, 0.21875, ((1, 32),)),
        "w_down": noise(streams_of[7], (2, FF, D), FF ** -0.5, 0.109375, ((1, 32),)),
        "gains": jnp.clip(1.0 + 0.1 * jax.random.normal(streams_of[8], (2, 2, D), jnp.float32), 0.5, 1.5).astype(jnp.bfloat16),
        "alpha_first": draw_alpha_first(jax.random.fold_in(streams_of[11], 71), 0),
        "alpha_second": draw_alpha_second(jax.random.fold_in(streams_of[11], 71), 0),
    }


@jax.custom_vjp
def low(v):
    return lax.optimization_barrier(v.astype(jnp.bfloat16)).astype(jnp.float32)

@jax.custom_vjp
def low_back(v):
    return v

def low_keep(v):
    return (low(v), None)

def low_pass(kept, grad):
    return (grad,)

def back_keep(v):
    return (v, None)

def back_low(kept, grad):
    return (low(grad),)
low.defvjp(low_keep, low_pass)
low_back.defvjp(back_keep, back_low)
norm_eps = 1e-05
gelu_coef = 0.044715
gelu_scale = math.sqrt(2.0 / math.pi)
highest = lax.Precision.HIGHEST

def matmul(left, right):
    return jnp.dot(left, right, precision=highest)

def layer_norm(hidden, gain_row):
    center = hidden - lax.optimization_barrier(jnp.mean(hidden, axis=-1, keepdims=True))
    spread = lax.optimization_barrier(jnp.mean(center * center, axis=-1, keepdims=True))
    return center * lax.rsqrt(spread + norm_eps) * gain_row

def gelu(values):
    return 0.5 * values * (1.0 + jnp.tanh(gelu_scale * (values + gelu_coef * values * values * values)))

def rotary_tables(seq_length, head_width):
    half_width = head_width // 2
    frequency = 10000.0 ** (-jnp.arange(half_width, dtype=jnp.float32) / half_width)
    angles = jnp.arange(seq_length, dtype=jnp.float32)[:, None] * frequency[None, :]
    return (jnp.cos(angles)[:, None, :], jnp.sin(angles)[:, None, :])

def rotate(values, cos_table, sin_table):
    half_width = values.shape[-1] // 2
    left_half = values[..., :half_width]
    right_half = values[..., half_width:]
    return jnp.concatenate([left_half * cos_table - right_half * sin_table, right_half * cos_table + left_half * sin_table], axis=-1)

def block(hidden, weights, length):
    layer_qkv, layer_out, layer_up, layer_down, layer_gains = weights
    seq_length = hidden.shape[0]
    head_width = D // HEADS
    normed = low(layer_norm(hidden, layer_gains[0]))
    joined = low_back(matmul(normed, layer_qkv)).reshape(seq_length, 3, HEADS, head_width)
    cos_table, sin_table = rotary_tables(seq_length, head_width)
    queries = low(rotate(joined[:, 0], cos_table, sin_table))
    key_rows = low(rotate(joined[:, 1], cos_table, sin_table))
    value_rows = low(joined[:, 2])
    scores = low_back(jnp.einsum('qhe,khe->hqk', queries, key_rows, precision=highest) * head_width ** (-0.5))
    places = jnp.arange(seq_length)
    allowed = (places[None, :] <= places[:, None]) & (places[None, :] < length)
    scores = jnp.where(allowed[None], scores, -1e+30)
    row_top = lax.optimization_barrier(jnp.max(scores, axis=-1, keepdims=True))
    exp_scores = jnp.exp(scores - row_top)
    prob_rows = exp_scores / lax.optimization_barrier(jnp.sum(exp_scores, axis=-1, keepdims=True))
    attended = jnp.einsum('hqk,khe->qhe', low(prob_rows), value_rows, precision=highest).reshape(seq_length, D)
    attended = low_back(low(attended))
    after_attn = hidden + low_back(matmul(attended, layer_out))
    normed_two = low(layer_norm(after_attn, layer_gains[1]))
    up_vals = low_back(matmul(normed_two, layer_up))
    active = low(gelu(up_vals))
    return after_attn + low_back(matmul(active, layer_down))

def forward(layer_input, past_outs, params, alphas, length):
    alpha_one, alpha_two = alphas
    all_qkv, all_out, all_up, all_down, all_gains = params
    first_layer = (all_qkv[0], all_out[0], all_up[0], all_down[0], all_gains[0])
    second_layer = (all_qkv[1], all_out[1], all_up[1], all_down[1], all_gains[1])
    kept_one = block(layer_input, first_layer, length)
    carried = jnp.einsum('j,jtd->td', alpha_one[:HIST], past_outs, precision=highest) + alpha_one[HIST] * kept_one
    kept_two = block(carried, second_layer, length)
    blended = jnp.einsum('j,jtd->td', alpha_two[:HIST], past_outs, precision=highest) + alpha_two[HIST] * kept_one + alpha_two[HIST + 1] * kept_two
    return (blended, jnp.stack([kept_one, kept_two]))

def reference(inputs, history, lengths, cotangent, w_qkv, w_out, w_up, w_down, gains, alpha_first, alpha_second):
    token_total = jnp.sum(lengths.astype(jnp.float32))
    params = (w_qkv.astype(jnp.float32), w_out.astype(jnp.float32), w_up.astype(jnp.float32), w_down.astype(jnp.float32), gains.astype(jnp.float32))
    alphas = (alpha_first, alpha_second)
    layer_inputs = inputs.astype(jnp.float32).reshape(BATCH, SEQ, D)
    past_all = jnp.moveaxis(history.astype(jnp.float32).reshape(HIST, BATCH, SEQ, D), 1, 0)
    out_grads = cotangent.astype(jnp.float32).reshape(BATCH, SEQ, D)
    zero_grads = jax.tree.map(jnp.zeros_like, (params, alphas))

    def per_sequence(running, seq_item):
        layer_input, past_outs, out_grad, length = seq_item

        def run_block(start_rows, past_rows, param_set, alpha_set):
            return forward(start_rows, past_rows, param_set, alpha_set, length)
        result, pullback, kept_rows = jax.vjp(run_block, layer_input, past_outs, params, alphas, has_aux=True)
        live_mask = (jnp.arange(SEQ) < length).astype(jnp.float32)[:, None]
        grad_start, grad_past, grad_params, grad_alphas = pullback(out_grad * live_mask / token_total)
        running = jax.tree.map(jnp.add, running, (grad_params, grad_alphas))
        return (running, (result, kept_rows, grad_start, grad_past))
    running, (results, kept_all, grad_starts, grad_pasts) = lax.scan(per_sequence, zero_grads, (layer_inputs, past_all, out_grads, lengths))
    grad_params, grad_alphas = running
    return (results.reshape(TOKENS, D), jnp.moveaxis(kept_all, 0, 1).reshape(2, TOKENS, D), grad_starts.reshape(TOKENS, D), jnp.moveaxis(grad_pasts, 0, 1).reshape(HIST, TOKENS, D), grad_params[0], grad_params[1], grad_params[2], grad_params[3], grad_params[4], grad_alphas[0], grad_alphas[1])
```

```python
import functools
import math

import jax
import jax.numpy as jnp
from jax import lax
from jax.experimental import pallas as pl
from jax.experimental.pallas import tpu as pltpu
from jax.sharding import PartitionSpec as P

MESH = pl.DeviceIdType.MESH
BF = jnp.bfloat16
F32 = jnp.float32

HEADS = 12


norm_eps = 1e-05
gelu_coef = 0.044715
gelu_scale = math.sqrt(2.0 / math.pi)
masked_score = -1e30


def product(left, right):
    return jnp.dot(left, right, preferred_element_type=jnp.float32)


def layer_norm(hidden, gain_row):
    center = hidden - jnp.mean(hidden, axis=-1, keepdims=True)
    inverse = lax.rsqrt(jnp.mean(center * center, axis=-1, keepdims=True) + norm_eps)
    standard = center * inverse
    return (standard * gain_row, standard, inverse)


def norm_back(grad_rows, standard, inverse, gain_row):
    scaled = grad_rows * gain_row
    grad_gain = jnp.sum(grad_rows * standard, axis=0)
    grad_in = inverse * (
        scaled
        - jnp.mean(scaled, axis=-1, keepdims=True)
        - standard * jnp.mean(scaled * standard, axis=-1, keepdims=True)
    )
    return (grad_in, grad_gain)


def gelu(values):
    return (
        0.5
        * values
        * (1.0 + jnp.tanh(gelu_scale * (values + gelu_coef * values * values * values)))
    )


def gelu_slope(values):
    tangent = jnp.tanh(gelu_scale * (values + gelu_coef * values * values * values))
    return 0.5 * (1.0 + tangent) + 0.5 * values * (1.0 - tangent * tangent) * gelu_scale * (
        1.0 + 3.0 * gelu_coef * values * values
    )


def rotary_tables(seq_length, head_width):
    half_width = head_width // 2
    frequency = 10000.0 ** (-jnp.arange(half_width, dtype=jnp.float32) / half_width)
    angles = jnp.arange(seq_length, dtype=jnp.float32)[:, None] * frequency[None, :]
    return (jnp.cos(angles)[:, None, :], jnp.sin(angles)[:, None, :])


def rotate(values, cos_table, sin_table):
    half_width = values.shape[-1] // 2
    left_half = values[..., :half_width]
    right_half = values[..., half_width:]
    return jnp.concatenate(
        [
            left_half * cos_table - right_half * sin_table,
            right_half * cos_table + left_half * sin_table,
        ],
        axis=-1,
    )


def rotate_back(grad_rows, cos_table, sin_table):
    half_width = grad_rows.shape[-1] // 2
    left_grad = grad_rows[..., :half_width]
    right_grad = grad_rows[..., half_width:]
    return jnp.concatenate(
        [
            left_grad * cos_table + right_grad * sin_table,
            right_grad * cos_table - left_grad * sin_table,
        ],
        axis=-1,
    )


def allowed_mask(block_rows, key_count, length):
    row_place = jnp.arange(block_rows)
    col_place = jnp.arange(key_count)
    return (col_place[None, :] <= row_place[:, None]) & (col_place[None, :] < length)


def attention_forward(queries, key_rows, value_rows, length):
    seq_length, head_count, head_width = queries.shape
    score_scale = head_width ** (-0.5)
    block_rows = min(512, seq_length)
    scores = (
        jnp.einsum("qhe,khe->hqk", queries, key_rows, preferred_element_type=jnp.float32)
        * score_scale
    )
    allowed = allowed_mask(block_rows, block_rows, length)
    scores = jnp.where(allowed[None], scores, masked_score)
    row_top = jnp.max(scores, axis=-1, keepdims=True)
    exp_scores = jnp.exp(scores - row_top)
    row_total = jnp.sum(exp_scores, axis=-1, keepdims=True)
    prob_rows = (exp_scores / row_total).astype(jnp.bfloat16)
    pieces = jnp.einsum("hqk,khe->qhe", prob_rows, value_rows, preferred_element_type=jnp.float32)
    log_sums = row_top + jnp.log(row_total)
    return (pieces, log_sums)


def attention_backward(queries, key_rows, value_rows, log_sums, grad_attended, length):
    seq_length, head_count, head_width = queries.shape
    score_scale = head_width ** (-0.5)
    grad_keys = jnp.zeros(queries.shape, jnp.float32)
    grad_values = jnp.zeros(queries.shape, jnp.float32)
    block_rows = min(512, seq_length)
    scores = (
        jnp.einsum("qhe,khe->hqk", queries, key_rows, preferred_element_type=jnp.float32)
        * score_scale
    )
    allowed = allowed_mask(block_rows, block_rows, length)
    prob_rows = jnp.where(allowed[None], jnp.exp(scores - log_sums), 0.0)
    grad_prob = jnp.einsum(
        "qhe,khe->hqk", grad_attended, value_rows, preferred_element_type=jnp.float32
    )
    inner_sum = jnp.sum(prob_rows * grad_prob, axis=-1, keepdims=True)
    grad_score = (prob_rows * (grad_prob - inner_sum)).astype(jnp.bfloat16)
    grad_pieces = (
        jnp.einsum("hqk,khe->qhe", grad_score, key_rows, preferred_element_type=jnp.float32)
        * score_scale
    )
    grad_keys = grad_keys.at[:block_rows].add(
        jnp.einsum("hqk,qhe->khe", grad_score, queries, preferred_element_type=jnp.float32)
        * score_scale
    )
    grad_values = grad_values.at[:block_rows].add(
        jnp.einsum(
            "hqk,qhe->khe",
            prob_rows.astype(jnp.bfloat16),
            grad_attended,
            preferred_element_type=jnp.float32,
        )
    )
    return (grad_pieces, grad_keys, grad_values)


def layer_forward(hidden, weights, length):
    layer_qkv, layer_out, layer_up, layer_down, layer_gains = weights
    seq_length = hidden.shape[0]
    head_width = layer_out.shape[0] // HEADS
    normed, unit_one, inverse_one = layer_norm(hidden, layer_gains[0])
    normed = normed.astype(jnp.bfloat16)
    joined = product(normed, layer_qkv).reshape(seq_length, 3, HEADS, head_width)
    cos_table, sin_table = rotary_tables(seq_length, head_width)
    queries = rotate(joined[:, 0], cos_table, sin_table).astype(jnp.bfloat16)
    key_rows = rotate(joined[:, 1], cos_table, sin_table).astype(jnp.bfloat16)
    value_rows = joined[:, 2].astype(jnp.bfloat16)
    attended, log_sums = attention_forward(queries, key_rows, value_rows, length)
    attended = attended.reshape(seq_length, HEADS * head_width).astype(jnp.bfloat16)
    after_attn = hidden + product(attended, layer_out)
    normed_two, unit_two, inverse_two = layer_norm(after_attn, layer_gains[1])
    normed_two = normed_two.astype(jnp.bfloat16)
    up_vals = product(normed_two, layer_up)
    result = after_attn + product(gelu(up_vals).astype(jnp.bfloat16), layer_down)
    kept_state = (
        normed,
        unit_one,
        inverse_one,
        queries,
        key_rows,
        value_rows,
        log_sums,
        attended,
        unit_two,
        inverse_two,
        normed_two,
        up_vals,
    )
    return (result, kept_state)


def layer_backward(grad_rows, weights, kept_state, length):
    layer_qkv, layer_out, layer_up, layer_down, layer_gains = weights
    (
        normed,
        unit_one,
        inverse_one,
        queries,
        key_rows,
        value_rows,
        log_sums,
        attended,
        unit_two,
        inverse_two,
        normed_two,
        up_vals,
    ) = kept_state
    seq_length, head_count, head_width = queries.shape
    grad_low = grad_rows.astype(jnp.bfloat16)
    active = gelu(up_vals).astype(jnp.bfloat16)
    grad_down = jnp.einsum("tf,td->fd", active, grad_low, preferred_element_type=jnp.float32)
    grad_active = jnp.einsum("td,fd->tf", grad_low, layer_down, preferred_element_type=jnp.float32)
    grad_upv = (grad_active * gelu_slope(up_vals)).astype(jnp.bfloat16)
    grad_up = jnp.einsum("td,tf->df", normed_two, grad_upv, preferred_element_type=jnp.float32)
    grad_norm_two = jnp.einsum("tf,df->td", grad_upv, layer_up, preferred_element_type=jnp.float32)
    grad_after, gain_two = norm_back(grad_norm_two, unit_two, inverse_two, layer_gains[1])
    grad_after = grad_rows + grad_after
    grad_branch = grad_after.astype(jnp.bfloat16)
    grad_wout = jnp.einsum("ta,td->ad", attended, grad_branch, preferred_element_type=jnp.float32)
    grad_attended = jnp.einsum(
        "td,ad->ta", grad_branch, layer_out, preferred_element_type=jnp.float32
    )
    grad_attended = grad_attended.astype(jnp.bfloat16).reshape(seq_length, head_count, head_width)
    grad_query, grad_keys, grad_values = attention_backward(
        queries, key_rows, value_rows, log_sums, grad_attended, length
    )
    cos_table, sin_table = rotary_tables(seq_length, head_width)
    grad_joined = jnp.stack(
        [
            rotate_back(grad_query, cos_table, sin_table),
            rotate_back(grad_keys, cos_table, sin_table),
            grad_values,
        ],
        axis=1,
    )
    grad_joined = grad_joined.reshape(seq_length, 3 * head_count * head_width).astype(jnp.bfloat16)
    grad_qkv = jnp.einsum("td,tj->dj", normed, grad_joined, preferred_element_type=jnp.float32)
    grad_norm_one = jnp.einsum(
        "tj,dj->td", grad_joined, layer_qkv, preferred_element_type=jnp.float32
    )
    grad_in, gain_one = norm_back(grad_norm_one, unit_one, inverse_one, layer_gains[0])
    return (
        grad_after + grad_in,
        (grad_qkv, grad_wout, grad_up, grad_down, jnp.stack([gain_one, gain_two])),
    )


def mix_history(alphas, history):
    blended = alphas[0] * history[0].astype(jnp.float32)
    for entry in range(1, history.shape[0]):
        blended = blended + alphas[entry] * history[entry].astype(jnp.float32)
    return blended


def plain_body(
    inputs,
    history,
    lengths,
    cotangent,
    w_qkv,
    w_out,
    w_up,
    w_down,
    gains,
    alpha_first,
    alpha_second,
):
    token_total = lax.psum(jnp.sum(lengths.astype(jnp.float32)), ("wide", "narrow"))
    length = lengths[0]
    hist_count = history.shape[0]

    def fetch_layer(layer_no):
        return (
            lax.all_gather(w_qkv[layer_no], ("wide", "narrow"), axis=0, tiled=True),
            lax.all_gather(w_out[layer_no], ("wide", "narrow"), axis=0, tiled=True),
            lax.all_gather(w_up[layer_no], ("wide", "narrow"), axis=0, tiled=True),
            lax.all_gather(w_down[layer_no], ("wide", "narrow"), axis=0, tiled=True),
            lax.all_gather(gains[layer_no], ("wide", "narrow"), axis=1, tiled=True),
        )

    def fetch_again(layer_no):
        return (
            lax.all_gather(w_qkv[layer_no], ("wide", "narrow"), axis=0, tiled=True),
            lax.all_gather(w_out[layer_no], ("wide", "narrow"), axis=0, tiled=True),
            lax.all_gather(w_up[layer_no], ("wide", "narrow"), axis=0, tiled=True),
            lax.all_gather(w_down[layer_no], ("wide", "narrow"), axis=0, tiled=True),
            lax.all_gather(gains[layer_no], ("wide", "narrow"), axis=1, tiled=True),
        )

    def reduce_grads(grad_set):
        return (
            lax.psum_scatter(grad_set[0], ("wide", "narrow"), scatter_dimension=0, tiled=True),
            lax.psum_scatter(grad_set[1], ("wide", "narrow"), scatter_dimension=0, tiled=True),
            lax.psum_scatter(grad_set[2], ("wide", "narrow"), scatter_dimension=0, tiled=True),
            lax.psum_scatter(grad_set[3], ("wide", "narrow"), scatter_dimension=0, tiled=True),
            lax.psum_scatter(grad_set[4], ("wide", "narrow"), scatter_dimension=1, tiled=True),
        )

    weights_one = fetch_layer(0)
    kept_one, state_one = layer_forward(inputs, weights_one, length)
    carried = mix_history(alpha_first, history) + alpha_first[hist_count] * kept_one
    weights_two = fetch_layer(1)
    kept_two, state_two = layer_forward(carried, weights_two, length)
    blended = (
        mix_history(alpha_second, history)
        + alpha_second[hist_count] * kept_one
        + alpha_second[hist_count + 1] * kept_two
    )
    seq_length = inputs.shape[0]
    live_mask = (jnp.arange(seq_length) < length).astype(jnp.float32)[:, None]
    grad_blend = cotangent * live_mask / token_total
    back_two = fetch_again(1)
    grad_carried, grads_two = layer_backward(
        alpha_second[hist_count + 1] * grad_blend, back_two, state_two, length
    )
    shard_two = reduce_grads(grads_two)
    grad_first = alpha_first[hist_count] * grad_carried + alpha_second[hist_count] * grad_blend
    back_one = fetch_again(0)
    grad_inputs, grads_one = layer_backward(grad_first, back_one, state_one, length)
    shard_one = reduce_grads(grads_one)
    grad_history = jnp.stack(
        [
            alpha_first[entry] * grad_carried + alpha_second[entry] * grad_blend
            for entry in range(hist_count)
        ]
    )
    first_terms = []
    second_terms = []
    for entry in range(hist_count):
        past_row = history[entry].astype(jnp.float32)
        first_terms.append(jnp.sum(past_row * grad_carried))
        second_terms.append(jnp.sum(past_row * grad_blend))
    first_terms.append(jnp.sum(kept_one * grad_carried))
    second_terms.append(jnp.sum(kept_one * grad_blend))
    second_terms.append(jnp.sum(kept_two * grad_blend))
    grad_alpha_first, grad_alpha_second = lax.psum(
        (jnp.stack(first_terms), jnp.stack(second_terms)), ("wide", "narrow")
    )
    return (
        blended,
        jnp.stack([kept_one, kept_two]),
        grad_inputs,
        grad_history,
        jnp.stack([shard_one[0], shard_two[0]]),
        jnp.stack([shard_one[1], shard_two[1]]),
        jnp.stack([shard_one[2], shard_two[2]]),
        jnp.stack([shard_one[3], shard_two[3]]),
        jnp.stack([shard_one[4], shard_two[4]]),
        grad_alpha_first,
        grad_alpha_second,
    )


GATHER_KINDS = "cacaca"
GATHER_ORDER = (
    0, 100, 10, 200, 130, 121, 40, 21, 50, 210, 140, 122, 150, 22, 131, 300, 41, 51, 221, 132, 240, 250, 123,
    42, 52, 321, 241, 141, 23, 400, 330, 251, 151, 142, 133, 222, 152, 223, 322, 331, 43, 53, 500, 323, 410,
    242, 252, 243, 143, 340, 253, 153, 350, 332, 521, 341, 333, 421, 351, 530, 522, 523, 342, 440, 422, 423,
    352, 450, 531, 441, 451, 532, 343, 540, 353, 550, 533, 442, 443, 453, 541, 452, 542, 551, 543, 552, 553,
)
SCATTER_KINDS = "caccac"
SCATTER_ORDER = (
    0, 100, 10, 200, 130, 121, 40, 21, 50, 210, 140, 122, 150, 22, 131, 41, 51, 221, 132, 240, 42, 250, 52,
    123, 241, 23, 141, 251, 151, 133, 142, 222, 152, 43, 223, 53, 300, 143, 153, 400, 242, 310, 252, 243, 253,
    430, 500, 421, 321, 340, 350, 431, 510, 341, 322, 422, 351, 423, 440, 450, 342, 432, 441, 352, 323, 433,
    451, 521, 540, 550, 522, 343, 541, 523, 353, 551, 442, 443, 452, 453, 542, 543, 552, 553,
)


def steps(codes):
    return [(v // 100, "oplaqd"[v // 10 % 10], v % 10) for v in codes]


def al(v, m): return pl.multiple_of(v, m)
def when(cond, fn): pl.when(cond)(fn)

class Place:
    def __init__(self, depth):
        self.depth = depth
        w = lax.axis_index("wide"); n = lax.axis_index("narrow")
        self.z, self.x = w // 2, lax.rem(w, 2)
        self.y, self.c = n // 2, lax.rem(n, 2)
        first = self.c == 0
        p = jnp.where(first, self.x, self.y)
        q = jnp.where(first, self.y, self.x)
        self.sib = (w, self.y * 2 + 1 - self.c)
        self.xn = (self.z * 2 + 1 - self.x, n)
        self.yn = (w, (1 - self.y) * 2 + self.c)
        self.pn = tuple(jnp.where(first, a, b) for a, b in zip(self.xn, self.yn))
        self.qn = tuple(jnp.where(first, b, a) for a, b in zip(self.xn, self.yn))
        self.has_up = self.z < depth - 1
        self.has_down = self.z > 0
        self.up = (w + 2, n)
        self.down = (w - 2, n)
        ways = jnp.where(first, 2, 1), jnp.where(first, 1, 2)
        self.chip = self.z * 4 + self.x * 2 + self.y
        self.planes = [self.plane(r) for r in range(depth)]
        self.chips = [[[z * 4 + jnp.where(first, 2, 1) * (1 - p if a else p) + jnp.where(first, 1, 2) * (1 - q if b else q)
                        for z in self.planes] for b in (0, 1)] for a in (0, 1)]
        self.onward_up = [(z < self.z) & self.has_up for z in self.planes]
        self.onward_down = [(z > self.z) & self.has_down for z in self.planes]
    def plane(self, r):
        if r == 0: return self.z
        z, last = self.z, self.depth - 1
        short = jnp.minimum(z, last - z)
        low = z * 2 < self.depth
        dist = jnp.where(r <= 2 * short, (r + 1) // 2, r - short)
        below = jnp.where((r <= 2 * short) & (r % 2 == 1), low, ~low)
        return jnp.where(below, z - dist, z + dist)
    def neighbours(self):
        return [self.sib, self.xn, self.yn]

class Gather:
    def __init__(self, me, chunks, ssem, rsem):
        self.me, self.chunks, self.ssem, self.rsem = me, chunks, ssem, rsem
    def copy(self, k, chip, way, target, sem):
        ref = self.chunks[k][1](chip, 1)
        return pltpu.make_async_remote_copy(src_ref=ref, dst_ref=ref, send_sem=self.ssem.at[k, way],
            recv_sem=self.rsem.at[k, sem], device_id=target, device_id_type=MESH)
    def plane_copy(self, k, r):
        ref = self.chunks[k][2](self.me.planes[r])
        return pltpu.make_async_remote_copy(src_ref=ref, dst_ref=ref, send_sem=self.ssem.at[k, 4],
            recv_sem=self.rsem.at[k, 3 * self.me.depth + self.me.planes[r]], device_id=self.me.sib, device_id_type=MESH)
    def p(self, k, chip, r): self.copy(k, chip, 0, self.me.pn, 2 * self.me.depth + self.me.planes[r]).start()
    def q(self, k, chip, r): self.copy(k, chip, 1, self.me.qn, self.me.planes[r]).start()
    def up(self, k, chip, r): self.copy(k, chip, 2, self.me.up, self.me.depth + self.me.planes[r]).start()
    def down(self, k, chip, r): self.copy(k, chip, 3, self.me.down, self.me.depth + self.me.planes[r]).start()
    def wait(self, k, n, sem):
        ref = self.chunks[k][1](0, n)
        pltpu.make_async_remote_copy(src_ref=ref, dst_ref=ref, send_sem=self.ssem.at[k, 0], recv_sem=self.rsem.at[k, sem],
            device_id=self.me.pn, device_id_type=MESH).wait_recv()
    def event(self, k, what, r):
        me, Z = self.me, self.me.depth
        kind = self.chunks[k][0]
        own, flip = me.chips[0][0][r], me.chips[1][0][r]
        if what == "o":
            when(me.has_up, lambda: self.up(k, own, 0))
            when(me.has_down, lambda: self.down(k, own, 0))
            self.p(k, own, 0)
            self.q(k, own, 0)
        elif what == "p":
            self.wait(k, 1, 2 * Z + me.planes[0])
            when(me.has_up, lambda: self.up(k, flip, 0))
            when(me.has_down, lambda: self.down(k, flip, 0))
            self.q(k, flip, 0)
        elif what == "l":
            both = (own, flip) if kind == "c" else (own,)
            self.wait(k, len(both), Z + me.planes[r])
            def fwd(send):
                for chip in both: send(k, chip, r)
            when(me.onward_up[r], lambda: fwd(self.up))
            when(me.onward_down[r], lambda: fwd(self.down))
            if kind == "a": self.p(k, own, r)
            for chip in both: self.q(k, chip, r)
        elif what == "a":
            self.wait(k, 1, 2 * Z + me.planes[r])
            self.q(k, flip, r)
        elif what == "q":
            self.wait(k, 2, me.planes[r])
            self.plane_copy(k, r).start()
        elif what == "d":
            self.plane_copy(k, r).wait_recv()
    def drain(self, k):
        me, Z = self.me, self.me.depth
        per = 2 if self.chunks[k][0] == "c" else 1
        counts = [1 if per == 2 else Z, 2 * Z, jnp.where(me.has_up, per * (me.z + 1), 0), jnp.where(me.has_down, per * (Z - me.z), 0)]
        for way, count in enumerate(counts):
            def one(_, carry):
                self.copy(k, 0, way, me.pn, 0).wait_send()
                return carry
            lax.fori_loop(0, count, one, 0)
        def one(_, carry):
            self.plane_copy(k, 0).wait_send()
            return carry
        lax.fori_loop(0, Z, one, 0)

def greet(me):
    bar = pltpu.get_barrier_semaphore()
    for d in me.neighbours():
        pl.semaphore_signal(bar, inc=1, device_id=d, device_id_type=MESH)
    when(me.has_up, lambda: pl.semaphore_signal(bar, inc=1, device_id=me.up, device_id_type=MESH))
    when(me.has_down, lambda: pl.semaphore_signal(bar, inc=1, device_id=me.down, device_id_type=MESH))
    return bar
def greeted(me, bar):
    pl.semaphore_wait(bar, 3 + me.has_up.astype(jnp.int32) + me.has_down.astype(jnp.int32))

def ag_kernel(depth, order, kinds, qkv_in, out_in, up_in, down_in, extra_in,
              mix_o, up_o, down_o, mix_b, up_b, down_b, mix_s, up_s, mix_t, up_t, ssem, rsem, esem, lsem):
    me = Place(depth)
    bar = greet(me)
    rows = qkv_in.shape[1]
    c = me.c
    wq, wo, wu = qkv_in.shape[2] // 2, out_in.shape[2] // 2, up_in.shape[2] // 2
    wx = extra_in.shape[2]
    mine = lambda w: pl.ds(al(c * w, 128), w)
    other = lambda w: pl.ds(al((1 - c) * w, 128), w)
    my_rows = pl.ds(al(c * rows, 8), rows)
    def stage(k):
        l, j = divmod(k, 3)
        if j == 0:
            for ref, at, pick in ((mix_s, (l, my_rows), mine), (mix_t, (l, slice(None)), other)):
                ref[at[0], at[1], 0:wq] = qkv_in[l, :, pick(wq)].astype(F32)
                ref[at[0], at[1], wq:wq + wo] = out_in[l, :, pick(wo)].astype(F32)
                ref[at[0], at[1], wq + wo:] = extra_in[l]
        elif j == 1:
            up_s[l, my_rows, :] = up_in[l, :, mine(wu)].astype(F32)
            up_t[l] = up_in[l, :, other(wu)].astype(F32)
    def exchange(k):
        l, j = divmod(k, 3)
        if j == 2: return None
        s, t = ((mix_s, mix_t), (up_s, up_t))[j]
        return pltpu.make_async_remote_copy(src_ref=t.at[l], dst_ref=s.at[l, my_rows, :], send_sem=esem.at[0, k],
            recv_sem=esem.at[1, k], device_id=me.sib, device_id_type=MESH)
    def ready(k):
        l, j = divmod(k, 3)
        if j == 2:
            down_b[l, me.chip, c] = down_in[l]
            return
        exchange(k).wait_recv()
        s, b = ((mix_s, mix_b), (up_s, up_b))[j]
        b[l, pl.ds(al(me.chip * 2 * rows, 16), 2 * rows), mine(s.shape[2])] = s[l].astype(BF)
    chunks = []
    for k in range(6):
        l, j = divmod(k, 3)
        if j == 2:
            chunks.append((kinds[k], lambda chip, n, l=l: down_b.at[l, pl.ds(chip, n), c], lambda z, l=l: down_b.at[l, pl.ds(z * 4, 4), c]))
        else:
            b = (mix_b, up_b)[j]
            half = b.shape[2] // 2
            chunks.append((kinds[k],
                lambda chip, n, b=b, l=l, half=half: b.at[l, pl.ds(al(chip * 2 * rows, 16), n * 2 * rows), mine(half)],
                lambda z, b=b, l=l, half=half: b.at[l, pl.ds(al(z * 8 * rows, 16), 8 * rows), mine(half)]))
    gather = Gather(me, chunks, ssem, rsem)
    stage(0)
    greeted(me, bar)
    exchange(0).start()
    for k in (1, 3, 4):
        stage(k)
        exchange(k).start()
    left = [depth] * 6
    pairs = ((mix_b, mix_o), (up_b, up_o), (down_b, down_o))
    def write(k):
        l, j = divmod(k, 3)
        b, o = pairs[j]
        return pltpu.make_async_copy(b.at[l], o.at[l], lsem.at[k])
    for k, what, r in order:
        if what == "o": ready(k)
        gather.event(k, what, r)
        if what == "d":
            left[k] -= 1
            if not left[k]: write(k).start()
    for k in range(6):
        gather.drain(k)
        if k % 3 < 2: exchange(k).wait_send()
    for k in range(6): write(k).wait()

def ag_call(mesh, order, kinds, w_qkv, w_out, w_up, w_down, extra):
    depth = mesh.shape["wide"] // 2
    rows = w_qkv.shape[1]
    D, FF = rows * mesh.size, w_down.shape[1] * mesh.size
    n = mesh.size // 2
    M = 4 * D + 256
    body = functools.partial(ag_kernel, depth, order, kinds)
    vm = pl.BlockSpec(memory_space=pltpu.VMEM); an = pl.BlockSpec(memory_space=pl.ANY)
    shapes = [((2, D, M), BF), ((2, D, FF), BF), ((2, n, 2, FF // n // 2, D), BF)]
    return pl.pallas_call(body,
        out_shape=[jax.ShapeDtypeStruct(s, d) for s, d in shapes],
        in_specs=[vm] * 5, out_specs=[an] * 3,
        scratch_shapes=[pltpu.VMEM(s, d) for s, d in shapes] + [
            pltpu.VMEM((2, 2 * rows, M // 2), F32), pltpu.VMEM((2, 2 * rows, FF // 2), F32),
            pltpu.VMEM((2, rows, M // 2), F32), pltpu.VMEM((2, rows, FF // 2), F32),
            pltpu.SemaphoreType.DMA((6, 5)), pltpu.SemaphoreType.DMA((6, 4 * depth)),
            pltpu.SemaphoreType.DMA((2, 6)), pltpu.SemaphoreType.DMA((6,))],
        compiler_params=pltpu.CompilerParams(collective_id=0, has_side_effects=True, vmem_limit_bytes=56 * 2**20),
    )(w_qkv, w_out, w_up, w_down, extra)

def make_extra(gains, lengths):
    rows = gains.shape[2]
    g = jnp.moveaxis(gains.astype(F32), 1, 2)
    n = jnp.broadcast_to(jnp.where(jnp.arange(rows) == 0, lengths[0].astype(F32), 0.0)[None, :, None], (2, rows, 1))
    return jnp.concatenate([g, n, jnp.zeros((2, rows, 125), F32)], axis=2)


def add_into(dst, sources, rows, out=None):
    @pl.loop(0, rows // 16)
    def _(i):
        at = pl.ds(al(i * 16, 16), 16)
        total = dst[at, :].astype(F32)
        for s in sources: total = total + s[at, :].astype(F32)
        if out is None: dst[at, :] = total.astype(dst.dtype)
        else: out[at, :] = total

class Scatter:
    def __init__(self, me, chunks, ssem, rsem):
        self.me, self.chunks, self.ssem, self.rsem = me, chunks, ssem, rsem
        Z = me.depth
        self.Z = Z
        self.q_slot = lambda flip, z: (Z if flip else 0) + z
        self.line_slot = lambda flip, z: 2 * Z + (Z if flip else 0) + z
        self.late_slot = lambda flip: 4 * Z + (1 if flip else 0)
        self.p_slot = lambda z: 4 * Z + 2 + z
        self.slots = 5 * Z + 2
    def land(self, k, slot): return self.chunks[k]["land"](slot)
    def copy(self, k, chip, way, target, slot):
        ch = self.chunks[k]
        return pltpu.make_async_remote_copy(src_ref=ch["share"](chip), dst_ref=ch["land"](slot), send_sem=self.ssem.at[k, way],
            recv_sem=self.rsem.at[k, slot], device_id=target, device_id_type=MESH)
    def plane_copy(self, k, r):
        ch, me = self.chunks[k], self.me
        z = me.planes[r]
        return pltpu.make_async_remote_copy(src_ref=ch["plane"](z, False), dst_ref=ch["plane_land"](z), send_sem=self.ssem.at[k, 4],
            recv_sem=self.rsem.at[k, self.slots + z], device_id=me.sib, device_id_type=MESH)
    def wait(self, k, slot):
        self.copy(k, 0, 0, self.me.pn, slot).wait_recv()
    def take(self, k, chip, slots, out=None):
        ch = self.chunks[k]
        for s in slots: self.wait(k, s)
        add_into(ch["share"](chip), [ch["land"](s) for s in slots], ch["rows"], out)
    def event(self, k, what, r):
        me, Z = self.me, self.Z
        ch = self.chunks[k]
        kind = ch["kind"]
        own, flip = me.chips[0][0][r], me.chips[1][0][r]
        z = me.planes[r]
        if what == "d":
            self.plane_copy(k, r).start()
        elif what == "q":
            self.plane_copy(k, r).wait_recv()
            ch["plane_add"](z)
            self.copy(k, me.chips[0][1][r], 1, me.qn, self.q_slot(False, z)).start()
            self.copy(k, me.chips[1][1][r], 1, me.qn, self.q_slot(True, z)).start()
        elif what == "a":
            self.take(k, flip, [self.q_slot(True, z)])
            self.copy(k, flip, 0, me.pn, self.p_slot(z)).start()
        elif what == "l":
            first = [self.q_slot(False, z)] + ([self.p_slot(z)] if kind == "a" else [])
            self.take(k, own, first)
            if kind == "c": self.take(k, flip, [self.q_slot(True, z)])
            flips = (False, True) if kind == "c" else (False,)
            def behind():
                for f in flips: self.take(k, flip if f else own, [self.line_slot(f, z)])
            when((z < me.z) & me.has_up, behind)
            when((z > me.z) & me.has_down, behind)
            def send(way, target, late):
                for f in flips:
                    self.copy(k, flip if f else own, way, target, self.late_slot(f) if late else self.line_slot(f, z)).start()
            when((z > me.z) & (z == me.z + 1), lambda: send(2, me.up, False))
            when((z > me.z) & (z != me.z + 1), lambda: send(2, me.up, False))
            when((z < me.z) & (z == me.z - 1), lambda: send(3, me.down, True))
            when((z < me.z) & (z != me.z - 1), lambda: send(3, me.down, False))
        elif what in "po":
            f = what == "p"
            chip = flip if f else own
            slots = [self.q_slot(f, z)]
            if not f: slots.append(self.p_slot(z))
            when(me.has_down, lambda: self.take(k, chip, [self.line_slot(f, z)]))
            when(me.has_up, lambda: self.take(k, chip, [self.late_slot(f)]))
            self.take(k, chip, slots, None if f else ch["result"])
            if f: self.copy(k, chip, 0, me.pn, self.p_slot(z)).start()
    def drain(self, k):
        me, Z = self.me, self.Z
        per = 2 if self.chunks[k]["kind"] == "c" else 1
        counts = [1 if per == 2 else Z, 2 * Z, jnp.where(me.has_up, per * (Z - 1 - me.z), 0), jnp.where(me.has_down, per * me.z, 0)]
        for way, count in enumerate(counts):
            def one(_, carry):
                self.copy(k, 0, way, me.pn, 0).wait_send()
                return carry
            lax.fori_loop(0, count, one, 0)
        def one(_, carry):
            self.plane_copy(k, 0).wait_send()
            return carry
        lax.fori_loop(0, Z, one, 0)

def rs_kernel(depth, order, kinds, mix_in, up_in, down_in, mix_r, up_r, down_r,
              mix_g, up_g, down_g, mix_d, up_d, down_d, mix_l, up_l, down_l, mix_f, up_f, mix_t, up_t,
              ssem, rsem, esem, lsem, credit):
    me = Place(depth)
    c = me.c
    bar = greet(me)
    rows = mix_r.shape[1]
    mine = lambda w: pl.ds(al(c * w, 128), w)
    other = lambda w: pl.ds(al((1 - c) * w, 128), w)
    chunks = {}
    for k in range(6):
        l, j = divmod(k, 3)
        if j == 2:
            R = down_g.shape[2]
            def plane_add(z):
                for i in range(4):
                    add_into(down_g.at[z * 4 + i, c], [down_d.at[z * 4 + i]], R)
            chunks[k] = dict(kind=kinds[k], rows=R, share=lambda chip: down_g.at[chip, c],
                plane=lambda z, own: down_g.at[pl.ds(z * 4, 4), c if own else 1 - c], plane_land=lambda z: down_d.at[pl.ds(z * 4, 4)],
                plane_add=plane_add, land=lambda s, l=l: down_l.at[l, s], result=down_r.at[l])
        else:
            g, d, land, f = ((mix_g, mix_d, mix_l, mix_f), (up_g, up_d, up_l, up_f))[j]
            half = g.shape[1] // 2
            def plane_add(z, g=g, d=d, half=half):
                at = pl.ds(al(z * 8 * rows, 16), 8 * rows)
                add_into(g.at[at, mine(half)], [d.at[at, :]], 8 * rows)
            chunks[k] = dict(kind=kinds[k], rows=2 * rows, share=lambda chip, g=g, half=half: g.at[pl.ds(al(chip * 2 * rows, 16), 2 * rows), mine(half)],
                plane=lambda z, own, g=g, half=half: g.at[pl.ds(al(z * 8 * rows, 16), 8 * rows), mine(half) if own else other(half)],
                plane_land=lambda z, d=d: d.at[pl.ds(al(z * 8 * rows, 16), 8 * rows), :],
                plane_add=plane_add, land=lambda s, land=land, l=l: land.at[l, s], result=f.at[l])
    sc = Scatter(me, chunks, ssem, rsem)
    ins = ((mix_in, mix_g), (up_in, up_g), (down_in, down_g))
    def fill(k):
        l, j = divmod(k, 3)
        cp = pltpu.make_async_copy(ins[j][0].at[l], ins[j][1], lsem.at[j])
        cp.start()
        cp.wait()
    def back(k):
        l, j = divmod(k, 3)
        f, t, r = ((mix_f, mix_t, mix_r), (up_f, up_t, up_r))[j]
        half = f.shape[2]
        return pltpu.make_async_remote_copy(src_ref=f.at[l, pl.ds(al((1 - c) * rows, 8), rows), :], dst_ref=t.at[l],
            send_sem=esem.at[0, k], recv_sem=esem.at[1, k], device_id=me.sib, device_id_type=MESH)
    greeted(me, bar)
    started, planes_left = set(), {k: depth for k in range(6)}
    for k, what, r in order:
        l, j = divmod(k, 3)
        if k not in started:
            started.add(k)
            if l == 0:
                sc.drain(k + 3)
                pl.semaphore_wait(credit.at[j], 1)
            fill(k)
        sc.event(k, what, r)
        if what == "q":
            planes_left[k] -= 1
            if l == 1 and planes_left[k] == 0:
                pl.semaphore_signal(credit.at[j], inc=1, device_id=me.sib, device_id_type=MESH)
        if what == "o" and j < 2:
            back(k).start()
    for k in range(6):
        l, j = divmod(k, 3)
        if j == 2: continue
        f, t, r = ((mix_f, mix_t, mix_r), (up_f, up_t, up_r))[j]
        half = f.shape[2]
        r[l, :, mine(half)] = f[l, pl.ds(al(c * rows, 8), rows), :]
        back(k).wait_recv()
        r[l, :, other(half)] = t[l]
        back(k).wait_send()
    for k in range(3): sc.drain(k)

def rs_call(mesh, order, kinds, mix, up, down):
    depth = mesh.shape["wide"] // 2
    D, M = mix.shape[1:]
    FF = up.shape[2]
    n = mesh.size // 2
    rows, drows = D // mesh.size, FF // mesh.size
    down = down.reshape(2, n, 2, drows, D)
    slots = 5 * depth + 2
    body = functools.partial(rs_kernel, depth, order, kinds)
    vm = pl.BlockSpec(memory_space=pltpu.VMEM); an = pl.BlockSpec(memory_space=pl.ANY)
    V = pltpu.VMEM
    return pl.pallas_call(body,
        out_shape=[jax.ShapeDtypeStruct(s, F32) for s in ((2, rows, M), (2, rows, FF), (2, drows, D))],
        in_specs=[an] * 3, out_specs=[vm] * 3,
        scratch_shapes=[V((D, M), BF), V((D, FF), BF), V((n, 2, drows, D), BF),
            V((D, M // 2), BF), V((D, FF // 2), BF), V((n, drows, D), BF),
            V((2, slots, 2 * rows, M // 2), BF), V((2, slots, 2 * rows, FF // 2), BF), V((2, slots, drows, D), BF),
            V((2, 2 * rows, M // 2), F32), V((2, 2 * rows, FF // 2), F32),
            V((2, rows, M // 2), F32), V((2, rows, FF // 2), F32),
            pltpu.SemaphoreType.DMA((6, 5)), pltpu.SemaphoreType.DMA((6, slots + depth)),
            pltpu.SemaphoreType.DMA((2, 6)), pltpu.SemaphoreType.DMA((3,)), pltpu.SemaphoreType.REGULAR((3,))],
        compiler_params=pltpu.CompilerParams(collective_id=1, has_side_effects=True, vmem_limit_bytes=60 * 2**20),
    )(mix, up, down)


def fast_body(mesh, inputs, history, lengths, cotangent, w_qkv, w_out, w_up, w_down, gains, alpha_first, alpha_second):
    gather_order, scatter_order = steps(GATHER_ORDER), steps(SCATTER_ORDER)[::-1]
    mix, up, down = ag_call(mesh, gather_order, GATHER_KINDS, w_qkv, w_out, w_up, w_down, make_extra(gains, lengths))
    D = inputs.shape[1]
    half = mix.shape[2] // 2
    q, o = 3 * D // 2, D // 2
    length = lengths[0]
    hist_count = history.shape[0]
    token_total = jnp.sum(mix[0, :, q + o + 2].astype(F32))

    def weights(l):
        m = mix[l]
        return (
            jnp.concatenate([m[:, :q], m[:, half:half + q]], axis=1),
            jnp.concatenate([m[:, q:q + o], m[:, half + q:half + q + o]], axis=1),
            up[l],
            down[l].reshape(-1, D),
            m[:, q + o:q + o + 2].T,
        )

    def packed(grads):
        g_qkv, g_out, g_up, g_down, g_gain = grads
        extra = jnp.concatenate([g_gain.T, jnp.zeros((D, 126), F32)], axis=1)
        m = jnp.concatenate([g_qkv[:, :q], g_out[:, :o], extra, g_qkv[:, q:], g_out[:, o:], jnp.zeros((D, 128), F32)], axis=1)
        return m.astype(BF), g_up.astype(BF), g_down.astype(BF)

    first, second = weights(0), weights(1)
    kept_one, state_one = layer_forward(inputs, first, length)
    carried = mix_history(alpha_first, history) + alpha_first[hist_count] * kept_one
    kept_two, state_two = layer_forward(carried, second, length)
    blended = (
        mix_history(alpha_second, history)
        + alpha_second[hist_count] * kept_one
        + alpha_second[hist_count + 1] * kept_two
    )
    seq_length = inputs.shape[0]
    live_mask = (jnp.arange(seq_length) < length).astype(jnp.float32)[:, None]
    grad_blend = cotangent * live_mask / token_total
    grad_carried, grads_two = layer_backward(alpha_second[hist_count + 1] * grad_blend, second, state_two, length)
    grad_first = alpha_first[hist_count] * grad_carried + alpha_second[hist_count] * grad_blend
    grad_inputs, grads_one = layer_backward(grad_first, first, state_one, length)
    mix_g, up_g, down_g = (jnp.stack(v) for v in zip(packed(grads_one), packed(grads_two)))
    mix_r, up_r, down_r = rs_call(mesh, scatter_order, SCATTER_KINDS, mix_g, up_g, down_g)
    grad_history = jnp.stack(
        [alpha_first[entry] * grad_carried + alpha_second[entry] * grad_blend for entry in range(hist_count)]
    )
    past = history.astype(F32)
    first_terms = [jnp.sum(past[e] * grad_carried) for e in range(hist_count)] + [jnp.sum(kept_one * grad_carried)]
    second_terms = [jnp.sum(past[e] * grad_blend) for e in range(hist_count)] + [
        jnp.sum(kept_one * grad_blend), jnp.sum(kept_two * grad_blend)]
    grad_alpha_first, grad_alpha_second = lax.psum((jnp.stack(first_terms), jnp.stack(second_terms)), ("wide", "narrow"))
    return (
        blended,
        jnp.stack([kept_one, kept_two]),
        grad_inputs,
        grad_history,
        jnp.concatenate([mix_r[:, :, :q], mix_r[:, :, half:half + q]], axis=2),
        jnp.concatenate([mix_r[:, :, q:q + o], mix_r[:, :, half + q:half + q + o]], axis=2),
        up_r,
        down_r,
        jnp.moveaxis(mix_r[:, :, q + o:q + o + 2], 2, 1),
        grad_alpha_first,
        grad_alpha_second,
    )


def solution(mesh):
    axes = ("wide", "narrow")
    split, row_split = P(None, axes, None), P(axes, None)
    placed = (row_split, split, P(axes), row_split, split, split, split, split, P(None, None, axes), P(), P())
    results = (row_split, split, row_split, split, split, split, split, split, P(None, None, axes), P(), P())

    def body(*args):
        rows = args[4].shape[1]
        tiled = mesh.shape["narrow"] == 4 and mesh.shape["wide"] == 8 and rows % 8 == 0
        return fast_body(mesh, *args) if tiled else plain_body(*args)

    return jax.shard_map(body, mesh=mesh, in_specs=placed, out_specs=results, check_vma=False)
```

```python
import functools
import math
from types import SimpleNamespace

import jax
import jax.numpy as jnp
import numpy as np
from jax import lax
from jax.experimental import pallas as pl
from jax.experimental.pallas import tpu as pltpu
from jax.sharding import PartitionSpec as P

MESH = pl.DeviceIdType.MESH
BF = jnp.bfloat16
F32 = jnp.float32


HEADS = 12


norm_eps = 1e-05
gelu_coef = 0.044715
gelu_scale = math.sqrt(2.0 / math.pi)
masked_score = -1e30


def product(left, right):
    return jnp.dot(left, right, preferred_element_type=jnp.float32)


def layer_norm(hidden, gain_row):
    center = hidden - jnp.mean(hidden, axis=-1, keepdims=True)
    inverse = lax.rsqrt(jnp.mean(center * center, axis=-1, keepdims=True) + norm_eps)
    standard = center * inverse
    return (standard * gain_row, standard, inverse)


def plain_norm_back(grad_rows, standard, inverse, gain_row):
    scaled = grad_rows * gain_row
    grad_gain = jnp.sum(grad_rows * standard, axis=0)
    grad_in = inverse * (
        scaled
        - jnp.mean(scaled, axis=-1, keepdims=True)
        - standard * jnp.mean(scaled * standard, axis=-1, keepdims=True)
    )
    return (grad_in, grad_gain)


def gelu(values):
    return (
        0.5
        * values
        * (1.0 + jnp.tanh(gelu_scale * (values + gelu_coef * values * values * values)))
    )


def gelu_slope(values):
    tangent = jnp.tanh(gelu_scale * (values + gelu_coef * values * values * values))
    return 0.5 * (1.0 + tangent) + 0.5 * values * (1.0 - tangent * tangent) * gelu_scale * (
        1.0 + 3.0 * gelu_coef * values * values
    )


def rotary_tables(seq_length, head_width):
    half_width = head_width // 2
    frequency = 10000.0 ** (-jnp.arange(half_width, dtype=jnp.float32) / half_width)
    angles = jnp.arange(seq_length, dtype=jnp.float32)[:, None] * frequency[None, :]
    return (jnp.cos(angles)[:, None, :], jnp.sin(angles)[:, None, :])


def rotate(values, cos_table, sin_table):
    half_width = values.shape[-1] // 2
    left_half = values[..., :half_width]
    right_half = values[..., half_width:]
    return jnp.concatenate(
        [
            left_half * cos_table - right_half * sin_table,
            right_half * cos_table + left_half * sin_table,
        ],
        axis=-1,
    )


def rotate_back(grad_rows, cos_table, sin_table):
    half_width = grad_rows.shape[-1] // 2
    left_grad = grad_rows[..., :half_width]
    right_grad = grad_rows[..., half_width:]
    return jnp.concatenate(
        [
            left_grad * cos_table + right_grad * sin_table,
            right_grad * cos_table - left_grad * sin_table,
        ],
        axis=-1,
    )


def allowed_mask(block_rows, key_count, length):
    row_place = jnp.arange(block_rows)
    col_place = jnp.arange(key_count)
    return (col_place[None, :] <= row_place[:, None]) & (col_place[None, :] < length)


def attention_forward(queries, key_rows, value_rows, length):
    seq_length, head_count, head_width = queries.shape
    score_scale = head_width ** (-0.5)
    block_rows = min(512, seq_length)
    scores = (
        jnp.einsum("qhe,khe->hqk", queries, key_rows, preferred_element_type=jnp.float32)
        * score_scale
    )
    allowed = allowed_mask(block_rows, block_rows, length)
    scores = jnp.where(allowed[None], scores, masked_score)
    row_top = jnp.max(scores, axis=-1, keepdims=True)
    exp_scores = jnp.exp(scores - row_top)
    row_total = jnp.sum(exp_scores, axis=-1, keepdims=True)
    prob_rows = (exp_scores / row_total).astype(jnp.bfloat16)
    pieces = jnp.einsum("hqk,khe->qhe", prob_rows, value_rows, preferred_element_type=jnp.float32)
    log_sums = row_top + jnp.log(row_total)
    return (pieces, log_sums)


def attention_backward(queries, key_rows, value_rows, log_sums, grad_attended, length):
    seq_length, head_count, head_width = queries.shape
    score_scale = head_width ** (-0.5)
    grad_keys = jnp.zeros(queries.shape, jnp.float32)
    grad_values = jnp.zeros(queries.shape, jnp.float32)
    block_rows = min(512, seq_length)
    scores = (
        jnp.einsum("qhe,khe->hqk", queries, key_rows, preferred_element_type=jnp.float32)
        * score_scale
    )
    allowed = allowed_mask(block_rows, block_rows, length)
    prob_rows = jnp.where(allowed[None], jnp.exp(scores - log_sums), 0.0)
    grad_prob = jnp.einsum(
        "qhe,khe->hqk", grad_attended, value_rows, preferred_element_type=jnp.float32
    )
    inner_sum = jnp.sum(prob_rows * grad_prob, axis=-1, keepdims=True)
    grad_score = (prob_rows * (grad_prob - inner_sum)).astype(jnp.bfloat16)
    grad_pieces = (
        jnp.einsum("hqk,khe->qhe", grad_score, key_rows, preferred_element_type=jnp.float32)
        * score_scale
    )
    grad_keys = grad_keys.at[:block_rows].add(
        jnp.einsum("hqk,qhe->khe", grad_score, queries, preferred_element_type=jnp.float32)
        * score_scale
    )
    grad_values = grad_values.at[:block_rows].add(
        jnp.einsum(
            "hqk,qhe->khe",
            prob_rows.astype(jnp.bfloat16),
            grad_attended,
            preferred_element_type=jnp.float32,
        )
    )
    return (grad_pieces, grad_keys, grad_values)


def layer_forward(hidden, weights, length):
    layer_qkv, layer_out, layer_up, layer_down, layer_gains = weights
    seq_length = hidden.shape[0]
    head_width = layer_out.shape[0] // HEADS
    normed, unit_one, inverse_one = layer_norm(hidden, layer_gains[0])
    normed = normed.astype(jnp.bfloat16)
    joined = product(normed, layer_qkv).reshape(seq_length, 3, HEADS, head_width)
    cos_table, sin_table = rotary_tables(seq_length, head_width)
    queries = rotate(joined[:, 0], cos_table, sin_table).astype(jnp.bfloat16)
    key_rows = rotate(joined[:, 1], cos_table, sin_table).astype(jnp.bfloat16)
    value_rows = joined[:, 2].astype(jnp.bfloat16)
    attended, log_sums = attention_forward(queries, key_rows, value_rows, length)
    attended = attended.reshape(seq_length, HEADS * head_width).astype(jnp.bfloat16)
    after_attn = hidden + product(attended, layer_out)
    normed_two, unit_two, inverse_two = layer_norm(after_attn, layer_gains[1])
    normed_two = normed_two.astype(jnp.bfloat16)
    up_vals = product(normed_two, layer_up)
    result = after_attn + product(gelu(up_vals).astype(jnp.bfloat16), layer_down)
    kept_state = (
        normed,
        unit_one,
        inverse_one,
        queries,
        key_rows,
        value_rows,
        log_sums,
        attended,
        unit_two,
        inverse_two,
        normed_two,
        up_vals,
    )
    return (result, kept_state)


def layer_backward(grad_rows, weights, kept_state, length):
    layer_qkv, layer_out, layer_up, layer_down, layer_gains = weights
    (
        normed,
        unit_one,
        inverse_one,
        queries,
        key_rows,
        value_rows,
        log_sums,
        attended,
        unit_two,
        inverse_two,
        normed_two,
        up_vals,
    ) = kept_state
    seq_length, head_count, head_width = queries.shape
    grad_low = grad_rows.astype(jnp.bfloat16)
    active = gelu(up_vals).astype(jnp.bfloat16)
    grad_down = jnp.einsum("tf,td->fd", active, grad_low, preferred_element_type=jnp.float32)
    grad_active = jnp.einsum("td,fd->tf", grad_low, layer_down, preferred_element_type=jnp.float32)
    grad_upv = (grad_active * gelu_slope(up_vals)).astype(jnp.bfloat16)
    grad_up = jnp.einsum("td,tf->df", normed_two, grad_upv, preferred_element_type=jnp.float32)
    grad_norm_two = jnp.einsum("tf,df->td", grad_upv, layer_up, preferred_element_type=jnp.float32)
    grad_after, gain_two = plain_norm_back(grad_norm_two, unit_two, inverse_two, layer_gains[1])
    grad_after = grad_rows + grad_after
    grad_branch = grad_after.astype(jnp.bfloat16)
    grad_wout = jnp.einsum("ta,td->ad", attended, grad_branch, preferred_element_type=jnp.float32)
    grad_attended = jnp.einsum(
        "td,ad->ta", grad_branch, layer_out, preferred_element_type=jnp.float32
    )
    grad_attended = grad_attended.astype(jnp.bfloat16).reshape(seq_length, head_count, head_width)
    grad_query, grad_keys, grad_values = attention_backward(
        queries, key_rows, value_rows, log_sums, grad_attended, length
    )
    cos_table, sin_table = rotary_tables(seq_length, head_width)
    grad_joined = jnp.stack(
        [
            rotate_back(grad_query, cos_table, sin_table),
            rotate_back(grad_keys, cos_table, sin_table),
            grad_values,
        ],
        axis=1,
    )
    grad_joined = grad_joined.reshape(seq_length, 3 * head_count * head_width).astype(jnp.bfloat16)
    grad_qkv = jnp.einsum("td,tj->dj", normed, grad_joined, preferred_element_type=jnp.float32)
    grad_norm_one = jnp.einsum(
        "tj,dj->td", grad_joined, layer_qkv, preferred_element_type=jnp.float32
    )
    grad_in, gain_one = plain_norm_back(grad_norm_one, unit_one, inverse_one, layer_gains[0])
    return (
        grad_after + grad_in,
        (grad_qkv, grad_wout, grad_up, grad_down, jnp.stack([gain_one, gain_two])),
    )


def mix_history(alphas, history):
    blended = alphas[0] * history[0].astype(jnp.float32)
    for entry in range(1, history.shape[0]):
        blended = blended + alphas[entry] * history[entry].astype(jnp.float32)
    return blended


def plain_body(
    inputs,
    history,
    lengths,
    cotangent,
    w_qkv,
    w_out,
    w_up,
    w_down,
    gains,
    alpha_first,
    alpha_second,
):
    token_total = lax.psum(jnp.sum(lengths.astype(jnp.float32)), ("wide", "narrow"))
    length = lengths[0]
    hist_count = history.shape[0]

    def fetch_layer(layer_no):
        return (
            lax.all_gather(w_qkv[layer_no], ("wide", "narrow"), axis=0, tiled=True),
            lax.all_gather(w_out[layer_no], ("wide", "narrow"), axis=0, tiled=True),
            lax.all_gather(w_up[layer_no], ("wide", "narrow"), axis=0, tiled=True),
            lax.all_gather(w_down[layer_no], ("wide", "narrow"), axis=0, tiled=True),
            lax.all_gather(gains[layer_no], ("wide", "narrow"), axis=1, tiled=True),
        )

    def fetch_again(layer_no):
        return (
            lax.all_gather(w_qkv[layer_no], ("wide", "narrow"), axis=0, tiled=True),
            lax.all_gather(w_out[layer_no], ("wide", "narrow"), axis=0, tiled=True),
            lax.all_gather(w_up[layer_no], ("wide", "narrow"), axis=0, tiled=True),
            lax.all_gather(w_down[layer_no], ("wide", "narrow"), axis=0, tiled=True),
            lax.all_gather(gains[layer_no], ("wide", "narrow"), axis=1, tiled=True),
        )

    def reduce_grads(grad_set):
        return (
            lax.psum_scatter(grad_set[0], ("wide", "narrow"), scatter_dimension=0, tiled=True),
            lax.psum_scatter(grad_set[1], ("wide", "narrow"), scatter_dimension=0, tiled=True),
            lax.psum_scatter(grad_set[2], ("wide", "narrow"), scatter_dimension=0, tiled=True),
            lax.psum_scatter(grad_set[3], ("wide", "narrow"), scatter_dimension=0, tiled=True),
            lax.psum_scatter(grad_set[4], ("wide", "narrow"), scatter_dimension=1, tiled=True),
        )

    weights_one = fetch_layer(0)
    kept_one, state_one = layer_forward(inputs, weights_one, length)
    carried = mix_history(alpha_first, history) + alpha_first[hist_count] * kept_one
    weights_two = fetch_layer(1)
    kept_two, state_two = layer_forward(carried, weights_two, length)
    blended = (
        mix_history(alpha_second, history)
        + alpha_second[hist_count] * kept_one
        + alpha_second[hist_count + 1] * kept_two
    )
    seq_length = inputs.shape[0]
    live_mask = (jnp.arange(seq_length) < length).astype(jnp.float32)[:, None]
    grad_blend = cotangent * live_mask / token_total
    back_two = fetch_again(1)
    grad_carried, grads_two = layer_backward(
        alpha_second[hist_count + 1] * grad_blend, back_two, state_two, length
    )
    shard_two = reduce_grads(grads_two)
    grad_first = alpha_first[hist_count] * grad_carried + alpha_second[hist_count] * grad_blend
    back_one = fetch_again(0)
    grad_inputs, grads_one = layer_backward(grad_first, back_one, state_one, length)
    shard_one = reduce_grads(grads_one)
    grad_history = jnp.stack(
        [
            alpha_first[entry] * grad_carried + alpha_second[entry] * grad_blend
            for entry in range(hist_count)
        ]
    )
    first_terms = []
    second_terms = []
    for entry in range(hist_count):
        past_row = history[entry].astype(jnp.float32)
        first_terms.append(jnp.sum(past_row * grad_carried))
        second_terms.append(jnp.sum(past_row * grad_blend))
    first_terms.append(jnp.sum(kept_one * grad_carried))
    second_terms.append(jnp.sum(kept_one * grad_blend))
    second_terms.append(jnp.sum(kept_two * grad_blend))
    grad_alpha_first, grad_alpha_second = lax.psum(
        (jnp.stack(first_terms), jnp.stack(second_terms)), ("wide", "narrow")
    )
    return (
        blended,
        jnp.stack([kept_one, kept_two]),
        grad_inputs,
        grad_history,
        jnp.stack([shard_one[0], shard_two[0]]),
        jnp.stack([shard_one[1], shard_two[1]]),
        jnp.stack([shard_one[2], shard_two[2]]),
        jnp.stack([shard_one[3], shard_two[3]]),
        jnp.stack([shard_one[4], shard_two[4]]),
        grad_alpha_first,
        grad_alpha_second,
    )


GATHER_KINDS = "caccac"
GATHER_ORDER = (
    0, 10, 100, 40, 21, 50, 130, 121, 41, 22, 200, 51, 140, 122, 131, 150, 42, 52, 210, 300, 23, 132, 123,
    141, 151, 43, 400, 53, 142, 221, 133, 310, 152, 240, 250, 500, 222, 223, 241, 251, 143, 421, 153, 430,
    321, 340, 242, 243, 253, 422, 350, 252, 431, 341, 423, 510, 322, 323, 351, 432, 440, 450, 433, 342, 343,
    353, 441, 521, 352, 451, 540, 442, 550, 452, 522, 523, 443, 541, 453, 551, 542, 543, 553, 552,
)
SCATTER_KINDS = "caccac"
SCATTER_ORDER = (
    0, 100, 10, 200, 130, 121, 40, 21, 50, 210, 140, 122, 150, 22, 131, 41, 51, 221, 132, 240, 42, 250, 52,
    123, 241, 23, 141, 251, 151, 133, 142, 222, 152, 43, 223, 53, 300, 143, 153, 400, 242, 310, 252, 243, 253,
    430, 500, 421, 321, 340, 350, 431, 510, 341, 322, 422, 351, 423, 440, 450, 342, 432, 441, 352, 323, 433,
    451, 521, 540, 550, 522, 343, 541, 523, 353, 551, 442, 443, 452, 453, 542, 543, 552, 553,
)


def steps(codes):
    return [(v // 100, "oplaqd"[v // 10 % 10], v % 10) for v in codes]


def al(v, m): return pl.multiple_of(v, m)
def when(cond, fn): pl.when(cond)(fn)

class Place:
    def __init__(self, depth):
        self.depth = depth
        w = lax.axis_index("wide"); n = lax.axis_index("narrow")
        self.z, self.x = w // 2, lax.rem(w, 2)
        self.y, self.c = n // 2, lax.rem(n, 2)
        first = self.c == 0
        p = jnp.where(first, self.x, self.y)
        q = jnp.where(first, self.y, self.x)
        self.sib = (w, self.y * 2 + 1 - self.c)
        self.xn = (self.z * 2 + 1 - self.x, n)
        self.yn = (w, (1 - self.y) * 2 + self.c)
        self.pn = tuple(jnp.where(first, a, b) for a, b in zip(self.xn, self.yn))
        self.qn = tuple(jnp.where(first, b, a) for a, b in zip(self.xn, self.yn))
        self.has_up = self.z < depth - 1
        self.has_down = self.z > 0
        self.up = (w + 2, n)
        self.down = (w - 2, n)
        self.line = [(lax.rem(w + 2 * i, 2 * depth), n) for i in range(1, depth)]
        self.chip = self.z * 4 + self.x * 2 + self.y
        self.planes = [self.plane(r) for r in range(depth)]
        self.chips = [[[z * 4 + jnp.where(first, 2, 1) * (1 - p if a else p) + jnp.where(first, 1, 2) * (1 - q if b else q)
                        for z in self.planes] for b in (0, 1)] for a in (0, 1)]
        self.onward_up = [(z < self.z) & self.has_up for z in self.planes]
        self.onward_down = [(z > self.z) & self.has_down for z in self.planes]
    def plane(self, r):
        if r == 0: return self.z
        z, last = self.z, self.depth - 1
        short = jnp.minimum(z, last - z)
        low = z * 2 < self.depth
        dist = jnp.where(r <= 2 * short, (r + 1) // 2, r - short)
        below = jnp.where((r <= 2 * short) & (r % 2 == 1), low, ~low)
        return jnp.where(below, z - dist, z + dist)

class Gather:
    def __init__(self, me, chunks, ssem, rsem):
        self.me, self.chunks, self.ssem, self.rsem = me, chunks, ssem, rsem
    def copy(self, k, chip, way, target, sem):
        ref = self.chunks[k][1](chip, 1)
        return pltpu.make_async_remote_copy(src_ref=ref, dst_ref=ref, send_sem=self.ssem.at[k, way],
            recv_sem=self.rsem.at[k, sem], device_id=target, device_id_type=MESH)
    def plane_copy(self, k, r):
        ref = self.chunks[k][2](self.me.planes[r])
        return pltpu.make_async_remote_copy(src_ref=ref, dst_ref=ref, send_sem=self.ssem.at[k, 4],
            recv_sem=self.rsem.at[k, 3 * self.me.depth + self.me.planes[r]], device_id=self.me.sib, device_id_type=MESH)
    def p(self, k, chip, r): self.copy(k, chip, 0, self.me.pn, 2 * self.me.depth + self.me.planes[r]).start()
    def q(self, k, chip, r): self.copy(k, chip, 1, self.me.qn, self.me.planes[r]).start()
    def up(self, k, chip, r): self.copy(k, chip, 2, self.me.up, self.me.depth + self.me.planes[r]).start()
    def down(self, k, chip, r): self.copy(k, chip, 3, self.me.down, self.me.depth + self.me.planes[r]).start()
    def wait(self, k, n, sem):
        ref = self.chunks[k][1](0, n)
        pltpu.make_async_remote_copy(src_ref=ref, dst_ref=ref, send_sem=self.ssem.at[k, 0], recv_sem=self.rsem.at[k, sem],
            device_id=self.me.pn, device_id_type=MESH).wait_recv()
    def event(self, k, what, r):
        me, Z = self.me, self.me.depth
        kind = self.chunks[k][0]
        own, flip = me.chips[0][0][r], me.chips[1][0][r]
        if what == "o":
            when(me.has_up, lambda: self.up(k, own, 0))
            when(me.has_down, lambda: self.down(k, own, 0))
            self.p(k, own, 0)
            self.q(k, own, 0)
        elif what == "p":
            self.wait(k, 1, 2 * Z + me.planes[0])
            when(me.has_up, lambda: self.up(k, flip, 0))
            when(me.has_down, lambda: self.down(k, flip, 0))
            self.q(k, flip, 0)
        elif what == "l":
            both = (own, flip) if kind == "c" else (own,)
            self.wait(k, len(both), Z + me.planes[r])
            def fwd(send):
                for chip in both: send(k, chip, r)
            when(me.onward_up[r], lambda: fwd(self.up))
            when(me.onward_down[r], lambda: fwd(self.down))
            if kind == "a": self.p(k, own, r)
            for chip in both: self.q(k, chip, r)
        elif what == "a":
            self.wait(k, 1, 2 * Z + me.planes[r])
            self.q(k, flip, r)
        elif what == "q":
            self.wait(k, 2, me.planes[r])
            self.plane_copy(k, r).start()
        elif what == "d":
            self.plane_copy(k, r).wait_recv()
    def drain(self, k):
        me, Z = self.me, self.me.depth
        per = 2 if self.chunks[k][0] == "c" else 1
        counts = [1 if per == 2 else Z, 2 * Z, jnp.where(me.has_up, per * (me.z + 1), 0), jnp.where(me.has_down, per * (Z - me.z), 0)]
        for way, count in enumerate(counts):
            def one(_, carry):
                self.copy(k, 0, way, me.pn, 0).wait_send()
                return carry
            lax.fori_loop(0, count, one, 0)
        def one(_, carry):
            self.plane_copy(k, 0).wait_send()
            return carry
        lax.fori_loop(0, Z, one, 0)

def greet(me, whole_line=False):
    bar = pltpu.get_barrier_semaphore()
    def signal(d): pl.semaphore_signal(bar, inc=1, device_id=d, device_id_type=MESH)
    for d in (me.sib, me.xn, me.yn): signal(d)
    if whole_line:
        for d in me.line: signal(d)
    else:
        when(me.has_up, lambda: signal(me.up))
        when(me.has_down, lambda: signal(me.down))
    return bar


def greeted(me, bar, whole_line=False):
    line = len(me.line) if whole_line else me.has_up.astype(jnp.int32) + me.has_down.astype(jnp.int32)
    pl.semaphore_wait(bar, 3 + line)


def add_into(dst, sources, rows, out=None):
    step = 48 if rows % 48 == 0 else 16
    @pl.loop(0, rows // step)
    def _(i):
        at = pl.ds(al(i * step, 16), step)
        if out is None and len(sources) == 1:
            dst[at, :] = dst[at, :] + sources[0][at, :]
            return
        total = dst[at, :].astype(F32)
        for s in sources: total = total + s[at, :].astype(F32)
        if out is None: dst[at, :] = total.astype(dst.dtype)
        else: out[at, :] = total


class Scatter:
    def __init__(self, me, chunks, ssem, rsem):
        self.me, self.chunks, self.ssem, self.rsem = me, chunks, ssem, rsem
        Z = me.depth
        self.Z = Z
        self.q_slot = lambda flip, z: (Z if flip else 0) + z
        self.line_slot = lambda flip, z: 2 * Z + (Z if flip else 0) + z
        self.late_slot = lambda flip: 4 * Z + (1 if flip else 0)
        self.p_slot = lambda z: 4 * Z + 2 + z
        self.slots = 5 * Z + 2
    def land(self, k, slot): return self.chunks[k].land(slot)
    def copy(self, k, chip, way, target, slot):
        ch = self.chunks[k]
        return pltpu.make_async_remote_copy(src_ref=ch.share(chip), dst_ref=ch.land(slot), send_sem=self.ssem.at[k, way],
            recv_sem=self.rsem.at[k, slot], device_id=target, device_id_type=MESH)
    def plane_copy(self, k, r):
        ch, me = self.chunks[k], self.me
        z = me.planes[r]
        return pltpu.make_async_remote_copy(src_ref=ch.plane(z, False), dst_ref=ch.plane_land(z), send_sem=self.ssem.at[k, 4],
            recv_sem=self.rsem.at[k, self.slots + z], device_id=me.sib, device_id_type=MESH)
    def wait(self, k, slot):
        self.copy(k, 0, 0, self.me.pn, slot).wait_recv()
    def take(self, k, chip, slots, out=None):
        ch = self.chunks[k]
        for s in slots: self.wait(k, s)
        add_into(ch.share(chip), [ch.land(s) for s in slots], ch.rows, out)
    def event(self, k, what, r):
        me, Z = self.me, self.Z
        ch = self.chunks[k]
        kind = ch.kind
        own, flip = me.chips[0][0][r], me.chips[1][0][r]
        z = me.planes[r]
        if what == "d":
            self.plane_copy(k, r).start()
        elif what == "q":
            self.plane_copy(k, r).wait_recv()
            ch.plane_add(z)
            self.copy(k, me.chips[0][1][r], 1, me.qn, self.q_slot(False, z)).start()
            self.copy(k, me.chips[1][1][r], 1, me.qn, self.q_slot(True, z)).start()
        elif what == "a":
            self.take(k, flip, [self.q_slot(True, z)])
            self.copy(k, flip, 0, me.pn, self.p_slot(z)).start()
        elif what == "l":
            first = [self.q_slot(False, z)] + ([self.p_slot(z)] if kind == "a" else [])
            self.take(k, own, first)
            if kind == "c": self.take(k, flip, [self.q_slot(True, z)])
            flips = (False, True) if kind == "c" else (False,)
            def behind():
                for f in flips: self.take(k, flip if f else own, [self.line_slot(f, z)])
            when((z < me.z) & me.has_up, behind)
            when((z > me.z) & me.has_down, behind)
            def send(way, target, late):
                for f in flips:
                    self.copy(k, flip if f else own, way, target, self.late_slot(f) if late else self.line_slot(f, z)).start()
            when((z > me.z) & (z == me.z + 1), lambda: send(2, me.up, False))
            when((z > me.z) & (z != me.z + 1), lambda: send(2, me.up, False))
            when((z < me.z) & (z == me.z - 1), lambda: send(3, me.down, True))
            when((z < me.z) & (z != me.z - 1), lambda: send(3, me.down, False))
        elif what in "po":
            f = what == "p"
            chip = flip if f else own
            slots = [self.q_slot(f, z)]
            if not f: slots.append(self.p_slot(z))
            when(me.has_down, lambda: self.take(k, chip, [self.line_slot(f, z)]))
            when(me.has_up, lambda: self.take(k, chip, [self.late_slot(f)]))
            self.take(k, chip, slots, None if f else ch.result)
            if f: self.copy(k, chip, 0, me.pn, self.p_slot(z)).start()
    def drain(self, k):
        me, Z = self.me, self.Z
        per = 2 if self.chunks[k].kind == "c" else 1
        counts = [1 if per == 2 else Z, 2 * Z, jnp.where(me.has_up, per * (Z - 1 - me.z), 0), jnp.where(me.has_down, per * me.z, 0)]
        for way, count in enumerate(counts):
            def one(_, carry):
                self.copy(k, 0, way, me.pn, 0).wait_send()
                return carry
            lax.fori_loop(0, count, one, 0)
        def one(_, carry):
            self.plane_copy(k, 0).wait_send()
            return carry
        lax.fori_loop(0, Z, one, 0)


def dot(a, b):
    return jnp.dot(a, b, preferred_element_type=F32)


def dot_nt(a, b):
    return lax.dot_general(a, b, (((1,), (1,)), ((), ())), preferred_element_type=F32)


def dot_tn(a, b):
    return lax.dot_general(a, b, (((0,), (0,)), ((), ())), preferred_element_type=F32)


def normalized(h):
    center = h - jnp.mean(h, axis=-1, keepdims=True)
    inverse = lax.rsqrt(jnp.mean(center * center, axis=-1, keepdims=True) + norm_eps)
    return center * inverse, inverse


def swap_halves(v, half):
    lanes = lax.broadcasted_iota(jnp.int32, v.shape, 1)
    width = v.shape[1]
    return jnp.where(lanes % (2 * half) < half, pltpu.roll(v, width - half, 1), pltpu.roll(v, half, 1))


def rotary_lanes(seq_length, head_width, lanes):
    half = head_width // 2
    frequency = (10000.0 ** (-np.arange(half, dtype=np.float32) / half)).astype(np.float32)
    angles = np.arange(seq_length, dtype=np.float32)[:, None] * frequency[None, :]
    cos, sin = np.cos(angles), np.sin(angles)
    both = np.stack([np.concatenate([cos, cos], 1), np.concatenate([-sin, sin], 1)])
    return np.tile(both, (1, 1, lanes // head_width)).astype(np.float32)


def add_sum(ref, row, lane, product):
    rows = lax.broadcasted_iota(jnp.int32, ref.shape, 0)
    lanes = lax.broadcasted_iota(jnp.int32, ref.shape, 1)
    total = jnp.sum(jnp.sum(product, axis=0, keepdims=True), axis=1, keepdims=True)
    ref[...] = ref[...] + jnp.where((rows == row) & (lanes == lane), total, 0.0)


class Forward:
    def __init__(self, w, io, s, length, first, second):
        self.w, self.io, self.s = w, io, s
        self.length, self.first, self.second = length, first, second
        self.T, self.D = io.h.shape
        self.width = self.D // HEADS
        self.q, self.o = 3 * self.D // 2, self.D // 2
        self.half = w.mix.shape[2] // 2
        self.writes = []

    def send(self, name, l=None):
        src, dst = getattr(self.s, name), getattr(self.io, name)
        if l is not None: src, dst = src.at[l], dst.at[l]
        n = len(self.writes)
        self.writes.append((src, dst, n))
        pltpu.make_async_copy(src, dst, self.io.wsem.at[n]).start()

    def finish(self):
        for src, dst, n in self.writes:
            pltpu.make_async_copy(src, dst, self.io.wsem.at[n]).wait()

    def setup(self):
        s, T = self.s, self.T
        row = lax.broadcasted_iota(jnp.int32, (T, T), 0)
        col = lax.broadcasted_iota(jnp.int32, (T, T), 1)
        s.bias[...] = jnp.where((col <= row) & (col < self.length), 0.0, masked_score)
        s.sums[...] = jnp.zeros_like(s.sums)

    def loss_grad(self):
        s, io = self.s, self.io
        count = jnp.sum(s.gain[0, 2:3, :])
        row = lax.broadcasted_iota(jnp.int32, (self.T, 1), 0)
        grad = jnp.where(row < self.length, io.cotangent[...], 0.0) / count
        s.gout[...] = grad
        self.send("gout")
        n = io.history.shape[0]
        for j in range(n): add_sum(s.sums, 1, j, io.history[j].astype(F32) * grad)

    def layer_in(self, l):
        return self.io.h if l == 0 else self.s.carried

    def norm_one(self, l):
        s, w = self.s, self.w
        g = w.mix[l, :, self.q + self.o:self.half].astype(F32)
        s.gain[l] = g.T[0:8, :]
        x, _ = normalized(self.layer_in(l)[...])
        s.n1[l] = (x * s.gain[l, 0:1, :]).astype(BF)
        self.send("n1", l)

    def project(self, l, t):
        s, w = self.s, self.w
        h, i = divmod(t, 3)
        W = self.q // 3
        at = h * self.half + i * W
        joined = dot(s.n1[l], w.mix[l, :, at:at + W])
        for j in range(W // 128):
            col = t * W + j * 128
            part = joined[:, j * 128:(j + 1) * 128]
            if col < 2 * self.D:
                part = part * s.cos[...] + swap_halves(part, self.width // 2) * s.sin[...]
                if col < self.D: part = part * self.width ** -0.5
            s.qkv[l, :, col:col + 128] = part.astype(BF)

    def attend(self, l, a):
        s, D = self.s, self.D
        q, k, v = (s.qkv[l, :, i * D + a * 128:i * D + a * 128 + 128] for i in range(3))
        lanes = lax.broadcasted_iota(jnp.int32, q.shape, 1)
        outs = []
        for e in range(2):
            mine = (lanes < self.width) if e == 0 else (lanes >= self.width)
            scores = dot_nt(jnp.where(mine, q, jnp.zeros_like(q)), k) + s.bias[...]
            top = jnp.max(scores, axis=-1, keepdims=True)
            weights = jnp.exp(scores - top)
            probs = (weights * (1.0 / jnp.sum(weights, axis=-1, keepdims=True))).astype(BF)
            s.probs[l, 2 * a + e] = probs
            outs.append(dot(probs, v))
        s.att[l, :, a * 128:a * 128 + 128] = jnp.where(lanes < self.width, outs[0], outs[1]).astype(BF)

    def attend_done(self, l):
        for name in ("qkv", "probs", "att"): self.send(name, l)

    def out(self, l, h):
        s, w = self.s, self.w
        cols = slice(h * self.o, (h + 1) * self.o)
        at = h * self.half + self.q
        s.after[l, :, cols] = self.layer_in(l)[:, cols] + dot(s.att[l], w.mix[l, :, at:at + self.o])

    def norm_two(self, l):
        s = self.s
        x, _ = normalized(s.after[l])
        s.n2[l] = (x * s.gain[l, 1:2, :]).astype(BF)
        self.send("n2", l)
        self.send("after", l)

    def raise_(self, l, t, W):
        s, w = self.s, self.w
        u = dot(s.n2[l], w.up[l, :, t * W:(t + 1) * W])
        tile, at = divmod(t * W, self.D)
        cols = slice(at, at + W)
        square = u * u
        tangent = jnp.tanh(gelu_scale * u * (1.0 + gelu_coef * square))
        s.act[l, tile, :, cols] = (0.5 * u * (1.0 + tangent)).astype(BF)
        s.slope[l, tile, :, cols] = (
            0.5 * (1.0 + tangent) + 0.5 * u * (1.0 - tangent * tangent) * gelu_scale * (1.0 + 3.0 * gelu_coef * square)
        ).astype(BF)

    def raise_done(self, l):
        for name in ("act", "slope"): self.send(name, l)

    def lower(self, l, t, W):
        s, w = self.s, self.w
        cols = slice(t * W, (t + 1) * W)
        total = s.after[l, :, cols]
        tiles = s.act.shape[1]
        chips = w.down.shape[1] // tiles
        for i in range(tiles):
            total = total + dot(s.act[l, i], w.down[l, i * chips:(i + 1) * chips, :, :, cols].reshape(-1, W))
        s.stored[l, :, cols] = total

    def mixed(self, l):
        s, io = self.s, self.io
        n = io.history.shape[0]
        if l == 0:
            s.carried[...] = mix_history([self.first[j] for j in range(n)], io.history) + self.first[n] * s.stored[0]
            self.send("carried")
        else:
            s.blended[...] = (
                mix_history([self.second[j] for j in range(n)], io.history)
                + self.second[n] * s.stored[0] + self.second[n + 1] * s.stored[1]
            )
            self.send("blended")
        self.send("stored", l)
        add_sum(s.sums, 1, n + l, s.stored[l] * s.gout[...])
        if l == 1: self.send("sums")

    def steps(self):
        out = [(-1, self.setup)]
        P = functools.partial
        for l in range(2):
            k = 3 * l
            out.append((k, P(self.norm_one, l)))
            out += [(k, P(self.project, l, t)) for t in range(6)]
            if l == 0: out.append((k, self.loss_grad))
            out += [(k, P(self.attend, l, a)) for a in range(self.D // 128)]
            out.append((k, P(self.attend_done, l)))
            out += [(k, P(self.out, l, h)) for h in range(2)]
            out.append((k, P(self.norm_two, l)))
            W = self.D // 2
            out += [(k + 1, P(self.raise_, l, t, W)) for t in range(4 * self.D // W)]
            out.append((k + 1, P(self.raise_done, l)))
            out += [(k + 2, P(self.lower, l, t, self.D // 3)) for t in range(3)]
            out.append((k + 2, P(self.mixed, l)))
        return out


def weave(order, work, per_event):
    left = {}
    for k, what, _ in order:
        if what == "d": left[k] = left.get(k, 0) + 1
    whole, done, queue = set([-1]), [], list(work)
    for k, what, r in order:
        done.append((k, what, r))
        if what == "d":
            left[k] -= 1
            if not left[k]: whole.add(k)
        for _ in range(per_event):
            if queue and all(j in whole for j in range(queue[0][0] + 1)):
                done.append(queue.pop(0)[1])
    return done + [act for _, act in queue]


def saved_shapes(T, D, FF):
    return dict(n1=((2, T, D), BF), qkv=((2, T, 3 * D), BF), probs=((2, HEADS, T, T), BF), att=((2, T, D), BF), after=((2, T, D), F32),
        n2=((2, T, D), BF), act=((2, FF // D, T, D), BF), slope=((2, FF // D, T, D), BF), stored=((2, T, D), F32), carried=((T, D), F32),
        blended=((T, D), F32), gout=((T, D), F32), sums=((8, 128), F32))


SAVED = tuple(saved_shapes(1, 1, 1))


def fwd_kernel(depth, order, kinds, qkv_in, out_in, up_in, down_in, extra_in, h_in, history_in, cotangent_in, rope_in, length, first, second,
              mix_o, up_o, down_o, *rest):
    n = len(SAVED)
    saved_o, rest = rest[:n], rest[n:]
    (mix_b, up_b, down_b, mix_s, up_s, mix_t, up_t, ssem, rsem, esem, lsem, wsem, bias, gain), saved_b = rest[:14], rest[14:]
    me = Place(depth)
    bar = greet(me)
    rows = qkv_in.shape[1]
    c = me.c
    wq, wo, wu = qkv_in.shape[2] // 2, out_in.shape[2] // 2, up_in.shape[2] // 2
    wx = extra_in.shape[2]
    mine = lambda w: pl.ds(al(c * w, 128), w)
    other = lambda w: pl.ds(al((1 - c) * w, 128), w)
    my_rows = pl.ds(al(c * rows, 8), rows)
    def stage(k):
        l, j = divmod(k, 3)
        if j == 0:
            for ref, at, pick in ((mix_s, (l, my_rows), mine), (mix_t, (l, slice(None)), other)):
                ref[at[0], at[1], 0:wq] = qkv_in[l, :, pick(wq)].astype(F32)
                ref[at[0], at[1], wq:wq + wo] = out_in[l, :, pick(wo)].astype(F32)
                ref[at[0], at[1], wq + wo:] = extra_in[l]
        elif j == 1:
            up_s[l, my_rows, :] = up_in[l, :, mine(wu)].astype(F32)
            up_t[l] = up_in[l, :, other(wu)].astype(F32)
    def exchange(k):
        l, j = divmod(k, 3)
        if j == 2: return None
        s, t = ((mix_s, mix_t), (up_s, up_t))[j]
        return pltpu.make_async_remote_copy(src_ref=t.at[l], dst_ref=s.at[l, my_rows, :], send_sem=esem.at[0, k],
            recv_sem=esem.at[1, k], device_id=me.sib, device_id_type=MESH)
    def ready(k):
        l, j = divmod(k, 3)
        if j == 2:
            down_b[l, me.chip, c] = down_in[l]
            return
        exchange(k).wait_recv()
        s, b = ((mix_s, mix_b), (up_s, up_b))[j]
        b[l, pl.ds(al(me.chip * 2 * rows, 16), 2 * rows), mine(s.shape[2])] = s[l].astype(BF)
    chunks = []
    for k in range(6):
        l, j = divmod(k, 3)
        if j == 2:
            chunks.append((kinds[k], lambda chip, n, l=l: down_b.at[l, pl.ds(chip, n), c], lambda z, l=l: down_b.at[l, pl.ds(z * 4, 4), c]))
        else:
            b = (mix_b, up_b)[j]
            half = b.shape[2] // 2
            chunks.append((kinds[k],
                lambda chip, n, b=b, l=l, half=half: b.at[l, pl.ds(al(chip * 2 * rows, 16), n * 2 * rows), mine(half)],
                lambda z, b=b, l=l, half=half: b.at[l, pl.ds(al(z * 8 * rows, 16), 8 * rows), mine(half)]))
    gather = Gather(me, chunks, ssem, rsem)
    stage(0)
    greeted(me, bar)
    exchange(0).start()
    for k in (1, 3, 4):
        stage(k)
        exchange(k).start()
    left = [depth] * 6
    pairs = ((mix_b, mix_o), (up_b, up_o), (down_b, down_o))
    def write(k):
        l, j = divmod(k, 3)
        b, o = pairs[j]
        return pltpu.make_async_copy(b.at[l], o.at[l], lsem.at[k])
    io = SimpleNamespace(**dict(zip(SAVED, saved_o)), h=h_in, history=history_in, cotangent=cotangent_in, wsem=wsem)
    scratch = SimpleNamespace(**dict(zip(SAVED, saved_b)), bias=bias, gain=gain, cos=rope_in.at[0], sin=rope_in.at[1])
    fwd = Forward(SimpleNamespace(mix=mix_b, up=up_b, down=down_b), io, scratch, length[0], first, second)
    for item in weave(order, fwd.steps(), 1):
        if not isinstance(item, tuple):
            item()
            continue
        k, what, r = item
        if what == "o": ready(k)
        gather.event(k, what, r)
        if what == "d":
            left[k] -= 1
            if not left[k]: write(k).start()
    for k in range(6):
        gather.drain(k)
        if k % 3 < 2: exchange(k).wait_send()
    for k in range(6): write(k).wait()
    fwd.finish()

def fwd_call(mesh, order, kinds, w_qkv, w_out, w_up, w_down, extra, h, history, cotangent, rope, lengths, first, second):
    depth = mesh.shape["wide"] // 2
    rows = w_qkv.shape[1]
    D, FF = rows * mesh.size, w_down.shape[1] * mesh.size
    T = h.shape[0]
    n = mesh.size // 2
    M = 4 * D + 256
    body = functools.partial(fwd_kernel, depth, order, kinds)
    vm = pl.BlockSpec(memory_space=pltpu.VMEM); an = pl.BlockSpec(memory_space=pl.ANY); sm = pl.BlockSpec(memory_space=pltpu.SMEM)
    shapes = [((2, D, M), BF), ((2, D, FF), BF), ((2, n, 2, FF // n // 2, D), BF)]
    saved = list(saved_shapes(T, D, FF).values())
    got = pl.pallas_call(body,
        out_shape=[jax.ShapeDtypeStruct(s, d) for s, d in shapes + saved],
        in_specs=[vm] * 9 + [sm] * 3, out_specs=[an] * (3 + len(saved)),
        scratch_shapes=[pltpu.VMEM(s, d) for s, d in shapes] + [
            pltpu.VMEM((2, 2 * rows, M // 2), F32), pltpu.VMEM((2, 2 * rows, FF // 2), F32),
            pltpu.VMEM((2, rows, M // 2), F32), pltpu.VMEM((2, rows, FF // 2), F32),
            pltpu.SemaphoreType.DMA((6, 5)), pltpu.SemaphoreType.DMA((6, 4 * depth)),
            pltpu.SemaphoreType.DMA((2, 6)), pltpu.SemaphoreType.DMA((6,)), pltpu.SemaphoreType.DMA((24,)),
            pltpu.VMEM((T, T), F32), pltpu.VMEM((2, 8, D), F32)] + [pltpu.VMEM(s, d) for s, d in saved],
        compiler_params=pltpu.CompilerParams(collective_id=0, has_side_effects=True, vmem_limit_bytes=62 * 2**20),
        cost_estimate=pl.CostEstimate(flops=16 * T * D * FF, bytes_accessed=2**26, transcendentals=2**21),
    )(w_qkv, w_out, w_up, w_down, extra, h, history, cotangent, rope, lengths, first, second)
    return got[:3], SimpleNamespace(**dict(zip(SAVED, got[3:])))


def norm_back(e, h, gain):
    unit, inverse = normalized(h)
    scaled = e * gain
    grad = inverse * (scaled - jnp.mean(scaled, axis=-1, keepdims=True) - unit * jnp.mean(scaled * unit, axis=-1, keepdims=True))
    return grad, jnp.sum(e * unit, axis=0, keepdims=True)


class Backward:
    def __init__(self, io, s, g, first, second):
        self.io, self.s, self.g = io, s, g
        self.first, self.second = first, second
        self.T, self.D = s.gy.shape
        self.width = self.D // HEADS
        self.q, self.o = 3 * self.D // 2, self.D // 2
        self.half = g.mix.shape[1] // 2
        self.tiles = s.act.shape[0]
        self.hist = io.history.shape[0]
        self.writes = []

    SLOTS = ("act", "slope", "n2", "n1", "att", "after", "h", "probs", "qkv", "mix")

    def load(self, name, src, dst=None):
        i = self.SLOTS.index(name)
        return pltpu.make_async_copy(src, getattr(self.s, name) if dst is None else dst, self.io.load_sem.at[i])

    def source(self, name, l):
        return getattr(self.io, name).at[l]

    def fetch(self, l, names):
        for name in names:
            src = (self.io.inputs if l == 0 else self.io.carried) if name == "h" else getattr(self.io, name).at[l]
            self.load(name, src).start()

    def here(self, l, *names):
        for name in names:
            src = (self.io.inputs if l == 0 else self.io.carried) if name == "h" else getattr(self.io, name).at[l]
            self.load(name, src).wait()

    def tile_copy(self, l, t, up):
        src = self.io.up.at[l, :, pl.ds(t * self.D, self.D)] if up else self.io.down.at[l, t]
        return pltpu.make_async_copy(src, self.s.tile.at[t], self.io.tile_sem.at[t])

    def send(self, src, dst):
        n = len(self.writes)
        self.writes.append((src, dst, n))
        pltpu.make_async_copy(src, dst, self.io.write_sem.at[n]).start()

    def finish(self):
        for src, dst, n in self.writes:
            pltpu.make_async_copy(src, dst, self.io.write_sem.at[n]).wait()

    def begin(self):
        for t in range(self.tiles): self.tile_copy(1, t, False).start()
        self.fetch(1, ("act", "slope", "n2", "after", "mix", "att", "probs", "qkv", "n1", "h"))
        s = self.s
        s.gy[...] = self.second[self.hist + 1] * self.io.gout[...]

    def gains(self, l):
        s = self.s
        g = s.mix[:, self.q + self.o:self.half].astype(F32)
        s.gain[...] = g.T[0:8, :]
        s.gain_grad[...] = jnp.zeros_like(s.gain_grad)

    def down_weight(self, l, t):
        s = self.s
        if t == self.tiles - 1:
            s.gm[...] = s.gy[...].astype(BF)
            self.here(l, "act")
        chips = self.g.down.shape[0] // self.tiles
        grad = dot_tn(s.act[t], s.gm[...])
        self.g.down[t * chips:(t + 1) * chips] = grad.astype(BF).reshape((chips,) + self.g.down.shape[1:])

    def act_grad(self, l, t):
        s = self.s
        if t == 0: self.here(l, "slope")
        self.tile_copy(l, t, False).wait()
        grad = dot_nt(s.gm[...], s.tile[t])
        s.slope[t] = (grad * s.slope[t].astype(F32)).astype(BF)
        self.tile_copy(l, t, True).start()

    def turned(self, l, name):
        self.here(l, name)
        self.s.turned[...] = getattr(self.s, name)[...].T

    def up_weight(self, l, t):
        s = self.s
        tile, at = divmod(t * self.o, self.D)
        self.g.up[:, t * self.o:(t + 1) * self.o] = dot(s.turned[...], s.slope[tile, :, at:at + self.o]).astype(BF)

    def norm_two_grad(self, l, t):
        s = self.s
        self.tile_copy(l, t, True).wait()
        part = dot_nt(s.slope[t], s.tile[t])
        if t == 0: s.gn[...] = part
        else: s.gn[...] = s.gn[...] + part
        if l == 1: self.tile_copy(0, t, False).start()

    def after_grad(self, l):
        s = self.s
        self.here(l, "after")
        grad, gain = norm_back(s.gn[...], s.after[...], s.gain[1:2, :])
        s.gain_grad[1:2, :] = gain
        s.gy[...] = s.gy[...] + grad
        s.gm[...] = s.gy[...].astype(BF)
        if l == 1:
            self.fetch(0, ("slope", "n2"))
            self.load("after", self.io.stored.at[0]).start()
            self.load("act", self.io.history).start()

    def out_weight(self, l, h):
        s = self.s
        if h == 0: self.turned(l, "att")
        at = h * self.half + self.q
        self.g.mix[:, at:at + self.o] = dot(s.turned[...], s.gm[:, h * self.o:(h + 1) * self.o]).astype(BF)

    def att_grad(self, l):
        s = self.s
        a, b = self.q, self.half + self.q
        grad = dot_nt(s.gm[:, :self.o], s.mix[:, a:a + self.o]) + dot_nt(s.gm[:, self.o:], s.mix[:, b:b + self.o])
        s.ga[...] = grad.astype(BF)
        if l == 1: self.fetch(0, ("att",))

    def attend(self, l, a):
        s, D = self.s, self.D
        if a == 0: self.here(l, "probs", "qkv")
        q, k, v = (s.qkv[:, i * D + a * 128:i * D + a * 128 + 128] for i in range(3))
        ga = s.ga[:, a * 128:a * 128 + 128]
        lanes = lax.broadcasted_iota(jnp.int32, q.shape, 1)
        got = []
        for e in range(2):
            mine = (lanes < self.width) if e == 0 else (lanes >= self.width)
            probs = s.probs[2 * a + e]
            wide = probs.astype(F32)
            gp = wide * dot_nt(jnp.where(mine, ga, jnp.zeros_like(ga)), v)
            gs = (gp - wide * jnp.sum(gp, axis=-1, keepdims=True)).astype(BF)
            got.append((dot(gs, k), dot_tn(gs, q), dot_tn(probs, ga)))
        gq, gk, gv = (jnp.where(lanes < self.width, x, y) for x, y in zip(*got))
        back = lambda g: g * s.cos[...] - swap_halves(g, self.width // 2) * s.sin[...]
        for i, g in enumerate((back(gq) * self.width ** -0.5, back(gk), gv)):
            s.gj[:, i * D + a * 128:i * D + a * 128 + 128] = g.astype(BF)

    def qkv_weight(self, l, t):
        s = self.s
        if t == 0:
            self.turned(l, "n1")
            if l == 1: self.fetch(0, ("probs", "qkv", "n1"))
        h, i = divmod(t, 3)
        W = self.q // 3
        at = h * self.half + i * W
        self.g.mix[:, at:at + W] = dot(s.turned[...], s.gj[:, t * W:(t + 1) * W]).astype(BF)

    def norm_one_grad(self, l, t):
        s = self.s
        W = self.D // 3
        rows = slice(t * W, (t + 1) * W)
        b = self.half
        s.gn[:, rows] = dot_nt(s.gj[:, :self.q], s.mix[rows, :self.q]) + dot_nt(s.gj[:, self.q:], s.mix[rows, b:b + self.q])

    def layer_grad(self, l):
        s = self.s
        self.here(l, "h")
        grad, gain = norm_back(s.gn[...], s.h[...], s.gain[0:1, :])
        s.gain_grad[0:1, :] = gain
        s.gy[...] = s.gy[...] + grad
        at = self.q + self.o
        self.g.mix[:, at:self.half] = s.gain_grad[...].T.astype(BF)
        self.g.mix[:, self.half + at:] = jnp.zeros((self.D, self.half - at), BF)
        if l == 1: self.fetch(0, ("mix", "h"))
        if l == 1:
            s.kept[...] = s.gy[...]
            self.send(s.kept, self.io.grad_carried)
        else: self.send(s.gy, self.io.grad_inputs)

    def between(self):
        s, n = self.s, self.hist
        self.load("act", self.io.history).wait()
        self.load("after", self.io.stored.at[0]).wait()
        grad = s.gy[...]
        for j in range(n): add_sum(s.sums, 0, j, s.act[j].astype(F32) * grad)
        add_sum(s.sums, 0, n, s.after[...] * grad)
        s.gy[...] = self.first[n] * grad + self.second[n] * self.io.gout[...]
        self.fetch(0, ("act", "after"))

    def steps(self):
        P = functools.partial
        out = [("do", -1, self.begin)]
        for l in (1, 0):
            k = 3 * l
            tiles = range(self.tiles)
            if l == 0: out.append(("sums", -1, self.between))
            out += [("make", k + 2, P(self.down_weight, l, t)) for t in reversed(tiles)]
            out += [("do", -1, P(self.act_grad, l, t)) for t in tiles]
            out.append(("do", -1, P(self.turned, l, "n2")))
            out += [("make", k + 1, P(self.up_weight, l, t)) for t in range(2 * self.tiles)]
            out += [("do", -1, P(self.norm_two_grad, l, t)) for t in tiles]
            out.append(("do", -1, P(lambda l: (self.here(l, "mix"), self.gains(l)), l)))
            out.append(("do", -1, P(self.after_grad, l)))
            out += [("make", k, P(self.out_weight, l, h)) for h in range(2)]
            out.append(("do", -1, P(self.att_grad, l)))
            out += [("do", -1, P(self.attend, l, a)) for a in range(self.D // 128)]
            out += [("make", k, P(self.qkv_weight, l, t)) for t in range(6)]
            out += [("do", -1, P(self.norm_one_grad, l, t)) for t in range(3)]
            out.append(("make", k, P(self.layer_grad, l)))
        return out


def weave_back(order, work, spread):
    to_make = {}
    for name, k, _ in work:
        if name == "make": to_make[k] = to_make.get(k, 0) + 1
    over, done, queue = set(), [], list(work)
    drained = set()
    def pop(force):
        name, k, act = queue[0]
        if name == "make" and k < 3 and k + 3 not in drained:
            if k + 3 not in over:
                assert not force
                return False
            drained.add(k + 3)
            done.append(("drain", k + 3))
        queue.pop(0)
        done.append(act)
        if name == "make": to_make[k] -= 1
        if name == "sums": done.append(("sums", 0))
        return True
    for n, (k, what, r) in enumerate(order):
        if what == "d":
            while to_make[k]: pop(True)
        done.append((k, what, r))
        if what == "o": over.add(k)
        for _ in range(spread):
            if queue: pop(False)
    while queue: pop(True)
    return done


class Total:
    def __init__(self, me, value, land, ssem, rsem):
        self.me, self.value, self.land, self.ssem, self.rsem = me, value, land, ssem, rsem
    def copy(self, i, src, target):
        return pltpu.make_async_remote_copy(src_ref=src, dst_ref=self.land.at[i], send_sem=self.ssem.at[i], recv_sem=self.rsem.at[i],
            device_id=target, device_id_type=MESH)
    def step(self, n):
        me, v = self.me, self.value
        targets = (me.sib, me.xn, me.yn)
        if 0 < n <= 3:
            self.copy(n - 1, v.at[n - 1], targets[n - 1]).wait()
            v[n] = v[n - 1] + self.land[n - 1]
        if n < 3: self.copy(n, v.at[n], targets[n]).start()
        elif n == 3:
            for i, t in enumerate(me.line): self.copy(3 + i, v.at[3], t).start()
        else:
            total = v[3]
            for i, t in enumerate(me.line):
                self.copy(3 + i, v.at[3], t).wait()
                total = total + self.land[3 + i]
            v[4] = total


def bwd_kernel(depth, order, kinds, gout_in, sums_in, rope_in, first, second, *rest):
    io, rest = SimpleNamespace(), rest
    (io.mix, io.up, io.down, io.n1, io.qkv, io.probs, io.att, io.after, io.n2, io.act, io.slope, io.stored, io.carried, io.inputs,
        io.history), rest = rest[:15], rest[15:]
    (mix_o, up_o, down_o, io.grad_carried, io.grad_inputs, sums_o), rest = rest[:6], rest[6:]
    (mix_g, up_g, down_g, mix_d, up_d, down_d, mix_l, up_l, down_l, mix_f, up_f, down_f,
        ssem, rsem, esem, credit, io.load_sem, io.tile_sem, io.write_sem, tsend, trecv, fsem), rest = rest[:22], rest[22:]
    io.gout = gout_in
    s = SimpleNamespace(cos=rope_in.at[0], sin=rope_in.at[1])
    (s.tile, s.mix, s.act, s.slope, s.n2, s.n1, s.att, s.after, s.h, s.probs, s.qkv, s.gy, s.gn, s.gm, s.ga, s.gj, s.turned, s.gain,
        s.gain_grad, s.kept, s.value, s.land) = rest
    scratch = s
    scratch.sums = scratch.value.at[0]
    me = Place(depth)
    c = me.c
    bar = greet(me, True)
    rows = mix_o.shape[1]
    mine = lambda w: pl.ds(al(c * w, 128), w)
    other = lambda w: pl.ds(al((1 - c) * w, 128), w)
    bwd = Backward(io, scratch, SimpleNamespace(mix=mix_g, up=up_g, down=down_g), first, second)
    scratch.value[0] = sums_in[...]
    chunks = {}
    for k in range(6):
        l, j = divmod(k, 3)
        if j == 2:
            R = down_g.shape[2]
            def plane_add(z):
                for i in range(4): add_into(down_g.at[z * 4 + i, c], [down_d.at[z * 4 + i]], R)
            chunks[k] = SimpleNamespace(kind=kinds[k], rows=R, share=lambda chip: down_g.at[chip, c],
                plane=lambda z, own: down_g.at[pl.ds(z * 4, 4), c if own else 1 - c], plane_land=lambda z: down_d.at[pl.ds(z * 4, 4)],
                plane_add=plane_add, land=lambda s: down_l.at[s], result=down_f.at[l])
        else:
            g, d, land, f = ((mix_g, mix_d, mix_l, mix_f), (up_g, up_d, up_l, up_f))[j]
            half = g.shape[1] // 2
            def plane_add(z, g=g, d=d, half=half):
                at = pl.ds(al(z * 8 * rows, 16), 8 * rows)
                add_into(g.at[at, mine(half)], [d.at[at, :]], 8 * rows)
            chunks[k] = SimpleNamespace(kind=kinds[k], rows=2 * rows, share=lambda chip, g=g, half=half: g.at[pl.ds(al(chip * 2 * rows, 16), 2 * rows), mine(half)],
                plane=lambda z, own, g=g, half=half: g.at[pl.ds(al(z * 8 * rows, 16), 8 * rows), mine(half) if own else other(half)],
                plane_land=lambda z, d=d: d.at[pl.ds(al(z * 8 * rows, 16), 8 * rows), :],
                plane_add=plane_add, land=lambda s, land=land: land.at[s], result=f.at[l])
    sc = Scatter(me, chunks, ssem, rsem)
    total = Total(me, scratch.value, scratch.land, tsend, trecv)
    def result(k):
        l, j = divmod(k, 3)
        if j == 2: return [pltpu.make_async_copy(down_f.at[l], down_o.at[l], fsem.at[k])]
        f, o = ((mix_f, mix_o), (up_f, up_o))[j]
        half = f.shape[2]
        return [pltpu.make_async_copy(f.at[l, pl.ds(al(c * rows, 8), rows), :], o.at[l, :, mine(half)], fsem.at[k]),
            pltpu.make_async_remote_copy(src_ref=f.at[l, pl.ds(al((1 - c) * rows, 8), rows), :], dst_ref=o.at[l, :, mine(half)],
                send_sem=esem.at[0, k], recv_sem=esem.at[1, k], device_id=me.sib, device_id_type=MESH)]
    def tell(j):
        for d in (me.xn, me.yn): pl.semaphore_signal(credit.at[1, j], inc=1, device_id=d, device_id_type=MESH)
        when(me.has_up, lambda: pl.semaphore_signal(credit.at[1, j], inc=1, device_id=me.up, device_id_type=MESH))
        when(me.has_down, lambda: pl.semaphore_signal(credit.at[1, j], inc=1, device_id=me.down, device_id_type=MESH))
    planes_left, told, totals = {k: depth for k in range(6)}, {}, []
    greeted_yet = []
    for n, item in enumerate(weave_back(order, bwd.steps(), 1)):
        if not isinstance(item, tuple):
            item()
            continue
        if not greeted_yet:
            greeted(me, bar, True)
            greeted_yet.append(1)
        if item[0] == "drain":
            sc.drain(item[1])
            continue
        if item[0] == "sums":
            totals = [0, 1, 2, 3, 4]
            since = 0
            continue
        k, what, r = item
        l, j = divmod(k, 3)
        if l == 0 and what == "d" and (0, j) not in told:
            told[0, j] = True
            pl.semaphore_wait(credit.at[0, j], 1)
        if l == 0 and what == "q" and (1, j) not in told:
            told[1, j] = True
            pl.semaphore_wait(credit.at[1, j], 2 + me.has_up.astype(jnp.int32) + me.has_down.astype(jnp.int32))
        sc.event(k, what, r)
        if what == "q":
            planes_left[k] -= 1
            if l == 1 and planes_left[k] == 0:
                pl.semaphore_signal(credit.at[0, j], inc=1, device_id=me.sib, device_id_type=MESH)
        if what == "o":
            for cp in result(k): cp.start()
            if l == 1: tell(j)
        if totals:
            since += 1
            if since % 4 == 0: total.step(totals.pop(0))
    for i in totals: total.step(i)
    sums_o[...] = scratch.value[4]
    for k in range(3): sc.drain(k)
    for k in range(6):
        for cp in result(k): cp.wait()
    bwd.finish()


def bwd_call(mesh, order, kinds, weights, saved, inputs, history, rope, first, second):
    mix, up, down = weights
    depth = mesh.shape["wide"] // 2
    D, M = mix.shape[1:]
    FF = up.shape[2]
    T = inputs.shape[0]
    n = mesh.size // 2
    rows, drows = D // mesh.size, FF // mesh.size
    down = down.reshape(2, FF // D, D, D)
    slots = 5 * depth + 2
    body = functools.partial(bwd_kernel, depth, order, kinds)
    vm = pl.BlockSpec(memory_space=pltpu.VMEM); an = pl.BlockSpec(memory_space=pl.ANY); sm = pl.BlockSpec(memory_space=pltpu.SMEM)
    V, S = pltpu.VMEM, pltpu.SemaphoreType.DMA
    return pl.pallas_call(body,
        out_shape=[jax.ShapeDtypeStruct(s, F32) for s in ((2, rows, M), (2, rows, FF), (2, drows, D), (T, D), (T, D), (8, 128))],
        in_specs=[vm] * 3 + [sm] * 2 + [an] * 15, out_specs=[an] * 5 + [vm],
        scratch_shapes=[V((D, M), BF), V((D, FF), BF), V((n, 2, drows, D), BF),
            V((D, M // 2), BF), V((D, FF // 2), BF), V((n, drows, D), BF),
            V((slots, 2 * rows, M // 2), BF), V((slots, 2 * rows, FF // 2), BF), V((slots, drows, D), BF),
            V((2, 2 * rows, M // 2), F32), V((2, 2 * rows, FF // 2), F32), V((2, drows, D), F32),
            S((6, 5)), S((6, slots + depth)), S((2, 6)), pltpu.SemaphoreType.REGULAR((2, 3)),
            S((len(Backward.SLOTS),)), S((FF // D,)), S((2,)), S((2 + depth,)), S((2 + depth,)), S((6,)),
            V((FF // D, D, D), BF), V((D, M), BF), V((FF // D, T, D), BF), V((FF // D, T, D), BF), V((T, D), BF), V((T, D), BF), V((T, D), BF),
            V((T, D), F32), V((T, D), F32), V((HEADS, T, T), BF), V((T, 3 * D), BF), V((T, D), F32), V((T, D), F32), V((T, D), BF),
            V((T, D), BF), V((T, 3 * D), BF), V((D, T), BF), V((8, D), F32), V((128, D), F32), V((T, D), F32), V((5, 8, 128), F32),
            V((2 + depth, 8, 128), F32)],
        compiler_params=pltpu.CompilerParams(collective_id=1, has_side_effects=True, vmem_limit_bytes=63 * 2**20),
        cost_estimate=pl.CostEstimate(flops=32 * T * D * FF, bytes_accessed=2**27, transcendentals=2**10),
    )(saved.gout, saved.sums, rope, first, second, mix, up, down, saved.n1, saved.qkv, saved.probs, saved.att,
        saved.after, saved.n2, saved.act, saved.slope, saved.stored, saved.carried, inputs, history)


def results_kernel(first, second, sums, grad_carried, gout, blended, stored, grad_inputs, mix, up, down,
                   blended_o, stored_o, inputs_o, history_o, qkv_o, out_o, up_o, down_o, gain_o, first_o, second_o,
                   mixed, blended_b, stored_b, inputs_b, mix_b, up_b, down_b, sem):
    q, o = qkv_o.shape[2] // 2, out_o.shape[2] // 2
    half = mix.shape[2] // 2
    ins = [(stored.at[0], stored_b.at[0]), (stored.at[1], stored_b.at[1]), (blended, blended_b), (grad_inputs, inputs_b), (mix, mix_b), (up, up_b), (down, down_b)]
    outs = [[(stored_b.at[0], stored_o.at[0])], [(stored_b.at[1], stored_o.at[1])], [(blended_b, blended_o)], [(inputs_b, inputs_o)], [], [(up_b, up_o)], [(down_b, down_o)]]
    for h in range(2):
        outs[4].append((mix_b.at[:, :, pl.ds(h * half, q)], qkv_o.at[:, :, pl.ds(h * q, q)]))
        outs[4].append((mix_b.at[:, :, pl.ds(h * half + q, o)], out_o.at[:, :, pl.ds(h * o, o)]))
    loads = [pltpu.make_async_copy(a, b, sem.at[i]) for i, (a, b) in enumerate(ins)]
    for cp in loads: cp.start()
    copies = []
    def leave(a, b):
        copies.append(pltpu.make_async_copy(a, b, sem.at[len(ins) + len(copies)]))
        copies[-1].start()
    hist = history_o.shape[0]
    for j in range(hist):
        mixed[j] = first[j] * grad_carried[...] + second[j] * gout[...]
        leave(mixed.at[j], history_o.at[j])
    for j in range(hist + 1): first_o[j] = sums[0, j]
    for j in range(hist + 2): second_o[j] = sums[1, j]
    for cp, pairs in zip(loads, outs):
        cp.wait()
        for a, b in pairs: leave(a, b)
    for l in range(2): gain_o[l] = mix_b[l, :, q + o:q + o + 128].T[0:2, :]
    for cp in copies: cp.wait()


def results_call(first, second, sums, grad_carried, saved, grad_inputs, mix, up, down, hist):
    T, D = grad_inputs.shape
    rows = mix.shape[1]
    vm = pl.BlockSpec(memory_space=pltpu.VMEM); an = pl.BlockSpec(memory_space=pl.ANY); sm = pl.BlockSpec(memory_space=pltpu.SMEM)
    shapes = [(T, D), (2, T, D), (T, D), (hist, T, D), (2, rows, 3 * D), (2, rows, D), up.shape, down.shape, (2, 2, rows), (hist + 1,), (hist + 2,)]
    return pl.pallas_call(results_kernel,
        out_shape=[jax.ShapeDtypeStruct(s, F32) for s in shapes],
        in_specs=[sm] * 3 + [vm] * 2 + [an] * 6, out_specs=[an] * 8 + [vm] + [sm] * 2,
        scratch_shapes=[pltpu.VMEM((hist, T, D), F32), pltpu.VMEM((T, D), F32), pltpu.VMEM((2, T, D), F32), pltpu.VMEM((T, D), F32),
            pltpu.VMEM(mix.shape, F32), pltpu.VMEM(up.shape, F32), pltpu.VMEM(down.shape, F32), pltpu.SemaphoreType.DMA((18 + hist,))],
        compiler_params=pltpu.CompilerParams(vmem_limit_bytes=60 * 2**20),
    )(first, second, sums, grad_carried, saved.gout, saved.blended, saved.stored, grad_inputs, mix, up, down)


def make_extra(gains, lengths):
    rows = gains.shape[2]
    g = jnp.moveaxis(gains.astype(F32), 1, 2)
    n = jnp.broadcast_to(jnp.where(jnp.arange(rows) == 0, lengths[0].astype(F32), 0.0)[None, :, None], (2, rows, 1))
    return jnp.concatenate([g, n, jnp.zeros((2, rows, 125), F32)], axis=2)


def fast_body(mesh, inputs, history, lengths, cotangent, w_qkv, w_out, w_up, w_down, gains, alpha_first, alpha_second):
    rope = jnp.asarray(rotary_lanes(inputs.shape[0], inputs.shape[1] // HEADS, 128))
    weights, saved = fwd_call(mesh, steps(GATHER_ORDER), GATHER_KINDS, w_qkv, w_out, w_up, w_down, make_extra(gains, lengths),
        inputs, history, cotangent, rope, lengths, alpha_first, alpha_second)
    mix, up, down, grad_carried, grad_inputs, sums = bwd_call(mesh, steps(SCATTER_ORDER)[::-1], SCATTER_KINDS, weights, saved,
        inputs, history, rope, alpha_first, alpha_second)
    return results_call(alpha_first, alpha_second, sums, grad_carried, saved, grad_inputs, mix, up, down, history.shape[0])


def solution(mesh):
    axes = ("wide", "narrow")
    split, row_split = P(None, axes, None), P(axes, None)
    placed = (row_split, split, P(axes), row_split, split, split, split, split, P(None, None, axes), P(), P())
    results = (row_split, split, row_split, split, split, split, split, split, P(None, None, axes), P(), P())

    def body(*args):
        rows, hist = args[4].shape[1], args[1].shape[0]
        fits = mesh.shape["narrow"] == 4 and mesh.shape["wide"] == 8 and rows % 8 == 0
        fits = fits and hist * args[4].shape[1] == args[7].shape[1]
        return fast_body(mesh, *args) if fits else plain_body(*args)

    return jax.shard_map(body, mesh=mesh, in_specs=placed, out_specs=results, check_vma=False)
```

```python
import functools
import math
from types import SimpleNamespace

import jax
import jax.numpy as jnp
import numpy as np
from jax import lax
from jax.experimental import pallas as pl
from jax.experimental.pallas import tpu as pltpu
from jax.sharding import PartitionSpec as P

MESH = pl.DeviceIdType.MESH
BF = jnp.bfloat16
F32 = jnp.float32


HEADS = 12


norm_eps = 1e-05
gelu_coef = 0.044715
gelu_scale = math.sqrt(2.0 / math.pi)
masked_score = -1e30


def product(left, right):
    return jnp.dot(left, right, preferred_element_type=jnp.float32)


def layer_norm(hidden, gain_row):
    center = hidden - jnp.mean(hidden, axis=-1, keepdims=True)
    inverse = lax.rsqrt(jnp.mean(center * center, axis=-1, keepdims=True) + norm_eps)
    standard = center * inverse
    return (standard * gain_row, standard, inverse)


def plain_norm_back(grad_rows, standard, inverse, gain_row):
    scaled = grad_rows * gain_row
    grad_gain = jnp.sum(grad_rows * standard, axis=0)
    grad_in = inverse * (
        scaled
        - jnp.mean(scaled, axis=-1, keepdims=True)
        - standard * jnp.mean(scaled * standard, axis=-1, keepdims=True)
    )
    return (grad_in, grad_gain)


def gelu(values):
    return (
        0.5
        * values
        * (1.0 + jnp.tanh(gelu_scale * (values + gelu_coef * values * values * values)))
    )


def gelu_slope(values):
    tangent = jnp.tanh(gelu_scale * (values + gelu_coef * values * values * values))
    return 0.5 * (1.0 + tangent) + 0.5 * values * (1.0 - tangent * tangent) * gelu_scale * (
        1.0 + 3.0 * gelu_coef * values * values
    )


def rotary_tables(seq_length, head_width):
    half_width = head_width // 2
    frequency = 10000.0 ** (-jnp.arange(half_width, dtype=jnp.float32) / half_width)
    angles = jnp.arange(seq_length, dtype=jnp.float32)[:, None] * frequency[None, :]
    return (jnp.cos(angles)[:, None, :], jnp.sin(angles)[:, None, :])


def rotate(values, cos_table, sin_table):
    half_width = values.shape[-1] // 2
    left_half = values[..., :half_width]
    right_half = values[..., half_width:]
    return jnp.concatenate(
        [
            left_half * cos_table - right_half * sin_table,
            right_half * cos_table + left_half * sin_table,
        ],
        axis=-1,
    )


def rotate_back(grad_rows, cos_table, sin_table):
    half_width = grad_rows.shape[-1] // 2
    left_grad = grad_rows[..., :half_width]
    right_grad = grad_rows[..., half_width:]
    return jnp.concatenate(
        [
            left_grad * cos_table + right_grad * sin_table,
            right_grad * cos_table - left_grad * sin_table,
        ],
        axis=-1,
    )


def allowed_mask(block_rows, key_count, length):
    row_place = jnp.arange(block_rows)
    col_place = jnp.arange(key_count)
    return (col_place[None, :] <= row_place[:, None]) & (col_place[None, :] < length)


def attention_forward(queries, key_rows, value_rows, length):
    seq_length, head_count, head_width = queries.shape
    score_scale = head_width ** (-0.5)
    block_rows = min(512, seq_length)
    scores = (
        jnp.einsum("qhe,khe->hqk", queries, key_rows, preferred_element_type=jnp.float32)
        * score_scale
    )
    allowed = allowed_mask(block_rows, block_rows, length)
    scores = jnp.where(allowed[None], scores, masked_score)
    row_top = jnp.max(scores, axis=-1, keepdims=True)
    exp_scores = jnp.exp(scores - row_top)
    row_total = jnp.sum(exp_scores, axis=-1, keepdims=True)
    prob_rows = (exp_scores / row_total).astype(jnp.bfloat16)
    pieces = jnp.einsum("hqk,khe->qhe", prob_rows, value_rows, preferred_element_type=jnp.float32)
    log_sums = row_top + jnp.log(row_total)
    return (pieces, log_sums)


def attention_backward(queries, key_rows, value_rows, log_sums, grad_attended, length):
    seq_length, head_count, head_width = queries.shape
    score_scale = head_width ** (-0.5)
    grad_keys = jnp.zeros(queries.shape, jnp.float32)
    grad_values = jnp.zeros(queries.shape, jnp.float32)
    block_rows = min(512, seq_length)
    scores = (
        jnp.einsum("qhe,khe->hqk", queries, key_rows, preferred_element_type=jnp.float32)
        * score_scale
    )
    allowed = allowed_mask(block_rows, block_rows, length)
    prob_rows = jnp.where(allowed[None], jnp.exp(scores - log_sums), 0.0)
    grad_prob = jnp.einsum(
        "qhe,khe->hqk", grad_attended, value_rows, preferred_element_type=jnp.float32
    )
    inner_sum = jnp.sum(prob_rows * grad_prob, axis=-1, keepdims=True)
    grad_score = (prob_rows * (grad_prob - inner_sum)).astype(jnp.bfloat16)
    grad_pieces = (
        jnp.einsum("hqk,khe->qhe", grad_score, key_rows, preferred_element_type=jnp.float32)
        * score_scale
    )
    grad_keys = grad_keys.at[:block_rows].add(
        jnp.einsum("hqk,qhe->khe", grad_score, queries, preferred_element_type=jnp.float32)
        * score_scale
    )
    grad_values = grad_values.at[:block_rows].add(
        jnp.einsum(
            "hqk,qhe->khe",
            prob_rows.astype(jnp.bfloat16),
            grad_attended,
            preferred_element_type=jnp.float32,
        )
    )
    return (grad_pieces, grad_keys, grad_values)


def layer_forward(hidden, weights, length):
    layer_qkv, layer_out, layer_up, layer_down, layer_gains = weights
    seq_length = hidden.shape[0]
    head_width = layer_out.shape[0] // HEADS
    normed, unit_one, inverse_one = layer_norm(hidden, layer_gains[0])
    normed = normed.astype(jnp.bfloat16)
    joined = product(normed, layer_qkv).reshape(seq_length, 3, HEADS, head_width)
    cos_table, sin_table = rotary_tables(seq_length, head_width)
    queries = rotate(joined[:, 0], cos_table, sin_table).astype(jnp.bfloat16)
    key_rows = rotate(joined[:, 1], cos_table, sin_table).astype(jnp.bfloat16)
    value_rows = joined[:, 2].astype(jnp.bfloat16)
    attended, log_sums = attention_forward(queries, key_rows, value_rows, length)
    attended = attended.reshape(seq_length, HEADS * head_width).astype(jnp.bfloat16)
    after_attn = hidden + product(attended, layer_out)
    normed_two, unit_two, inverse_two = layer_norm(after_attn, layer_gains[1])
    normed_two = normed_two.astype(jnp.bfloat16)
    up_vals = product(normed_two, layer_up)
    result = after_attn + product(gelu(up_vals).astype(jnp.bfloat16), layer_down)
    kept_state = (
        normed,
        unit_one,
        inverse_one,
        queries,
        key_rows,
        value_rows,
        log_sums,
        attended,
        unit_two,
        inverse_two,
        normed_two,
        up_vals,
    )
    return (result, kept_state)


def layer_backward(grad_rows, weights, kept_state, length):
    layer_qkv, layer_out, layer_up, layer_down, layer_gains = weights
    (
        normed,
        unit_one,
        inverse_one,
        queries,
        key_rows,
        value_rows,
        log_sums,
        attended,
        unit_two,
        inverse_two,
        normed_two,
        up_vals,
    ) = kept_state
    seq_length, head_count, head_width = queries.shape
    grad_low = grad_rows.astype(jnp.bfloat16)
    active = gelu(up_vals).astype(jnp.bfloat16)
    grad_down = jnp.einsum("tf,td->fd", active, grad_low, preferred_element_type=jnp.float32)
    grad_active = jnp.einsum("td,fd->tf", grad_low, layer_down, preferred_element_type=jnp.float32)
    grad_upv = (grad_active * gelu_slope(up_vals)).astype(jnp.bfloat16)
    grad_up = jnp.einsum("td,tf->df", normed_two, grad_upv, preferred_element_type=jnp.float32)
    grad_norm_two = jnp.einsum("tf,df->td", grad_upv, layer_up, preferred_element_type=jnp.float32)
    grad_after, gain_two = plain_norm_back(grad_norm_two, unit_two, inverse_two, layer_gains[1])
    grad_after = grad_rows + grad_after
    grad_branch = grad_after.astype(jnp.bfloat16)
    grad_wout = jnp.einsum("ta,td->ad", attended, grad_branch, preferred_element_type=jnp.float32)
    grad_attended = jnp.einsum(
        "td,ad->ta", grad_branch, layer_out, preferred_element_type=jnp.float32
    )
    grad_attended = grad_attended.astype(jnp.bfloat16).reshape(seq_length, head_count, head_width)
    grad_query, grad_keys, grad_values = attention_backward(
        queries, key_rows, value_rows, log_sums, grad_attended, length
    )
    cos_table, sin_table = rotary_tables(seq_length, head_width)
    grad_joined = jnp.stack(
        [
            rotate_back(grad_query, cos_table, sin_table),
            rotate_back(grad_keys, cos_table, sin_table),
            grad_values,
        ],
        axis=1,
    )
    grad_joined = grad_joined.reshape(seq_length, 3 * head_count * head_width).astype(jnp.bfloat16)
    grad_qkv = jnp.einsum("td,tj->dj", normed, grad_joined, preferred_element_type=jnp.float32)
    grad_norm_one = jnp.einsum(
        "tj,dj->td", grad_joined, layer_qkv, preferred_element_type=jnp.float32
    )
    grad_in, gain_one = plain_norm_back(grad_norm_one, unit_one, inverse_one, layer_gains[0])
    return (
        grad_after + grad_in,
        (grad_qkv, grad_wout, grad_up, grad_down, jnp.stack([gain_one, gain_two])),
    )


def mix_history(alphas, history):
    blended = alphas[0] * history[0].astype(jnp.float32)
    for entry in range(1, history.shape[0]):
        blended = blended + alphas[entry] * history[entry].astype(jnp.float32)
    return blended


def plain_body(
    inputs,
    history,
    lengths,
    cotangent,
    w_qkv,
    w_out,
    w_up,
    w_down,
    gains,
    alpha_first,
    alpha_second,
):
    token_total = lax.psum(jnp.sum(lengths.astype(jnp.float32)), ("wide", "narrow"))
    length = lengths[0]
    hist_count = history.shape[0]

    def fetch_layer(layer_no):
        return (
            lax.all_gather(w_qkv[layer_no], ("wide", "narrow"), axis=0, tiled=True),
            lax.all_gather(w_out[layer_no], ("wide", "narrow"), axis=0, tiled=True),
            lax.all_gather(w_up[layer_no], ("wide", "narrow"), axis=0, tiled=True),
            lax.all_gather(w_down[layer_no], ("wide", "narrow"), axis=0, tiled=True),
            lax.all_gather(gains[layer_no], ("wide", "narrow"), axis=1, tiled=True),
        )

    def fetch_again(layer_no):
        return (
            lax.all_gather(w_qkv[layer_no], ("wide", "narrow"), axis=0, tiled=True),
            lax.all_gather(w_out[layer_no], ("wide", "narrow"), axis=0, tiled=True),
            lax.all_gather(w_up[layer_no], ("wide", "narrow"), axis=0, tiled=True),
            lax.all_gather(w_down[layer_no], ("wide", "narrow"), axis=0, tiled=True),
            lax.all_gather(gains[layer_no], ("wide", "narrow"), axis=1, tiled=True),
        )

    def reduce_grads(grad_set):
        return (
            lax.psum_scatter(grad_set[0], ("wide", "narrow"), scatter_dimension=0, tiled=True),
            lax.psum_scatter(grad_set[1], ("wide", "narrow"), scatter_dimension=0, tiled=True),
            lax.psum_scatter(grad_set[2], ("wide", "narrow"), scatter_dimension=0, tiled=True),
            lax.psum_scatter(grad_set[3], ("wide", "narrow"), scatter_dimension=0, tiled=True),
            lax.psum_scatter(grad_set[4], ("wide", "narrow"), scatter_dimension=1, tiled=True),
        )

    weights_one = fetch_layer(0)
    kept_one, state_one = layer_forward(inputs, weights_one, length)
    carried = mix_history(alpha_first, history) + alpha_first[hist_count] * kept_one
    weights_two = fetch_layer(1)
    kept_two, state_two = layer_forward(carried, weights_two, length)
    blended = (
        mix_history(alpha_second, history)
        + alpha_second[hist_count] * kept_one
        + alpha_second[hist_count + 1] * kept_two
    )
    seq_length = inputs.shape[0]
    live_mask = (jnp.arange(seq_length) < length).astype(jnp.float32)[:, None]
    grad_blend = cotangent * live_mask / token_total
    back_two = fetch_again(1)
    grad_carried, grads_two = layer_backward(
        alpha_second[hist_count + 1] * grad_blend, back_two, state_two, length
    )
    shard_two = reduce_grads(grads_two)
    grad_first = alpha_first[hist_count] * grad_carried + alpha_second[hist_count] * grad_blend
    back_one = fetch_again(0)
    grad_inputs, grads_one = layer_backward(grad_first, back_one, state_one, length)
    shard_one = reduce_grads(grads_one)
    grad_history = jnp.stack(
        [
            alpha_first[entry] * grad_carried + alpha_second[entry] * grad_blend
            for entry in range(hist_count)
        ]
    )
    first_terms = []
    second_terms = []
    for entry in range(hist_count):
        past_row = history[entry].astype(jnp.float32)
        first_terms.append(jnp.sum(past_row * grad_carried))
        second_terms.append(jnp.sum(past_row * grad_blend))
    first_terms.append(jnp.sum(kept_one * grad_carried))
    second_terms.append(jnp.sum(kept_one * grad_blend))
    second_terms.append(jnp.sum(kept_two * grad_blend))
    grad_alpha_first, grad_alpha_second = lax.psum(
        (jnp.stack(first_terms), jnp.stack(second_terms)), ("wide", "narrow")
    )
    return (
        blended,
        jnp.stack([kept_one, kept_two]),
        grad_inputs,
        grad_history,
        jnp.stack([shard_one[0], shard_two[0]]),
        jnp.stack([shard_one[1], shard_two[1]]),
        jnp.stack([shard_one[2], shard_two[2]]),
        jnp.stack([shard_one[3], shard_two[3]]),
        jnp.stack([shard_one[4], shard_two[4]]),
        grad_alpha_first,
        grad_alpha_second,
    )


GATHER_KINDS = "accacc"
GATHER_ORDER = (
    400, 200, 100, 210, 110, 0, 30, 140, 121, 122, 141, 410, 21, 22, 31, 23, 151, -1, 142, 152, 123, 300, 40,
    50, 41, 51, 500, 32, 33, 143, 153, 330, 221, 222, 42, 52, 223, 321, 43, 53, -1, -1, -1, 150, 240, 241,
    322, 323, 510, 250, 251, -1, -1, -1, -1, -1, -1, -1, -1, -1, -1, -1, -1, -1, -1, 331, 332, 333, 421, 422,
    -1, -1, 242, 243, -1, -1, -1, 340, 350, 341, 351, 342, 343, 253, 440, 423, 252, -1, -1, -1, -1, -1, -1,
    -1, -1, -1, -1, 353, 450, 441, 442, 521, 522, 540, 451, 352, -1, -1, -1, -1, -1, -1, -1, -1, -1, -1, -1,
    -1, 443, -1, -1, -1, -1, -1, 523, 541, 542, 453, 550, 452, -1, -1, -1, -1, -1, -1, -1, -1, -1, -1, 551,
    -1, 552, -1, 543, 553, -1, -1,
)
SCATTER_KINDS = "acacac"
SCATTER_ORDER = (
    -1, -1, -1, 553, -1, 552, 543, -1, 551, 542, -1, 550, -1, -1, -1, -1, -1, 523, 541, 540, -1, -1, -1, -1,
    -1, -1, -1, -1, 452, 453, 451, 450, -1, 443, -1, 442, -1, 441, -1, 440, -1, -1, 522, 521, 433, -1, -1, -1,
    -1, -1, -1, -1, -1, -1, -1, -1, -1, -1, 432, 431, 430, 423, -1, -1, -1, -1, -1, 353, 351, 350, -1, 343,
    422, 421, 510, 352, 342, 341, 340, 323, 500, -1, -1, 253, -1, 252, 243, -1, 251, 242, -1, 250, 241, -1,
    240, -1, -1, -1, 322, 321, 400, -1, -1, -1, -1, -1, -1, -1, -1, -1, 153, 152, 151, 150, -1, 143, -1, 142,
    -1, -1, -1, -1, -1, -1, -1, -1, -1, -1, 123, 310, 141, 140, 233, 232, 231, 230, 300, -1, -1, -1, -1, -1,
    -1, -1, -1, -1, -1, -1, -1, 53, 52, 51, 122, 121, 50, 43, 42, 41, 33, 223, 222, 221, 32, 31, 110, 40, 23,
    22, 21, 100, 200, 30, 0,
)
NEXT = -1


def steps(codes):
    return [v if v == NEXT else (v // 100, "oplaqd"[v // 10 % 10], v % 10) for v in codes]


def al(v, m): return pl.multiple_of(v, m)
def when(cond, fn): pl.when(cond)(fn)

class Place:
    def __init__(self, depth):
        self.depth = depth
        w = lax.axis_index("wide"); n = lax.axis_index("narrow")
        self.z, self.x = w // 2, lax.rem(w, 2)
        self.y, self.c = n // 2, lax.rem(n, 2)
        first = self.c == 0
        p = jnp.where(first, self.x, self.y)
        q = jnp.where(first, self.y, self.x)
        self.sib = (w, self.y * 2 + 1 - self.c)
        self.xn = (self.z * 2 + 1 - self.x, n)
        self.yn = (w, (1 - self.y) * 2 + self.c)
        self.pn = tuple(jnp.where(first, a, b) for a, b in zip(self.xn, self.yn))
        self.qn = tuple(jnp.where(first, b, a) for a, b in zip(self.xn, self.yn))
        self.has_up = self.z < depth - 1
        self.has_down = self.z > 0
        self.up = (w + 2, n)
        self.down = (w - 2, n)
        self.line = [(lax.rem(w + 2 * i, 2 * depth), n) for i in range(1, depth)]
        self.chip = self.z * 4 + self.x * 2 + self.y
        self.planes = [self.plane(r) for r in range(depth)]
        self.chips = [[[z * 4 + jnp.where(first, 2, 1) * (1 - p if a else p) + jnp.where(first, 1, 2) * (1 - q if b else q)
                        for z in self.planes] for b in (0, 1)] for a in (0, 1)]
        self.onward_up = [(z < self.z) & self.has_up for z in self.planes]
        self.onward_down = [(z > self.z) & self.has_down for z in self.planes]
    def plane(self, r):
        if r == 0: return self.z
        z, last = self.z, self.depth - 1
        short = jnp.minimum(z, last - z)
        low = z * 2 < self.depth
        dist = jnp.where(r <= 2 * short, (r + 1) // 2, r - short)
        below = jnp.where((r <= 2 * short) & (r % 2 == 1), low, ~low)
        return jnp.where(below, z - dist, z + dist)

class Gather:
    def __init__(self, me, chunks, ssem, rsem):
        self.me, self.chunks, self.ssem, self.rsem = me, chunks, ssem, rsem
    def copy(self, k, chip, way, target, sem):
        ref = self.chunks[k][1](chip, 1)
        return pltpu.make_async_remote_copy(src_ref=ref, dst_ref=ref, send_sem=self.ssem.at[k, way],
            recv_sem=self.rsem.at[k, sem], device_id=target, device_id_type=MESH)
    def plane_copy(self, k, r):
        ref = self.chunks[k][2](self.me.planes[r])
        return pltpu.make_async_remote_copy(src_ref=ref, dst_ref=ref, send_sem=self.ssem.at[k, 4],
            recv_sem=self.rsem.at[k, 3 * self.me.depth + self.me.planes[r]], device_id=self.me.sib, device_id_type=MESH)
    def p(self, k, chip, r): self.copy(k, chip, 0, self.me.pn, 2 * self.me.depth + self.me.planes[r]).start()
    def q(self, k, chip, r): self.copy(k, chip, 1, self.me.qn, self.me.planes[r]).start()
    def up(self, k, chip, r): self.copy(k, chip, 2, self.me.up, self.me.depth + self.me.planes[r]).start()
    def down(self, k, chip, r): self.copy(k, chip, 3, self.me.down, self.me.depth + self.me.planes[r]).start()
    def wait(self, k, n, sem):
        ref = self.chunks[k][1](0, n)
        pltpu.make_async_remote_copy(src_ref=ref, dst_ref=ref, send_sem=self.ssem.at[k, 0], recv_sem=self.rsem.at[k, sem],
            device_id=self.me.pn, device_id_type=MESH).wait_recv()
    def event(self, k, what, r):
        me, Z = self.me, self.me.depth
        kind = self.chunks[k][0]
        own, flip = me.chips[0][0][r], me.chips[1][0][r]
        if what == "o":
            when(me.has_up, lambda: self.up(k, own, 0))
            when(me.has_down, lambda: self.down(k, own, 0))
            self.p(k, own, 0)
            self.q(k, own, 0)
        elif what == "p":
            self.wait(k, 1, 2 * Z + me.planes[0])
            when(me.has_up, lambda: self.up(k, flip, 0))
            when(me.has_down, lambda: self.down(k, flip, 0))
            self.q(k, flip, 0)
        elif what == "l":
            both = (own, flip) if kind == "c" else (own,)
            self.wait(k, len(both), Z + me.planes[r])
            def fwd(send):
                for chip in both: send(k, chip, r)
            when(me.onward_up[r], lambda: fwd(self.up))
            when(me.onward_down[r], lambda: fwd(self.down))
            if kind == "a": self.p(k, own, r)
            for chip in both: self.q(k, chip, r)
        elif what == "a":
            self.wait(k, 1, 2 * Z + me.planes[r])
            self.q(k, flip, r)
        elif what == "q":
            self.wait(k, 2, me.planes[r])
            self.plane_copy(k, r).start()
        elif what == "d":
            self.plane_copy(k, r).wait_recv()
    def drain(self, k):
        me, Z = self.me, self.me.depth
        per = 2 if self.chunks[k][0] == "c" else 1
        counts = [1 if per == 2 else Z, 2 * Z, jnp.where(me.has_up, per * (me.z + 1), 0), jnp.where(me.has_down, per * (Z - me.z), 0)]
        for way, count in enumerate(counts):
            def one(_, carry):
                self.copy(k, 0, way, me.pn, 0).wait_send()
                return carry
            lax.fori_loop(0, count, one, 0)
        def one(_, carry):
            self.plane_copy(k, 0).wait_send()
            return carry
        lax.fori_loop(0, Z, one, 0)

def greet(me, whole_line=False):
    bar = pltpu.get_barrier_semaphore()
    def signal(d): pl.semaphore_signal(bar, inc=1, device_id=d, device_id_type=MESH)
    for d in (me.sib, me.xn, me.yn): signal(d)
    if whole_line:
        for d in me.line: signal(d)
    else:
        when(me.has_up, lambda: signal(me.up))
        when(me.has_down, lambda: signal(me.down))
    return bar


def greeted(me, bar, whole_line=False):
    line = len(me.line) if whole_line else me.has_up.astype(jnp.int32) + me.has_down.astype(jnp.int32)
    pl.semaphore_wait(bar, 3 + line)


def add_into(dst, sources, rows, out=None):
    step = 48 if rows % 48 == 0 else 16
    @pl.loop(0, rows // step)
    def _(i):
        at = pl.ds(al(i * step, 16), step)
        if out is None and len(sources) == 1:
            dst[at, :] = dst[at, :] + sources[0][at, :]
            return
        total = dst[at, :].astype(F32)
        for s in sources: total = total + s[at, :].astype(F32)
        if out is None: dst[at, :] = total.astype(dst.dtype)
        else: out[at, :] = total


class Scatter:
    def __init__(self, me, chunks, ssem, rsem):
        self.me, self.chunks, self.ssem, self.rsem = me, chunks, ssem, rsem
        Z = me.depth
        self.Z = Z
        self.q_slot = lambda flip, z: (Z if flip else 0) + z
        self.line_slot = lambda flip, z: 2 * Z + (Z if flip else 0) + z
        self.late_slot = lambda flip: 4 * Z + (1 if flip else 0)
        self.p_slot = lambda z: 4 * Z + 2 + z
        self.slots = 5 * Z + 2
    def land(self, k, slot): return self.chunks[k].land(slot)
    def copy(self, k, chip, way, target, slot):
        ch = self.chunks[k]
        return pltpu.make_async_remote_copy(src_ref=ch.share(chip), dst_ref=ch.land(slot), send_sem=self.ssem.at[k, way],
            recv_sem=self.rsem.at[k, slot], device_id=target, device_id_type=MESH)
    def plane_copy(self, k, r):
        ch, me = self.chunks[k], self.me
        z = me.planes[r]
        return pltpu.make_async_remote_copy(src_ref=ch.plane(z, False), dst_ref=ch.plane_land(z), send_sem=self.ssem.at[k, 4],
            recv_sem=self.rsem.at[k, self.slots + z], device_id=me.sib, device_id_type=MESH)
    def wait(self, k, slot):
        self.copy(k, 0, 0, self.me.pn, slot).wait_recv()
    def take(self, k, chip, slots, out=None):
        ch = self.chunks[k]
        for s in slots: self.wait(k, s)
        add_into(ch.share(chip), [ch.land(s) for s in slots], ch.rows, out)
    def event(self, k, what, r):
        me, Z = self.me, self.Z
        ch = self.chunks[k]
        kind = ch.kind
        own, flip = me.chips[0][0][r], me.chips[1][0][r]
        z = me.planes[r]
        if what == "d":
            self.plane_copy(k, r).start()
        elif what == "q":
            self.plane_copy(k, r).wait_recv()
            ch.plane_add(z)
            self.copy(k, me.chips[0][1][r], 1, me.qn, self.q_slot(False, z)).start()
            self.copy(k, me.chips[1][1][r], 1, me.qn, self.q_slot(True, z)).start()
        elif what == "a":
            self.take(k, flip, [self.q_slot(True, z)])
            self.copy(k, flip, 0, me.pn, self.p_slot(z)).start()
        elif what == "l":
            first = [self.q_slot(False, z)] + ([self.p_slot(z)] if kind == "a" else [])
            self.take(k, own, first)
            if kind == "c": self.take(k, flip, [self.q_slot(True, z)])
            flips = (False, True) if kind == "c" else (False,)
            def behind():
                for f in flips: self.take(k, flip if f else own, [self.line_slot(f, z)])
            when((z < me.z) & me.has_up, behind)
            when((z > me.z) & me.has_down, behind)
            def send(way, target, late):
                for f in flips:
                    self.copy(k, flip if f else own, way, target, self.late_slot(f) if late else self.line_slot(f, z)).start()
            when((z > me.z) & (z == me.z + 1), lambda: send(2, me.up, False))
            when((z > me.z) & (z != me.z + 1), lambda: send(2, me.up, False))
            when((z < me.z) & (z == me.z - 1), lambda: send(3, me.down, True))
            when((z < me.z) & (z != me.z - 1), lambda: send(3, me.down, False))
        elif what in "po":
            f = what == "p"
            chip = flip if f else own
            slots = [self.q_slot(f, z)]
            if not f: slots.append(self.p_slot(z))
            when(me.has_down, lambda: self.take(k, chip, [self.line_slot(f, z)]))
            when(me.has_up, lambda: self.take(k, chip, [self.late_slot(f)]))
            self.take(k, chip, slots, None if f else ch.result)
            if f: self.copy(k, chip, 0, me.pn, self.p_slot(z)).start()
    def drain(self, k):
        me, Z = self.me, self.Z
        per = 2 if self.chunks[k].kind == "c" else 1
        counts = [1 if per == 2 else Z, 2 * Z, jnp.where(me.has_up, per * (Z - 1 - me.z), 0), jnp.where(me.has_down, per * me.z, 0)]
        for way, count in enumerate(counts):
            def one(_, carry):
                self.copy(k, 0, way, me.pn, 0).wait_send()
                return carry
            lax.fori_loop(0, count, one, 0)
        def one(_, carry):
            self.plane_copy(k, 0).wait_send()
            return carry
        lax.fori_loop(0, Z, one, 0)


def dot(a, b):
    return jnp.dot(a, b, preferred_element_type=F32)


def dot_nt(a, b):
    return lax.dot_general(a, b, (((1,), (1,)), ((), ())), preferred_element_type=F32)


def dot_tn(a, b):
    return lax.dot_general(a, b, (((0,), (0,)), ((), ())), preferred_element_type=F32)


def normalized(h):
    center = h - jnp.mean(h, axis=-1, keepdims=True)
    inverse = lax.rsqrt(jnp.mean(center * center, axis=-1, keepdims=True) + norm_eps)
    return center * inverse, inverse


def swap_halves(v, half):
    lanes = lax.broadcasted_iota(jnp.int32, v.shape, 1)
    width = v.shape[1]
    return jnp.where(lanes % (2 * half) < half, pltpu.roll(v, width - half, 1), pltpu.roll(v, half, 1))


def rotary_lanes(seq_length, head_width, lanes):
    half = head_width // 2
    frequency = (10000.0 ** (-np.arange(half, dtype=np.float32) / half)).astype(np.float32)
    angles = np.arange(seq_length, dtype=np.float32)[:, None] * frequency[None, :]
    cos, sin = np.cos(angles), np.sin(angles)
    both = np.stack([np.concatenate([cos, cos], 1), np.concatenate([-sin, sin], 1)])
    return np.tile(both, (1, 1, lanes // head_width)).astype(np.float32)


def add_sum(ref, row, lane, product):
    rows = lax.broadcasted_iota(jnp.int32, ref.shape, 0)
    lanes = lax.broadcasted_iota(jnp.int32, ref.shape, 1)
    total = jnp.sum(jnp.sum(product, axis=0, keepdims=True), axis=1, keepdims=True)
    ref[...] = ref[...] + jnp.where((rows == row) & (lanes == lane), total, 0.0)


class Forward:
    def __init__(self, w, io, s, planes, length, first, second):
        self.planes = planes
        self.w, self.io, self.s = w, io, s
        self.length, self.first, self.second = length, first, second
        self.T, self.D = s.h.shape
        self.width = self.D // HEADS
        self.q, self.o = 3 * self.D // 2, self.D // 2
        self.half = w.mix.shape[2] // 2
        self.writes = []

    def send(self, name, l=None):
        src, dst = getattr(self.s, name), getattr(self.io, name)
        if l is not None: src, dst = src.at[l], dst.at[l]
        n = len(self.writes)
        self.writes.append((src, dst, n))
        pltpu.make_async_copy(src, dst, self.io.wsem.at[n]).start()

    def finish(self):
        for src, dst, n in self.writes:
            pltpu.make_async_copy(src, dst, self.io.wsem.at[n]).wait()

    def load(self, i):
        s, io = self.s, self.io
        src, dst = ((io.h, s.h), (io.rope, s.rope), (io.cotangent, s.cotangent), (io.history, s.history))[i]
        return pltpu.make_async_copy(src, dst, io.isem.at[i])

    def setup(self):
        s, T = self.s, self.T
        row = lax.broadcasted_iota(jnp.int32, (T, T), 0)
        col = lax.broadcasted_iota(jnp.int32, (T, T), 1)
        s.bias[...] = jnp.where((col <= row) & (col < self.length), 0.0, masked_score)
        s.sums[...] = jnp.zeros_like(s.sums)

    def loss_grad(self):
        s, io = self.s, self.io
        count = jnp.sum(s.gain[0, 2:3, :])
        row = lax.broadcasted_iota(jnp.int32, (self.T, 1), 0)
        grad = jnp.where(row < self.length, s.cotangent[...], 0.0) / count
        s.gout[...] = grad
        self.send("gout")
        n = s.history.shape[0]
        for j in range(n): add_sum(s.sums, 1, j, s.history[j].astype(F32) * grad)

    def layer_in(self, l):
        return self.s.h if l == 0 else self.s.carried

    def norm_one(self, l):
        s, w = self.s, self.w
        g = w.mix[l, :, self.q + self.o:self.half].astype(F32)
        s.gain[l] = g.T[0:8, :]
        if l == 0:
            for i in range(4): self.load(i).wait()
        x, _ = normalized(self.layer_in(l)[...])
        s.n1[l] = (x * s.gain[l, 0:1, :]).astype(BF)
        self.send("n1", l)

    def project(self, l, t):
        s, w = self.s, self.w
        h, i = divmod(t, 3)
        W = self.q // 3
        at = h * self.half + i * W
        joined = dot(s.n1[l], w.mix[l, :, at:at + W])
        for j in range(W // 128):
            col = t * W + j * 128
            part = joined[:, j * 128:(j + 1) * 128]
            if col < 2 * self.D:
                part = part * s.cos[...] + swap_halves(part, self.width // 2) * s.sin[...]
                if col < self.D: part = part * self.width ** -0.5
            s.qkv[l, :, col:col + 128] = part.astype(BF)

    def attend(self, l, a):
        s, D = self.s, self.D
        q, k, v = (s.qkv[l, :, i * D + a * 128:i * D + a * 128 + 128] for i in range(3))
        lanes = lax.broadcasted_iota(jnp.int32, q.shape, 1)
        outs = []
        for e in range(2):
            mine = (lanes < self.width) if e == 0 else (lanes >= self.width)
            scores = dot_nt(jnp.where(mine, q, jnp.zeros_like(q)), k) + s.bias[...]
            top = jnp.max(scores, axis=-1, keepdims=True)
            weights = jnp.exp(scores - top)
            probs = (weights * (1.0 / jnp.sum(weights, axis=-1, keepdims=True))).astype(BF)
            s.probs[l, 2 * a + e] = probs
            outs.append(dot(probs, v))
        s.att[l, :, a * 128:a * 128 + 128] = jnp.where(lanes < self.width, outs[0], outs[1]).astype(BF)

    def attend_done(self, l):
        for name in ("qkv", "probs", "att"): self.send(name, l)

    def out(self, l, h):
        s, w = self.s, self.w
        cols = slice(h * self.o, (h + 1) * self.o)
        at = h * self.half + self.q
        s.after[l, :, cols] = self.layer_in(l)[:, cols] + dot(s.att[l], w.mix[l, :, at:at + self.o])

    def norm_two(self, l):
        s = self.s
        x, _ = normalized(s.after[l])
        s.n2[l] = (x * s.gain[l, 1:2, :]).astype(BF)
        self.send("n2", l)
        self.send("after", l)

    def raise_(self, l, t, W):
        s, w = self.s, self.w
        u = dot(s.n2[l], w.up[l, :, t * W:(t + 1) * W])
        tile, at = divmod(t * W, self.D)
        cols = slice(at, at + W)
        square = u * u
        tangent = jnp.tanh(gelu_scale * u * (1.0 + gelu_coef * square))
        s.act[l, tile, :, cols] = (0.5 * u * (1.0 + tangent)).astype(BF)
        s.slope[l, tile, :, cols] = (
            0.5 * (1.0 + tangent) + 0.5 * u * (1.0 - tangent * tangent) * gelu_scale * (1.0 + 3.0 * gelu_coef * square)
        ).astype(BF)

    def raise_done(self, l):
        for name in ("act", "slope"): self.send(name, l)

    def lower(self, l, r):
        s, w = self.s, self.w
        z = self.planes[r]
        chips = w.down.shape[1] // len(self.planes)
        part = dot(s.act[l, z], w.down[l, pl.ds(z * chips, chips)].reshape(-1, self.D))
        s.stored[l] = (s.after[l] if r == 0 else s.stored[l]) + part

    def mixed(self, l):
        s, io = self.s, self.io
        n = s.history.shape[0]
        if l == 0:
            s.carried[...] = mix_history([self.first[j] for j in range(n)], s.history) + self.first[n] * s.stored[0]
            self.send("carried")
        else:
            s.blended[...] = (
                mix_history([self.second[j] for j in range(n)], s.history)
                + self.second[n] * s.stored[0] + self.second[n + 1] * s.stored[1]
            )
            self.send("blended")
        self.send("stored", l)
        add_sum(s.sums, 1, n + l, s.stored[l] * s.gout[...])
        if l == 1: self.send("sums")

    def steps(self):
        out = [(-1, self.setup)]
        P = functools.partial
        for l in range(2):
            k = 3 * l
            out.append((k, P(self.norm_one, l)))
            out += [(k, P(self.project, l, t)) for t in range(6)]
            if l == 0: out.append((k, self.loss_grad))
            out += [(k, P(self.attend, l, a)) for a in range(self.D // 128)]
            out.append((k, P(self.attend_done, l)))
            out += [(k, P(self.out, l, h)) for h in range(2)]
            out.append((k, P(self.norm_two, l)))
            W = self.D // 2
            out += [(k + 1, P(self.raise_, l, t, W)) for t in range(4 * self.D // W)]
            out.append((k + 1, P(self.raise_done, l)))
            out += [((k + 2, r), P(self.lower, l, r)) for r in range(len(self.planes))]
            out.append((k + 2, P(self.mixed, l)))
        return out


def weave(order, work):
    left, whole, done, queue = {}, set([-1]), [], list(work)
    for v in order:
        if v != NEXT and v[1] == "d": left[v[0]] = left.get(v[0], 0) + 1
    for v in order:
        if v == NEXT:
            need, act = queue.pop(0)
            assert need in whole
            done.append(act)
            continue
        done.append(v)
        k, what, r = v
        if what == "d":
            whole.add((k, r))
            left[k] -= 1
            if not left[k]: whole.add(k)
    assert not queue
    return done


def saved_shapes(T, D, FF):
    return dict(n1=((2, T, D), BF), qkv=((2, T, 3 * D), BF), probs=((2, HEADS, T, T), BF), att=((2, T, D), BF), after=((2, T, D), F32),
        n2=((2, T, D), BF), act=((2, FF // D, T, D), BF), slope=((2, FF // D, T, D), BF), stored=((2, T, D), F32), carried=((T, D), F32),
        blended=((T, D), F32), gout=((T, D), F32), sums=((8, 128), F32))


SAVED = tuple(saved_shapes(1, 1, 1))


def fwd_kernel(depth, order, kinds, qkv_in, out_in, up_in, down_in, gain_in, h_in, history_in, cotangent_in, rope_in, length, first, second,
              mix_o, up_o, down_o, *rest):
    n = len(SAVED)
    saved_o, rest = rest[:n], rest[n:]
    (mix_b, up_b, down_b, mix_s, up_s, mix_t, up_t, ssem, rsem, esem, lsem, wsem, isem, bias, gain, turn, h_b, history_b, cotangent_b,
        rope_b), saved_b = rest[:20], rest[20:]
    me = Place(depth)
    bar = greet(me)
    rows = qkv_in.shape[1]
    c = me.c
    wq, wo, wu = qkv_in.shape[2] // 2, out_in.shape[2] // 2, up_in.shape[2] // 2
    mine = lambda w: pl.ds(al(c * w, 128), w)
    other = lambda w: pl.ds(al((1 - c) * w, 128), w)
    my_rows = pl.ds(al(c * rows, 8), rows)
    def stage(k):
        l, j = divmod(k, 3)
        if j == 0:
            turn[...] = jnp.zeros_like(turn)
            turn[0:2, 0:rows] = gain_in[l].astype(F32)
            row = lax.broadcasted_iota(jnp.int32, turn.shape, 0)
            col = lax.broadcasted_iota(jnp.int32, turn.shape, 1)
            turn[...] = jnp.where((row == 2) & (col == 0), length[0].astype(F32), turn[...]).T
            for ref, at, pick in ((mix_s, (l, my_rows), mine), (mix_t, (l, slice(None)), other)):
                ref[at[0], at[1], 0:wq] = qkv_in[l, :, pick(wq)].astype(F32)
                ref[at[0], at[1], wq:wq + wo] = out_in[l, :, pick(wo)].astype(F32)
                ref[at[0], at[1], wq + wo:] = turn[0:rows, :]
        elif j == 1:
            up_s[l, my_rows, :] = up_in[l, :, mine(wu)].astype(F32)
            up_t[l] = up_in[l, :, other(wu)].astype(F32)
    def exchange(k):
        l, j = divmod(k, 3)
        if j == 2: return None
        s, t = ((mix_s, mix_t), (up_s, up_t))[j]
        return pltpu.make_async_remote_copy(src_ref=t.at[l], dst_ref=s.at[l, my_rows, :], send_sem=esem.at[0, k],
            recv_sem=esem.at[1, k], device_id=me.sib, device_id_type=MESH)
    def ready(k):
        l, j = divmod(k, 3)
        if j == 2:
            down_b[l, me.chip, c] = down_in[l]
            return
        exchange(k).wait_recv()
        s, b = ((mix_s, mix_b), (up_s, up_b))[j]
        b[l, pl.ds(al(me.chip * 2 * rows, 16), 2 * rows), mine(s.shape[2])] = s[l].astype(BF)
    chunks = []
    for k in range(6):
        l, j = divmod(k, 3)
        if j == 2:
            chunks.append((kinds[k], lambda chip, n, l=l: down_b.at[l, pl.ds(chip, n), c], lambda z, l=l: down_b.at[l, pl.ds(z * 4, 4), c]))
        else:
            b = (mix_b, up_b)[j]
            half = b.shape[2] // 2
            chunks.append((kinds[k],
                lambda chip, n, b=b, l=l, half=half: b.at[l, pl.ds(al(chip * 2 * rows, 16), n * 2 * rows), mine(half)],
                lambda z, b=b, l=l, half=half: b.at[l, pl.ds(al(z * 8 * rows, 16), 8 * rows), mine(half)]))
    gather = Gather(me, chunks, ssem, rsem)
    io = SimpleNamespace(**dict(zip(SAVED, saved_o)), h=h_in, history=history_in, cotangent=cotangent_in, rope=rope_in,
        wsem=wsem, isem=isem)
    scratch = SimpleNamespace(**dict(zip(SAVED, saved_b)), bias=bias, gain=gain, h=h_b, history=history_b,
        cotangent=cotangent_b, rope=rope_b, cos=rope_b.at[0], sin=rope_b.at[1])
    fwd = Forward(SimpleNamespace(mix=mix_b, up=up_b, down=down_b), io, scratch, me.planes, length[0], first, second)
    stage(0)
    greeted(me, bar)
    exchange(0).start()
    for i in range(4): fwd.load(i).start()
    for k in (1, 3, 4):
        stage(k)
        exchange(k).start()
    left = [depth] * 6
    pairs = ((mix_b, mix_o), (up_b, up_o), (down_b, down_o))
    def write(k):
        l, j = divmod(k, 3)
        b, o = pairs[j]
        return pltpu.make_async_copy(b.at[l], o.at[l], lsem.at[k])
    for item in weave(order, fwd.steps()):
        if not isinstance(item, tuple):
            item()
            continue
        k, what, r = item
        if what == "o": ready(k)
        gather.event(k, what, r)
        if what == "d":
            left[k] -= 1
            if not left[k]: write(k).start()
    for k in range(6):
        gather.drain(k)
        if k % 3 < 2: exchange(k).wait_send()
    for k in range(6): write(k).wait()
    fwd.finish()

def fwd_call(mesh, order, kinds, w_qkv, w_out, w_up, w_down, gains, h, history, cotangent, rope, lengths, first, second):
    depth = mesh.shape["wide"] // 2
    rows = w_qkv.shape[1]
    D, FF = rows * mesh.size, w_down.shape[1] * mesh.size
    T = h.shape[0]
    n = mesh.size // 2
    M = 4 * D + 256
    body = functools.partial(fwd_kernel, depth, order, kinds)
    vm = pl.BlockSpec(memory_space=pltpu.VMEM); an = pl.BlockSpec(memory_space=pl.ANY); sm = pl.BlockSpec(memory_space=pltpu.SMEM)
    shapes = [((2, D, M), BF), ((2, D, FF), BF), ((2, n, 2, FF // n // 2, D), BF)]
    saved = list(saved_shapes(T, D, FF).values())
    got = pl.pallas_call(body,
        out_shape=[jax.ShapeDtypeStruct(s, d) for s, d in shapes + saved],
        in_specs=[vm] * 5 + [an] * 4 + [sm] * 3, out_specs=[an] * (3 + len(saved)),
        scratch_shapes=[pltpu.VMEM(s, d) for s, d in shapes] + [
            pltpu.VMEM((2, 2 * rows, M // 2), F32), pltpu.VMEM((2, 2 * rows, FF // 2), F32),
            pltpu.VMEM((2, rows, M // 2), F32), pltpu.VMEM((2, rows, FF // 2), F32),
            pltpu.SemaphoreType.DMA((6, 5)), pltpu.SemaphoreType.DMA((6, 4 * depth)),
            pltpu.SemaphoreType.DMA((2, 6)), pltpu.SemaphoreType.DMA((6,)), pltpu.SemaphoreType.DMA((24,)),
            pltpu.SemaphoreType.DMA((4,)), pltpu.VMEM((T, T), F32), pltpu.VMEM((2, 8, D), F32), pltpu.VMEM((128, 128), F32),
            pltpu.VMEM(h.shape, F32), pltpu.VMEM(history.shape, BF), pltpu.VMEM(cotangent.shape, F32), pltpu.VMEM(rope.shape, F32)] + [pltpu.VMEM(s, d) for s, d in saved],
        compiler_params=pltpu.CompilerParams(collective_id=0, has_side_effects=True, vmem_limit_bytes=62 * 2**20),
        cost_estimate=pl.CostEstimate(flops=16 * T * D * FF, bytes_accessed=2**26, transcendentals=2**21),
    )(w_qkv, w_out, w_up, w_down, gains, h, history, cotangent, rope, lengths, first, second)
    return got[:3], SimpleNamespace(**dict(zip(SAVED, got[3:])))


def norm_back(e, h, gain):
    unit, inverse = normalized(h)
    scaled = e * gain
    grad = inverse * (scaled - jnp.mean(scaled, axis=-1, keepdims=True) - unit * jnp.mean(scaled * unit, axis=-1, keepdims=True))
    return grad, jnp.sum(e * unit, axis=0, keepdims=True)


class Backward:
    def __init__(self, io, s, g, planes, first, second):
        self.planes = planes
        self.io, self.s, self.g = io, s, g
        self.first, self.second = first, second
        self.T, self.D = s.gy.shape
        self.width = self.D // HEADS
        self.q, self.o = 3 * self.D // 2, self.D // 2
        self.half = g.mix.shape[1] // 2
        self.tiles = s.act.shape[0]
        self.hist = io.history.shape[0]
        self.writes = []

    SLOTS = ("act", "slope", "n2", "n1", "att", "after", "h", "probs", "qkv", "mix")

    def load(self, name, src, dst=None):
        i = self.SLOTS.index(name)
        return pltpu.make_async_copy(src, getattr(self.s, name) if dst is None else dst, self.io.load_sem.at[i])

    def source(self, name, l):
        return getattr(self.io, name).at[l]

    def fetch(self, l, names):
        for name in names:
            src = (self.io.inputs if l == 0 else self.io.carried) if name == "h" else getattr(self.io, name).at[l]
            self.load(name, src).start()

    def here(self, l, *names):
        for name in names:
            src = (self.io.inputs if l == 0 else self.io.carried) if name == "h" else getattr(self.io, name).at[l]
            self.load(name, src).wait()

    def tile_copy(self, l, t, up):
        src = self.io.up.at[l, :, pl.ds(t * self.D, self.D)] if up else self.io.down.at[l, t]
        return pltpu.make_async_copy(src, self.s.tile.at[t], self.io.tile_sem.at[t])

    def send(self, src, dst):
        n = len(self.writes)
        self.writes.append((src, dst, n))
        pltpu.make_async_copy(src, dst, self.io.write_sem.at[n]).start()

    def finish(self):
        for src, dst, n in self.writes:
            pltpu.make_async_copy(src, dst, self.io.write_sem.at[n]).wait()

    def begin(self):
        for t in range(self.tiles): self.tile_copy(1, t, False).start()
        self.fetch(1, ("act", "slope", "n2", "after", "mix", "att", "probs", "qkv", "n1", "h"))
        s = self.s
        s.gy[...] = self.second[self.hist + 1] * self.io.gout[...]

    def gains(self, l):
        s = self.s
        g = s.mix[:, self.q + self.o:self.half].astype(F32)
        s.gain[...] = g.T[0:8, :]
        s.gain_grad[...] = jnp.zeros_like(s.gain_grad)

    def down_weight(self, l, r):
        s = self.s
        if r == len(self.planes) - 1:
            s.gm[...] = s.gy[...].astype(BF)
            self.here(l, "act")
        z = self.planes[r]
        chips = self.g.down.shape[0] // len(self.planes)
        grad = dot_tn(s.act[z], s.gm[...])
        self.g.down[pl.ds(z * chips, chips)] = grad.astype(BF).reshape((chips,) + self.g.down.shape[1:])

    def act_grad(self, l, t):
        s = self.s
        if t == 0: self.here(l, "slope")
        self.tile_copy(l, t, False).wait()
        grad = dot_nt(s.gm[...], s.tile[t])
        s.slope[t] = (grad * s.slope[t].astype(F32)).astype(BF)
        self.tile_copy(l, t, True).start()

    def turned(self, l, name):
        self.here(l, name)
        self.s.turned[...] = getattr(self.s, name)[...].T

    def up_weight(self, l, t):
        s = self.s
        tile, at = divmod(t * self.o, self.D)
        self.g.up[:, t * self.o:(t + 1) * self.o] = dot(s.turned[...], s.slope[tile, :, at:at + self.o]).astype(BF)

    def norm_two_grad(self, l, t):
        s = self.s
        self.tile_copy(l, t, True).wait()
        part = dot_nt(s.slope[t], s.tile[t])
        if t == 0: s.gn[...] = part
        else: s.gn[...] = s.gn[...] + part
        if l == 1: self.tile_copy(0, t, False).start()

    def after_grad(self, l):
        s = self.s
        self.here(l, "after")
        grad, gain = norm_back(s.gn[...], s.after[...], s.gain[1:2, :])
        s.gain_grad[1:2, :] = gain
        s.gy[...] = s.gy[...] + grad
        s.gm[...] = s.gy[...].astype(BF)
        if l == 1:
            self.fetch(0, ("slope", "n2"))
            self.load("after", self.io.stored.at[0]).start()
            self.load("act", self.io.history).start()

    def out_weight(self, l, h):
        s = self.s
        if h == 0: self.turned(l, "att")
        at = h * self.half + self.q
        self.g.mix[:, at:at + self.o] = dot(s.turned[...], s.gm[:, h * self.o:(h + 1) * self.o]).astype(BF)

    def att_grad(self, l):
        s = self.s
        a, b = self.q, self.half + self.q
        grad = dot_nt(s.gm[:, :self.o], s.mix[:, a:a + self.o]) + dot_nt(s.gm[:, self.o:], s.mix[:, b:b + self.o])
        s.ga[...] = grad.astype(BF)

    def attend(self, l, a):
        s, D = self.s, self.D
        if a == 0: self.here(l, "probs", "qkv")
        q, k, v = (s.qkv[:, i * D + a * 128:i * D + a * 128 + 128] for i in range(3))
        ga = s.ga[:, a * 128:a * 128 + 128]
        lanes = lax.broadcasted_iota(jnp.int32, q.shape, 1)
        got = []
        for e in range(2):
            mine = (lanes < self.width) if e == 0 else (lanes >= self.width)
            probs = s.probs[2 * a + e]
            wide = probs.astype(F32)
            gp = wide * dot_nt(jnp.where(mine, ga, jnp.zeros_like(ga)), v)
            gs = (gp - wide * jnp.sum(gp, axis=-1, keepdims=True)).astype(BF)
            got.append((dot(gs, k), dot_tn(gs, q), dot_tn(probs, ga)))
        gq, gk, gv = (jnp.where(lanes < self.width, x, y) for x, y in zip(*got))
        back = lambda g: g * s.cos[...] - swap_halves(g, self.width // 2) * s.sin[...]
        for i, g in enumerate((back(gq) * self.width ** -0.5, back(gk), gv)):
            s.gj[:, i * D + a * 128:i * D + a * 128 + 128] = g.astype(BF)

    def qkv_weight(self, l, t):
        s = self.s
        if t == 0:
            self.turned(l, "n1")
            if l == 1: self.fetch(0, ("probs", "qkv", "n1", "att"))
        h, i = divmod(t, 3)
        W = self.q // 3
        at = h * self.half + i * W
        self.g.mix[:, at:at + W] = dot(s.turned[...], s.gj[:, t * W:(t + 1) * W]).astype(BF)

    def norm_one_grad(self, l, t):
        s = self.s
        W = self.D // 3
        rows = slice(t * W, (t + 1) * W)
        b = self.half
        s.gn[:, rows] = dot_nt(s.gj[:, :self.q], s.mix[rows, :self.q]) + dot_nt(s.gj[:, self.q:], s.mix[rows, b:b + self.q])

    def layer_grad(self, l):
        s = self.s
        self.here(l, "h")
        grad, gain = norm_back(s.gn[...], s.h[...], s.gain[0:1, :])
        s.gain_grad[0:1, :] = gain
        s.gy[...] = s.gy[...] + grad
        at = self.q + self.o
        self.g.mix[:, at:self.half] = s.gain_grad[...].T.astype(BF)
        self.g.mix[:, self.half + at:] = jnp.zeros((self.D, self.half - at), BF)
        if l == 1: self.fetch(0, ("mix", "h"))
        if l == 1:
            s.kept[...] = s.gy[...]
            self.send(s.kept, self.io.grad_carried)
        else: self.send(s.gy, self.io.grad_inputs)

    def between(self):
        s, n = self.s, self.hist
        self.load("act", self.io.history).wait()
        self.load("after", self.io.stored.at[0]).wait()
        grad = s.gy[...]
        for j in range(n): add_sum(s.sums, 0, j, s.act[j].astype(F32) * grad)
        add_sum(s.sums, 0, n, s.after[...] * grad)
        s.gy[...] = self.first[n] * grad + self.second[n] * self.io.gout[...]
        self.fetch(0, ("act", "after"))

    def steps(self):
        P = functools.partial
        out = [("do", -1, self.begin)]
        for l in (1, 0):
            k = 3 * l
            tiles = range(self.tiles)
            if l == 0: out.append(("sums", -1, self.between))
            out += [("make", (k + 2, r), P(self.down_weight, l, r)) for r in reversed(range(len(self.planes)))]
            out += [("do", -1, P(self.act_grad, l, t)) for t in tiles]
            out.append(("do", -1, P(self.turned, l, "n2")))
            out += [("make", (k + 1, -1), P(self.up_weight, l, t)) for t in range(2 * self.tiles)]
            out += [("do", -1, P(self.norm_two_grad, l, t)) for t in tiles]
            out.append(("do", -1, P(lambda l: (self.here(l, "mix"), self.gains(l)), l)))
            out.append(("do", -1, P(self.after_grad, l)))
            out.append(("do", -1, P(self.att_grad, l)))
            out += [("do", -1, P(self.attend, l, a)) for a in range(self.D // 128)]
            out += [("make", (k, -1), P(self.out_weight, l, h)) for h in range(2)]
            out += [("make", (k, -1), P(self.qkv_weight, l, t)) for t in range(6)]
            out += [("do", -1, P(self.norm_one_grad, l, t)) for t in range(3)]
            out.append(("make", (k, -1), P(self.layer_grad, l)))
        return out


def weave_back(order, work):
    to_make, over, drained, done, queue = {}, set(), set(), [], list(work)
    for name, k, _ in work:
        if name == "make": to_make[k] = to_make.get(k, 0) + 1
    for v in order:
        if v == NEXT:
            name, k, act = queue.pop(0)
            if name == "make":
                before = k[0] + 3
                if k[0] < 3 and before not in drained:
                    assert before in over
                    drained.add(before)
                    done.append(("drain", before))
                to_make[k] -= 1
            done.append(act)
            if name == "sums": done.append(("sums", 0))
            continue
        k, what, r = v
        if what == "d": assert not to_make.get((k, r), 0) and not to_make.get((k, -1), 0)
        if what == "o": over.add(k)
        done.append(v)
    assert not queue
    return done


class Total:
    def __init__(self, me, value, land, ssem, rsem):
        self.me, self.value, self.land, self.ssem, self.rsem = me, value, land, ssem, rsem
    def copy(self, i, src, target):
        return pltpu.make_async_remote_copy(src_ref=src, dst_ref=self.land.at[i], send_sem=self.ssem.at[i], recv_sem=self.rsem.at[i],
            device_id=target, device_id_type=MESH)
    def step(self, n):
        me, v = self.me, self.value
        targets = (me.sib, me.xn, me.yn)
        if 0 < n <= 3:
            self.copy(n - 1, v.at[n - 1], targets[n - 1]).wait()
            v[n] = v[n - 1] + self.land[n - 1]
        if n < 3: self.copy(n, v.at[n], targets[n]).start()
        elif n == 3:
            for i, t in enumerate(me.line): self.copy(3 + i, v.at[3], t).start()
        else:
            total = v[3]
            for i, t in enumerate(me.line):
                self.copy(3 + i, v.at[3], t).wait()
                total = total + self.land[3 + i]
            v[4] = total


def bwd_kernel(depth, order, kinds, gout_in, sums_in, rope_in, first, second, *rest):
    io, rest = SimpleNamespace(), rest
    (io.mix, io.up, io.down, io.n1, io.qkv, io.probs, io.att, io.after, io.n2, io.act, io.slope, io.stored, io.carried, io.inputs,
        io.history), rest = rest[:15], rest[15:]
    (mix_o, up_o, down_o, io.grad_carried, io.grad_inputs, sums_o), rest = rest[:6], rest[6:]
    (mix_g, up_g, down_g, mix_d, up_d, down_d, mix_l, up_l, down_l, mix_f, up_f, down_f,
        ssem, rsem, esem, credit, io.load_sem, io.tile_sem, io.write_sem, tsend, trecv, fsem), rest = rest[:22], rest[22:]
    io.gout = gout_in
    s = SimpleNamespace(cos=rope_in.at[0], sin=rope_in.at[1])
    (s.tile, s.mix, s.act, s.slope, s.n2, s.n1, s.att, s.after, s.h, s.probs, s.qkv, s.gy, s.gn, s.gm, s.ga, s.gj, s.turned, s.gain,
        s.gain_grad, s.kept, s.value, s.land) = rest
    scratch = s
    scratch.sums = scratch.value.at[0]
    me = Place(depth)
    c = me.c
    bar = greet(me, True)
    rows = mix_o.shape[1]
    mine = lambda w: pl.ds(al(c * w, 128), w)
    other = lambda w: pl.ds(al((1 - c) * w, 128), w)
    bwd = Backward(io, scratch, SimpleNamespace(mix=mix_g, up=up_g, down=down_g), me.planes, first, second)
    scratch.value[0] = sums_in[...]
    chunks = {}
    for k in range(6):
        l, j = divmod(k, 3)
        if j == 2:
            R = down_g.shape[2]
            def plane_add(z):
                for i in range(4): add_into(down_g.at[z * 4 + i, c], [down_d.at[z * 4 + i]], R)
            chunks[k] = SimpleNamespace(kind=kinds[k], rows=R, share=lambda chip: down_g.at[chip, c],
                plane=lambda z, own: down_g.at[pl.ds(z * 4, 4), c if own else 1 - c], plane_land=lambda z: down_d.at[pl.ds(z * 4, 4)],
                plane_add=plane_add, land=lambda s: down_l.at[s], result=down_f.at[l])
        else:
            g, d, land, f = ((mix_g, mix_d, mix_l, mix_f), (up_g, up_d, up_l, up_f))[j]
            half = g.shape[1] // 2
            def plane_add(z, g=g, d=d, half=half):
                at = pl.ds(al(z * 8 * rows, 16), 8 * rows)
                add_into(g.at[at, mine(half)], [d.at[at, :]], 8 * rows)
            chunks[k] = SimpleNamespace(kind=kinds[k], rows=2 * rows, share=lambda chip, g=g, half=half: g.at[pl.ds(al(chip * 2 * rows, 16), 2 * rows), mine(half)],
                plane=lambda z, own, g=g, half=half: g.at[pl.ds(al(z * 8 * rows, 16), 8 * rows), mine(half) if own else other(half)],
                plane_land=lambda z, d=d: d.at[pl.ds(al(z * 8 * rows, 16), 8 * rows), :],
                plane_add=plane_add, land=lambda s, land=land: land.at[s], result=f.at[l])
    sc = Scatter(me, chunks, ssem, rsem)
    total = Total(me, scratch.value, scratch.land, tsend, trecv)
    def result(k):
        l, j = divmod(k, 3)
        if j == 2: return [pltpu.make_async_copy(down_f.at[l], down_o.at[l], fsem.at[k])]
        f, o = ((mix_f, mix_o), (up_f, up_o))[j]
        half = f.shape[2]
        return [pltpu.make_async_copy(f.at[l, pl.ds(al(c * rows, 8), rows), :], o.at[l, :, mine(half)], fsem.at[k]),
            pltpu.make_async_remote_copy(src_ref=f.at[l, pl.ds(al((1 - c) * rows, 8), rows), :], dst_ref=o.at[l, :, mine(half)],
                send_sem=esem.at[0, k], recv_sem=esem.at[1, k], device_id=me.sib, device_id_type=MESH)]
    def tell(j):
        for d in (me.xn, me.yn): pl.semaphore_signal(credit.at[1, j], inc=1, device_id=d, device_id_type=MESH)
        when(me.has_up, lambda: pl.semaphore_signal(credit.at[1, j], inc=1, device_id=me.up, device_id_type=MESH))
        when(me.has_down, lambda: pl.semaphore_signal(credit.at[1, j], inc=1, device_id=me.down, device_id_type=MESH))
    planes_left, told, totals = {k: depth for k in range(6)}, {}, []
    greeted_yet = []
    for n, item in enumerate(weave_back(order, bwd.steps())):
        if not isinstance(item, tuple):
            item()
            continue
        if not greeted_yet:
            greeted(me, bar, True)
            greeted_yet.append(1)
        if item[0] == "drain":
            sc.drain(item[1])
            continue
        if item[0] == "sums":
            totals = [0, 1, 2, 3, 4]
            since = 0
            continue
        k, what, r = item
        l, j = divmod(k, 3)
        if l == 0 and what == "d" and (0, j) not in told:
            told[0, j] = True
            pl.semaphore_wait(credit.at[0, j], 1)
        if l == 0 and what == "q" and (1, j) not in told:
            told[1, j] = True
            pl.semaphore_wait(credit.at[1, j], 2 + me.has_up.astype(jnp.int32) + me.has_down.astype(jnp.int32))
        sc.event(k, what, r)
        if what == "q":
            planes_left[k] -= 1
            if l == 1 and planes_left[k] == 0:
                pl.semaphore_signal(credit.at[0, j], inc=1, device_id=me.sib, device_id_type=MESH)
        if what == "o":
            for cp in result(k): cp.start()
            if l == 1: tell(j)
        if totals:
            since += 1
            if since % 4 == 0: total.step(totals.pop(0))
    for i in totals: total.step(i)
    sums_o[...] = scratch.value[4]
    for k in range(3): sc.drain(k)
    for k in range(6):
        for cp in result(k): cp.wait()
    bwd.finish()


def bwd_call(mesh, order, kinds, weights, saved, inputs, history, rope, first, second):
    mix, up, down = weights
    depth = mesh.shape["wide"] // 2
    D, M = mix.shape[1:]
    FF = up.shape[2]
    T = inputs.shape[0]
    n = mesh.size // 2
    rows, drows = D // mesh.size, FF // mesh.size
    down = down.reshape(2, FF // D, D, D)
    slots = 5 * depth + 2
    body = functools.partial(bwd_kernel, depth, order, kinds)
    vm = pl.BlockSpec(memory_space=pltpu.VMEM); an = pl.BlockSpec(memory_space=pl.ANY); sm = pl.BlockSpec(memory_space=pltpu.SMEM)
    V, S = pltpu.VMEM, pltpu.SemaphoreType.DMA
    return pl.pallas_call(body,
        out_shape=[jax.ShapeDtypeStruct(s, F32) for s in ((2, rows, M), (2, rows, FF), (2, drows, D), (T, D), (T, D), (8, 128))],
        in_specs=[vm] * 3 + [sm] * 2 + [an] * 15, out_specs=[an] * 5 + [vm],
        scratch_shapes=[V((D, M), BF), V((D, FF), BF), V((n, 2, drows, D), BF),
            V((D, M // 2), BF), V((D, FF // 2), BF), V((n, drows, D), BF),
            V((slots, 2 * rows, M // 2), BF), V((slots, 2 * rows, FF // 2), BF), V((slots, drows, D), BF),
            V((2, 2 * rows, M // 2), F32), V((2, 2 * rows, FF // 2), F32), V((2, drows, D), F32),
            S((6, 5)), S((6, slots + depth)), S((2, 6)), pltpu.SemaphoreType.REGULAR((2, 3)),
            S((len(Backward.SLOTS),)), S((FF // D,)), S((2,)), S((2 + depth,)), S((2 + depth,)), S((6,)),
            V((FF // D, D, D), BF), V((D, M), BF), V((FF // D, T, D), BF), V((FF // D, T, D), BF), V((T, D), BF), V((T, D), BF), V((T, D), BF),
            V((T, D), F32), V((T, D), F32), V((HEADS, T, T), BF), V((T, 3 * D), BF), V((T, D), F32), V((T, D), F32), V((T, D), BF),
            V((T, D), BF), V((T, 3 * D), BF), V((D, T), BF), V((8, D), F32), V((128, D), F32), V((T, D), F32), V((5, 8, 128), F32),
            V((2 + depth, 8, 128), F32)],
        compiler_params=pltpu.CompilerParams(collective_id=1, has_side_effects=True, vmem_limit_bytes=63 * 2**20),
        cost_estimate=pl.CostEstimate(flops=32 * T * D * FF, bytes_accessed=2**27, transcendentals=2**10),
    )(saved.gout, saved.sums, rope, first, second, mix, up, down, saved.n1, saved.qkv, saved.probs, saved.att,
        saved.after, saved.n2, saved.act, saved.slope, saved.stored, saved.carried, inputs, history)


def results_kernel(first, second, sums, grad_carried, gout, blended, stored, grad_inputs, mix, up, down,
                   blended_o, stored_o, inputs_o, history_o, qkv_o, out_o, up_o, down_o, gain_o, first_o, second_o,
                   mixed, blended_b, stored_b, inputs_b, mix_b, up_b, down_b, sem):
    q, o = qkv_o.shape[2] // 2, out_o.shape[2] // 2
    half = mix.shape[2] // 2
    ins = [(stored.at[0], stored_b.at[0]), (stored.at[1], stored_b.at[1]), (blended, blended_b), (grad_inputs, inputs_b), (mix, mix_b), (up, up_b), (down, down_b)]
    outs = [[(stored_b.at[0], stored_o.at[0])], [(stored_b.at[1], stored_o.at[1])], [(blended_b, blended_o)], [(inputs_b, inputs_o)], [], [(up_b, up_o)], [(down_b, down_o)]]
    for h in range(2):
        outs[4].append((mix_b.at[:, :, pl.ds(h * half, q)], qkv_o.at[:, :, pl.ds(h * q, q)]))
        outs[4].append((mix_b.at[:, :, pl.ds(h * half + q, o)], out_o.at[:, :, pl.ds(h * o, o)]))
    loads = [pltpu.make_async_copy(a, b, sem.at[i]) for i, (a, b) in enumerate(ins)]
    for cp in loads: cp.start()
    copies = []
    def leave(a, b):
        copies.append(pltpu.make_async_copy(a, b, sem.at[len(ins) + len(copies)]))
        copies[-1].start()
    hist = history_o.shape[0]
    for j in range(hist):
        mixed[j] = first[j] * grad_carried[...] + second[j] * gout[...]
        leave(mixed.at[j], history_o.at[j])
    for j in range(hist + 1): first_o[j] = sums[0, j]
    for j in range(hist + 2): second_o[j] = sums[1, j]
    for cp, pairs in zip(loads, outs):
        cp.wait()
        for a, b in pairs: leave(a, b)
    for l in range(2): gain_o[l] = mix_b[l, :, q + o:q + o + 128].T[0:2, :]
    for cp in copies: cp.wait()


def results_call(first, second, sums, grad_carried, saved, grad_inputs, mix, up, down, hist):
    T, D = grad_inputs.shape
    rows = mix.shape[1]
    vm = pl.BlockSpec(memory_space=pltpu.VMEM); an = pl.BlockSpec(memory_space=pl.ANY); sm = pl.BlockSpec(memory_space=pltpu.SMEM)
    shapes = [(T, D), (2, T, D), (T, D), (hist, T, D), (2, rows, 3 * D), (2, rows, D), up.shape, down.shape, (2, 2, rows), (hist + 1,), (hist + 2,)]
    return pl.pallas_call(results_kernel,
        out_shape=[jax.ShapeDtypeStruct(s, F32) for s in shapes],
        in_specs=[sm] * 3 + [vm] * 2 + [an] * 6, out_specs=[an] * 8 + [vm] + [sm] * 2,
        scratch_shapes=[pltpu.VMEM((hist, T, D), F32), pltpu.VMEM((T, D), F32), pltpu.VMEM((2, T, D), F32), pltpu.VMEM((T, D), F32),
            pltpu.VMEM(mix.shape, F32), pltpu.VMEM(up.shape, F32), pltpu.VMEM(down.shape, F32), pltpu.SemaphoreType.DMA((18 + hist,))],
        compiler_params=pltpu.CompilerParams(vmem_limit_bytes=60 * 2**20),
    )(first, second, sums, grad_carried, saved.gout, saved.blended, saved.stored, grad_inputs, mix, up, down)


def fast_body(mesh, inputs, history, lengths, cotangent, w_qkv, w_out, w_up, w_down, gains, alpha_first, alpha_second):
    rope = jnp.asarray(rotary_lanes(inputs.shape[0], inputs.shape[1] // HEADS, 128))
    weights, saved = fwd_call(mesh, steps(GATHER_ORDER), GATHER_KINDS, w_qkv, w_out, w_up, w_down, gains,
        inputs, history, cotangent, rope, lengths, alpha_first, alpha_second)
    mix, up, down, grad_carried, grad_inputs, sums = bwd_call(mesh, steps(SCATTER_ORDER), SCATTER_KINDS, weights, saved,
        inputs, history, rope, alpha_first, alpha_second)
    return results_call(alpha_first, alpha_second, sums, grad_carried, saved, grad_inputs, mix, up, down, history.shape[0])


def solution(mesh):
    axes = ("wide", "narrow")
    split, row_split = P(None, axes, None), P(axes, None)
    placed = (row_split, split, P(axes), row_split, split, split, split, split, P(None, None, axes), P(), P())
    results = (row_split, split, row_split, split, split, split, split, split, P(None, None, axes), P(), P())

    def body(*args):
        rows, hist = args[4].shape[1], args[1].shape[0]
        fits = mesh.shape["narrow"] == 4 and mesh.shape["wide"] == 8 and rows % 8 == 0
        fits = fits and hist * args[4].shape[1] == args[7].shape[1]
        return fast_body(mesh, *args) if fits else plain_body(*args)

    return jax.shard_map(body, mesh=mesh, in_specs=placed, out_specs=results, check_vma=False)
```

```python
import functools
import math
from types import SimpleNamespace

import jax
import jax.numpy as jnp
import numpy as np
from jax import lax
from jax.experimental import pallas as pl
from jax.experimental.pallas import tpu as pltpu
from jax.sharding import PartitionSpec as P

MESH = pl.DeviceIdType.MESH
BF = jnp.bfloat16
F32 = jnp.float32


HEADS = 12


norm_eps = 1e-05
gelu_coef = 0.044715
gelu_scale = math.sqrt(2.0 / math.pi)
masked_score = -1e30


def product(left, right):
    return jnp.dot(left, right, preferred_element_type=jnp.float32)


def layer_norm(hidden, gain_row):
    center = hidden - jnp.mean(hidden, axis=-1, keepdims=True)
    inverse = lax.rsqrt(jnp.mean(center * center, axis=-1, keepdims=True) + norm_eps)
    standard = center * inverse
    return (standard * gain_row, standard, inverse)


def plain_norm_back(grad_rows, standard, inverse, gain_row):
    scaled = grad_rows * gain_row
    grad_gain = jnp.sum(grad_rows * standard, axis=0)
    grad_in = inverse * (
        scaled
        - jnp.mean(scaled, axis=-1, keepdims=True)
        - standard * jnp.mean(scaled * standard, axis=-1, keepdims=True)
    )
    return (grad_in, grad_gain)


def gelu(values):
    return (
        0.5
        * values
        * (1.0 + jnp.tanh(gelu_scale * (values + gelu_coef * values * values * values)))
    )


def gelu_slope(values):
    tangent = jnp.tanh(gelu_scale * (values + gelu_coef * values * values * values))
    return 0.5 * (1.0 + tangent) + 0.5 * values * (1.0 - tangent * tangent) * gelu_scale * (
        1.0 + 3.0 * gelu_coef * values * values
    )


def rotary_tables(seq_length, head_width):
    half_width = head_width // 2
    frequency = 10000.0 ** (-jnp.arange(half_width, dtype=jnp.float32) / half_width)
    angles = jnp.arange(seq_length, dtype=jnp.float32)[:, None] * frequency[None, :]
    return (jnp.cos(angles)[:, None, :], jnp.sin(angles)[:, None, :])


def rotate(values, cos_table, sin_table):
    half_width = values.shape[-1] // 2
    left_half = values[..., :half_width]
    right_half = values[..., half_width:]
    return jnp.concatenate(
        [
            left_half * cos_table - right_half * sin_table,
            right_half * cos_table + left_half * sin_table,
        ],
        axis=-1,
    )


def rotate_back(grad_rows, cos_table, sin_table):
    half_width = grad_rows.shape[-1] // 2
    left_grad = grad_rows[..., :half_width]
    right_grad = grad_rows[..., half_width:]
    return jnp.concatenate(
        [
            left_grad * cos_table + right_grad * sin_table,
            right_grad * cos_table - left_grad * sin_table,
        ],
        axis=-1,
    )


def allowed_mask(block_rows, key_count, length):
    row_place = jnp.arange(block_rows)
    col_place = jnp.arange(key_count)
    return (col_place[None, :] <= row_place[:, None]) & (col_place[None, :] < length)


def attention_forward(queries, key_rows, value_rows, length):
    seq_length, head_count, head_width = queries.shape
    score_scale = head_width ** (-0.5)
    block_rows = min(512, seq_length)
    scores = (
        jnp.einsum("qhe,khe->hqk", queries, key_rows, preferred_element_type=jnp.float32)
        * score_scale
    )
    allowed = allowed_mask(block_rows, block_rows, length)
    scores = jnp.where(allowed[None], scores, masked_score)
    row_top = jnp.max(scores, axis=-1, keepdims=True)
    exp_scores = jnp.exp(scores - row_top)
    row_total = jnp.sum(exp_scores, axis=-1, keepdims=True)
    prob_rows = (exp_scores / row_total).astype(jnp.bfloat16)
    pieces = jnp.einsum("hqk,khe->qhe", prob_rows, value_rows, preferred_element_type=jnp.float32)
    log_sums = row_top + jnp.log(row_total)
    return (pieces, log_sums)


def attention_backward(queries, key_rows, value_rows, log_sums, grad_attended, length):
    seq_length, head_count, head_width = queries.shape
    score_scale = head_width ** (-0.5)
    grad_keys = jnp.zeros(queries.shape, jnp.float32)
    grad_values = jnp.zeros(queries.shape, jnp.float32)
    block_rows = min(512, seq_length)
    scores = (
        jnp.einsum("qhe,khe->hqk", queries, key_rows, preferred_element_type=jnp.float32)
        * score_scale
    )
    allowed = allowed_mask(block_rows, block_rows, length)
    prob_rows = jnp.where(allowed[None], jnp.exp(scores - log_sums), 0.0)
    grad_prob = jnp.einsum(
        "qhe,khe->hqk", grad_attended, value_rows, preferred_element_type=jnp.float32
    )
    inner_sum = jnp.sum(prob_rows * grad_prob, axis=-1, keepdims=True)
    grad_score = (prob_rows * (grad_prob - inner_sum)).astype(jnp.bfloat16)
    grad_pieces = (
        jnp.einsum("hqk,khe->qhe", grad_score, key_rows, preferred_element_type=jnp.float32)
        * score_scale
    )
    grad_keys = grad_keys.at[:block_rows].add(
        jnp.einsum("hqk,qhe->khe", grad_score, queries, preferred_element_type=jnp.float32)
        * score_scale
    )
    grad_values = grad_values.at[:block_rows].add(
        jnp.einsum(
            "hqk,qhe->khe",
            prob_rows.astype(jnp.bfloat16),
            grad_attended,
            preferred_element_type=jnp.float32,
        )
    )
    return (grad_pieces, grad_keys, grad_values)


def layer_forward(hidden, weights, length):
    layer_qkv, layer_out, layer_up, layer_down, layer_gains = weights
    seq_length = hidden.shape[0]
    head_width = layer_out.shape[0] // HEADS
    normed, unit_one, inverse_one = layer_norm(hidden, layer_gains[0])
    normed = normed.astype(jnp.bfloat16)
    joined = product(normed, layer_qkv).reshape(seq_length, 3, HEADS, head_width)
    cos_table, sin_table = rotary_tables(seq_length, head_width)
    queries = rotate(joined[:, 0], cos_table, sin_table).astype(jnp.bfloat16)
    key_rows = rotate(joined[:, 1], cos_table, sin_table).astype(jnp.bfloat16)
    value_rows = joined[:, 2].astype(jnp.bfloat16)
    attended, log_sums = attention_forward(queries, key_rows, value_rows, length)
    attended = attended.reshape(seq_length, HEADS * head_width).astype(jnp.bfloat16)
    after_attn = hidden + product(attended, layer_out)
    normed_two, unit_two, inverse_two = layer_norm(after_attn, layer_gains[1])
    normed_two = normed_two.astype(jnp.bfloat16)
    up_vals = product(normed_two, layer_up)
    result = after_attn + product(gelu(up_vals).astype(jnp.bfloat16), layer_down)
    kept_state = (
        normed,
        unit_one,
        inverse_one,
        queries,
        key_rows,
        value_rows,
        log_sums,
        attended,
        unit_two,
        inverse_two,
        normed_two,
        up_vals,
    )
    return (result, kept_state)


def layer_backward(grad_rows, weights, kept_state, length):
    layer_qkv, layer_out, layer_up, layer_down, layer_gains = weights
    (
        normed,
        unit_one,
        inverse_one,
        queries,
        key_rows,
        value_rows,
        log_sums,
        attended,
        unit_two,
        inverse_two,
        normed_two,
        up_vals,
    ) = kept_state
    seq_length, head_count, head_width = queries.shape
    grad_low = grad_rows.astype(jnp.bfloat16)
    active = gelu(up_vals).astype(jnp.bfloat16)
    grad_down = jnp.einsum("tf,td->fd", active, grad_low, preferred_element_type=jnp.float32)
    grad_active = jnp.einsum("td,fd->tf", grad_low, layer_down, preferred_element_type=jnp.float32)
    grad_upv = (grad_active * gelu_slope(up_vals)).astype(jnp.bfloat16)
    grad_up = jnp.einsum("td,tf->df", normed_two, grad_upv, preferred_element_type=jnp.float32)
    grad_norm_two = jnp.einsum("tf,df->td", grad_upv, layer_up, preferred_element_type=jnp.float32)
    grad_after, gain_two = plain_norm_back(grad_norm_two, unit_two, inverse_two, layer_gains[1])
    grad_after = grad_rows + grad_after
    grad_branch = grad_after.astype(jnp.bfloat16)
    grad_wout = jnp.einsum("ta,td->ad", attended, grad_branch, preferred_element_type=jnp.float32)
    grad_attended = jnp.einsum(
        "td,ad->ta", grad_branch, layer_out, preferred_element_type=jnp.float32
    )
    grad_attended = grad_attended.astype(jnp.bfloat16).reshape(seq_length, head_count, head_width)
    grad_query, grad_keys, grad_values = attention_backward(
        queries, key_rows, value_rows, log_sums, grad_attended, length
    )
    cos_table, sin_table = rotary_tables(seq_length, head_width)
    grad_joined = jnp.stack(
        [
            rotate_back(grad_query, cos_table, sin_table),
            rotate_back(grad_keys, cos_table, sin_table),
            grad_values,
        ],
        axis=1,
    )
    grad_joined = grad_joined.reshape(seq_length, 3 * head_count * head_width).astype(jnp.bfloat16)
    grad_qkv = jnp.einsum("td,tj->dj", normed, grad_joined, preferred_element_type=jnp.float32)
    grad_norm_one = jnp.einsum(
        "tj,dj->td", grad_joined, layer_qkv, preferred_element_type=jnp.float32
    )
    grad_in, gain_one = plain_norm_back(grad_norm_one, unit_one, inverse_one, layer_gains[0])
    return (
        grad_after + grad_in,
        (grad_qkv, grad_wout, grad_up, grad_down, jnp.stack([gain_one, gain_two])),
    )


def mix_history(alphas, history):
    blended = alphas[0] * history[0].astype(jnp.float32)
    for entry in range(1, history.shape[0]):
        blended = blended + alphas[entry] * history[entry].astype(jnp.float32)
    return blended


def plain_body(
    inputs,
    history,
    lengths,
    cotangent,
    w_qkv,
    w_out,
    w_up,
    w_down,
    gains,
    alpha_first,
    alpha_second,
):
    token_total = lax.psum(jnp.sum(lengths.astype(jnp.float32)), ("wide", "narrow"))
    length = lengths[0]
    hist_count = history.shape[0]

    def fetch_layer(layer_no):
        return (
            lax.all_gather(w_qkv[layer_no], ("wide", "narrow"), axis=0, tiled=True),
            lax.all_gather(w_out[layer_no], ("wide", "narrow"), axis=0, tiled=True),
            lax.all_gather(w_up[layer_no], ("wide", "narrow"), axis=0, tiled=True),
            lax.all_gather(w_down[layer_no], ("wide", "narrow"), axis=0, tiled=True),
            lax.all_gather(gains[layer_no], ("wide", "narrow"), axis=1, tiled=True),
        )

    def fetch_again(layer_no):
        return (
            lax.all_gather(w_qkv[layer_no], ("wide", "narrow"), axis=0, tiled=True),
            lax.all_gather(w_out[layer_no], ("wide", "narrow"), axis=0, tiled=True),
            lax.all_gather(w_up[layer_no], ("wide", "narrow"), axis=0, tiled=True),
            lax.all_gather(w_down[layer_no], ("wide", "narrow"), axis=0, tiled=True),
            lax.all_gather(gains[layer_no], ("wide", "narrow"), axis=1, tiled=True),
        )

    def reduce_grads(grad_set):
        return (
            lax.psum_scatter(grad_set[0], ("wide", "narrow"), scatter_dimension=0, tiled=True),
            lax.psum_scatter(grad_set[1], ("wide", "narrow"), scatter_dimension=0, tiled=True),
            lax.psum_scatter(grad_set[2], ("wide", "narrow"), scatter_dimension=0, tiled=True),
            lax.psum_scatter(grad_set[3], ("wide", "narrow"), scatter_dimension=0, tiled=True),
            lax.psum_scatter(grad_set[4], ("wide", "narrow"), scatter_dimension=1, tiled=True),
        )

    weights_one = fetch_layer(0)
    kept_one, state_one = layer_forward(inputs, weights_one, length)
    carried = mix_history(alpha_first, history) + alpha_first[hist_count] * kept_one
    weights_two = fetch_layer(1)
    kept_two, state_two = layer_forward(carried, weights_two, length)
    blended = (
        mix_history(alpha_second, history)
        + alpha_second[hist_count] * kept_one
        + alpha_second[hist_count + 1] * kept_two
    )
    seq_length = inputs.shape[0]
    live_mask = (jnp.arange(seq_length) < length).astype(jnp.float32)[:, None]
    grad_blend = cotangent * live_mask / token_total
    back_two = fetch_again(1)
    grad_carried, grads_two = layer_backward(
        alpha_second[hist_count + 1] * grad_blend, back_two, state_two, length
    )
    shard_two = reduce_grads(grads_two)
    grad_first = alpha_first[hist_count] * grad_carried + alpha_second[hist_count] * grad_blend
    back_one = fetch_again(0)
    grad_inputs, grads_one = layer_backward(grad_first, back_one, state_one, length)
    shard_one = reduce_grads(grads_one)
    grad_history = jnp.stack(
        [
            alpha_first[entry] * grad_carried + alpha_second[entry] * grad_blend
            for entry in range(hist_count)
        ]
    )
    first_terms = []
    second_terms = []
    for entry in range(hist_count):
        past_row = history[entry].astype(jnp.float32)
        first_terms.append(jnp.sum(past_row * grad_carried))
        second_terms.append(jnp.sum(past_row * grad_blend))
    first_terms.append(jnp.sum(kept_one * grad_carried))
    second_terms.append(jnp.sum(kept_one * grad_blend))
    second_terms.append(jnp.sum(kept_two * grad_blend))
    grad_alpha_first, grad_alpha_second = lax.psum(
        (jnp.stack(first_terms), jnp.stack(second_terms)), ("wide", "narrow")
    )
    return (
        blended,
        jnp.stack([kept_one, kept_two]),
        grad_inputs,
        grad_history,
        jnp.stack([shard_one[0], shard_two[0]]),
        jnp.stack([shard_one[1], shard_two[1]]),
        jnp.stack([shard_one[2], shard_two[2]]),
        jnp.stack([shard_one[3], shard_two[3]]),
        jnp.stack([shard_one[4], shard_two[4]]),
        grad_alpha_first,
        grad_alpha_second,
    )


GATHER_KINDS = "accacc"
GATHER_ORDER = (
    200, 100, 210, 0, 30, 400, 110, 40, 21, 22, 31, 300, 240, 32, 23, 121, -1, 122, 123, 140, 150, 33, 321,
    141, 142, 322, 41, 42, 323, 500, 410, 50, 43, 53, 330, 331, 221, 222, 223, 152, 51, 143, 52, -1, 332, 333,
    340, 350, 341, 351, 440, 421, 422, -1, -1, -1, 510, -1, -1, -1, -1, -1, -1, -1, -1, -1, -1, -1, -1, -1,
    -1, 151, 342, 343, 423, 250, 241, 242, 243, 352, 153, -1, -1, -1, -1, -1, -1, -1, -1, -1, -1, 450, 252,
    353, 251, -1, -1, 441, 442, 521, 522, 253, -1, -1, -1, -1, -1, -1, -1, -1, -1, -1, -1, -1, -1, -1, -1, -1,
    -1, -1, -1, 523, 451, 443, 453, 540, 550, 541, 542, 543, 452, -1, -1, -1, -1, -1, -1, -1, -1, -1, -1, 551,
    -1, 552, -1, 553, -1, -1,
)
SCATTER_KINDS = "acacac"
SCATTER_ORDER = (
    -1, -1, 553, -1, -1, 551, 543, 552, -1, -1, 550, -1, -1, -1, 542, 541, 540, -1, -1, -1, -1, -1, -1, 523,
    -1, -1, -1, 453, 452, 451, 450, -1, 443, -1, 442, -1, 441, -1, -1, -1, -1, -1, -1, -1, -1, 522, 521, 440,
    433, 432, -1, -1, -1, -1, -1, -1, -1, -1, -1, -1, 351, 352, 353, -1, -1, -1, -1, 431, 350, 343, 423, 422,
    510, 342, 341, 340, 323, 421, 430, 500, -1, -1, 253, -1, 243, 252, -1, 242, 251, -1, 241, 250, -1, -1, -1,
    -1, 322, 321, 233, 400, -1, -1, -1, -1, -1, -1, -1, -1, -1, 152, 153, 151, -1, 143, -1, 142, -1, 141, -1,
    -1, -1, -1, -1, -1, -1, -1, 310, 240, 123, 232, 231, 150, 140, 223, 300, -1, -1, -1, -1, -1, -1, -1, -1,
    53, 52, 50, -1, -1, -1, -1, 43, 42, 122, 121, 33, 51, 41, 40, 230, 23, 222, 221, 110, 32, 31, 22, 30, 21,
    100, 200, 0,
)
NEXT = -1


def steps(codes):
    return [v if v == NEXT else (v // 100, "oplaqd"[v // 10 % 10], v % 10) for v in codes]


def al(v, m): return pl.multiple_of(v, m)
def when(cond, fn): pl.when(cond)(fn)

class Place:
    def __init__(self, depth):
        self.depth = depth
        w = lax.axis_index("wide"); n = lax.axis_index("narrow")
        self.w, self.n = w, n
        self.z, self.x = w // 2, lax.rem(w, 2)
        self.y, self.c = n // 2, lax.rem(n, 2)
        first = self.c == 0
        p = jnp.where(first, self.x, self.y)
        q = jnp.where(first, self.y, self.x)
        self.sib = (w, self.y * 2 + 1 - self.c)
        self.xn = (self.z * 2 + 1 - self.x, n)
        self.yn = (w, (1 - self.y) * 2 + self.c)
        self.pn = tuple(jnp.where(first, a, b) for a, b in zip(self.xn, self.yn))
        self.qn = tuple(jnp.where(first, b, a) for a, b in zip(self.xn, self.yn))
        self.has_up = self.z < depth - 1
        self.has_down = self.z > 0
        self.up = (w + 2, n)
        self.down = (w - 2, n)
        self.line = [(lax.rem(w + 2 * i, 2 * depth), n) for i in range(1, depth)]
        self.chip = self.z * 4 + self.x * 2 + self.y
        self.planes = [self.plane(r) for r in range(depth)]
        self.chips = [[[z * 4 + jnp.where(first, 2, 1) * (1 - p if a else p) + jnp.where(first, 1, 2) * (1 - q if b else q)
                        for z in self.planes] for b in (0, 1)] for a in (0, 1)]
        self.onward_up = [(z < self.z) & self.has_up for z in self.planes]
        self.onward_down = [(z > self.z) & self.has_down for z in self.planes]
    def plane(self, r):
        if r == 0: return self.z
        z, last = self.z, self.depth - 1
        short = jnp.minimum(z, last - z)
        low = z * 2 < self.depth
        dist = jnp.where(r <= 2 * short, (r + 1) // 2, r - short)
        below = jnp.where((r <= 2 * short) & (r % 2 == 1), low, ~low)
        return jnp.where(below, z - dist, z + dist)

class Gather:
    def __init__(self, me, chunks, ssem, rsem):
        self.me, self.chunks, self.ssem, self.rsem = me, chunks, ssem, rsem
    def copy(self, k, chip, way, target, sem):
        ref = self.chunks[k][1](chip, 1)
        return pltpu.make_async_remote_copy(src_ref=ref, dst_ref=ref, send_sem=self.ssem.at[k, way],
            recv_sem=self.rsem.at[k, sem], device_id=target, device_id_type=MESH)
    def plane_copy(self, k, r):
        ref = self.chunks[k][2](self.me.planes[r])
        return pltpu.make_async_remote_copy(src_ref=ref, dst_ref=ref, send_sem=self.ssem.at[k, 4],
            recv_sem=self.rsem.at[k, 3 * self.me.depth + self.me.planes[r]], device_id=self.me.sib, device_id_type=MESH)
    def p(self, k, chip, r): self.copy(k, chip, 0, self.me.pn, 2 * self.me.depth + self.me.planes[r]).start()
    def q(self, k, chip, r): self.copy(k, chip, 1, self.me.qn, self.me.planes[r]).start()
    def up(self, k, chip, r): self.copy(k, chip, 2, self.me.up, self.me.depth + self.me.planes[r]).start()
    def down(self, k, chip, r): self.copy(k, chip, 3, self.me.down, self.me.depth + self.me.planes[r]).start()
    def wait(self, k, n, sem):
        ref = self.chunks[k][1](0, n)
        pltpu.make_async_remote_copy(src_ref=ref, dst_ref=ref, send_sem=self.ssem.at[k, 0], recv_sem=self.rsem.at[k, sem],
            device_id=self.me.pn, device_id_type=MESH).wait_recv()
    def event(self, k, what, r):
        me, Z = self.me, self.me.depth
        kind = self.chunks[k][0]
        own, flip = me.chips[0][0][r], me.chips[1][0][r]
        if what == "o":
            when(me.has_up, lambda: self.up(k, own, 0))
            when(me.has_down, lambda: self.down(k, own, 0))
            self.p(k, own, 0)
            self.q(k, own, 0)
        elif what == "p":
            self.wait(k, 1, 2 * Z + me.planes[0])
            when(me.has_up, lambda: self.up(k, flip, 0))
            when(me.has_down, lambda: self.down(k, flip, 0))
            self.q(k, flip, 0)
        elif what == "l":
            both = (own, flip) if kind == "c" else (own,)
            self.wait(k, len(both), Z + me.planes[r])
            def fwd(send):
                for chip in both: send(k, chip, r)
            when(me.onward_up[r], lambda: fwd(self.up))
            when(me.onward_down[r], lambda: fwd(self.down))
            if kind == "a": self.p(k, own, r)
            for chip in both: self.q(k, chip, r)
        elif what == "a":
            self.wait(k, 1, 2 * Z + me.planes[r])
            self.q(k, flip, r)
        elif what == "q":
            self.wait(k, 2, me.planes[r])
            self.plane_copy(k, r).start()
        elif what == "d":
            self.plane_copy(k, r).wait_recv()
    def drain(self, k):
        me, Z = self.me, self.me.depth
        per = 2 if self.chunks[k][0] == "c" else 1
        counts = [1 if per == 2 else Z, 2 * Z, jnp.where(me.has_up, per * (me.z + 1), 0), jnp.where(me.has_down, per * (Z - me.z), 0)]
        for way, count in enumerate(counts):
            def one(_, carry):
                self.copy(k, 0, way, me.pn, 0).wait_send()
                return carry
            lax.fori_loop(0, count, one, 0)
        def one(_, carry):
            self.plane_copy(k, 0).wait_send()
            return carry
        lax.fori_loop(0, Z, one, 0)

def greet(me, whole_line=False):
    bar = pltpu.get_barrier_semaphore()
    def signal(d): pl.semaphore_signal(bar, inc=1, device_id=d, device_id_type=MESH)
    for d in (me.sib, me.xn, me.yn): signal(d)
    if whole_line:
        for d in me.line: signal(d)
    else:
        when(me.has_up, lambda: signal(me.up))
        when(me.has_down, lambda: signal(me.down))
    return bar


def greeted(me, bar, whole_line=False):
    line = len(me.line) if whole_line else me.has_up.astype(jnp.int32) + me.has_down.astype(jnp.int32)
    pl.semaphore_wait(bar, 3 + line)


def add_into(dst, sources, rows, out=None):
    step = 48 if rows % 48 == 0 else 16
    @pl.loop(0, rows // step)
    def _(i):
        at = pl.ds(al(i * step, 16), step)
        if out is None and len(sources) == 1:
            dst[at, :] = dst[at, :] + sources[0][at, :]
            return
        total = dst[at, :].astype(F32)
        for s in sources: total = total + s[at, :].astype(F32)
        if out is None: dst[at, :] = total.astype(dst.dtype)
        else: out[at, :] = total


class Scatter:
    def __init__(self, me, chunks, ssem, rsem):
        self.me, self.chunks, self.ssem, self.rsem = me, chunks, ssem, rsem
        Z = me.depth
        self.Z = Z
        self.q_slot = lambda flip, z: (Z if flip else 0) + z
        self.line_slot = lambda flip, z: 2 * Z + (Z if flip else 0) + z
        self.late_slot = lambda flip: 4 * Z + (1 if flip else 0)
        self.p_slot = lambda kind, z: 3 * Z + z if kind == "a" else 4 * Z + 2
        self.slots = 4 * Z + 3
    def land(self, k, slot): return self.chunks[k].land(slot)
    def copy(self, k, chip, way, target, slot):
        ch = self.chunks[k]
        return pltpu.make_async_remote_copy(src_ref=ch.share(chip), dst_ref=ch.land(slot), send_sem=self.ssem.at[k, way],
            recv_sem=self.rsem.at[k, slot], device_id=target, device_id_type=MESH)
    def plane_copy(self, k, r):
        ch, me = self.chunks[k], self.me
        z = me.planes[r]
        return pltpu.make_async_remote_copy(src_ref=ch.plane(z, False), dst_ref=ch.plane_land(z), send_sem=self.ssem.at[k, 4],
            recv_sem=self.rsem.at[k, self.slots + z], device_id=me.sib, device_id_type=MESH)
    def wait(self, k, slot):
        self.copy(k, 0, 0, self.me.pn, slot).wait_recv()
    def take(self, k, chip, slots, out=None):
        ch = self.chunks[k]
        for s in slots: self.wait(k, s)
        add_into(ch.share(chip), [ch.land(s) for s in slots], ch.rows, out)
    def event(self, k, what, r):
        me, Z = self.me, self.Z
        ch = self.chunks[k]
        kind = ch.kind
        own, flip = me.chips[0][0][r], me.chips[1][0][r]
        z = me.planes[r]
        if what == "d":
            self.plane_copy(k, r).start()
        elif what == "q":
            self.plane_copy(k, r).wait_recv()
            ch.plane_add(z)
            self.copy(k, me.chips[0][1][r], 1, me.qn, self.q_slot(False, z)).start()
            self.copy(k, me.chips[1][1][r], 1, me.qn, self.q_slot(True, z)).start()
        elif what == "a":
            self.take(k, flip, [self.q_slot(True, z)])
            self.copy(k, flip, 0, me.pn, self.p_slot(kind, z)).start()
        elif what == "l":
            first = [self.q_slot(False, z)] + ([self.p_slot(kind, z)] if kind == "a" else [])
            self.take(k, own, first)
            if kind == "c": self.take(k, flip, [self.q_slot(True, z)])
            flips = (False, True) if kind == "c" else (False,)
            def behind():
                for f in flips: self.take(k, flip if f else own, [self.line_slot(f, z)])
            when((z < me.z) & me.has_up, behind)
            when((z > me.z) & me.has_down, behind)
            def send(way, target, late):
                for f in flips:
                    self.copy(k, flip if f else own, way, target, self.late_slot(f) if late else self.line_slot(f, z)).start()
            when((z > me.z) & (z == me.z + 1), lambda: send(2, me.up, False))
            when((z > me.z) & (z != me.z + 1), lambda: send(2, me.up, False))
            when((z < me.z) & (z == me.z - 1), lambda: send(3, me.down, True))
            when((z < me.z) & (z != me.z - 1), lambda: send(3, me.down, False))
        elif what in "po":
            f = what == "p"
            chip = flip if f else own
            slots = [self.q_slot(f, z)]
            if not f: slots.append(self.p_slot(kind, z))
            when(me.has_down, lambda: self.take(k, chip, [self.line_slot(f, z)]))
            when(me.has_up, lambda: self.take(k, chip, [self.late_slot(f)]))
            self.take(k, chip, slots, None if f else ch.result)
            if f: self.copy(k, chip, 0, me.pn, self.p_slot(kind, z)).start()
    def drain(self, k):
        me, Z = self.me, self.Z
        per = 2 if self.chunks[k].kind == "c" else 1
        counts = [1 if per == 2 else Z, 2 * Z, jnp.where(me.has_up, per * (Z - 1 - me.z), 0), jnp.where(me.has_down, per * me.z, 0)]
        for way, count in enumerate(counts):
            def one(_, carry):
                self.copy(k, 0, way, me.pn, 0).wait_send()
                return carry
            lax.fori_loop(0, count, one, 0)
        def one(_, carry):
            self.plane_copy(k, 0).wait_send()
            return carry
        lax.fori_loop(0, Z, one, 0)


def dot(a, b):
    return jnp.dot(a, b, preferred_element_type=F32)


def dot_nt(a, b):
    return lax.dot_general(a, b, (((1,), (1,)), ((), ())), preferred_element_type=F32)


def dot_tn(a, b):
    return lax.dot_general(a, b, (((0,), (0,)), ((), ())), preferred_element_type=F32)


def normalized(h):
    center = h - jnp.mean(h, axis=-1, keepdims=True)
    inverse = lax.rsqrt(jnp.mean(center * center, axis=-1, keepdims=True) + norm_eps)
    return center * inverse, inverse


def swap_halves(v, half):
    lanes = lax.broadcasted_iota(jnp.int32, v.shape, 1)
    width = v.shape[1]
    return jnp.where(lanes % (2 * half) < half, pltpu.roll(v, width - half, 1), pltpu.roll(v, half, 1))


def rotary_lanes(seq_length, head_width, lanes):
    half = head_width // 2
    frequency = (10000.0 ** (-np.arange(half, dtype=np.float32) / half)).astype(np.float32)
    angles = np.arange(seq_length, dtype=np.float32)[:, None] * frequency[None, :]
    cos, sin = np.cos(angles), np.sin(angles)
    both = np.stack([np.concatenate([cos, cos], 1), np.concatenate([-sin, sin], 1)])
    return np.tile(both, (1, 1, lanes // head_width)).astype(np.float32)


def add_sum(ref, row, lane, product):
    rows = lax.broadcasted_iota(jnp.int32, ref.shape, 0)
    lanes = lax.broadcasted_iota(jnp.int32, ref.shape, 1)
    total = jnp.sum(jnp.sum(product, axis=0, keepdims=True), axis=1, keepdims=True)
    ref[...] = ref[...] + jnp.where((rows == row) & (lanes == lane), total, 0.0)


class Forward:
    def __init__(self, w, io, s, planes, length, first, second):
        self.planes = planes
        self.w, self.io, self.s = w, io, s
        self.length, self.first, self.second = length, first, second
        self.T, self.D = s.h.shape
        self.width = self.D // HEADS
        self.q, self.o = 3 * self.D // 2, self.D // 2
        self.half = w.mix.shape[2] // 2
        self.writes = []

    def send(self, name, l=None):
        src, dst = getattr(self.s, name), getattr(self.io, name)
        if l is not None: src, dst = src.at[l], dst.at[l]
        n = len(self.writes)
        self.writes.append((src, dst, n))
        pltpu.make_async_copy(src, dst, self.io.wsem.at[n]).start()

    def finish(self):
        for src, dst, n in self.writes:
            pltpu.make_async_copy(src, dst, self.io.wsem.at[n]).wait()

    def load(self, i):
        s, io = self.s, self.io
        src, dst = ((io.h, s.h), (io.rope, s.rope), (io.cotangent, s.cotangent), (io.history, s.history))[i]
        return pltpu.make_async_copy(src, dst, io.isem.at[i])

    def setup(self):
        s, T = self.s, self.T
        row = lax.broadcasted_iota(jnp.int32, (T, T), 0)
        col = lax.broadcasted_iota(jnp.int32, (T, T), 1)
        s.bias[...] = jnp.where((col <= row) & (col < self.length), 0.0, masked_score)
        s.sums[...] = jnp.zeros_like(s.sums)

    def loss_grad(self):
        s, io = self.s, self.io
        count = jnp.sum(s.gain[4:5, :])
        row = lax.broadcasted_iota(jnp.int32, (self.T, 1), 0)
        grad = jnp.where(row < self.length, s.cotangent[...], 0.0) / count
        s.gout[...] = grad
        self.send("gout")
        n = s.history.shape[0]
        for j in range(n): add_sum(s.sums, 1, j, s.history[j].astype(F32) * grad)

    def layer_in(self, l):
        return self.s.h if l == 0 else self.s.carried

    def norm_one(self, l):
        s, w = self.s, self.w
        if l == 0:
            s.gain[...] = s.total[...]
            self.send("gain")
            for i in range(4): self.load(i).wait()
        x, _ = normalized(self.layer_in(l)[...])
        s.n1[l] = (x * s.gain[2 * l:2 * l + 1, :]).astype(BF)
        self.send("n1", l)

    def project(self, l, t):
        s, w = self.s, self.w
        h, i = divmod(t, 3)
        W = self.q // 3
        at = h * self.half + i * W
        joined = dot(s.n1[l], w.mix[l, :, at:at + W])
        for j in range(W // 128):
            col = t * W + j * 128
            part = joined[:, j * 128:(j + 1) * 128]
            if col < 2 * self.D:
                part = part * s.cos[...] + swap_halves(part, self.width // 2) * s.sin[...]
                if col < self.D: part = part * self.width ** -0.5
            s.qkv[l, :, col:col + 128] = part.astype(BF)

    def attend(self, l, a):
        s, D = self.s, self.D
        q, k, v = (s.qkv[l, :, i * D + a * 128:i * D + a * 128 + 128] for i in range(3))
        lanes = lax.broadcasted_iota(jnp.int32, q.shape, 1)
        outs = []
        for e in range(2):
            mine = (lanes < self.width) if e == 0 else (lanes >= self.width)
            scores = dot_nt(jnp.where(mine, q, jnp.zeros_like(q)), k) + s.bias[...]
            top = jnp.max(scores, axis=-1, keepdims=True)
            weights = jnp.exp(scores - top)
            probs = (weights * (1.0 / jnp.sum(weights, axis=-1, keepdims=True))).astype(BF)
            s.probs[l, 2 * a + e] = probs
            outs.append(dot(probs, v))
        s.att[l, :, a * 128:a * 128 + 128] = jnp.where(lanes < self.width, outs[0], outs[1]).astype(BF)

    def attend_done(self, l):
        for name in ("qkv", "probs", "att"): self.send(name, l)

    def out(self, l, h):
        s, w = self.s, self.w
        cols = slice(h * self.o, (h + 1) * self.o)
        at = h * self.half + self.q
        s.after[l, :, cols] = self.layer_in(l)[:, cols] + dot(s.att[l], w.mix[l, :, at:at + self.o])

    def norm_two(self, l):
        s = self.s
        x, _ = normalized(s.after[l])
        s.n2[l] = (x * s.gain[2 * l + 1:2 * l + 2, :]).astype(BF)
        self.send("n2", l)
        self.send("after", l)

    def raise_(self, l, t, W):
        s, w = self.s, self.w
        u = dot(s.n2[l], w.up[l, :, t * W:(t + 1) * W])
        tile, at = divmod(t * W, self.D)
        cols = slice(at, at + W)
        square = u * u
        tangent = jnp.tanh(gelu_scale * u * (1.0 + gelu_coef * square))
        s.act[l, tile, :, cols] = (0.5 * u * (1.0 + tangent)).astype(BF)
        s.slope[l, tile, :, cols] = (
            0.5 * (1.0 + tangent) + 0.5 * u * (1.0 - tangent * tangent) * gelu_scale * (1.0 + 3.0 * gelu_coef * square)
        ).astype(BF)

    def raise_done(self, l):
        for name in ("act", "slope"): self.send(name, l)

    def lower(self, l, r):
        s, w = self.s, self.w
        z = self.planes[r]
        chips = w.down.shape[1] // len(self.planes)
        part = dot(s.act[l, z], w.down[l, pl.ds(z * chips, chips)].reshape(-1, self.D))
        s.stored[l] = (s.after[l] if r == 0 else s.stored[l]) + part

    def mixed(self, l):
        s, io = self.s, self.io
        n = s.history.shape[0]
        if l == 0:
            s.carried[...] = mix_history([self.first[j] for j in range(n)], s.history) + self.first[n] * s.stored[0]
            self.send("carried")
        else:
            s.blended[...] = (
                mix_history([self.second[j] for j in range(n)], s.history)
                + self.second[n] * s.stored[0] + self.second[n + 1] * s.stored[1]
            )
            self.send("blended")
        self.send("stored", l)
        add_sum(s.sums, 1, n + l, s.stored[l] * s.gout[...])
        if l == 1: self.send("sums")

    def steps(self):
        out = [(-1, self.setup)]
        P = functools.partial
        for l in range(2):
            k = 3 * l
            out.append((k, P(self.norm_one, l)))
            out += [(k, P(self.project, l, t)) for t in range(6)]
            if l == 0: out.append((k, self.loss_grad))
            out += [(k, P(self.attend, l, a)) for a in range(self.D // 128)]
            out.append((k, P(self.attend_done, l)))
            out += [(k, P(self.out, l, h)) for h in range(2)]
            out.append((k, P(self.norm_two, l)))
            W = self.D // 2
            out += [(k + 1, P(self.raise_, l, t, W)) for t in range(4 * self.D // W)]
            out.append((k + 1, P(self.raise_done, l)))
            out += [((k + 2, r), P(self.lower, l, r)) for r in range(len(self.planes))]
            out.append((k + 2, P(self.mixed, l)))
        return out


def weave(order, work):
    left, whole, done, queue = {}, set([-1]), [], list(work)
    for v in order:
        if v != NEXT and v[1] == "d": left[v[0]] = left.get(v[0], 0) + 1
    for v in order:
        if v == NEXT:
            need, act = queue.pop(0)
            assert need in whole
            done.append(act)
            continue
        done.append(v)
        k, what, r = v
        if what == "d":
            whole.add((k, r))
            left[k] -= 1
            if not left[k]: whole.add(k)
    assert not queue
    return done


def saved_shapes(T, D, FF):
    return dict(n1=((2, T, D), BF), qkv=((2, T, 3 * D), BF), probs=((2, HEADS, T, T), BF), att=((2, T, D), BF), after=((2, T, D), F32),
        n2=((2, T, D), BF), act=((2, FF // D, T, D), BF), slope=((2, FF // D, T, D), BF), stored=((2, T, D), F32), carried=((T, D), F32),
        blended=((T, D), F32), gout=((T, D), F32), sums=((8, D), F32), gain=((8, D), F32))


SAVED = tuple(saved_shapes(1, 1, 1))


def fwd_kernel(depth, order, kinds, qkv_in, out_in, up_in, down_in, gain_in, h_in, history_in, cotangent_in, rope_in, length, first, second,
              mix_o, up_o, down_o, *rest):
    n = len(SAVED)
    saved_o, rest = rest[:n], rest[n:]
    (mix_b, up_b, down_b, mix_s, up_s, mix_t, up_t, ssem, rsem, esem, lsem, wsem, isem, bias, value, land, h_b, history_b, cotangent_b,
        rope_b, tsend, trecv), saved_b = rest[:22], rest[22:]
    me = Place(depth)
    bar = greet(me, True)
    rows = qkv_in.shape[1]
    c = me.c
    wq, wo, wu = qkv_in.shape[2] // 2, out_in.shape[2] // 2, up_in.shape[2] // 2
    mine = lambda w: pl.ds(al(c * w, 128), w)
    other = lambda w: pl.ds(al((1 - c) * w, 128), w)
    my_rows = pl.ds(al(c * rows, 8), rows)
    def stage(k):
        l, j = divmod(k, 3)
        if j == 0:
            for ref, at, pick in ((mix_s, (l, my_rows), mine), (mix_t, (l, slice(None)), other)):
                ref[at[0], at[1], 0:wq] = qkv_in[l, :, pick(wq)].astype(F32)
                ref[at[0], at[1], wq:wq + wo] = out_in[l, :, pick(wo)].astype(F32)
        elif j == 1:
            up_s[l, my_rows, :] = up_in[l, :, mine(wu)].astype(F32)
            up_t[l] = up_in[l, :, other(wu)].astype(F32)
    def place_gains():
        small = value.at[2]
        small[...] = jnp.zeros_like(small)
        for l in range(2): small[2 * l:2 * l + 2, 0:rows] = gain_in[l].astype(F32)
        n = value.shape[2]
        at = rows * (me.w * 4 + me.n)
        one = lax.broadcasted_iota(jnp.int32, (128, n), 1) == lax.broadcasted_iota(jnp.int32, (128, n), 0) + at
        own = dot(small[:, 0:128].astype(BF), one.astype(BF))
        row = lax.broadcasted_iota(jnp.int32, own.shape, 0)
        col = lax.broadcasted_iota(jnp.int32, own.shape, 1)
        value[0] = own + jnp.where((row == 4) & (col == 0), length[0].astype(F32), 0.0)
    def exchange(k):
        l, j = divmod(k, 3)
        if j == 2: return None
        s, t = ((mix_s, mix_t), (up_s, up_t))[j]
        return pltpu.make_async_remote_copy(src_ref=t.at[l], dst_ref=s.at[l, my_rows, :], send_sem=esem.at[0, k],
            recv_sem=esem.at[1, k], device_id=me.sib, device_id_type=MESH)
    def ready(k):
        l, j = divmod(k, 3)
        if j == 2:
            down_b[l, me.chip, c] = down_in[l]
            return
        exchange(k).wait_recv()
        s, b = ((mix_s, mix_b), (up_s, up_b))[j]
        b[l, pl.ds(al(me.chip * 2 * rows, 16), 2 * rows), mine(s.shape[2])] = s[l].astype(BF)
    chunks = []
    for k in range(6):
        l, j = divmod(k, 3)
        if j == 2:
            chunks.append((kinds[k], lambda chip, n, l=l: down_b.at[l, pl.ds(chip, n), c], lambda z, l=l: down_b.at[l, pl.ds(z * 4, 4), c]))
        else:
            b = (mix_b, up_b)[j]
            half = b.shape[2] // 2
            chunks.append((kinds[k],
                lambda chip, n, b=b, l=l, half=half: b.at[l, pl.ds(al(chip * 2 * rows, 16), n * 2 * rows), mine(half)],
                lambda z, b=b, l=l, half=half: b.at[l, pl.ds(al(z * 8 * rows, 16), 8 * rows), mine(half)]))
    gather = Gather(me, chunks, ssem, rsem)
    io = SimpleNamespace(**dict(zip(SAVED, saved_o)), h=h_in, history=history_in, cotangent=cotangent_in, rope=rope_in,
        wsem=wsem, isem=isem)
    scratch = SimpleNamespace(**dict(zip(SAVED, saved_b)), bias=bias, total=value.at[4], h=h_b, history=history_b,
        cotangent=cotangent_b, rope=rope_b, cos=rope_b.at[0], sin=rope_b.at[1])
    fwd = Forward(SimpleNamespace(mix=mix_b, up=up_b, down=down_b), io, scratch, me.planes, length[0], first, second)
    first_out = []
    for v in order:
        if v != NEXT and v[1] == "o" and v[0] % 3 < 2: first_out.append(v[0])
    stage(first_out[0])
    greeted(me, bar, True)
    exchange(first_out[0]).start()
    place_gains()
    total = Total(me, value, land, tsend, trecv)
    total.step(0)
    for k in first_out[1:]:
        stage(k)
        exchange(k).start()
    for i in range(4): fwd.load(i).start()
    pairs = ((mix_b, mix_o), (up_b, up_o), (down_b, down_o))
    def write(k, r):
        l, j = divmod(k, 3)
        b, o = pairs[j]
        n = b.shape[1] // depth
        at = pl.ds(al(me.planes[r] * n, n), n)
        return pltpu.make_async_copy(b.at[l, at], o.at[l, at], lsem.at[k, r])
    totals, count = [1, 2, 3, 4], 0
    for item in weave(order, fwd.steps()):
        if not isinstance(item, tuple):
            item()
            continue
        k, what, r = item
        if what == "o": ready(k)
        gather.event(k, what, r)
        if what == "d": write(k, r).start()
        count += 1
        if totals and count % 5 == 0: total.step(totals.pop(0))
    for k in range(6):
        gather.drain(k)
        if k % 3 < 2: exchange(k).wait_send()
    for k in range(6):
        for r in range(depth): write(k, r).wait()
    fwd.finish()

def fwd_call(mesh, order, kinds, w_qkv, w_out, w_up, w_down, gains, h, history, cotangent, rope, lengths, first, second):
    depth = mesh.shape["wide"] // 2
    rows = w_qkv.shape[1]
    D, FF = rows * mesh.size, w_down.shape[1] * mesh.size
    T = h.shape[0]
    n = mesh.size // 2
    M = 4 * D
    body = functools.partial(fwd_kernel, depth, order, kinds)
    vm = pl.BlockSpec(memory_space=pltpu.VMEM); an = pl.BlockSpec(memory_space=pl.ANY); sm = pl.BlockSpec(memory_space=pltpu.SMEM)
    shapes = [((2, D, M), BF), ((2, D, FF), BF), ((2, n, 2, FF // n // 2, D), BF)]
    saved = list(saved_shapes(T, D, FF).values())
    got = pl.pallas_call(body,
        out_shape=[jax.ShapeDtypeStruct(s, d) for s, d in shapes + saved],
        in_specs=[vm] * 5 + [an] * 4 + [sm] * 3, out_specs=[an] * (3 + len(saved)),
        scratch_shapes=[pltpu.VMEM(s, d) for s, d in shapes] + [
            pltpu.VMEM((2, 2 * rows, M // 2), F32), pltpu.VMEM((2, 2 * rows, FF // 2), F32),
            pltpu.VMEM((2, rows, M // 2), F32), pltpu.VMEM((2, rows, FF // 2), F32),
            pltpu.SemaphoreType.DMA((6, 5)), pltpu.SemaphoreType.DMA((6, 4 * depth)),
            pltpu.SemaphoreType.DMA((2, 6)), pltpu.SemaphoreType.DMA((6, depth)), pltpu.SemaphoreType.DMA((24,)),
            pltpu.SemaphoreType.DMA((4,)), pltpu.VMEM((T, T), F32), pltpu.VMEM((5, 8, D), F32), pltpu.VMEM((2 + depth, 8, D), F32),
            pltpu.VMEM(h.shape, F32), pltpu.VMEM(history.shape, BF), pltpu.VMEM(cotangent.shape, F32), pltpu.VMEM(rope.shape, F32), pltpu.SemaphoreType.DMA((2 + depth,)), pltpu.SemaphoreType.DMA((2 + depth,))] + [pltpu.VMEM(s, d) for s, d in saved],
        compiler_params=pltpu.CompilerParams(collective_id=0, has_side_effects=True, vmem_limit_bytes=62 * 2**20),
        cost_estimate=pl.CostEstimate(flops=16 * T * D * FF, bytes_accessed=2**26, transcendentals=2**21),
    )(w_qkv, w_out, w_up, w_down, gains, h, history, cotangent, rope, lengths, first, second)
    return got[:3], SimpleNamespace(**dict(zip(SAVED, got[3:])))


def norm_back(e, h, gain):
    unit, inverse = normalized(h)
    scaled = e * gain
    grad = inverse * (scaled - jnp.mean(scaled, axis=-1, keepdims=True) - unit * jnp.mean(scaled * unit, axis=-1, keepdims=True))
    return grad, jnp.sum(e * unit, axis=0, keepdims=True)


class Backward:
    def __init__(self, io, s, g, planes, first, second):
        self.planes = planes
        self.io, self.s, self.g = io, s, g
        self.first, self.second = first, second
        self.T, self.D = s.gy.shape
        self.width = self.D // HEADS
        self.q, self.o = 3 * self.D // 2, self.D // 2
        self.half = g.mix.shape[1] // 2
        self.tiles = s.act.shape[0]
        self.hist = io.history.shape[0]
        self.writes = []

    SLOTS = ("act", "slope", "n2", "n1", "att", "after", "h", "probs", "qkv", "mix", "history")

    def load(self, name, src, dst=None):
        i = self.SLOTS.index(name)
        return pltpu.make_async_copy(src, getattr(self.s, name) if dst is None else dst, self.io.load_sem.at[i])

    def source(self, name, l):
        return getattr(self.io, name).at[l]

    def fetch(self, l, names):
        for name in names:
            src = (self.io.inputs if l == 0 else self.io.carried) if name == "h" else getattr(self.io, name).at[l]
            self.load(name, src).start()

    def here(self, l, *names):
        for name in names:
            src = (self.io.inputs if l == 0 else self.io.carried) if name == "h" else getattr(self.io, name).at[l]
            self.load(name, src).wait()

    def tile_copy(self, l, t, up):
        src = self.io.up.at[l, :, pl.ds(t * self.D, self.D)] if up else self.io.down.at[l, t]
        return pltpu.make_async_copy(src, self.s.tile.at[t], self.io.tile_sem.at[t])

    def send(self, src, dst):
        n = len(self.writes)
        self.writes.append((src, dst, n))
        pltpu.make_async_copy(src, dst, self.io.write_sem.at[n]).start()

    def finish(self):
        for src, dst, n in self.writes:
            pltpu.make_async_copy(src, dst, self.io.write_sem.at[n]).wait()

    def begin(self):
        self.fetch(1, ("act",))
        for t in range(self.tiles): self.tile_copy(1, t, False).start()
        self.fetch(1, ("slope", "n2", "after", "mix", "att", "probs", "qkv", "n1", "h"))
        self.load("history", self.io.history).start()
        s = self.s
        s.gy[...] = self.second[self.hist + 1] * self.io.gout[...]

    def down_weight(self, l, r):
        s = self.s
        if r == len(self.planes) - 1:
            s.gm[...] = s.gy[...].astype(BF)
            self.here(l, "act")
        z = self.planes[r]
        chips = self.g.down.shape[0] // len(self.planes)
        grad = dot_tn(s.act[z], s.gm[...])
        self.g.down[pl.ds(z * chips, chips)] = grad.astype(BF).reshape((chips,) + self.g.down.shape[1:])

    def act_grad(self, l, t):
        s = self.s
        if t == 0: self.here(l, "slope")
        self.tile_copy(l, t, False).wait()
        grad = dot_nt(s.gm[...], s.tile[t])
        s.slope[t] = (grad * s.slope[t].astype(F32)).astype(BF)
        self.tile_copy(l, t, True).start()

    def turned(self, l, name):
        self.here(l, name)
        self.s.turned[...] = getattr(self.s, name)[...].T

    def up_weight(self, l, t):
        s = self.s
        tile, at = divmod(t * self.o, self.D)
        self.g.up[:, t * self.o:(t + 1) * self.o] = dot(s.turned[...], s.slope[tile, :, at:at + self.o]).astype(BF)

    def norm_two_grad(self, l, t):
        s = self.s
        self.tile_copy(l, t, True).wait()
        part = dot_nt(s.slope[t], s.tile[t])
        if t == 0: s.gn[...] = part
        else: s.gn[...] = s.gn[...] + part
        if l == 1: self.tile_copy(0, t, False).start()

    def after_grad(self, l):
        s = self.s
        self.here(l, "after")
        grad, gain = norm_back(s.gn[...], s.after[...], self.io.gain[2 * l + 1:2 * l + 2, :])
        s.sums[3 + 2 * l:4 + 2 * l, :] = gain
        s.gy[...] = s.gy[...] + grad
        s.gm[...] = s.gy[...].astype(BF)
        if l == 1:
            self.fetch(0, ("slope", "n2", "act"))
            self.load("after", self.io.stored.at[0]).start()

    def out_weight(self, l, h):
        s = self.s
        if h == 0: self.turned(l, "att")
        at = h * self.half + self.q
        self.g.mix[:, at:at + self.o] = dot(s.turned[...], s.gm[:, h * self.o:(h + 1) * self.o]).astype(BF)

    def att_grad(self, l):
        s = self.s
        self.here(l, "mix")
        a, b = self.q, self.half + self.q
        grad = dot_nt(s.gm[:, :self.o], s.mix[:, a:a + self.o]) + dot_nt(s.gm[:, self.o:], s.mix[:, b:b + self.o])
        s.ga[...] = grad.astype(BF)

    def attend(self, l, a):
        s, D = self.s, self.D
        if a == 0: self.here(l, "probs", "qkv")
        q, k, v = (s.qkv[:, i * D + a * 128:i * D + a * 128 + 128] for i in range(3))
        ga = s.ga[:, a * 128:a * 128 + 128]
        lanes = lax.broadcasted_iota(jnp.int32, q.shape, 1)
        got = []
        for e in range(2):
            mine = (lanes < self.width) if e == 0 else (lanes >= self.width)
            probs = s.probs[2 * a + e]
            wide = probs.astype(F32)
            gp = wide * dot_nt(jnp.where(mine, ga, jnp.zeros_like(ga)), v)
            gs = (gp - wide * jnp.sum(gp, axis=-1, keepdims=True)).astype(BF)
            got.append((dot(gs, k), dot_tn(gs, q), dot_tn(probs, ga)))
        gq, gk, gv = (jnp.where(lanes < self.width, x, y) for x, y in zip(*got))
        back = lambda g: g * s.cos[...] - swap_halves(g, self.width // 2) * s.sin[...]
        for i, g in enumerate((back(gq) * self.width ** -0.5, back(gk), gv)):
            s.gj[:, i * D + a * 128:i * D + a * 128 + 128] = g.astype(BF)

    def qkv_weight(self, l, t):
        s = self.s
        if t == 0:
            self.turned(l, "n1")
            if l == 1: self.fetch(0, ("probs", "qkv", "n1", "att"))
        h, i = divmod(t, 3)
        W = self.q // 3
        at = h * self.half + i * W
        self.g.mix[:, at:at + W] = dot(s.turned[...], s.gj[:, t * W:(t + 1) * W]).astype(BF)

    def norm_one_grad(self, l, t):
        s = self.s
        W = self.D // 3
        rows = slice(t * W, (t + 1) * W)
        b = self.half
        s.gn[:, rows] = dot_nt(s.gj[:, :self.q], s.mix[rows, :self.q]) + dot_nt(s.gj[:, self.q:], s.mix[rows, b:b + self.q])

    def layer_grad(self, l):
        s = self.s
        self.here(l, "h")
        grad, gain = norm_back(s.gn[...], s.h[...], self.io.gain[2 * l:2 * l + 1, :])
        s.sums[2 + 2 * l:3 + 2 * l, :] = gain
        s.gy[...] = s.gy[...] + grad
        if l == 1: self.fetch(0, ("mix", "h"))
        if l == 1:
            s.kept[...] = s.gy[...]
            self.send(s.kept, self.io.grad_carried)
        else: self.send(s.gy, self.io.grad_inputs)

    def between(self):
        s, n = self.s, self.hist
        self.load("history", self.io.history).wait()
        self.load("after", self.io.stored.at[0]).wait()
        grad = s.gy[...]
        for j in range(n): add_sum(s.sums, 0, j, s.history[j].astype(F32) * grad)
        add_sum(s.sums, 0, n, s.after[...] * grad)
        s.gy[...] = self.first[n] * grad + self.second[n] * self.io.gout[...]
        self.fetch(0, ("after",))

    def steps(self):
        P = functools.partial
        out = [("do", -1, self.begin)]
        for l in (1, 0):
            k = 3 * l
            tiles = range(self.tiles)
            if l == 0: out.append(("do", -1, self.between))
            out += [("make", (k + 2, r), P(self.down_weight, l, r)) for r in reversed(range(len(self.planes)))]
            out += [("do", -1, P(self.act_grad, l, t)) for t in tiles]
            out.append(("do", -1, P(self.turned, l, "n2")))
            out += [("make", (k + 1, -1), P(self.up_weight, l, t)) for t in range(2 * self.tiles)]
            out += [("do", -1, P(self.norm_two_grad, l, t)) for t in tiles]
            out.append(("do", -1, P(self.after_grad, l)))
            out.append(("do", -1, P(self.att_grad, l)))
            out += [("do", -1, P(self.attend, l, a)) for a in range(self.D // 128)]
            out += [("make", (k, -1), P(self.out_weight, l, h)) for h in range(2)]
            out += [("make", (k, -1), P(self.qkv_weight, l, t)) for t in range(6)]
            out += [("do", -1, P(self.norm_one_grad, l, t)) for t in range(3)]
            out.append(("sums" if l == 0 else "do", -1, P(self.layer_grad, l)))
        return out


def weave_back(order, work):
    to_make, over, drained, done, queue = {}, set(), set(), [], list(work)
    for name, k, _ in work:
        if name == "make": to_make[k] = to_make.get(k, 0) + 1
    for v in order:
        if v == NEXT:
            name, k, act = queue.pop(0)
            if name == "make":
                before = k[0] + 3
                if k[0] < 3 and before not in drained:
                    assert before in over
                    drained.add(before)
                    done.append(("drain", before))
                to_make[k] -= 1
            done.append(act)
            if name == "sums": done.append(("sums", 0))
            continue
        k, what, r = v
        if what == "d": assert not to_make.get((k, r), 0) and not to_make.get((k, -1), 0)
        if what == "o": over.add(k)
        done.append(v)
    assert not queue
    return done


class Total:
    def __init__(self, me, value, land, ssem, rsem):
        self.me, self.value, self.land, self.ssem, self.rsem = me, value, land, ssem, rsem
    def copy(self, i, src, target):
        return pltpu.make_async_remote_copy(src_ref=src, dst_ref=self.land.at[i], send_sem=self.ssem.at[i], recv_sem=self.rsem.at[i],
            device_id=target, device_id_type=MESH)
    def step(self, n):
        me, v = self.me, self.value
        targets = (me.sib, me.xn, me.yn)
        if 0 < n <= 3:
            self.copy(n - 1, v.at[n - 1], targets[n - 1]).wait()
            v[n] = v[n - 1] + self.land[n - 1]
        if n < 3: self.copy(n, v.at[n], targets[n]).start()
        elif n == 3:
            for i, t in enumerate(me.line): self.copy(3 + i, v.at[3], t).start()
        else:
            total = v[3]
            for i, t in enumerate(me.line):
                self.copy(3 + i, v.at[3], t).wait()
                total = total + self.land[3 + i]
            v[4] = total


def bwd_kernel(depth, order, kinds, gout_in, sums_in, gain_in, rope_in, first, second, *rest):
    io, rest = SimpleNamespace(), rest
    (io.mix, io.up, io.down, io.n1, io.qkv, io.probs, io.att, io.after, io.n2, io.act, io.slope, io.stored, io.carried, io.inputs,
        io.history), rest = rest[:15], rest[15:]
    (mix_o, up_o, down_o, io.grad_carried, io.grad_inputs, sums_o), rest = rest[:6], rest[6:]
    (mix_g, up_g, down_g, mix_d, up_d, down_d, mix_l, up_l, down_l, mix_f, up_f, down_f,
        ssem, rsem, esem, credit, io.load_sem, io.tile_sem, io.write_sem, tsend, trecv, fsem), rest = rest[:22], rest[22:]
    io.gout, io.gain = gout_in, gain_in
    s = SimpleNamespace(cos=rope_in.at[0], sin=rope_in.at[1])
    (s.tile, s.mix, s.act, s.slope, s.n2, s.n1, s.att, s.after, s.h, s.probs, s.qkv, s.gy, s.gn, s.gm, s.ga, s.gj, s.turned, s.history,
        s.kept, s.value, s.land) = rest
    scratch = s
    scratch.sums = scratch.value.at[0]
    me = Place(depth)
    c = me.c
    bar = greet(me, True)
    rows = mix_o.shape[1]
    mine = lambda w: pl.ds(al(c * w, 128), w)
    other = lambda w: pl.ds(al((1 - c) * w, 128), w)
    bwd = Backward(io, scratch, SimpleNamespace(mix=mix_g, up=up_g, down=down_g), me.planes, first, second)
    scratch.value[0] = sums_in[...]
    chunks = {}
    for k in range(6):
        l, j = divmod(k, 3)
        if j == 2:
            R = down_g.shape[2]
            def plane_add(z):
                for i in range(4): add_into(down_g.at[z * 4 + i, c], [down_d.at[z * 4 + i]], R)
            chunks[k] = SimpleNamespace(kind=kinds[k], rows=R, share=lambda chip: down_g.at[chip, c],
                plane=lambda z, own: down_g.at[pl.ds(z * 4, 4), c if own else 1 - c], plane_land=lambda z: down_d.at[pl.ds(z * 4, 4)],
                plane_add=plane_add, land=lambda s: down_l.at[s], result=down_f.at[l])
        else:
            g, d, land, f = ((mix_g, mix_d, mix_l, mix_f), (up_g, up_d, up_l, up_f))[j]
            half = g.shape[1] // 2
            def plane_add(z, g=g, d=d, half=half):
                at = pl.ds(al(z * 8 * rows, 16), 8 * rows)
                add_into(g.at[at, mine(half)], [d.at[at, :]], 8 * rows)
            chunks[k] = SimpleNamespace(kind=kinds[k], rows=2 * rows, share=lambda chip, g=g, half=half: g.at[pl.ds(al(chip * 2 * rows, 16), 2 * rows), mine(half)],
                plane=lambda z, own, g=g, half=half: g.at[pl.ds(al(z * 8 * rows, 16), 8 * rows), mine(half) if own else other(half)],
                plane_land=lambda z, d=d: d.at[pl.ds(al(z * 8 * rows, 16), 8 * rows), :],
                plane_add=plane_add, land=lambda s, land=land: land.at[s], result=f.at[l])
    sc = Scatter(me, chunks, ssem, rsem)
    total = Total(me, scratch.value, scratch.land, tsend, trecv)
    def result(k):
        l, j = divmod(k, 3)
        if j == 2: return [pltpu.make_async_copy(down_f.at[l], down_o.at[l], fsem.at[k])]
        f, o = ((mix_f, mix_o), (up_f, up_o))[j]
        half = f.shape[2]
        return [pltpu.make_async_copy(f.at[l, pl.ds(al(c * rows, 8), rows), :], o.at[l, :, mine(half)], fsem.at[k]),
            pltpu.make_async_remote_copy(src_ref=f.at[l, pl.ds(al((1 - c) * rows, 8), rows), :], dst_ref=o.at[l, :, mine(half)],
                send_sem=esem.at[0, k], recv_sem=esem.at[1, k], device_id=me.sib, device_id_type=MESH)]
    def tell(j):
        for d in (me.xn, me.yn): pl.semaphore_signal(credit.at[1, j], inc=1, device_id=d, device_id_type=MESH)
        when(me.has_up, lambda: pl.semaphore_signal(credit.at[1, j], inc=1, device_id=me.up, device_id_type=MESH))
        when(me.has_down, lambda: pl.semaphore_signal(credit.at[1, j], inc=1, device_id=me.down, device_id_type=MESH))
    planes_left, told, totals = {k: depth for k in range(6)}, {}, []
    greeted_yet = []
    for n, item in enumerate(weave_back(order, bwd.steps())):
        if not isinstance(item, tuple):
            item()
            continue
        if not greeted_yet:
            greeted(me, bar, True)
            greeted_yet.append(1)
        if item[0] == "drain":
            sc.drain(item[1])
            continue
        if item[0] == "sums":
            totals = [0, 1, 2, 3, 4]
            since = 0
            continue
        k, what, r = item
        l, j = divmod(k, 3)
        if l == 0 and what == "d" and (0, j) not in told:
            told[0, j] = True
            pl.semaphore_wait(credit.at[0, j], 1)
        if l == 0 and what == "q" and (1, j) not in told:
            told[1, j] = True
            pl.semaphore_wait(credit.at[1, j], 2 + me.has_up.astype(jnp.int32) + me.has_down.astype(jnp.int32))
        sc.event(k, what, r)
        if what == "q":
            planes_left[k] -= 1
            if l == 1 and planes_left[k] == 0:
                pl.semaphore_signal(credit.at[0, j], inc=1, device_id=me.sib, device_id_type=MESH)
        if what == "o":
            for cp in result(k): cp.start()
            if l == 1: tell(j)
        if totals:
            since += 1
            if since % 4 == 0: total.step(totals.pop(0))
    for i in totals: total.step(i)
    sums_o[...] = scratch.value[4]
    for k in range(3): sc.drain(k)
    for k in range(6):
        for cp in result(k): cp.wait()
    bwd.finish()


def bwd_call(mesh, order, kinds, weights, saved, inputs, history, rope, first, second):
    mix, up, down = weights
    depth = mesh.shape["wide"] // 2
    D, M = mix.shape[1:]
    FF = up.shape[2]
    T = inputs.shape[0]
    n = mesh.size // 2
    rows, drows = D // mesh.size, FF // mesh.size
    down = down.reshape(2, FF // D, D, D)
    slots = 4 * depth + 3
    body = functools.partial(bwd_kernel, depth, order, kinds)
    vm = pl.BlockSpec(memory_space=pltpu.VMEM); an = pl.BlockSpec(memory_space=pl.ANY); sm = pl.BlockSpec(memory_space=pltpu.SMEM)
    V, S = pltpu.VMEM, pltpu.SemaphoreType.DMA
    return pl.pallas_call(body,
        out_shape=[jax.ShapeDtypeStruct(s, F32) for s in ((2, rows, M), (2, rows, FF), (2, drows, D), (T, D), (T, D), (8, D))],
        in_specs=[vm] * 4 + [sm] * 2 + [an] * 15, out_specs=[an] * 5 + [vm],
        scratch_shapes=[V((D, M), BF), V((D, FF), BF), V((n, 2, drows, D), BF),
            V((D, M // 2), BF), V((D, FF // 2), BF), V((n, drows, D), BF),
            V((slots, 2 * rows, M // 2), BF), V((slots, 2 * rows, FF // 2), BF), V((slots, drows, D), BF),
            V((2, 2 * rows, M // 2), F32), V((2, 2 * rows, FF // 2), F32), V((2, drows, D), F32),
            S((6, 5)), S((6, slots + depth)), S((2, 6)), pltpu.SemaphoreType.REGULAR((2, 3)),
            S((len(Backward.SLOTS),)), S((FF // D,)), S((2,)), S((2 + depth,)), S((2 + depth,)), S((6,)),
            V((FF // D, D, D), BF), V((D, M), BF), V((FF // D, T, D), BF), V((FF // D, T, D), BF), V((T, D), BF), V((T, D), BF), V((T, D), BF),
            V((T, D), F32), V((T, D), F32), V((HEADS, T, T), BF), V((T, 3 * D), BF), V((T, D), F32), V((T, D), F32), V((T, D), BF),
            V((T, D), BF), V((T, 3 * D), BF), V((D, T), BF), V(history.shape, BF), V((T, D), F32), V((5, 8, D), F32),
            V((2 + depth, 8, D), F32)],
        compiler_params=pltpu.CompilerParams(collective_id=1, has_side_effects=True, vmem_limit_bytes=63 * 2**20),
        cost_estimate=pl.CostEstimate(flops=32 * T * D * FF, bytes_accessed=2**27, transcendentals=2**10),
    )(saved.gout, saved.sums, saved.gain, rope, first, second, mix, up, down, saved.n1, saved.qkv, saved.probs, saved.att,
        saved.after, saved.n2, saved.act, saved.slope, saved.stored, saved.carried, inputs, history)


def results_kernel(first, second, sums, sums_v, grad_carried, gout, blended, stored, grad_inputs, mix, up, down,
                   blended_o, stored_o, inputs_o, history_o, qkv_o, out_o, up_o, down_o, gain_o, first_o, second_o,
                   mixed, carried_b, gout_b, blended_b, stored_b, inputs_b, mix_b, up_b, down_b, sem):
    q, o = qkv_o.shape[2] // 2, out_o.shape[2] // 2
    half = mix.shape[2] // 2
    ins = [(grad_carried, carried_b), (gout, gout_b), (stored.at[0], stored_b.at[0]), (stored.at[1], stored_b.at[1]), (blended, blended_b), (grad_inputs, inputs_b), (mix, mix_b), (up, up_b), (down, down_b)]
    outs = [[], [], [(stored_b.at[0], stored_o.at[0])], [(stored_b.at[1], stored_o.at[1])], [(blended_b, blended_o)], [(inputs_b, inputs_o)], [], [(up_b, up_o)], [(down_b, down_o)]]
    for h in range(2):
        outs[6].append((mix_b.at[:, :, pl.ds(h * half, q)], qkv_o.at[:, :, pl.ds(h * q, q)]))
        outs[6].append((mix_b.at[:, :, pl.ds(h * half + q, o)], out_o.at[:, :, pl.ds(h * o, o)]))
    loads = [pltpu.make_async_copy(a, b, sem.at[i]) for i, (a, b) in enumerate(ins)]
    for cp in loads: cp.start()
    copies = []
    def leave(a, b):
        copies.append(pltpu.make_async_copy(a, b, sem.at[len(ins) + len(copies)]))
        copies[-1].start()
    hist = history_o.shape[0]
    for cp in loads[:2]: cp.wait()
    for j in range(hist):
        mixed[j] = first[j] * carried_b[...] + second[j] * gout_b[...]
        leave(mixed.at[j], history_o.at[j])
    for j in range(hist + 1): first_o[j] = sums[0, j]
    for j in range(hist + 2): second_o[j] = sums[1, j]
    for cp, pairs in list(zip(loads, outs))[2:]:
        cp.wait()
        for a, b in pairs: leave(a, b)
    rows = gain_o.shape[2]
    device = lax.axis_index("wide") * lax.axis_size("narrow") + lax.axis_index("narrow")
    own = pltpu.roll(sums_v[...], lax.rem(sums_v.shape[1] - device * rows, sums_v.shape[1]), 1)
    for l in range(2): gain_o[l] = own[2 + 2 * l:4 + 2 * l, 0:rows]
    for cp in copies: cp.wait()


def results_call(first, second, sums, grad_carried, saved, grad_inputs, mix, up, down, hist):
    T, D = grad_inputs.shape
    rows = mix.shape[1]
    vm = pl.BlockSpec(memory_space=pltpu.VMEM); an = pl.BlockSpec(memory_space=pl.ANY); sm = pl.BlockSpec(memory_space=pltpu.SMEM)
    shapes = [(T, D), (2, T, D), (T, D), (hist, T, D), (2, rows, 3 * D), (2, rows, D), up.shape, down.shape, (2, 2, rows), (hist + 1,), (hist + 2,)]
    return pl.pallas_call(results_kernel,
        out_shape=[jax.ShapeDtypeStruct(s, F32) for s in shapes],
        in_specs=[sm] * 3 + [vm] + [an] * 8, out_specs=[an] * 8 + [vm] + [sm] * 2,
        scratch_shapes=[pltpu.VMEM((hist, T, D), F32), pltpu.VMEM((T, D), F32), pltpu.VMEM((T, D), F32), pltpu.VMEM((T, D), F32), pltpu.VMEM((2, T, D), F32), pltpu.VMEM((T, D), F32),
            pltpu.VMEM(mix.shape, F32), pltpu.VMEM(up.shape, F32), pltpu.VMEM(down.shape, F32), pltpu.SemaphoreType.DMA((20 + hist,))],
        compiler_params=pltpu.CompilerParams(vmem_limit_bytes=60 * 2**20),
    )(first, second, sums, sums, grad_carried, saved.gout, saved.blended, saved.stored, grad_inputs, mix, up, down)


def fast_body(mesh, inputs, history, lengths, cotangent, w_qkv, w_out, w_up, w_down, gains, alpha_first, alpha_second):
    rope = jnp.asarray(rotary_lanes(inputs.shape[0], inputs.shape[1] // HEADS, 128))
    weights, saved = fwd_call(mesh, steps(GATHER_ORDER), GATHER_KINDS, w_qkv, w_out, w_up, w_down, gains,
        inputs, history, cotangent, rope, lengths, alpha_first, alpha_second)
    mix, up, down, grad_carried, grad_inputs, sums = bwd_call(mesh, steps(SCATTER_ORDER), SCATTER_KINDS, weights, saved,
        inputs, history, rope, alpha_first, alpha_second)
    return results_call(alpha_first, alpha_second, sums, grad_carried, saved, grad_inputs, mix, up, down, history.shape[0])


def solution(mesh):
    axes = ("wide", "narrow")
    split, row_split = P(None, axes, None), P(axes, None)
    placed = (row_split, split, P(axes), row_split, split, split, split, split, P(None, None, axes), P(), P())
    results = (row_split, split, row_split, split, split, split, split, split, P(None, None, axes), P(), P())

    def body(*args):
        rows, hist = args[4].shape[1], args[1].shape[0]
        fits = mesh.shape["narrow"] == 4 and mesh.shape["wide"] == 8 and rows % 8 == 0
        fits = fits and hist * args[4].shape[1] == args[7].shape[1]
        return fast_body(mesh, *args) if fits else plain_body(*args)

    return jax.shard_map(body, mesh=mesh, in_specs=placed, out_specs=results, check_vma=False)
```

```python
import functools
import math
from types import SimpleNamespace

import jax
import jax.numpy as jnp
import numpy as np
from jax import lax
from jax.experimental import pallas as pl
from jax.experimental.pallas import tpu as pltpu
from jax.sharding import PartitionSpec as P

MESH = pl.DeviceIdType.MESH
BF = jnp.bfloat16
F32 = jnp.float32


HEADS = 12


norm_eps = 1e-05
gelu_coef = 0.044715
gelu_scale = math.sqrt(2.0 / math.pi)
masked_score = -1e30


def product(left, right):
    return jnp.dot(left, right, preferred_element_type=jnp.float32)


def layer_norm(hidden, gain_row):
    center = hidden - jnp.mean(hidden, axis=-1, keepdims=True)
    inverse = lax.rsqrt(jnp.mean(center * center, axis=-1, keepdims=True) + norm_eps)
    standard = center * inverse
    return (standard * gain_row, standard, inverse)


def plain_norm_back(grad_rows, standard, inverse, gain_row):
    scaled = grad_rows * gain_row
    grad_gain = jnp.sum(grad_rows * standard, axis=0)
    grad_in = inverse * (
        scaled
        - jnp.mean(scaled, axis=-1, keepdims=True)
        - standard * jnp.mean(scaled * standard, axis=-1, keepdims=True)
    )
    return (grad_in, grad_gain)


def gelu(values):
    return (
        0.5
        * values
        * (1.0 + jnp.tanh(gelu_scale * (values + gelu_coef * values * values * values)))
    )


def gelu_slope(values):
    tangent = jnp.tanh(gelu_scale * (values + gelu_coef * values * values * values))
    return 0.5 * (1.0 + tangent) + 0.5 * values * (1.0 - tangent * tangent) * gelu_scale * (
        1.0 + 3.0 * gelu_coef * values * values
    )


def rotary_tables(seq_length, head_width):
    half_width = head_width // 2
    frequency = 10000.0 ** (-jnp.arange(half_width, dtype=jnp.float32) / half_width)
    angles = jnp.arange(seq_length, dtype=jnp.float32)[:, None] * frequency[None, :]
    return (jnp.cos(angles)[:, None, :], jnp.sin(angles)[:, None, :])


def rotate(values, cos_table, sin_table):
    half_width = values.shape[-1] // 2
    left_half = values[..., :half_width]
    right_half = values[..., half_width:]
    return jnp.concatenate(
        [
            left_half * cos_table - right_half * sin_table,
            right_half * cos_table + left_half * sin_table,
        ],
        axis=-1,
    )


def rotate_back(grad_rows, cos_table, sin_table):
    half_width = grad_rows.shape[-1] // 2
    left_grad = grad_rows[..., :half_width]
    right_grad = grad_rows[..., half_width:]
    return jnp.concatenate(
        [
            left_grad * cos_table + right_grad * sin_table,
            right_grad * cos_table - left_grad * sin_table,
        ],
        axis=-1,
    )


def allowed_mask(block_rows, key_count, length):
    row_place = jnp.arange(block_rows)
    col_place = jnp.arange(key_count)
    return (col_place[None, :] <= row_place[:, None]) & (col_place[None, :] < length)


def attention_forward(queries, key_rows, value_rows, length):
    seq_length, head_count, head_width = queries.shape
    score_scale = head_width ** (-0.5)
    block_rows = min(512, seq_length)
    scores = (
        jnp.einsum("qhe,khe->hqk", queries, key_rows, preferred_element_type=jnp.float32)
        * score_scale
    )
    allowed = allowed_mask(block_rows, block_rows, length)
    scores = jnp.where(allowed[None], scores, masked_score)
    row_top = jnp.max(scores, axis=-1, keepdims=True)
    exp_scores = jnp.exp(scores - row_top)
    row_total = jnp.sum(exp_scores, axis=-1, keepdims=True)
    prob_rows = (exp_scores / row_total).astype(jnp.bfloat16)
    pieces = jnp.einsum("hqk,khe->qhe", prob_rows, value_rows, preferred_element_type=jnp.float32)
    log_sums = row_top + jnp.log(row_total)
    return (pieces, log_sums)


def attention_backward(queries, key_rows, value_rows, log_sums, grad_attended, length):
    seq_length, head_count, head_width = queries.shape
    score_scale = head_width ** (-0.5)
    grad_keys = jnp.zeros(queries.shape, jnp.float32)
    grad_values = jnp.zeros(queries.shape, jnp.float32)
    block_rows = min(512, seq_length)
    scores = (
        jnp.einsum("qhe,khe->hqk", queries, key_rows, preferred_element_type=jnp.float32)
        * score_scale
    )
    allowed = allowed_mask(block_rows, block_rows, length)
    prob_rows = jnp.where(allowed[None], jnp.exp(scores - log_sums), 0.0)
    grad_prob = jnp.einsum(
        "qhe,khe->hqk", grad_attended, value_rows, preferred_element_type=jnp.float32
    )
    inner_sum = jnp.sum(prob_rows * grad_prob, axis=-1, keepdims=True)
    grad_score = (prob_rows * (grad_prob - inner_sum)).astype(jnp.bfloat16)
    grad_pieces = (
        jnp.einsum("hqk,khe->qhe", grad_score, key_rows, preferred_element_type=jnp.float32)
        * score_scale
    )
    grad_keys = grad_keys.at[:block_rows].add(
        jnp.einsum("hqk,qhe->khe", grad_score, queries, preferred_element_type=jnp.float32)
        * score_scale
    )
    grad_values = grad_values.at[:block_rows].add(
        jnp.einsum(
            "hqk,qhe->khe",
            prob_rows.astype(jnp.bfloat16),
            grad_attended,
            preferred_element_type=jnp.float32,
        )
    )
    return (grad_pieces, grad_keys, grad_values)


def layer_forward(hidden, weights, length):
    layer_qkv, layer_out, layer_up, layer_down, layer_gains = weights
    seq_length = hidden.shape[0]
    head_width = layer_out.shape[0] // HEADS
    normed, unit_one, inverse_one = layer_norm(hidden, layer_gains[0])
    normed = normed.astype(jnp.bfloat16)
    joined = product(normed, layer_qkv).reshape(seq_length, 3, HEADS, head_width)
    cos_table, sin_table = rotary_tables(seq_length, head_width)
    queries = rotate(joined[:, 0], cos_table, sin_table).astype(jnp.bfloat16)
    key_rows = rotate(joined[:, 1], cos_table, sin_table).astype(jnp.bfloat16)
    value_rows = joined[:, 2].astype(jnp.bfloat16)
    attended, log_sums = attention_forward(queries, key_rows, value_rows, length)
    attended = attended.reshape(seq_length, HEADS * head_width).astype(jnp.bfloat16)
    after_attn = hidden + product(attended, layer_out)
    normed_two, unit_two, inverse_two = layer_norm(after_attn, layer_gains[1])
    normed_two = normed_two.astype(jnp.bfloat16)
    up_vals = product(normed_two, layer_up)
    result = after_attn + product(gelu(up_vals).astype(jnp.bfloat16), layer_down)
    kept_state = (
        normed,
        unit_one,
        inverse_one,
        queries,
        key_rows,
        value_rows,
        log_sums,
        attended,
        unit_two,
        inverse_two,
        normed_two,
        up_vals,
    )
    return (result, kept_state)


def layer_backward(grad_rows, weights, kept_state, length):
    layer_qkv, layer_out, layer_up, layer_down, layer_gains = weights
    (
        normed,
        unit_one,
        inverse_one,
        queries,
        key_rows,
        value_rows,
        log_sums,
        attended,
        unit_two,
        inverse_two,
        normed_two,
        up_vals,
    ) = kept_state
    seq_length, head_count, head_width = queries.shape
    grad_low = grad_rows.astype(jnp.bfloat16)
    active = gelu(up_vals).astype(jnp.bfloat16)
    grad_down = jnp.einsum("tf,td->fd", active, grad_low, preferred_element_type=jnp.float32)
    grad_active = jnp.einsum("td,fd->tf", grad_low, layer_down, preferred_element_type=jnp.float32)
    grad_upv = (grad_active * gelu_slope(up_vals)).astype(jnp.bfloat16)
    grad_up = jnp.einsum("td,tf->df", normed_two, grad_upv, preferred_element_type=jnp.float32)
    grad_norm_two = jnp.einsum("tf,df->td", grad_upv, layer_up, preferred_element_type=jnp.float32)
    grad_after, gain_two = plain_norm_back(grad_norm_two, unit_two, inverse_two, layer_gains[1])
    grad_after = grad_rows + grad_after
    grad_branch = grad_after.astype(jnp.bfloat16)
    grad_wout = jnp.einsum("ta,td->ad", attended, grad_branch, preferred_element_type=jnp.float32)
    grad_attended = jnp.einsum(
        "td,ad->ta", grad_branch, layer_out, preferred_element_type=jnp.float32
    )
    grad_attended = grad_attended.astype(jnp.bfloat16).reshape(seq_length, head_count, head_width)
    grad_query, grad_keys, grad_values = attention_backward(
        queries, key_rows, value_rows, log_sums, grad_attended, length
    )
    cos_table, sin_table = rotary_tables(seq_length, head_width)
    grad_joined = jnp.stack(
        [
            rotate_back(grad_query, cos_table, sin_table),
            rotate_back(grad_keys, cos_table, sin_table),
            grad_values,
        ],
        axis=1,
    )
    grad_joined = grad_joined.reshape(seq_length, 3 * head_count * head_width).astype(jnp.bfloat16)
    grad_qkv = jnp.einsum("td,tj->dj", normed, grad_joined, preferred_element_type=jnp.float32)
    grad_norm_one = jnp.einsum(
        "tj,dj->td", grad_joined, layer_qkv, preferred_element_type=jnp.float32
    )
    grad_in, gain_one = plain_norm_back(grad_norm_one, unit_one, inverse_one, layer_gains[0])
    return (
        grad_after + grad_in,
        (grad_qkv, grad_wout, grad_up, grad_down, jnp.stack([gain_one, gain_two])),
    )


def mix_history(alphas, history):
    blended = alphas[0] * history[0].astype(jnp.float32)
    for entry in range(1, history.shape[0]):
        blended = blended + alphas[entry] * history[entry].astype(jnp.float32)
    return blended


def plain_body(
    inputs,
    history,
    lengths,
    cotangent,
    w_qkv,
    w_out,
    w_up,
    w_down,
    gains,
    alpha_first,
    alpha_second,
):
    token_total = lax.psum(jnp.sum(lengths.astype(jnp.float32)), ("wide", "narrow"))
    length = lengths[0]
    hist_count = history.shape[0]

    def fetch_layer(layer_no):
        return (
            lax.all_gather(w_qkv[layer_no], ("wide", "narrow"), axis=0, tiled=True),
            lax.all_gather(w_out[layer_no], ("wide", "narrow"), axis=0, tiled=True),
            lax.all_gather(w_up[layer_no], ("wide", "narrow"), axis=0, tiled=True),
            lax.all_gather(w_down[layer_no], ("wide", "narrow"), axis=0, tiled=True),
            lax.all_gather(gains[layer_no], ("wide", "narrow"), axis=1, tiled=True),
        )

    def fetch_again(layer_no):
        return (
            lax.all_gather(w_qkv[layer_no], ("wide", "narrow"), axis=0, tiled=True),
            lax.all_gather(w_out[layer_no], ("wide", "narrow"), axis=0, tiled=True),
            lax.all_gather(w_up[layer_no], ("wide", "narrow"), axis=0, tiled=True),
            lax.all_gather(w_down[layer_no], ("wide", "narrow"), axis=0, tiled=True),
            lax.all_gather(gains[layer_no], ("wide", "narrow"), axis=1, tiled=True),
        )

    def reduce_grads(grad_set):
        return (
            lax.psum_scatter(grad_set[0], ("wide", "narrow"), scatter_dimension=0, tiled=True),
            lax.psum_scatter(grad_set[1], ("wide", "narrow"), scatter_dimension=0, tiled=True),
            lax.psum_scatter(grad_set[2], ("wide", "narrow"), scatter_dimension=0, tiled=True),
            lax.psum_scatter(grad_set[3], ("wide", "narrow"), scatter_dimension=0, tiled=True),
            lax.psum_scatter(grad_set[4], ("wide", "narrow"), scatter_dimension=1, tiled=True),
        )

    weights_one = fetch_layer(0)
    kept_one, state_one = layer_forward(inputs, weights_one, length)
    carried = mix_history(alpha_first, history) + alpha_first[hist_count] * kept_one
    weights_two = fetch_layer(1)
    kept_two, state_two = layer_forward(carried, weights_two, length)
    blended = (
        mix_history(alpha_second, history)
        + alpha_second[hist_count] * kept_one
        + alpha_second[hist_count + 1] * kept_two
    )
    seq_length = inputs.shape[0]
    live_mask = (jnp.arange(seq_length) < length).astype(jnp.float32)[:, None]
    grad_blend = cotangent * live_mask / token_total
    back_two = fetch_again(1)
    grad_carried, grads_two = layer_backward(
        alpha_second[hist_count + 1] * grad_blend, back_two, state_two, length
    )
    shard_two = reduce_grads(grads_two)
    grad_first = alpha_first[hist_count] * grad_carried + alpha_second[hist_count] * grad_blend
    back_one = fetch_again(0)
    grad_inputs, grads_one = layer_backward(grad_first, back_one, state_one, length)
    shard_one = reduce_grads(grads_one)
    grad_history = jnp.stack(
        [
            alpha_first[entry] * grad_carried + alpha_second[entry] * grad_blend
            for entry in range(hist_count)
        ]
    )
    first_terms = []
    second_terms = []
    for entry in range(hist_count):
        past_row = history[entry].astype(jnp.float32)
        first_terms.append(jnp.sum(past_row * grad_carried))
        second_terms.append(jnp.sum(past_row * grad_blend))
    first_terms.append(jnp.sum(kept_one * grad_carried))
    second_terms.append(jnp.sum(kept_one * grad_blend))
    second_terms.append(jnp.sum(kept_two * grad_blend))
    grad_alpha_first, grad_alpha_second = lax.psum(
        (jnp.stack(first_terms), jnp.stack(second_terms)), ("wide", "narrow")
    )
    return (
        blended,
        jnp.stack([kept_one, kept_two]),
        grad_inputs,
        grad_history,
        jnp.stack([shard_one[0], shard_two[0]]),
        jnp.stack([shard_one[1], shard_two[1]]),
        jnp.stack([shard_one[2], shard_two[2]]),
        jnp.stack([shard_one[3], shard_two[3]]),
        jnp.stack([shard_one[4], shard_two[4]]),
        grad_alpha_first,
        grad_alpha_second,
    )


GATHER_KINDS = "accacc"
GATHER_ORDER = (
    200, 400, 100, 0, 110, 21, 22, 500, -1, 30, 210, 23, 300, 121, 31, 32, 33, 122, 123, 40, 41, 51, 510, 321,
    140, 410, 42, 52, 50, 150, 330, 240, 250, 43, 53, -1, 322, 323, 141, 142, 221, 143, 153, 222, -1, -1, -1,
    -1, -1, -1, -1, -1, -1, -1, 440, 223, -1, -1, -1, -1, -1, 331, 332, 333, 151, 540, 152, -1, -1, -1, 340,
    350, 521, 421, 422, 241, 251, 242, -1, -1, -1, -1, -1, -1, -1, 522, -1, -1, -1, 252, -1, 341, 351, 342,
    343, 243, 353, 423, 352, 253, -1, -1, -1, -1, -1, -1, -1, -1, -1, -1, -1, -1, 441, 523, 442, 443, 550,
    541, 542, -1, -1, -1, -1, -1, -1, -1, 451, 452, 453, 450, -1, -1, -1, 543, -1, -1, -1, -1, -1, -1, -1,
    552, 553, 551, -1, -1, -1, -1,
)
SCATTER_KINDS = "acacac"
SCATTER_ORDER = (
    -1, -1, 553, -1, -1, 552, -1, 551, 550, 543, -1, -1, -1, -1, -1, -1, -1, -1, 542, 541, -1, -1, -1, -1, -1,
    451, 452, 453, 450, 523, 443, 442, 441, -1, -1, -1, -1, 522, 540, -1, -1, -1, 521, -1, -1, -1, -1, -1,
    433, 432, 431, -1, -1, -1, -1, -1, -1, -1, -1, 353, 352, 351, 350, 343, 440, 423, 422, -1, -1, -1, -1, -1,
    510, 342, 341, 323, 421, 500, -1, -1, 253, -1, 252, 243, -1, 251, 242, -1, 250, -1, -1, -1, -1, 430, 241,
    240, 322, 321, 340, 233, 232, 400, -1, -1, -1, -1, -1, -1, -1, -1, -1, 153, 151, 150, -1, 143, -1, -1, -1,
    -1, -1, -1, -1, -1, -1, -1, 223, 310, 231, 152, 142, 141, 140, 123, 230, 222, 221, 300, -1, -1, -1, -1,
    -1, -1, -1, -1, 53, 52, 51, 50, -1, 43, -1, 42, -1, 41, -1, 122, 121, 33, 32, 23, 31, 40, 200, 110, 22,
    21, 30, 100, 0,
)
NEXT = -1


def steps(codes):
    return [v if v == NEXT else (v // 100, "oplaqd"[v // 10 % 10], v % 10) for v in codes]


def al(v, m): return pl.multiple_of(v, m)
def when(cond, fn): pl.when(cond)(fn)

class Place:
    def __init__(self, depth):
        self.depth = depth
        w = lax.axis_index("wide"); n = lax.axis_index("narrow")
        self.w, self.n = w, n
        self.z, self.x = w // 2, lax.rem(w, 2)
        self.y, self.c = n // 2, lax.rem(n, 2)
        first = self.c == 0
        p = jnp.where(first, self.x, self.y)
        q = jnp.where(first, self.y, self.x)
        self.sib = (w, self.y * 2 + 1 - self.c)
        self.xn = (self.z * 2 + 1 - self.x, n)
        self.yn = (w, (1 - self.y) * 2 + self.c)
        self.pn = tuple(jnp.where(first, a, b) for a, b in zip(self.xn, self.yn))
        self.qn = tuple(jnp.where(first, b, a) for a, b in zip(self.xn, self.yn))
        self.has_up = self.z < depth - 1
        self.has_down = self.z > 0
        self.up = (w + 2, n)
        self.down = (w - 2, n)
        self.line = [(lax.rem(w + 2 * i, 2 * depth), n) for i in range(1, depth)]
        self.chip = self.z * 4 + self.x * 2 + self.y
        self.planes = [self.plane(r) for r in range(depth)]
        self.chips = [[[z * 4 + jnp.where(first, 2, 1) * (1 - p if a else p) + jnp.where(first, 1, 2) * (1 - q if b else q)
                        for z in self.planes] for b in (0, 1)] for a in (0, 1)]
        self.onward_up = [(z < self.z) & self.has_up for z in self.planes]
        self.onward_down = [(z > self.z) & self.has_down for z in self.planes]
    def plane(self, r):
        if r == 0: return self.z
        z, last = self.z, self.depth - 1
        short = jnp.minimum(z, last - z)
        low = z * 2 < self.depth
        dist = jnp.where(r <= 2 * short, (r + 1) // 2, r - short)
        below = jnp.where((r <= 2 * short) & (r % 2 == 1), low, ~low)
        return jnp.where(below, z - dist, z + dist)

class Gather:
    def __init__(self, me, chunks, ssem, rsem):
        self.me, self.chunks, self.ssem, self.rsem = me, chunks, ssem, rsem
    def copy(self, k, chip, way, target, sem):
        ref = self.chunks[k][1](chip, 1)
        return pltpu.make_async_remote_copy(src_ref=ref, dst_ref=ref, send_sem=self.ssem.at[k, way],
            recv_sem=self.rsem.at[k, sem], device_id=target, device_id_type=MESH)
    def plane_copy(self, k, r):
        ref = self.chunks[k][2](self.me.planes[r])
        return pltpu.make_async_remote_copy(src_ref=ref, dst_ref=ref, send_sem=self.ssem.at[k, 4],
            recv_sem=self.rsem.at[k, 3 * self.me.depth + self.me.planes[r]], device_id=self.me.sib, device_id_type=MESH)
    def p(self, k, chip, r): self.copy(k, chip, 0, self.me.pn, 2 * self.me.depth + self.me.planes[r]).start()
    def q(self, k, chip, r): self.copy(k, chip, 1, self.me.qn, self.me.planes[r]).start()
    def up(self, k, chip, r): self.copy(k, chip, 2, self.me.up, self.me.depth + self.me.planes[r]).start()
    def down(self, k, chip, r): self.copy(k, chip, 3, self.me.down, self.me.depth + self.me.planes[r]).start()
    def wait(self, k, n, sem):
        ref = self.chunks[k][1](0, n)
        pltpu.make_async_remote_copy(src_ref=ref, dst_ref=ref, send_sem=self.ssem.at[k, 0], recv_sem=self.rsem.at[k, sem],
            device_id=self.me.pn, device_id_type=MESH).wait_recv()
    def event(self, k, what, r):
        me, Z = self.me, self.me.depth
        kind = self.chunks[k][0]
        own, flip = me.chips[0][0][r], me.chips[1][0][r]
        if what == "o":
            when(me.has_up, lambda: self.up(k, own, 0))
            when(me.has_down, lambda: self.down(k, own, 0))
            self.p(k, own, 0)
            self.q(k, own, 0)
        elif what == "p":
            self.wait(k, 1, 2 * Z + me.planes[0])
            when(me.has_up, lambda: self.up(k, flip, 0))
            when(me.has_down, lambda: self.down(k, flip, 0))
            self.q(k, flip, 0)
        elif what == "l":
            both = (own, flip) if kind == "c" else (own,)
            self.wait(k, len(both), Z + me.planes[r])
            def fwd(send):
                for chip in both: send(k, chip, r)
            when(me.onward_up[r], lambda: fwd(self.up))
            when(me.onward_down[r], lambda: fwd(self.down))
            if kind == "a": self.p(k, own, r)
            for chip in both: self.q(k, chip, r)
        elif what == "a":
            self.wait(k, 1, 2 * Z + me.planes[r])
            self.q(k, flip, r)
        elif what == "q":
            self.wait(k, 2, me.planes[r])
            self.plane_copy(k, r).start()
        elif what == "d":
            self.plane_copy(k, r).wait_recv()
    def drain(self, k):
        me, Z = self.me, self.me.depth
        per = 2 if self.chunks[k][0] == "c" else 1
        counts = [1 if per == 2 else Z, 2 * Z, jnp.where(me.has_up, per * (me.z + 1), 0), jnp.where(me.has_down, per * (Z - me.z), 0)]
        for way, count in enumerate(counts):
            def one(_, carry):
                self.copy(k, 0, way, me.pn, 0).wait_send()
                return carry
            lax.fori_loop(0, count, one, 0)
        def one(_, carry):
            self.plane_copy(k, 0).wait_send()
            return carry
        lax.fori_loop(0, Z, one, 0)

def greet(me, whole_line=False):
    bar = pltpu.get_barrier_semaphore()
    def signal(d): pl.semaphore_signal(bar, inc=1, device_id=d, device_id_type=MESH)
    for d in (me.sib, me.xn, me.yn): signal(d)
    if whole_line:
        for d in me.line: signal(d)
    else:
        when(me.has_up, lambda: signal(me.up))
        when(me.has_down, lambda: signal(me.down))
    return bar


def greeted(me, bar, whole_line=False):
    line = len(me.line) if whole_line else me.has_up.astype(jnp.int32) + me.has_down.astype(jnp.int32)
    pl.semaphore_wait(bar, 3 + line)


def add_into(dst, sources, rows, out=None):
    step = 48 if rows % 48 == 0 else 16
    @pl.loop(0, rows // step)
    def _(i):
        at = pl.ds(al(i * step, 16), step)
        if out is None and len(sources) == 1:
            dst[at, :] = dst[at, :] + sources[0][at, :]
            return
        total = dst[at, :].astype(F32)
        for s in sources: total = total + s[at, :].astype(F32)
        if out is None: dst[at, :] = total.astype(dst.dtype)
        else: out[at, :] = total


class Scatter:
    def __init__(self, me, chunks, ssem, rsem):
        self.me, self.chunks, self.ssem, self.rsem = me, chunks, ssem, rsem
        Z = me.depth
        self.Z = Z
        self.q_slot = lambda flip, z: (Z if flip else 0) + z
        self.line_slot = lambda flip, z: 2 * Z + (Z if flip else 0) + z
        self.late_slot = lambda flip: 4 * Z + (1 if flip else 0)
        self.p_slot = lambda kind, z: 3 * Z + z if kind == "a" else 4 * Z + 2
        self.slots = 4 * Z + 3
    def land(self, k, slot): return self.chunks[k].land(slot)
    def copy(self, k, chip, way, target, slot):
        ch = self.chunks[k]
        return pltpu.make_async_remote_copy(src_ref=ch.share(chip), dst_ref=ch.land(slot), send_sem=self.ssem.at[k, way],
            recv_sem=self.rsem.at[k, slot], device_id=target, device_id_type=MESH)
    def plane_copy(self, k, r):
        ch, me = self.chunks[k], self.me
        z = me.planes[r]
        return pltpu.make_async_remote_copy(src_ref=ch.plane(z, False), dst_ref=ch.plane_land(z), send_sem=self.ssem.at[k, 4],
            recv_sem=self.rsem.at[k, self.slots + z], device_id=me.sib, device_id_type=MESH)
    def wait(self, k, slot):
        self.copy(k, 0, 0, self.me.pn, slot).wait_recv()
    def take(self, k, chip, slots, out=None):
        ch = self.chunks[k]
        for s in slots: self.wait(k, s)
        add_into(ch.share(chip), [ch.land(s) for s in slots], ch.rows, out)
    def event(self, k, what, r):
        me, Z = self.me, self.Z
        ch = self.chunks[k]
        kind = ch.kind
        own, flip = me.chips[0][0][r], me.chips[1][0][r]
        z = me.planes[r]
        if what == "d":
            self.plane_copy(k, r).start()
        elif what == "q":
            self.plane_copy(k, r).wait_recv()
            ch.plane_add(z)
            self.copy(k, me.chips[0][1][r], 1, me.qn, self.q_slot(False, z)).start()
            self.copy(k, me.chips[1][1][r], 1, me.qn, self.q_slot(True, z)).start()
        elif what == "a":
            self.take(k, flip, [self.q_slot(True, z)])
            self.copy(k, flip, 0, me.pn, self.p_slot(kind, z)).start()
        elif what == "l":
            first = [self.q_slot(False, z)] + ([self.p_slot(kind, z)] if kind == "a" else [])
            self.take(k, own, first)
            if kind == "c": self.take(k, flip, [self.q_slot(True, z)])
            flips = (False, True) if kind == "c" else (False,)
            def behind():
                for f in flips: self.take(k, flip if f else own, [self.line_slot(f, z)])
            when((z < me.z) & me.has_up, behind)
            when((z > me.z) & me.has_down, behind)
            def send(way, target, late):
                for f in flips:
                    self.copy(k, flip if f else own, way, target, self.late_slot(f) if late else self.line_slot(f, z)).start()
            when((z > me.z) & (z == me.z + 1), lambda: send(2, me.up, False))
            when((z > me.z) & (z != me.z + 1), lambda: send(2, me.up, False))
            when((z < me.z) & (z == me.z - 1), lambda: send(3, me.down, True))
            when((z < me.z) & (z != me.z - 1), lambda: send(3, me.down, False))
        elif what in "po":
            f = what == "p"
            chip = flip if f else own
            slots = [self.q_slot(f, z)]
            if not f: slots.append(self.p_slot(kind, z))
            when(me.has_down, lambda: self.take(k, chip, [self.line_slot(f, z)]))
            when(me.has_up, lambda: self.take(k, chip, [self.late_slot(f)]))
            self.take(k, chip, slots, None if f else ch.result)
            if f: self.copy(k, chip, 0, me.pn, self.p_slot(kind, z)).start()
    def drain(self, k):
        me, Z = self.me, self.Z
        per = 2 if self.chunks[k].kind == "c" else 1
        counts = [1 if per == 2 else Z, 2 * Z, jnp.where(me.has_up, per * (Z - 1 - me.z), 0), jnp.where(me.has_down, per * me.z, 0)]
        for way, count in enumerate(counts):
            def one(_, carry):
                self.copy(k, 0, way, me.pn, 0).wait_send()
                return carry
            lax.fori_loop(0, count, one, 0)
        def one(_, carry):
            self.plane_copy(k, 0).wait_send()
            return carry
        lax.fori_loop(0, Z, one, 0)


def dot(a, b):
    return jnp.dot(a, b, preferred_element_type=F32)


def dot_nt(a, b):
    return lax.dot_general(a, b, (((1,), (1,)), ((), ())), preferred_element_type=F32)


def dot_tn(a, b):
    return lax.dot_general(a, b, (((0,), (0,)), ((), ())), preferred_element_type=F32)


def normalized(h):
    center = h - jnp.mean(h, axis=-1, keepdims=True)
    inverse = lax.rsqrt(jnp.mean(center * center, axis=-1, keepdims=True) + norm_eps)
    return center * inverse, inverse


def swap_halves(v, half):
    lanes = lax.broadcasted_iota(jnp.int32, v.shape, 1)
    width = v.shape[1]
    return jnp.where(lanes % (2 * half) < half, pltpu.roll(v, width - half, 1), pltpu.roll(v, half, 1))


def rotary_lanes(seq_length, head_width, lanes):
    half = head_width // 2
    frequency = (10000.0 ** (-np.arange(half, dtype=np.float32) / half)).astype(np.float32)
    angles = np.arange(seq_length, dtype=np.float32)[:, None] * frequency[None, :]
    cos, sin = np.cos(angles), np.sin(angles)
    both = np.stack([np.concatenate([cos, cos], 1), np.concatenate([-sin, sin], 1)])
    return np.tile(both, (1, 1, lanes // head_width)).astype(np.float32)


def add_sum(ref, row, lane, product):
    rows = lax.broadcasted_iota(jnp.int32, ref.shape, 0)
    lanes = lax.broadcasted_iota(jnp.int32, ref.shape, 1)
    total = jnp.sum(jnp.sum(product, axis=0, keepdims=True), axis=1, keepdims=True)
    ref[...] = ref[...] + jnp.where((rows == row) & (lanes == lane), total, 0.0)


class Forward:
    def __init__(self, w, io, s, planes, length, first, second):
        self.planes = planes
        self.w, self.io, self.s = w, io, s
        self.length, self.first, self.second = length, first, second
        self.T, self.D = s.h.shape
        self.width = self.D // HEADS
        self.q, self.o = 3 * self.D // 2, self.D // 2
        self.half = w.mix.shape[2] // 2
        self.writes = []

    def send(self, name, l=None):
        src, dst = getattr(self.s, name), getattr(self.io, name)
        if l is not None: src, dst = src.at[l], dst.at[l]
        n = len(self.writes)
        self.writes.append((src, dst, n))
        pltpu.make_async_copy(src, dst, self.io.wsem.at[n]).start()

    def finish(self):
        for src, dst, n in self.writes:
            pltpu.make_async_copy(src, dst, self.io.wsem.at[n]).wait()

    def load(self, i):
        s, io = self.s, self.io
        src, dst = ((io.h, s.h), (io.rope, s.rope), (io.cotangent, s.cotangent), (io.history, s.history))[i]
        return pltpu.make_async_copy(src, dst, io.isem.at[i])

    def setup(self):
        s, T = self.s, self.T
        row = lax.broadcasted_iota(jnp.int32, (T, T), 0)
        col = lax.broadcasted_iota(jnp.int32, (T, T), 1)
        s.bias[...] = jnp.where((col <= row) & (col < self.length), 0.0, masked_score)
        s.sums[...] = jnp.zeros_like(s.sums)

    def loss_grad(self):
        s, io = self.s, self.io
        count = jnp.sum(s.gain[4:5, :])
        row = lax.broadcasted_iota(jnp.int32, (self.T, 1), 0)
        grad = jnp.where(row < self.length, s.cotangent[...], 0.0) / count
        s.gout[...] = grad
        self.send("gout")
        n = s.history.shape[0]
        for j in range(n): add_sum(s.sums, 1, j, s.history[j].astype(F32) * grad)

    def layer_in(self, l):
        return self.s.h if l == 0 else self.s.carried

    def norm_one(self, l):
        s, w = self.s, self.w
        if l == 0:
            s.gain[...] = s.total[...]
            self.send("gain")
            for i in range(4): self.load(i).wait()
        x, _ = normalized(self.layer_in(l)[...])
        s.n1[l] = (x * s.gain[2 * l:2 * l + 1, :]).astype(BF)
        self.send("n1", l)

    def project(self, l, t):
        s, w = self.s, self.w
        h, i = divmod(t, 3)
        W = self.q // 3
        at = h * self.half + i * W
        joined = dot(s.n1[l], w.mix[l, :, at:at + W])
        for j in range(W // 128):
            col = t * W + j * 128
            part = joined[:, j * 128:(j + 1) * 128]
            if col < 2 * self.D:
                part = part * s.cos[...] + swap_halves(part, self.width // 2) * s.sin[...]
                if col < self.D: part = part * self.width ** -0.5
            s.qkv[l, :, col:col + 128] = part.astype(BF)

    def attend(self, l, a):
        s, D = self.s, self.D
        q, k, v = (s.qkv[l, :, i * D + a * 128:i * D + a * 128 + 128] for i in range(3))
        lanes = lax.broadcasted_iota(jnp.int32, q.shape, 1)
        outs = []
        for e in range(2):
            mine = (lanes < self.width) if e == 0 else (lanes >= self.width)
            scores = dot_nt(jnp.where(mine, q, jnp.zeros_like(q)), k) + s.bias[...]
            top = jnp.max(scores, axis=-1, keepdims=True)
            weights = jnp.exp(scores - top)
            probs = (weights * (1.0 / jnp.sum(weights, axis=-1, keepdims=True))).astype(BF)
            s.probs[l, 2 * a + e] = probs
            outs.append(dot(probs, v))
        s.att[l, :, a * 128:a * 128 + 128] = jnp.where(lanes < self.width, outs[0], outs[1]).astype(BF)

    def attend_done(self, l):
        for name in ("qkv", "probs", "att"): self.send(name, l)

    def out(self, l, h):
        s, w = self.s, self.w
        cols = slice(h * self.o, (h + 1) * self.o)
        at = h * self.half + self.q
        s.after[l, :, cols] = self.layer_in(l)[:, cols] + dot(s.att[l], w.mix[l, :, at:at + self.o])

    def norm_two(self, l):
        s = self.s
        x, _ = normalized(s.after[l])
        s.n2[l] = (x * s.gain[2 * l + 1:2 * l + 2, :]).astype(BF)
        self.send("n2", l)
        self.send("after", l)

    def raise_(self, l, t, W):
        s, w = self.s, self.w
        u = dot(s.n2[l], w.up[l, :, t * W:(t + 1) * W])
        tile, at = divmod(t * W, self.D)
        cols = slice(at, at + W)
        square = u * u
        tangent = jnp.tanh(gelu_scale * u * (1.0 + gelu_coef * square))
        s.act[l, tile, :, cols] = (0.5 * u * (1.0 + tangent)).astype(BF)
        s.slope[l, tile, :, cols] = (
            0.5 * (1.0 + tangent) + 0.5 * u * (1.0 - tangent * tangent) * gelu_scale * (1.0 + 3.0 * gelu_coef * square)
        ).astype(BF)

    def raise_done(self, l):
        for name in ("act", "slope"): self.send(name, l)

    def lower(self, l, r):
        s, w = self.s, self.w
        z = self.planes[r]
        chips = w.down.shape[1] // len(self.planes)
        part = dot(s.act[l, z], w.down[l, pl.ds(z * chips, chips)].reshape(-1, self.D))
        s.stored[l] = (s.after[l] if r == 0 else s.stored[l]) + part

    def mixed(self, l):
        s, io = self.s, self.io
        n = s.history.shape[0]
        if l == 0:
            s.carried[...] = mix_history([self.first[j] for j in range(n)], s.history) + self.first[n] * s.stored[0]
            self.send("carried")
        else:
            s.blended[...] = (
                mix_history([self.second[j] for j in range(n)], s.history)
                + self.second[n] * s.stored[0] + self.second[n + 1] * s.stored[1]
            )
            self.send("blended")
        self.send("stored", l)
        add_sum(s.sums, 1, n + l, s.stored[l] * s.gout[...])
        if l == 1: self.send("sums")

    def steps(self):
        out = [(-1, self.setup)]
        P = functools.partial
        for l in range(2):
            k = 3 * l
            out.append((k, P(self.norm_one, l)))
            out += [(k, P(self.project, l, t)) for t in range(6)]
            if l == 0: out.append((k, self.loss_grad))
            out += [(k, P(self.attend, l, a)) for a in range(self.D // 128)]
            out.append((k, P(self.attend_done, l)))
            out += [(k, P(self.out, l, h)) for h in range(2)]
            out.append((k, P(self.norm_two, l)))
            W = self.D // 2
            out += [(k + 1, P(self.raise_, l, t, W)) for t in range(4 * self.D // W)]
            out.append((k + 1, P(self.raise_done, l)))
            out += [((k + 2, r), P(self.lower, l, r)) for r in range(len(self.planes))]
            out.append((k + 2, P(self.mixed, l)))
        return out


def weave(order, work):
    left, whole, done, queue = {}, set([-1]), [], list(work)
    for v in order:
        if v != NEXT and v[1] == "d": left[v[0]] = left.get(v[0], 0) + 1
    for v in order:
        if v == NEXT:
            need, act = queue.pop(0)
            assert need in whole
            done.append(act)
            continue
        done.append(v)
        k, what, r = v
        if what == "d":
            whole.add((k, r))
            left[k] -= 1
            if not left[k]: whole.add(k)
    assert not queue
    return done


def saved_shapes(T, D, FF):
    return dict(n1=((2, T, D), BF), qkv=((2, T, 3 * D), BF), probs=((2, HEADS, T, T), BF), att=((2, T, D), BF), after=((2, T, D), F32),
        n2=((2, T, D), BF), act=((2, FF // D, T, D), BF), slope=((2, FF // D, T, D), BF), stored=((2, T, D), F32), carried=((T, D), F32),
        blended=((T, D), F32), gout=((T, D), F32), sums=((8, D), F32), gain=((8, D), F32))


SAVED = tuple(saved_shapes(1, 1, 1))


def fwd_kernel(depth, order, kinds, qkv_in, out_in, up_in, down_in, gain_in, h_in, history_in, cotangent_in, rope_in, length, first, second,
              mix_o, up_o, down_o, *rest):
    n = len(SAVED)
    saved_o, rest = rest[:n], rest[n:]
    (mix_b, up_b, down_b, mix_s, up_s, mix_t, up_t, ssem, rsem, esem, lsem, wsem, isem, bias, value, land, h_b, history_b, cotangent_b,
        rope_b, tsend, trecv), saved_b = rest[:22], rest[22:]
    me = Place(depth)
    bar = greet(me, True)
    rows = qkv_in.shape[1]
    c = me.c
    wq, wo, wu = qkv_in.shape[2] // 2, out_in.shape[2] // 2, up_in.shape[2] // 2
    mine = lambda w: pl.ds(al(c * w, 128), w)
    other = lambda w: pl.ds(al((1 - c) * w, 128), w)
    my_rows = pl.ds(al(c * rows, 8), rows)
    def stage(k):
        l, j = divmod(k, 3)
        if j == 0:
            for ref, at, pick in ((mix_s, (l, my_rows), mine), (mix_t, (l, slice(None)), other)):
                ref[at[0], at[1], 0:wq] = qkv_in[l, :, pick(wq)].astype(F32)
                ref[at[0], at[1], wq:wq + wo] = out_in[l, :, pick(wo)].astype(F32)
        elif j == 1:
            up_s[l, my_rows, :] = up_in[l, :, mine(wu)].astype(F32)
            up_t[l] = up_in[l, :, other(wu)].astype(F32)
    def place_gains():
        small = value.at[2]
        small[...] = jnp.zeros_like(small)
        for l in range(2): small[2 * l:2 * l + 2, 0:rows] = gain_in[l].astype(F32)
        n = value.shape[2]
        at = rows * (me.w * 4 + me.n)
        one = lax.broadcasted_iota(jnp.int32, (128, n), 1) == lax.broadcasted_iota(jnp.int32, (128, n), 0) + at
        own = dot(small[:, 0:128].astype(BF), one.astype(BF))
        row = lax.broadcasted_iota(jnp.int32, own.shape, 0)
        col = lax.broadcasted_iota(jnp.int32, own.shape, 1)
        value[0] = own + jnp.where((row == 4) & (col == 0), length[0].astype(F32), 0.0)
    def exchange(k):
        l, j = divmod(k, 3)
        if j == 2: return None
        s, t = ((mix_s, mix_t), (up_s, up_t))[j]
        return pltpu.make_async_remote_copy(src_ref=t.at[l], dst_ref=s.at[l, my_rows, :], send_sem=esem.at[0, k],
            recv_sem=esem.at[1, k], device_id=me.sib, device_id_type=MESH)
    def ready(k):
        l, j = divmod(k, 3)
        if j == 2:
            down_b[l, me.chip, c] = down_in[l]
            return
        exchange(k).wait_recv()
        s, b = ((mix_s, mix_b), (up_s, up_b))[j]
        b[l, pl.ds(al(me.chip * 2 * rows, 16), 2 * rows), mine(s.shape[2])] = s[l].astype(BF)
    chunks = []
    for k in range(6):
        l, j = divmod(k, 3)
        if j == 2:
            chunks.append((kinds[k], lambda chip, n, l=l: down_b.at[l, pl.ds(chip, n), c], lambda z, l=l: down_b.at[l, pl.ds(z * 4, 4), c]))
        else:
            b = (mix_b, up_b)[j]
            half = b.shape[2] // 2
            chunks.append((kinds[k],
                lambda chip, n, b=b, l=l, half=half: b.at[l, pl.ds(al(chip * 2 * rows, 16), n * 2 * rows), mine(half)],
                lambda z, b=b, l=l, half=half: b.at[l, pl.ds(al(z * 8 * rows, 16), 8 * rows), mine(half)]))
    gather = Gather(me, chunks, ssem, rsem)
    io = SimpleNamespace(**dict(zip(SAVED, saved_o)), h=h_in, history=history_in, cotangent=cotangent_in, rope=rope_in,
        wsem=wsem, isem=isem)
    scratch = SimpleNamespace(**dict(zip(SAVED, saved_b)), bias=bias, total=value.at[4], h=h_b, history=history_b,
        cotangent=cotangent_b, rope=rope_b, cos=rope_b.at[0], sin=rope_b.at[1])
    fwd = Forward(SimpleNamespace(mix=mix_b, up=up_b, down=down_b), io, scratch, me.planes, length[0], first, second)
    first_out = []
    for v in order:
        if v != NEXT and v[1] == "o" and v[0] % 3 < 2: first_out.append(v[0])
    for k in first_out[:2]: stage(k)
    greeted(me, bar, True)
    for k in first_out[:2]: exchange(k).start()
    total = Total(me, value, land, tsend, trecv)
    def settle():
        place_gains()
        total.step(0)
        for i in range(4): fwd.load(i).start()
        for k in first_out[2:]:
            stage(k)
            exchange(k).start()
    pairs = ((mix_b, mix_o), (up_b, up_o), (down_b, down_o))
    def write(k, r):
        l, j = divmod(k, 3)
        b, o = pairs[j]
        n = b.shape[1] // depth
        at = pl.ds(al(me.planes[r] * n, n), n)
        return pltpu.make_async_copy(b.at[l, at], o.at[l, at], lsem.at[k, r])
    totals, count, sent = [1, 2, 3, 4], 0, 0
    for item in weave(order, fwd.steps()):
        if not isinstance(item, tuple):
            item()
            continue
        k, what, r = item
        if what == "o":
            if settle and k in first_out[2:]:
                settle()
                settle = None
            ready(k)
        gather.event(k, what, r)
        if what == "o" and settle:
            if k % 3 < 2: sent += 1
            if sent == 2:
                settle()
                settle = None
        if what == "d": write(k, r).start()
        count += 1
        if totals and not settle and count % 5 == 0: total.step(totals.pop(0))
    for k in range(6):
        gather.drain(k)
        if k % 3 < 2: exchange(k).wait_send()
    for k in range(6):
        for r in range(depth): write(k, r).wait()
    fwd.finish()

def fwd_call(mesh, order, kinds, w_qkv, w_out, w_up, w_down, gains, h, history, cotangent, rope, lengths, first, second):
    depth = mesh.shape["wide"] // 2
    rows = w_qkv.shape[1]
    D, FF = rows * mesh.size, w_down.shape[1] * mesh.size
    T = h.shape[0]
    n = mesh.size // 2
    M = 4 * D
    body = functools.partial(fwd_kernel, depth, order, kinds)
    vm = pl.BlockSpec(memory_space=pltpu.VMEM); an = pl.BlockSpec(memory_space=pl.ANY); sm = pl.BlockSpec(memory_space=pltpu.SMEM)
    shapes = [((2, D, M), BF), ((2, D, FF), BF), ((2, n, 2, FF // n // 2, D), BF)]
    saved = list(saved_shapes(T, D, FF).values())
    got = pl.pallas_call(body,
        out_shape=[jax.ShapeDtypeStruct(s, d) for s, d in shapes + saved],
        in_specs=[vm] * 5 + [an] * 4 + [sm] * 3, out_specs=[an] * (3 + len(saved)),
        scratch_shapes=[pltpu.VMEM(s, d) for s, d in shapes] + [
            pltpu.VMEM((2, 2 * rows, M // 2), F32), pltpu.VMEM((2, 2 * rows, FF // 2), F32),
            pltpu.VMEM((2, rows, M // 2), F32), pltpu.VMEM((2, rows, FF // 2), F32),
            pltpu.SemaphoreType.DMA((6, 5)), pltpu.SemaphoreType.DMA((6, 4 * depth)),
            pltpu.SemaphoreType.DMA((2, 6)), pltpu.SemaphoreType.DMA((6, depth)), pltpu.SemaphoreType.DMA((24,)),
            pltpu.SemaphoreType.DMA((4,)), pltpu.VMEM((T, T), F32), pltpu.VMEM((5, 8, D), F32), pltpu.VMEM((2 + depth, 8, D), F32),
            pltpu.VMEM(h.shape, F32), pltpu.VMEM(history.shape, BF), pltpu.VMEM(cotangent.shape, F32), pltpu.VMEM(rope.shape, F32), pltpu.SemaphoreType.DMA((2 + depth,)), pltpu.SemaphoreType.DMA((2 + depth,))] + [pltpu.VMEM(s, d) for s, d in saved],
        compiler_params=pltpu.CompilerParams(collective_id=0, has_side_effects=True, vmem_limit_bytes=62 * 2**20),
        cost_estimate=pl.CostEstimate(flops=16 * T * D * FF, bytes_accessed=2**26, transcendentals=2**21),
    )(w_qkv, w_out, w_up, w_down, gains, h, history, cotangent, rope, lengths, first, second)
    return got[:3], SimpleNamespace(**dict(zip(SAVED, got[3:])))


def norm_back(e, h, gain):
    unit, inverse = normalized(h)
    scaled = e * gain
    grad = inverse * (scaled - jnp.mean(scaled, axis=-1, keepdims=True) - unit * jnp.mean(scaled * unit, axis=-1, keepdims=True))
    return grad, jnp.sum(e * unit, axis=0, keepdims=True)


class Backward:
    def __init__(self, io, s, g, planes, first, second):
        self.planes = planes
        self.io, self.s, self.g = io, s, g
        self.first, self.second = first, second
        self.T, self.D = s.gy.shape
        self.width = self.D // HEADS
        self.q, self.o = 3 * self.D // 2, self.D // 2
        self.half = g.mix.shape[1] // 2
        self.tiles = s.act.shape[0]
        self.hist = io.history.shape[0]
        self.writes = []

    SLOTS = ("act", "slope", "n2", "n1", "att", "after", "h", "probs", "qkv", "mix", "history")

    def load(self, name, src, dst=None):
        i = self.SLOTS.index(name)
        return pltpu.make_async_copy(src, getattr(self.s, name) if dst is None else dst, self.io.load_sem.at[i])

    def source(self, name, l):
        return getattr(self.io, name).at[l]

    def fetch(self, l, names):
        for name in names:
            src = (self.io.inputs if l == 0 else self.io.carried) if name == "h" else getattr(self.io, name).at[l]
            self.load(name, src).start()

    def here(self, l, *names):
        for name in names:
            src = (self.io.inputs if l == 0 else self.io.carried) if name == "h" else getattr(self.io, name).at[l]
            self.load(name, src).wait()

    def tile_copy(self, l, t, up):
        src = self.io.up.at[l, :, pl.ds(t * self.D, self.D)] if up else self.io.down.at[l, t]
        return pltpu.make_async_copy(src, self.s.tile.at[t], self.io.tile_sem.at[t])

    def send(self, src, dst):
        n = len(self.writes)
        self.writes.append((src, dst, n))
        pltpu.make_async_copy(src, dst, self.io.write_sem.at[n]).start()

    def finish(self):
        for src, dst, n in self.writes:
            pltpu.make_async_copy(src, dst, self.io.write_sem.at[n]).wait()

    def begin(self):
        self.fetch(1, ("act",))
        for t in range(self.tiles): self.tile_copy(1, t, False).start()
        self.fetch(1, ("slope", "n2"))
        s = self.s
        s.gy[...] = self.second[self.hist + 1] * self.io.gout[...]

    def down_weight(self, l, r):
        s = self.s
        if r == len(self.planes) - 1:
            s.gm[...] = s.gy[...].astype(BF)
            self.here(l, "act")
        z = self.planes[r]
        chips = self.g.down.shape[0] // len(self.planes)
        grad = dot_tn(s.act[z], s.gm[...])
        self.g.down[pl.ds(z * chips, chips)] = grad.astype(BF).reshape((chips,) + self.g.down.shape[1:])

    def act_grad(self, l, t):
        s = self.s
        if t == 0: self.here(l, "slope")
        if l == 1 and t == 1: self.fetch(1, ("after", "mix", "probs", "qkv"))
        self.tile_copy(l, t, False).wait()
        grad = dot_nt(s.gm[...], s.tile[t])
        s.slope[t] = (grad * s.slope[t].astype(F32)).astype(BF)
        self.tile_copy(l, t, True).start()

    def turned(self, l, name):
        self.here(l, name)
        self.s.turned[...] = getattr(self.s, name)[...].T

    def up_weight(self, l, t):
        s = self.s
        tile, at = divmod(t * self.o, self.D)
        self.g.up[:, t * self.o:(t + 1) * self.o] = dot(s.turned[...], s.slope[tile, :, at:at + self.o]).astype(BF)

    def norm_two_grad(self, l, t):
        s = self.s
        self.tile_copy(l, t, True).wait()
        part = dot_nt(s.slope[t], s.tile[t])
        if l == 1 and t == 1:
            self.fetch(1, ("att", "n1", "h"))
            self.load("history", self.io.history).start()
        if t == 0: s.gn[...] = part
        else: s.gn[...] = s.gn[...] + part
        if l == 1: self.tile_copy(0, t, False).start()

    def after_grad(self, l):
        s = self.s
        self.here(l, "after")
        grad, gain = norm_back(s.gn[...], s.after[...], self.io.gain[2 * l + 1:2 * l + 2, :])
        s.sums[3 + 2 * l:4 + 2 * l, :] = gain
        s.gy[...] = s.gy[...] + grad
        s.gm[...] = s.gy[...].astype(BF)
        if l == 1:
            self.fetch(0, ("slope", "n2", "act"))
            self.load("after", self.io.stored.at[0]).start()

    def out_weight(self, l, h):
        s = self.s
        if h == 0: self.turned(l, "att")
        at = h * self.half + self.q
        self.g.mix[:, at:at + self.o] = dot(s.turned[...], s.gm[:, h * self.o:(h + 1) * self.o]).astype(BF)

    def att_grad(self, l):
        s = self.s
        self.here(l, "mix")
        a, b = self.q, self.half + self.q
        grad = dot_nt(s.gm[:, :self.o], s.mix[:, a:a + self.o]) + dot_nt(s.gm[:, self.o:], s.mix[:, b:b + self.o])
        s.ga[...] = grad.astype(BF)

    def attend(self, l, a):
        s, D = self.s, self.D
        if a == 0: self.here(l, "probs", "qkv")
        q, k, v = (s.qkv[:, i * D + a * 128:i * D + a * 128 + 128] for i in range(3))
        ga = s.ga[:, a * 128:a * 128 + 128]
        lanes = lax.broadcasted_iota(jnp.int32, q.shape, 1)
        got = []
        for e in range(2):
            mine = (lanes < self.width) if e == 0 else (lanes >= self.width)
            probs = s.probs[2 * a + e]
            wide = probs.astype(F32)
            gp = wide * dot_nt(jnp.where(mine, ga, jnp.zeros_like(ga)), v)
            gs = (gp - wide * jnp.sum(gp, axis=-1, keepdims=True)).astype(BF)
            got.append((dot(gs, k), dot_tn(gs, q), dot_tn(probs, ga)))
        gq, gk, gv = (jnp.where(lanes < self.width, x, y) for x, y in zip(*got))
        back = lambda g: g * s.cos[...] - swap_halves(g, self.width // 2) * s.sin[...]
        for i, g in enumerate((back(gq) * self.width ** -0.5, back(gk), gv)):
            s.gj[:, i * D + a * 128:i * D + a * 128 + 128] = g.astype(BF)

    def qkv_weight(self, l, t):
        s = self.s
        if t == 0:
            self.turned(l, "n1")
            if l == 1: self.fetch(0, ("probs", "qkv", "n1", "att"))
        h, i = divmod(t, 3)
        W = self.q // 3
        at = h * self.half + i * W
        self.g.mix[:, at:at + W] = dot(s.turned[...], s.gj[:, t * W:(t + 1) * W]).astype(BF)

    def norm_one_grad(self, l, t):
        s = self.s
        W = self.D // 3
        rows = slice(t * W, (t + 1) * W)
        b = self.half
        s.gn[:, rows] = dot_nt(s.gj[:, :self.q], s.mix[rows, :self.q]) + dot_nt(s.gj[:, self.q:], s.mix[rows, b:b + self.q])

    def layer_grad(self, l):
        s = self.s
        self.here(l, "h")
        grad, gain = norm_back(s.gn[...], s.h[...], self.io.gain[2 * l:2 * l + 1, :])
        s.sums[2 + 2 * l:3 + 2 * l, :] = gain
        s.gy[...] = s.gy[...] + grad
        if l == 1: self.fetch(0, ("mix", "h"))
        if l == 1:
            s.kept[...] = s.gy[...]
            self.send(s.kept, self.io.grad_carried)
        else: self.send(s.gy, self.io.grad_inputs)

    def between(self):
        s, n = self.s, self.hist
        self.load("history", self.io.history).wait()
        self.load("after", self.io.stored.at[0]).wait()
        grad = s.gy[...]
        for j in range(n): add_sum(s.sums, 0, j, s.history[j].astype(F32) * grad)
        add_sum(s.sums, 0, n, s.after[...] * grad)
        s.gy[...] = self.first[n] * grad + self.second[n] * self.io.gout[...]
        self.fetch(0, ("after",))

    def steps(self):
        P = functools.partial
        out = [("do", -1, self.begin)]
        for l in (1, 0):
            k = 3 * l
            tiles = range(self.tiles)
            if l == 0: out.append(("do", -1, self.between))
            out += [("make", (k + 2, r), P(self.down_weight, l, r)) for r in reversed(range(len(self.planes)))]
            out += [("do", -1, P(self.act_grad, l, t)) for t in tiles]
            out.append(("do", -1, P(self.turned, l, "n2")))
            out += [("make", (k + 1, -1), P(self.up_weight, l, t)) for t in range(2 * self.tiles)]
            out += [("do", -1, P(self.norm_two_grad, l, t)) for t in tiles]
            out.append(("do", -1, P(self.after_grad, l)))
            out.append(("do", -1, P(self.att_grad, l)))
            out += [("do", -1, P(self.attend, l, a)) for a in range(self.D // 128)]
            out += [("make", (k, -1), P(self.out_weight, l, h)) for h in range(2)]
            out += [("make", (k, -1), P(self.qkv_weight, l, t)) for t in range(6)]
            out += [("do", -1, P(self.norm_one_grad, l, t)) for t in range(3)]
            out.append(("sums" if l == 0 else "do", -1, P(self.layer_grad, l)))
        return out


def weave_back(order, work):
    to_make, over, drained, done, queue = {}, set(), set(), [], list(work)
    for name, k, _ in work:
        if name == "make": to_make[k] = to_make.get(k, 0) + 1
    for v in order:
        if v == NEXT:
            name, k, act = queue.pop(0)
            if name == "make":
                before = k[0] + 3
                if k[0] < 3 and before not in drained:
                    assert before in over
                    drained.add(before)
                    done.append(("drain", before))
                to_make[k] -= 1
            done.append(act)
            if name == "sums": done.append(("sums", 0))
            continue
        k, what, r = v
        if what == "d": assert not to_make.get((k, r), 0) and not to_make.get((k, -1), 0)
        if what == "o": over.add(k)
        done.append(v)
    assert not queue
    return done


class Total:
    def __init__(self, me, value, land, ssem, rsem):
        self.me, self.value, self.land, self.ssem, self.rsem = me, value, land, ssem, rsem
    def copy(self, i, src, target):
        return pltpu.make_async_remote_copy(src_ref=src, dst_ref=self.land.at[i], send_sem=self.ssem.at[i], recv_sem=self.rsem.at[i],
            device_id=target, device_id_type=MESH)
    def step(self, n):
        me, v = self.me, self.value
        targets = (me.sib, me.xn, me.yn)
        if 0 < n <= 3:
            self.copy(n - 1, v.at[n - 1], targets[n - 1]).wait()
            v[n] = v[n - 1] + self.land[n - 1]
        if n < 3: self.copy(n, v.at[n], targets[n]).start()
        elif n == 3:
            for i, t in enumerate(me.line): self.copy(3 + i, v.at[3], t).start()
        else:
            total = v[3]
            for i, t in enumerate(me.line):
                self.copy(3 + i, v.at[3], t).wait()
                total = total + self.land[3 + i]
            v[4] = total


def bwd_kernel(depth, order, kinds, gout_in, sums_in, gain_in, rope_in, first, second, *rest):
    io, rest = SimpleNamespace(), rest
    (io.mix, io.up, io.down, io.n1, io.qkv, io.probs, io.att, io.after, io.n2, io.act, io.slope, io.stored, io.carried, io.inputs,
        io.history), rest = rest[:15], rest[15:]
    (mix_o, up_o, down_o, io.grad_carried, io.grad_inputs, sums_o), rest = rest[:6], rest[6:]
    (mix_g, up_g, down_g, mix_d, up_d, down_d, mix_l, up_l, down_l, mix_f, up_f, down_f,
        ssem, rsem, esem, credit, io.load_sem, io.tile_sem, io.write_sem, tsend, trecv, fsem), rest = rest[:22], rest[22:]
    io.gout, io.gain = gout_in, gain_in
    s = SimpleNamespace(cos=rope_in.at[0], sin=rope_in.at[1])
    (s.tile, s.mix, s.act, s.slope, s.n2, s.n1, s.att, s.after, s.h, s.probs, s.qkv, s.gy, s.gn, s.gm, s.ga, s.gj, s.turned, s.history,
        s.kept, s.value, s.land) = rest
    scratch = s
    scratch.sums = scratch.value.at[0]
    me = Place(depth)
    c = me.c
    bar = greet(me, True)
    rows = mix_o.shape[1]
    mine = lambda w: pl.ds(al(c * w, 128), w)
    other = lambda w: pl.ds(al((1 - c) * w, 128), w)
    bwd = Backward(io, scratch, SimpleNamespace(mix=mix_g, up=up_g, down=down_g), me.planes, first, second)
    scratch.value[0] = sums_in[...]
    chunks = {}
    for k in range(6):
        l, j = divmod(k, 3)
        if j == 2:
            R = down_g.shape[2]
            def plane_add(z):
                for i in range(4): add_into(down_g.at[z * 4 + i, c], [down_d.at[z * 4 + i]], R)
            chunks[k] = SimpleNamespace(kind=kinds[k], rows=R, share=lambda chip: down_g.at[chip, c],
                plane=lambda z, own: down_g.at[pl.ds(z * 4, 4), c if own else 1 - c], plane_land=lambda z: down_d.at[pl.ds(z * 4, 4)],
                plane_add=plane_add, land=lambda s: down_l.at[s], result=down_f.at[l])
        else:
            g, d, land, f = ((mix_g, mix_d, mix_l, mix_f), (up_g, up_d, up_l, up_f))[j]
            half = g.shape[1] // 2
            def plane_add(z, g=g, d=d, half=half):
                at = pl.ds(al(z * 8 * rows, 16), 8 * rows)
                add_into(g.at[at, mine(half)], [d.at[at, :]], 8 * rows)
            chunks[k] = SimpleNamespace(kind=kinds[k], rows=2 * rows, share=lambda chip, g=g, half=half: g.at[pl.ds(al(chip * 2 * rows, 16), 2 * rows), mine(half)],
                plane=lambda z, own, g=g, half=half: g.at[pl.ds(al(z * 8 * rows, 16), 8 * rows), mine(half) if own else other(half)],
                plane_land=lambda z, d=d: d.at[pl.ds(al(z * 8 * rows, 16), 8 * rows), :],
                plane_add=plane_add, land=lambda s, land=land: land.at[s], result=f.at[l])
    sc = Scatter(me, chunks, ssem, rsem)
    total = Total(me, scratch.value, scratch.land, tsend, trecv)
    def result(k):
        l, j = divmod(k, 3)
        if j == 2: return [pltpu.make_async_copy(down_f.at[l], down_o.at[l], fsem.at[k])]
        f, o = ((mix_f, mix_o), (up_f, up_o))[j]
        half = f.shape[2]
        return [pltpu.make_async_copy(f.at[l, pl.ds(al(c * rows, 8), rows), :], o.at[l, :, mine(half)], fsem.at[k]),
            pltpu.make_async_remote_copy(src_ref=f.at[l, pl.ds(al((1 - c) * rows, 8), rows), :], dst_ref=o.at[l, :, mine(half)],
                send_sem=esem.at[0, k], recv_sem=esem.at[1, k], device_id=me.sib, device_id_type=MESH)]
    def tell(j):
        for d in (me.xn, me.yn): pl.semaphore_signal(credit.at[1, j], inc=1, device_id=d, device_id_type=MESH)
        when(me.has_up, lambda: pl.semaphore_signal(credit.at[2, j], inc=1, device_id=me.up, device_id_type=MESH))
        when(me.has_down, lambda: pl.semaphore_signal(credit.at[2, j], inc=1, device_id=me.down, device_id_type=MESH))
    planes_left, told, totals = {k: depth for k in range(6)}, {}, []
    greeted_yet = []
    for n, item in enumerate(weave_back(order, bwd.steps())):
        if not isinstance(item, tuple):
            item()
            continue
        if not greeted_yet:
            greeted(me, bar, True)
            greeted_yet.append(1)
        if item[0] == "drain":
            sc.drain(item[1])
            continue
        if item[0] == "sums":
            totals = [0, 1, 2, 3, 4]
            since = 0
            continue
        k, what, r = item
        l, j = divmod(k, 3)
        if l == 0 and what == "d" and (0, j) not in told:
            told[0, j] = True
            pl.semaphore_wait(credit.at[0, j], 1)
        if l == 0 and what == "q" and (1, j) not in told:
            told[1, j] = True
            pl.semaphore_wait(credit.at[1, j], 2)
        if l == 0 and what == "l" and (2, j) not in told:
            told[2, j] = True
            pl.semaphore_wait(credit.at[2, j], me.has_up.astype(jnp.int32) + me.has_down.astype(jnp.int32))
        sc.event(k, what, r)
        if what == "q":
            planes_left[k] -= 1
            if l == 1 and planes_left[k] == 0:
                pl.semaphore_signal(credit.at[0, j], inc=1, device_id=me.sib, device_id_type=MESH)
        if what == "o":
            for cp in result(k): cp.start()
            if l == 1: tell(j)
        if totals:
            since += 1
            if since % 4 == 0: total.step(totals.pop(0))
    for i in totals: total.step(i)
    sums_o[...] = scratch.value[4]
    for k in range(3): sc.drain(k)
    for k in range(6):
        for cp in result(k): cp.wait()
    bwd.finish()


def bwd_call(mesh, order, kinds, weights, saved, inputs, history, rope, first, second):
    mix, up, down = weights
    depth = mesh.shape["wide"] // 2
    D, M = mix.shape[1:]
    FF = up.shape[2]
    T = inputs.shape[0]
    n = mesh.size // 2
    rows, drows = D // mesh.size, FF // mesh.size
    down = down.reshape(2, FF // D, D, D)
    slots = 4 * depth + 3
    body = functools.partial(bwd_kernel, depth, order, kinds)
    vm = pl.BlockSpec(memory_space=pltpu.VMEM); an = pl.BlockSpec(memory_space=pl.ANY); sm = pl.BlockSpec(memory_space=pltpu.SMEM)
    V, S = pltpu.VMEM, pltpu.SemaphoreType.DMA
    return pl.pallas_call(body,
        out_shape=[jax.ShapeDtypeStruct(s, F32) for s in ((2, rows, M), (2, rows, FF), (2, drows, D), (T, D), (T, D), (8, D))],
        in_specs=[vm] * 4 + [sm] * 2 + [an] * 15, out_specs=[an] * 5 + [vm],
        scratch_shapes=[V((D, M), BF), V((D, FF), BF), V((n, 2, drows, D), BF),
            V((D, M // 2), BF), V((D, FF // 2), BF), V((n, drows, D), BF),
            V((slots, 2 * rows, M // 2), BF), V((slots, 2 * rows, FF // 2), BF), V((slots, drows, D), BF),
            V((2, 2 * rows, M // 2), F32), V((2, 2 * rows, FF // 2), F32), V((2, drows, D), F32),
            S((6, 5)), S((6, slots + depth)), S((2, 6)), pltpu.SemaphoreType.REGULAR((3, 3)),
            S((len(Backward.SLOTS),)), S((FF // D,)), S((2,)), S((2 + depth,)), S((2 + depth,)), S((6,)),
            V((FF // D, D, D), BF), V((D, M), BF), V((FF // D, T, D), BF), V((FF // D, T, D), BF), V((T, D), BF), V((T, D), BF), V((T, D), BF),
            V((T, D), F32), V((T, D), F32), V((HEADS, T, T), BF), V((T, 3 * D), BF), V((T, D), F32), V((T, D), F32), V((T, D), BF),
            V((T, D), BF), V((T, 3 * D), BF), V((D, T), BF), V(history.shape, BF), V((T, D), F32), V((5, 8, D), F32),
            V((2 + depth, 8, D), F32)],
        compiler_params=pltpu.CompilerParams(collective_id=1, has_side_effects=True, vmem_limit_bytes=63 * 2**20),
        cost_estimate=pl.CostEstimate(flops=32 * T * D * FF, bytes_accessed=2**27, transcendentals=2**10),
    )(saved.gout, saved.sums, saved.gain, rope, first, second, mix, up, down, saved.n1, saved.qkv, saved.probs, saved.att,
        saved.after, saved.n2, saved.act, saved.slope, saved.stored, saved.carried, inputs, history)


def results_kernel(first, second, sums, sums_v, grad_carried, gout, blended, stored, grad_inputs, mix, up, down,
                   blended_o, stored_o, inputs_o, history_o, qkv_o, out_o, up_o, down_o, gain_o, first_o, second_o,
                   mixed, carried_b, gout_b, blended_b, stored_b, inputs_b, mix_b, up_b, down_b, sem):
    q, o = qkv_o.shape[2] // 2, out_o.shape[2] // 2
    half = mix.shape[2] // 2
    ins = [(grad_carried, carried_b), (gout, gout_b), (stored.at[0], stored_b.at[0]), (stored.at[1], stored_b.at[1]), (blended, blended_b), (grad_inputs, inputs_b), (mix, mix_b), (up, up_b), (down, down_b)]
    outs = [[], [], [(stored_b.at[0], stored_o.at[0])], [(stored_b.at[1], stored_o.at[1])], [(blended_b, blended_o)], [(inputs_b, inputs_o)], [], [(up_b, up_o)], [(down_b, down_o)]]
    for h in range(2):
        outs[6].append((mix_b.at[:, :, pl.ds(h * half, q)], qkv_o.at[:, :, pl.ds(h * q, q)]))
        outs[6].append((mix_b.at[:, :, pl.ds(h * half + q, o)], out_o.at[:, :, pl.ds(h * o, o)]))
    loads = [pltpu.make_async_copy(a, b, sem.at[i]) for i, (a, b) in enumerate(ins)]
    for cp in loads: cp.start()
    copies = []
    def leave(a, b):
        copies.append(pltpu.make_async_copy(a, b, sem.at[len(ins) + len(copies)]))
        copies[-1].start()
    hist = history_o.shape[0]
    for cp in loads[:2]: cp.wait()
    for j in range(hist):
        mixed[j] = first[j] * carried_b[...] + second[j] * gout_b[...]
        leave(mixed.at[j], history_o.at[j])
    for j in range(hist + 1): first_o[j] = sums[0, j]
    for j in range(hist + 2): second_o[j] = sums[1, j]
    for cp, pairs in list(zip(loads, outs))[2:]:
        cp.wait()
        for a, b in pairs: leave(a, b)
    rows = gain_o.shape[2]
    device = lax.axis_index("wide") * lax.axis_size("narrow") + lax.axis_index("narrow")
    own = pltpu.roll(sums_v[...], lax.rem(sums_v.shape[1] - device * rows, sums_v.shape[1]), 1)
    for l in range(2): gain_o[l] = own[2 + 2 * l:4 + 2 * l, 0:rows]
    for cp in copies: cp.wait()


def results_call(first, second, sums, grad_carried, saved, grad_inputs, mix, up, down, hist):
    T, D = grad_inputs.shape
    rows = mix.shape[1]
    vm = pl.BlockSpec(memory_space=pltpu.VMEM); an = pl.BlockSpec(memory_space=pl.ANY); sm = pl.BlockSpec(memory_space=pltpu.SMEM)
    shapes = [(T, D), (2, T, D), (T, D), (hist, T, D), (2, rows, 3 * D), (2, rows, D), up.shape, down.shape, (2, 2, rows), (hist + 1,), (hist + 2,)]
    return pl.pallas_call(results_kernel,
        out_shape=[jax.ShapeDtypeStruct(s, F32) for s in shapes],
        in_specs=[sm] * 3 + [vm] + [an] * 8, out_specs=[an] * 8 + [vm] + [sm] * 2,
        scratch_shapes=[pltpu.VMEM((hist, T, D), F32), pltpu.VMEM((T, D), F32), pltpu.VMEM((T, D), F32), pltpu.VMEM((T, D), F32), pltpu.VMEM((2, T, D), F32), pltpu.VMEM((T, D), F32),
            pltpu.VMEM(mix.shape, F32), pltpu.VMEM(up.shape, F32), pltpu.VMEM(down.shape, F32), pltpu.SemaphoreType.DMA((20 + hist,))],
        compiler_params=pltpu.CompilerParams(vmem_limit_bytes=60 * 2**20),
    )(first, second, sums, sums, grad_carried, saved.gout, saved.blended, saved.stored, grad_inputs, mix, up, down)


def fast_body(mesh, inputs, history, lengths, cotangent, w_qkv, w_out, w_up, w_down, gains, alpha_first, alpha_second):
    rope = jnp.asarray(rotary_lanes(inputs.shape[0], inputs.shape[1] // HEADS, 128))
    weights, saved = fwd_call(mesh, steps(GATHER_ORDER), GATHER_KINDS, w_qkv, w_out, w_up, w_down, gains,
        inputs, history, cotangent, rope, lengths, alpha_first, alpha_second)
    mix, up, down, grad_carried, grad_inputs, sums = bwd_call(mesh, steps(SCATTER_ORDER), SCATTER_KINDS, weights, saved,
        inputs, history, rope, alpha_first, alpha_second)
    return results_call(alpha_first, alpha_second, sums, grad_carried, saved, grad_inputs, mix, up, down, history.shape[0])


def solution(mesh):
    axes = ("wide", "narrow")
    split, row_split = P(None, axes, None), P(axes, None)
    placed = (row_split, split, P(axes), row_split, split, split, split, split, P(None, None, axes), P(), P())
    results = (row_split, split, row_split, split, split, split, split, split, P(None, None, axes), P(), P())

    def body(*args):
        rows, hist = args[4].shape[1], args[1].shape[0]
        fits = mesh.shape["narrow"] == 4 and mesh.shape["wide"] == 8 and rows % 8 == 0
        fits = fits and hist * args[4].shape[1] == args[7].shape[1]
        return fast_body(mesh, *args) if fits else plain_body(*args)

    return jax.shard_map(body, mesh=mesh, in_specs=placed, out_specs=results, check_vma=False)
```

```python
import functools
import math
from types import SimpleNamespace

import jax
import jax.numpy as jnp
import numpy as np
from jax import lax
from jax.experimental import pallas as pl
from jax.experimental.pallas import tpu as pltpu
from jax.sharding import PartitionSpec as P

MESH = pl.DeviceIdType.MESH
BF = jnp.bfloat16
F32 = jnp.float32


HEADS = 12


norm_eps = 1e-05
gelu_coef = 0.044715
gelu_scale = math.sqrt(2.0 / math.pi)
masked_score = -1e30


def product(left, right):
    return jnp.dot(left, right, preferred_element_type=jnp.float32)


def layer_norm(hidden, gain_row):
    center = hidden - jnp.mean(hidden, axis=-1, keepdims=True)
    inverse = lax.rsqrt(jnp.mean(center * center, axis=-1, keepdims=True) + norm_eps)
    standard = center * inverse
    return (standard * gain_row, standard, inverse)


def plain_norm_back(grad_rows, standard, inverse, gain_row):
    scaled = grad_rows * gain_row
    grad_gain = jnp.sum(grad_rows * standard, axis=0)
    grad_in = inverse * (
        scaled
        - jnp.mean(scaled, axis=-1, keepdims=True)
        - standard * jnp.mean(scaled * standard, axis=-1, keepdims=True)
    )
    return (grad_in, grad_gain)


def gelu(values):
    return (
        0.5
        * values
        * (1.0 + jnp.tanh(gelu_scale * (values + gelu_coef * values * values * values)))
    )


def gelu_slope(values):
    tangent = jnp.tanh(gelu_scale * (values + gelu_coef * values * values * values))
    return 0.5 * (1.0 + tangent) + 0.5 * values * (1.0 - tangent * tangent) * gelu_scale * (
        1.0 + 3.0 * gelu_coef * values * values
    )


def rotary_tables(seq_length, head_width):
    half_width = head_width // 2
    frequency = 10000.0 ** (-jnp.arange(half_width, dtype=jnp.float32) / half_width)
    angles = jnp.arange(seq_length, dtype=jnp.float32)[:, None] * frequency[None, :]
    return (jnp.cos(angles)[:, None, :], jnp.sin(angles)[:, None, :])


def rotate(values, cos_table, sin_table):
    half_width = values.shape[-1] // 2
    left_half = values[..., :half_width]
    right_half = values[..., half_width:]
    return jnp.concatenate(
        [
            left_half * cos_table - right_half * sin_table,
            right_half * cos_table + left_half * sin_table,
        ],
        axis=-1,
    )


def rotate_back(grad_rows, cos_table, sin_table):
    half_width = grad_rows.shape[-1] // 2
    left_grad = grad_rows[..., :half_width]
    right_grad = grad_rows[..., half_width:]
    return jnp.concatenate(
        [
            left_grad * cos_table + right_grad * sin_table,
            right_grad * cos_table - left_grad * sin_table,
        ],
        axis=-1,
    )


def allowed_mask(block_rows, key_count, length):
    row_place = jnp.arange(block_rows)
    col_place = jnp.arange(key_count)
    return (col_place[None, :] <= row_place[:, None]) & (col_place[None, :] < length)


def attention_forward(queries, key_rows, value_rows, length):
    seq_length, head_count, head_width = queries.shape
    score_scale = head_width ** (-0.5)
    block_rows = min(512, seq_length)
    scores = (
        jnp.einsum("qhe,khe->hqk", queries, key_rows, preferred_element_type=jnp.float32)
        * score_scale
    )
    allowed = allowed_mask(block_rows, block_rows, length)
    scores = jnp.where(allowed[None], scores, masked_score)
    row_top = jnp.max(scores, axis=-1, keepdims=True)
    exp_scores = jnp.exp(scores - row_top)
    row_total = jnp.sum(exp_scores, axis=-1, keepdims=True)
    prob_rows = (exp_scores / row_total).astype(jnp.bfloat16)
    pieces = jnp.einsum("hqk,khe->qhe", prob_rows, value_rows, preferred_element_type=jnp.float32)
    log_sums = row_top + jnp.log(row_total)
    return (pieces, log_sums)


def attention_backward(queries, key_rows, value_rows, log_sums, grad_attended, length):
    seq_length, head_count, head_width = queries.shape
    score_scale = head_width ** (-0.5)
    grad_keys = jnp.zeros(queries.shape, jnp.float32)
    grad_values = jnp.zeros(queries.shape, jnp.float32)
    block_rows = min(512, seq_length)
    scores = (
        jnp.einsum("qhe,khe->hqk", queries, key_rows, preferred_element_type=jnp.float32)
        * score_scale
    )
    allowed = allowed_mask(block_rows, block_rows, length)
    prob_rows = jnp.where(allowed[None], jnp.exp(scores - log_sums), 0.0)
    grad_prob = jnp.einsum(
        "qhe,khe->hqk", grad_attended, value_rows, preferred_element_type=jnp.float32
    )
    inner_sum = jnp.sum(prob_rows * grad_prob, axis=-1, keepdims=True)
    grad_score = (prob_rows * (grad_prob - inner_sum)).astype(jnp.bfloat16)
    grad_pieces = (
        jnp.einsum("hqk,khe->qhe", grad_score, key_rows, preferred_element_type=jnp.float32)
        * score_scale
    )
    grad_keys = grad_keys.at[:block_rows].add(
        jnp.einsum("hqk,qhe->khe", grad_score, queries, preferred_element_type=jnp.float32)
        * score_scale
    )
    grad_values = grad_values.at[:block_rows].add(
        jnp.einsum(
            "hqk,qhe->khe",
            prob_rows.astype(jnp.bfloat16),
            grad_attended,
            preferred_element_type=jnp.float32,
        )
    )
    return (grad_pieces, grad_keys, grad_values)


def layer_forward(hidden, weights, length):
    layer_qkv, layer_out, layer_up, layer_down, layer_gains = weights
    seq_length = hidden.shape[0]
    head_width = layer_out.shape[0] // HEADS
    normed, unit_one, inverse_one = layer_norm(hidden, layer_gains[0])
    normed = normed.astype(jnp.bfloat16)
    joined = product(normed, layer_qkv).reshape(seq_length, 3, HEADS, head_width)
    cos_table, sin_table = rotary_tables(seq_length, head_width)
    queries = rotate(joined[:, 0], cos_table, sin_table).astype(jnp.bfloat16)
    key_rows = rotate(joined[:, 1], cos_table, sin_table).astype(jnp.bfloat16)
    value_rows = joined[:, 2].astype(jnp.bfloat16)
    attended, log_sums = attention_forward(queries, key_rows, value_rows, length)
    attended = attended.reshape(seq_length, HEADS * head_width).astype(jnp.bfloat16)
    after_attn = hidden + product(attended, layer_out)
    normed_two, unit_two, inverse_two = layer_norm(after_attn, layer_gains[1])
    normed_two = normed_two.astype(jnp.bfloat16)
    up_vals = product(normed_two, layer_up)
    result = after_attn + product(gelu(up_vals).astype(jnp.bfloat16), layer_down)
    kept_state = (
        normed,
        unit_one,
        inverse_one,
        queries,
        key_rows,
        value_rows,
        log_sums,
        attended,
        unit_two,
        inverse_two,
        normed_two,
        up_vals,
    )
    return (result, kept_state)


def layer_backward(grad_rows, weights, kept_state, length):
    layer_qkv, layer_out, layer_up, layer_down, layer_gains = weights
    (
        normed,
        unit_one,
        inverse_one,
        queries,
        key_rows,
        value_rows,
        log_sums,
        attended,
        unit_two,
        inverse_two,
        normed_two,
        up_vals,
    ) = kept_state
    seq_length, head_count, head_width = queries.shape
    grad_low = grad_rows.astype(jnp.bfloat16)
    active = gelu(up_vals).astype(jnp.bfloat16)
    grad_down = jnp.einsum("tf,td->fd", active, grad_low, preferred_element_type=jnp.float32)
    grad_active = jnp.einsum("td,fd->tf", grad_low, layer_down, preferred_element_type=jnp.float32)
    grad_upv = (grad_active * gelu_slope(up_vals)).astype(jnp.bfloat16)
    grad_up = jnp.einsum("td,tf->df", normed_two, grad_upv, preferred_element_type=jnp.float32)
    grad_norm_two = jnp.einsum("tf,df->td", grad_upv, layer_up, preferred_element_type=jnp.float32)
    grad_after, gain_two = plain_norm_back(grad_norm_two, unit_two, inverse_two, layer_gains[1])
    grad_after = grad_rows + grad_after
    grad_branch = grad_after.astype(jnp.bfloat16)
    grad_wout = jnp.einsum("ta,td->ad", attended, grad_branch, preferred_element_type=jnp.float32)
    grad_attended = jnp.einsum(
        "td,ad->ta", grad_branch, layer_out, preferred_element_type=jnp.float32
    )
    grad_attended = grad_attended.astype(jnp.bfloat16).reshape(seq_length, head_count, head_width)
    grad_query, grad_keys, grad_values = attention_backward(
        queries, key_rows, value_rows, log_sums, grad_attended, length
    )
    cos_table, sin_table = rotary_tables(seq_length, head_width)
    grad_joined = jnp.stack(
        [
            rotate_back(grad_query, cos_table, sin_table),
            rotate_back(grad_keys, cos_table, sin_table),
            grad_values,
        ],
        axis=1,
    )
    grad_joined = grad_joined.reshape(seq_length, 3 * head_count * head_width).astype(jnp.bfloat16)
    grad_qkv = jnp.einsum("td,tj->dj", normed, grad_joined, preferred_element_type=jnp.float32)
    grad_norm_one = jnp.einsum(
        "tj,dj->td", grad_joined, layer_qkv, preferred_element_type=jnp.float32
    )
    grad_in, gain_one = plain_norm_back(grad_norm_one, unit_one, inverse_one, layer_gains[0])
    return (
        grad_after + grad_in,
        (grad_qkv, grad_wout, grad_up, grad_down, jnp.stack([gain_one, gain_two])),
    )


def mix_history(alphas, history):
    blended = alphas[0] * history[0].astype(jnp.float32)
    for entry in range(1, history.shape[0]):
        blended = blended + alphas[entry] * history[entry].astype(jnp.float32)
    return blended


def plain_body(
    inputs,
    history,
    lengths,
    cotangent,
    w_qkv,
    w_out,
    w_up,
    w_down,
    gains,
    alpha_first,
    alpha_second,
):
    token_total = lax.psum(jnp.sum(lengths.astype(jnp.float32)), ("wide", "narrow"))
    length = lengths[0]
    hist_count = history.shape[0]

    def fetch_layer(layer_no):
        return (
            lax.all_gather(w_qkv[layer_no], ("wide", "narrow"), axis=0, tiled=True),
            lax.all_gather(w_out[layer_no], ("wide", "narrow"), axis=0, tiled=True),
            lax.all_gather(w_up[layer_no], ("wide", "narrow"), axis=0, tiled=True),
            lax.all_gather(w_down[layer_no], ("wide", "narrow"), axis=0, tiled=True),
            lax.all_gather(gains[layer_no], ("wide", "narrow"), axis=1, tiled=True),
        )

    def fetch_again(layer_no):
        return (
            lax.all_gather(w_qkv[layer_no], ("wide", "narrow"), axis=0, tiled=True),
            lax.all_gather(w_out[layer_no], ("wide", "narrow"), axis=0, tiled=True),
            lax.all_gather(w_up[layer_no], ("wide", "narrow"), axis=0, tiled=True),
            lax.all_gather(w_down[layer_no], ("wide", "narrow"), axis=0, tiled=True),
            lax.all_gather(gains[layer_no], ("wide", "narrow"), axis=1, tiled=True),
        )

    def reduce_grads(grad_set):
        return (
            lax.psum_scatter(grad_set[0], ("wide", "narrow"), scatter_dimension=0, tiled=True),
            lax.psum_scatter(grad_set[1], ("wide", "narrow"), scatter_dimension=0, tiled=True),
            lax.psum_scatter(grad_set[2], ("wide", "narrow"), scatter_dimension=0, tiled=True),
            lax.psum_scatter(grad_set[3], ("wide", "narrow"), scatter_dimension=0, tiled=True),
            lax.psum_scatter(grad_set[4], ("wide", "narrow"), scatter_dimension=1, tiled=True),
        )

    weights_one = fetch_layer(0)
    kept_one, state_one = layer_forward(inputs, weights_one, length)
    carried = mix_history(alpha_first, history) + alpha_first[hist_count] * kept_one
    weights_two = fetch_layer(1)
    kept_two, state_two = layer_forward(carried, weights_two, length)
    blended = (
        mix_history(alpha_second, history)
        + alpha_second[hist_count] * kept_one
        + alpha_second[hist_count + 1] * kept_two
    )
    seq_length = inputs.shape[0]
    live_mask = (jnp.arange(seq_length) < length).astype(jnp.float32)[:, None]
    grad_blend = cotangent * live_mask / token_total
    back_two = fetch_again(1)
    grad_carried, grads_two = layer_backward(
        alpha_second[hist_count + 1] * grad_blend, back_two, state_two, length
    )
    shard_two = reduce_grads(grads_two)
    grad_first = alpha_first[hist_count] * grad_carried + alpha_second[hist_count] * grad_blend
    back_one = fetch_again(0)
    grad_inputs, grads_one = layer_backward(grad_first, back_one, state_one, length)
    shard_one = reduce_grads(grads_one)
    grad_history = jnp.stack(
        [
            alpha_first[entry] * grad_carried + alpha_second[entry] * grad_blend
            for entry in range(hist_count)
        ]
    )
    first_terms = []
    second_terms = []
    for entry in range(hist_count):
        past_row = history[entry].astype(jnp.float32)
        first_terms.append(jnp.sum(past_row * grad_carried))
        second_terms.append(jnp.sum(past_row * grad_blend))
    first_terms.append(jnp.sum(kept_one * grad_carried))
    second_terms.append(jnp.sum(kept_one * grad_blend))
    second_terms.append(jnp.sum(kept_two * grad_blend))
    grad_alpha_first, grad_alpha_second = lax.psum(
        (jnp.stack(first_terms), jnp.stack(second_terms)), ("wide", "narrow")
    )
    return (
        blended,
        jnp.stack([kept_one, kept_two]),
        grad_inputs,
        grad_history,
        jnp.stack([shard_one[0], shard_two[0]]),
        jnp.stack([shard_one[1], shard_two[1]]),
        jnp.stack([shard_one[2], shard_two[2]]),
        jnp.stack([shard_one[3], shard_two[3]]),
        jnp.stack([shard_one[4], shard_two[4]]),
        grad_alpha_first,
        grad_alpha_second,
    )


GATHER_KINDS = "accacc"
GATHER_ORDER = (
    200, 400, 100, 0, 110, 21, 22, 500, -1, 30, 210, 23, 300, 121, 31, 32, 33, 122, 123, 40, 41, 51, 510, 321,
    140, 410, 42, 52, 50, 150, 330, 240, 250, 43, 53, -1, 322, 323, 141, 142, 221, 143, 153, 222, -1, -1, -1,
    -1, -1, -1, -1, -1, -1, -1, 440, 223, -1, -1, -1, -1, -1, 331, 332, 333, 151, 540, 152, -1, -1, -1, 340,
    350, 521, 421, 422, 241, 251, 242, -1, -1, -1, -1, -1, -1, -1, 522, -1, -1, -1, 252, -1, 341, 351, 342,
    343, 243, 353, 423, 352, 253, -1, -1, -1, -1, -1, -1, -1, -1, -1, -1, -1, -1, 441, 523, 442, 443, 550,
    541, 542, -1, -1, -1, -1, -1, -1, -1, 451, 452, 453, 450, -1, -1, -1, 543, -1, -1, -1, -1, -1, -1, -1,
    552, 553, 551, -1, -1, -1, -1,
)
SCATTER_KINDS = "acacac"
SCATTER_ORDER = (
    -1, -1, -1, 553, -1, 551, 552, 543, -1, -1, 550, -1, -1, -1, -1, 542, 541, 540, -1, -1, -1, 523, -1, -1,
    -1, -1, -1, 453, 452, 450, -1, -1, -1, -1, -1, -1, 451, 443, 442, 441, 522, 521, -1, -1, -1, -1, -1, 433,
    -1, 432, 440, -1, -1, -1, -1, -1, -1, -1, -1, 353, 431, 350, 423, 422, 343, -1, -1, -1, -1, 352, 351, 510,
    421, 430, -1, 342, 341, 340, 323, 500, -1, 253, -1, 252, -1, 251, -1, 250, -1, -1, -1, -1, 243, -1, 242,
    241, 322, 321, 400, -1, -1, -1, -1, -1, -1, -1, -1, 150, -1, 151, 152, 153, 143, -1, 142, -1, 141, -1,
    140, -1, -1, 123, -1, 310, 240, -1, -1, -1, -1, 122, -1, 121, 233, 232, 231, 300, -1, -1, -1, -1, -1, -1,
    -1, -1, 53, 43, -1, 52, -1, 42, -1, 50, -1, 223, 51, 33, 41, 40, 222, 221, 32, 31, 23, 230, 30, 22, 110,
    21, 200, 100, 0,
)
NEXT = -1


def steps(codes):
    return [v if v == NEXT else (v // 100, "oplaqd"[v // 10 % 10], v % 10) for v in codes]


def al(v, m): return pl.multiple_of(v, m)
def when(cond, fn): pl.when(cond)(fn)

class Place:
    def __init__(self, depth):
        self.depth = depth
        w = lax.axis_index("wide"); n = lax.axis_index("narrow")
        self.w, self.n = w, n
        self.z, self.x = w // 2, lax.rem(w, 2)
        self.y, self.c = n // 2, lax.rem(n, 2)
        first = self.c == 0
        p = jnp.where(first, self.x, self.y)
        q = jnp.where(first, self.y, self.x)
        self.sib = (w, self.y * 2 + 1 - self.c)
        self.xn = (self.z * 2 + 1 - self.x, n)
        self.yn = (w, (1 - self.y) * 2 + self.c)
        self.pn = tuple(jnp.where(first, a, b) for a, b in zip(self.xn, self.yn))
        self.qn = tuple(jnp.where(first, b, a) for a, b in zip(self.xn, self.yn))
        self.has_up = self.z < depth - 1
        self.has_down = self.z > 0
        self.up = (w + 2, n)
        self.down = (w - 2, n)
        self.line = [(lax.rem(w + 2 * i, 2 * depth), n) for i in range(1, depth)]
        self.chip = self.z * 4 + self.x * 2 + self.y
        self.planes = [self.plane(r) for r in range(depth)]
        self.chips = [[[z * 4 + jnp.where(first, 2, 1) * (1 - p if a else p) + jnp.where(first, 1, 2) * (1 - q if b else q)
                        for z in self.planes] for b in (0, 1)] for a in (0, 1)]
        self.onward_up = [(z < self.z) & self.has_up for z in self.planes]
        self.onward_down = [(z > self.z) & self.has_down for z in self.planes]
    def plane(self, r):
        if r == 0: return self.z
        z, last = self.z, self.depth - 1
        short = jnp.minimum(z, last - z)
        low = z * 2 < self.depth
        dist = jnp.where(r <= 2 * short, (r + 1) // 2, r - short)
        below = jnp.where((r <= 2 * short) & (r % 2 == 1), low, ~low)
        return jnp.where(below, z - dist, z + dist)

class Gather:
    def __init__(self, me, chunks, ssem, rsem):
        self.me, self.chunks, self.ssem, self.rsem = me, chunks, ssem, rsem
    def copy(self, k, chip, way, target, sem):
        ref = self.chunks[k][1](chip, 1)
        return pltpu.make_async_remote_copy(src_ref=ref, dst_ref=ref, send_sem=self.ssem.at[k, way],
            recv_sem=self.rsem.at[k, sem], device_id=target, device_id_type=MESH)
    def plane_copy(self, k, r):
        ref = self.chunks[k][2](self.me.planes[r])
        return pltpu.make_async_remote_copy(src_ref=ref, dst_ref=ref, send_sem=self.ssem.at[k, 4],
            recv_sem=self.rsem.at[k, 3 * self.me.depth + self.me.planes[r]], device_id=self.me.sib, device_id_type=MESH)
    def p(self, k, chip, r): self.copy(k, chip, 0, self.me.pn, 2 * self.me.depth + self.me.planes[r]).start()
    def q(self, k, chip, r): self.copy(k, chip, 1, self.me.qn, self.me.planes[r]).start()
    def up(self, k, chip, r): self.copy(k, chip, 2, self.me.up, self.me.depth + self.me.planes[r]).start()
    def down(self, k, chip, r): self.copy(k, chip, 3, self.me.down, self.me.depth + self.me.planes[r]).start()
    def wait(self, k, n, sem):
        ref = self.chunks[k][1](0, n)
        pltpu.make_async_remote_copy(src_ref=ref, dst_ref=ref, send_sem=self.ssem.at[k, 0], recv_sem=self.rsem.at[k, sem],
            device_id=self.me.pn, device_id_type=MESH).wait_recv()
    def event(self, k, what, r):
        me, Z = self.me, self.me.depth
        kind = self.chunks[k][0]
        own, flip = me.chips[0][0][r], me.chips[1][0][r]
        if what == "o":
            when(me.has_up, lambda: self.up(k, own, 0))
            when(me.has_down, lambda: self.down(k, own, 0))
            self.p(k, own, 0)
            self.q(k, own, 0)
        elif what == "p":
            self.wait(k, 1, 2 * Z + me.planes[0])
            when(me.has_up, lambda: self.up(k, flip, 0))
            when(me.has_down, lambda: self.down(k, flip, 0))
            self.q(k, flip, 0)
        elif what == "l":
            both = (own, flip) if kind == "c" else (own,)
            self.wait(k, len(both), Z + me.planes[r])
            def fwd(send):
                for chip in both: send(k, chip, r)
            when(me.onward_up[r], lambda: fwd(self.up))
            when(me.onward_down[r], lambda: fwd(self.down))
            if kind == "a": self.p(k, own, r)
            for chip in both: self.q(k, chip, r)
        elif what == "a":
            self.wait(k, 1, 2 * Z + me.planes[r])
            self.q(k, flip, r)
        elif what == "q":
            self.wait(k, 2, me.planes[r])
            self.plane_copy(k, r).start()
        elif what == "d":
            self.plane_copy(k, r).wait_recv()
    def drain(self, k):
        me, Z = self.me, self.me.depth
        per = 2 if self.chunks[k][0] == "c" else 1
        counts = [1 if per == 2 else Z, 2 * Z, jnp.where(me.has_up, per * (me.z + 1), 0), jnp.where(me.has_down, per * (Z - me.z), 0)]
        for way, count in enumerate(counts):
            def one(_, carry):
                self.copy(k, 0, way, me.pn, 0).wait_send()
                return carry
            lax.fori_loop(0, count, one, 0)
        def one(_, carry):
            self.plane_copy(k, 0).wait_send()
            return carry
        lax.fori_loop(0, Z, one, 0)

def greet(me, whole_line=False):
    bar = pltpu.get_barrier_semaphore()
    def signal(d): pl.semaphore_signal(bar, inc=1, device_id=d, device_id_type=MESH)
    for d in (me.sib, me.xn, me.yn): signal(d)
    if whole_line:
        for d in me.line: signal(d)
    else:
        when(me.has_up, lambda: signal(me.up))
        when(me.has_down, lambda: signal(me.down))
    return bar


def greeted(me, bar, whole_line=False):
    line = len(me.line) if whole_line else me.has_up.astype(jnp.int32) + me.has_down.astype(jnp.int32)
    pl.semaphore_wait(bar, 3 + line)


def add_into(dst, sources, rows, out=None):
    step = 48 if rows % 48 == 0 else 16
    @pl.loop(0, rows // step)
    def _(i):
        at = pl.ds(al(i * step, 16), step)
        if out is None and len(sources) == 1:
            dst[at, :] = dst[at, :] + sources[0][at, :]
            return
        total = dst[at, :].astype(F32)
        for s in sources: total = total + s[at, :].astype(F32)
        if out is None: dst[at, :] = total.astype(dst.dtype)
        else: out[at, :] = total


class Scatter:
    def __init__(self, me, chunks, ssem, rsem):
        self.me, self.chunks, self.ssem, self.rsem = me, chunks, ssem, rsem
        Z = me.depth
        self.Z = Z
        self.q_slot = lambda flip, z: (Z if flip else 0) + z
        self.line_slot = lambda flip, z: 2 * Z + (Z if flip else 0) + z
        self.late_slot = lambda flip: 4 * Z + (1 if flip else 0)
        self.p_slot = lambda kind, z: 3 * Z + z if kind == "a" else 4 * Z + 2
        self.slots = 4 * Z + 3
    def land(self, k, slot): return self.chunks[k].land(slot)
    def copy(self, k, chip, way, target, slot):
        ch = self.chunks[k]
        return pltpu.make_async_remote_copy(src_ref=ch.share(chip), dst_ref=ch.land(slot), send_sem=self.ssem.at[k, way],
            recv_sem=self.rsem.at[k, slot], device_id=target, device_id_type=MESH)
    def plane_copy(self, k, r):
        ch, me = self.chunks[k], self.me
        z = me.planes[r]
        return pltpu.make_async_remote_copy(src_ref=ch.plane(z, False), dst_ref=ch.plane_land(z), send_sem=self.ssem.at[k, 4],
            recv_sem=self.rsem.at[k, self.slots + z], device_id=me.sib, device_id_type=MESH)
    def wait(self, k, slot):
        self.copy(k, 0, 0, self.me.pn, slot).wait_recv()
    def take(self, k, chip, slots, out=None):
        ch = self.chunks[k]
        for s in slots: self.wait(k, s)
        add_into(ch.share(chip), [ch.land(s) for s in slots], ch.rows, out)
    def event(self, k, what, r):
        me, Z = self.me, self.Z
        ch = self.chunks[k]
        kind = ch.kind
        own, flip = me.chips[0][0][r], me.chips[1][0][r]
        z = me.planes[r]
        if what == "d":
            self.plane_copy(k, r).start()
        elif what == "q":
            self.plane_copy(k, r).wait_recv()
            ch.plane_add(z)
            self.copy(k, me.chips[0][1][r], 1, me.qn, self.q_slot(False, z)).start()
            self.copy(k, me.chips[1][1][r], 1, me.qn, self.q_slot(True, z)).start()
        elif what == "a":
            self.take(k, flip, [self.q_slot(True, z)])
            self.copy(k, flip, 0, me.pn, self.p_slot(kind, z)).start()
        elif what == "l":
            first = [self.q_slot(False, z)] + ([self.p_slot(kind, z)] if kind == "a" else [])
            self.take(k, own, first)
            if kind == "c": self.take(k, flip, [self.q_slot(True, z)])
            flips = (False, True) if kind == "c" else (False,)
            def behind():
                for f in flips: self.take(k, flip if f else own, [self.line_slot(f, z)])
            when((z < me.z) & me.has_up, behind)
            when((z > me.z) & me.has_down, behind)
            def send(way, target, late):
                for f in flips:
                    self.copy(k, flip if f else own, way, target, self.late_slot(f) if late else self.line_slot(f, z)).start()
            when((z > me.z) & (z == me.z + 1), lambda: send(2, me.up, False))
            when((z > me.z) & (z != me.z + 1), lambda: send(2, me.up, False))
            when((z < me.z) & (z == me.z - 1), lambda: send(3, me.down, True))
            when((z < me.z) & (z != me.z - 1), lambda: send(3, me.down, False))
        elif what in "po":
            f = what == "p"
            chip = flip if f else own
            slots = [self.q_slot(f, z)]
            if not f: slots.append(self.p_slot(kind, z))
            when(me.has_down, lambda: self.take(k, chip, [self.line_slot(f, z)]))
            when(me.has_up, lambda: self.take(k, chip, [self.late_slot(f)]))
            self.take(k, chip, slots, None if f else ch.result)
            if f: self.copy(k, chip, 0, me.pn, self.p_slot(kind, z)).start()
    def drain(self, k):
        me, Z = self.me, self.Z
        per = 2 if self.chunks[k].kind == "c" else 1
        counts = [1 if per == 2 else Z, 2 * Z, jnp.where(me.has_up, per * (Z - 1 - me.z), 0), jnp.where(me.has_down, per * me.z, 0)]
        for way, count in enumerate(counts):
            def one(_, carry):
                self.copy(k, 0, way, me.pn, 0).wait_send()
                return carry
            lax.fori_loop(0, count, one, 0)
        def one(_, carry):
            self.plane_copy(k, 0).wait_send()
            return carry
        lax.fori_loop(0, Z, one, 0)


def dot(a, b):
    return jnp.dot(a, b, preferred_element_type=F32)


def dot_nt(a, b):
    return lax.dot_general(a, b, (((1,), (1,)), ((), ())), preferred_element_type=F32)


def dot_tn(a, b):
    return lax.dot_general(a, b, (((0,), (0,)), ((), ())), preferred_element_type=F32)


def normalized(h):
    center = h - jnp.mean(h, axis=-1, keepdims=True)
    inverse = lax.rsqrt(jnp.mean(center * center, axis=-1, keepdims=True) + norm_eps)
    return center * inverse, inverse


def swap_halves(v, half):
    lanes = lax.broadcasted_iota(jnp.int32, v.shape, 1)
    width = v.shape[1]
    return jnp.where(lanes % (2 * half) < half, pltpu.roll(v, width - half, 1), pltpu.roll(v, half, 1))


def rotary_lanes(seq_length, head_width, lanes):
    half = head_width // 2
    frequency = (10000.0 ** (-np.arange(half, dtype=np.float32) / half)).astype(np.float32)
    angles = np.arange(seq_length, dtype=np.float32)[:, None] * frequency[None, :]
    cos, sin = np.cos(angles), np.sin(angles)
    both = np.stack([np.concatenate([cos, cos], 1), np.concatenate([-sin, sin], 1)])
    return np.tile(both, (1, 1, lanes // head_width)).astype(np.float32)


def add_sum(ref, row, lane, product):
    rows = lax.broadcasted_iota(jnp.int32, ref.shape, 0)
    lanes = lax.broadcasted_iota(jnp.int32, ref.shape, 1)
    total = jnp.sum(jnp.sum(product, axis=0, keepdims=True), axis=1, keepdims=True)
    ref[...] = ref[...] + jnp.where((rows == row) & (lanes == lane), total, 0.0)


class Forward:
    def __init__(self, w, io, s, planes, length, first, second):
        self.planes = planes
        self.w, self.io, self.s = w, io, s
        self.length, self.first, self.second = length, first, second
        self.T, self.D = s.h.shape
        self.width = self.D // HEADS
        self.q, self.o = 3 * self.D // 2, self.D // 2
        self.half = w.mix.shape[2] // 2
        self.writes = []

    def send(self, name, l=None):
        src, dst = getattr(self.s, name), getattr(self.io, name)
        if l is not None: src, dst = src.at[l], dst.at[l]
        n = len(self.writes)
        self.writes.append((src, dst, n))
        pltpu.make_async_copy(src, dst, self.io.wsem.at[n]).start()

    def finish(self):
        for src, dst, n in self.writes:
            pltpu.make_async_copy(src, dst, self.io.wsem.at[n]).wait()

    def load(self, i):
        s, io = self.s, self.io
        src, dst = ((io.h, s.h), (io.rope, s.rope), (io.cotangent, s.cotangent), (io.history, s.history))[i]
        return pltpu.make_async_copy(src, dst, io.isem.at[i])

    def setup(self):
        s, T = self.s, self.T
        row = lax.broadcasted_iota(jnp.int32, (T, T), 0)
        col = lax.broadcasted_iota(jnp.int32, (T, T), 1)
        s.bias[...] = jnp.where((col <= row) & (col < self.length), 0.0, masked_score)
        s.sums[...] = jnp.zeros_like(s.sums)

    def loss_grad(self):
        s, io = self.s, self.io
        count = jnp.sum(s.gain[4:5, :])
        row = lax.broadcasted_iota(jnp.int32, (self.T, 1), 0)
        grad = jnp.where(row < self.length, s.cotangent[...], 0.0) / count
        s.gout[...] = grad
        self.send("gout")
        n = s.history.shape[0]
        for j in range(n): add_sum(s.sums, 1, j, s.history[j].astype(F32) * grad)

    def layer_in(self, l):
        return self.s.h if l == 0 else self.s.carried

    def norm_one(self, l):
        s, w = self.s, self.w
        if l == 0:
            s.gain[...] = s.total[...]
            self.send("gain")
            for i in range(4): self.load(i).wait()
        x, _ = normalized(self.layer_in(l)[...])
        s.n1[l] = (x * s.gain[2 * l:2 * l + 1, :]).astype(BF)
        self.send("n1", l)

    def project(self, l, t):
        s, w = self.s, self.w
        h, i = divmod(t, 3)
        W = self.q // 3
        at = h * self.half + i * W
        joined = dot(s.n1[l], w.mix[l, :, at:at + W])
        for j in range(W // 128):
            col = t * W + j * 128
            part = joined[:, j * 128:(j + 1) * 128]
            if col < 2 * self.D:
                part = part * s.cos[...] + swap_halves(part, self.width // 2) * s.sin[...]
                if col < self.D: part = part * self.width ** -0.5
            s.qkv[l, :, col:col + 128] = part.astype(BF)

    def attend(self, l, a):
        s, D = self.s, self.D
        q, k, v = (s.qkv[l, :, i * D + a * 128:i * D + a * 128 + 128] for i in range(3))
        lanes = lax.broadcasted_iota(jnp.int32, q.shape, 1)
        outs = []
        for e in range(2):
            mine = (lanes < self.width) if e == 0 else (lanes >= self.width)
            scores = dot_nt(jnp.where(mine, q, jnp.zeros_like(q)), k) + s.bias[...]
            top = jnp.max(scores, axis=-1, keepdims=True)
            weights = jnp.exp(scores - top)
            probs = (weights * (1.0 / jnp.sum(weights, axis=-1, keepdims=True))).astype(BF)
            s.probs[l, 2 * a + e] = probs
            outs.append(dot(probs, v))
        s.att[l, :, a * 128:a * 128 + 128] = jnp.where(lanes < self.width, outs[0], outs[1]).astype(BF)

    def attend_done(self, l):
        for name in ("qkv", "probs", "att"): self.send(name, l)

    def out(self, l, h):
        s, w = self.s, self.w
        cols = slice(h * self.o, (h + 1) * self.o)
        at = h * self.half + self.q
        s.after[l, :, cols] = self.layer_in(l)[:, cols] + dot(s.att[l], w.mix[l, :, at:at + self.o])

    def norm_two(self, l):
        s = self.s
        x, _ = normalized(s.after[l])
        s.n2[l] = (x * s.gain[2 * l + 1:2 * l + 2, :]).astype(BF)
        self.send("n2", l)
        self.send("after", l)

    def raise_(self, l, t, W):
        s, w = self.s, self.w
        u = dot(s.n2[l], w.up[l, :, t * W:(t + 1) * W])
        tile, at = divmod(t * W, self.D)
        cols = slice(at, at + W)
        square = u * u
        tangent = jnp.tanh(gelu_scale * u * (1.0 + gelu_coef * square))
        s.act[l, tile, :, cols] = (0.5 * u * (1.0 + tangent)).astype(BF)
        s.slope[l, tile, :, cols] = (
            0.5 * (1.0 + tangent) + 0.5 * u * (1.0 - tangent * tangent) * gelu_scale * (1.0 + 3.0 * gelu_coef * square)
        ).astype(BF)

    def raise_done(self, l):
        for name in ("act", "slope"): self.send(name, l)

    def lower(self, l, r):
        s, w = self.s, self.w
        z = self.planes[r]
        chips = w.down.shape[1] // len(self.planes)
        part = dot(s.act[l, z], w.down[l, pl.ds(z * chips, chips)].reshape(-1, self.D))
        s.stored[l] = (s.after[l] if r == 0 else s.stored[l]) + part

    def mixed(self, l):
        s, io = self.s, self.io
        n = s.history.shape[0]
        if l == 0:
            s.carried[...] = mix_history([self.first[j] for j in range(n)], s.history) + self.first[n] * s.stored[0]
            self.send("carried")
        else:
            s.blended[...] = (
                mix_history([self.second[j] for j in range(n)], s.history)
                + self.second[n] * s.stored[0] + self.second[n + 1] * s.stored[1]
            )
            self.send("blended")
        self.send("stored", l)
        add_sum(s.sums, 1, n + l, s.stored[l] * s.gout[...])
        if l == 1: self.send("sums")

    def steps(self):
        out = [(-1, self.setup)]
        P = functools.partial
        for l in range(2):
            k = 3 * l
            out.append((k, P(self.norm_one, l)))
            out += [(k, P(self.project, l, t)) for t in range(6)]
            if l == 0: out.append((k, self.loss_grad))
            out += [(k, P(self.attend, l, a)) for a in range(self.D // 128)]
            out.append((k, P(self.attend_done, l)))
            out += [(k, P(self.out, l, h)) for h in range(2)]
            out.append((k, P(self.norm_two, l)))
            W = self.D // 2
            out += [(k + 1, P(self.raise_, l, t, W)) for t in range(4 * self.D // W)]
            out.append((k + 1, P(self.raise_done, l)))
            out += [((k + 2, r), P(self.lower, l, r)) for r in range(len(self.planes))]
            out.append((k + 2, P(self.mixed, l)))
        return out


def weave(order, work):
    left, whole, done, queue = {}, set([-1]), [], list(work)
    for v in order:
        if v != NEXT and v[1] == "d": left[v[0]] = left.get(v[0], 0) + 1
    for v in order:
        if v == NEXT:
            need, act = queue.pop(0)
            assert need in whole
            done.append(act)
            continue
        done.append(v)
        k, what, r = v
        if what == "d":
            whole.add((k, r))
            left[k] -= 1
            if not left[k]: whole.add(k)
    assert not queue
    return done


def saved_shapes(T, D, FF):
    return dict(n1=((2, T, D), BF), qkv=((2, T, 3 * D), BF), probs=((2, HEADS, T, T), BF), att=((2, T, D), BF), after=((2, T, D), F32),
        n2=((2, T, D), BF), act=((2, FF // D, T, D), BF), slope=((2, FF // D, T, D), BF), stored=((2, T, D), F32), carried=((T, D), F32),
        blended=((T, D), F32), gout=((T, D), F32), sums=((8, D), F32), gain=((8, D), F32))


SAVED = tuple(saved_shapes(1, 1, 1))


def fwd_kernel(depth, order, kinds, qkv_in, out_in, up_in, down_in, gain_in, h_in, history_in, cotangent_in, rope_in, length, first, second,
              mix_o, up_o, down_o, *rest):
    n = len(SAVED)
    saved_o, rest = rest[:n], rest[n:]
    (mix_b, up_b, down_b, mix_s, up_s, mix_t, up_t, ssem, rsem, esem, lsem, wsem, isem, bias, value, land, h_b, history_b, cotangent_b,
        rope_b, tsend, trecv), saved_b = rest[:22], rest[22:]
    me = Place(depth)
    bar = greet(me, True)
    rows = qkv_in.shape[1]
    c = me.c
    wq, wo, wu = qkv_in.shape[2] // 2, out_in.shape[2] // 2, up_in.shape[2] // 2
    mine = lambda w: pl.ds(al(c * w, 128), w)
    other = lambda w: pl.ds(al((1 - c) * w, 128), w)
    my_rows = pl.ds(al(c * rows, 8), rows)
    def stage(k):
        l, j = divmod(k, 3)
        if j == 0:
            for ref, at, pick in ((mix_s, (l, my_rows), mine), (mix_t, (l, slice(None)), other)):
                ref[at[0], at[1], 0:wq] = qkv_in[l, :, pick(wq)].astype(F32)
                ref[at[0], at[1], wq:wq + wo] = out_in[l, :, pick(wo)].astype(F32)
        elif j == 1:
            up_s[l, my_rows, :] = up_in[l, :, mine(wu)].astype(F32)
            up_t[l] = up_in[l, :, other(wu)].astype(F32)
    def place_gains():
        small = value.at[2]
        small[...] = jnp.zeros_like(small)
        for l in range(2): small[2 * l:2 * l + 2, 0:rows] = gain_in[l].astype(F32)
        n = value.shape[2]
        at = rows * (me.w * 4 + me.n)
        one = lax.broadcasted_iota(jnp.int32, (128, n), 1) == lax.broadcasted_iota(jnp.int32, (128, n), 0) + at
        own = dot(small[:, 0:128].astype(BF), one.astype(BF))
        row = lax.broadcasted_iota(jnp.int32, own.shape, 0)
        col = lax.broadcasted_iota(jnp.int32, own.shape, 1)
        value[0] = own + jnp.where((row == 4) & (col == 0), length[0].astype(F32), 0.0)
    def exchange(k):
        l, j = divmod(k, 3)
        if j == 2: return None
        s, t = ((mix_s, mix_t), (up_s, up_t))[j]
        return pltpu.make_async_remote_copy(src_ref=t.at[l], dst_ref=s.at[l, my_rows, :], send_sem=esem.at[0, k],
            recv_sem=esem.at[1, k], device_id=me.sib, device_id_type=MESH)
    def ready(k):
        l, j = divmod(k, 3)
        if j == 2:
            down_b[l, me.chip, c] = down_in[l]
            return
        exchange(k).wait_recv()
        s, b = ((mix_s, mix_b), (up_s, up_b))[j]
        b[l, pl.ds(al(me.chip * 2 * rows, 16), 2 * rows), mine(s.shape[2])] = s[l].astype(BF)
    chunks = []
    for k in range(6):
        l, j = divmod(k, 3)
        if j == 2:
            chunks.append((kinds[k], lambda chip, n, l=l: down_b.at[l, pl.ds(chip, n), c], lambda z, l=l: down_b.at[l, pl.ds(z * 4, 4), c]))
        else:
            b = (mix_b, up_b)[j]
            half = b.shape[2] // 2
            chunks.append((kinds[k],
                lambda chip, n, b=b, l=l, half=half: b.at[l, pl.ds(al(chip * 2 * rows, 16), n * 2 * rows), mine(half)],
                lambda z, b=b, l=l, half=half: b.at[l, pl.ds(al(z * 8 * rows, 16), 8 * rows), mine(half)]))
    gather = Gather(me, chunks, ssem, rsem)
    io = SimpleNamespace(**dict(zip(SAVED, saved_o)), h=h_in, history=history_in, cotangent=cotangent_in, rope=rope_in,
        wsem=wsem, isem=isem)
    scratch = SimpleNamespace(**dict(zip(SAVED, saved_b)), bias=bias, total=value.at[4], h=h_b, history=history_b,
        cotangent=cotangent_b, rope=rope_b, cos=rope_b.at[0], sin=rope_b.at[1])
    fwd = Forward(SimpleNamespace(mix=mix_b, up=up_b, down=down_b), io, scratch, me.planes, length[0], first, second)
    first_out = []
    for v in order:
        if v != NEXT and v[1] == "o" and v[0] % 3 < 2: first_out.append(v[0])
    for k in first_out[:2]: stage(k)
    greeted(me, bar, True)
    for k in first_out[:2]: exchange(k).start()
    total = Total(me, value, land, tsend, trecv)
    def settle():
        place_gains()
        total.step(0)
        for i in range(4): fwd.load(i).start()
        for k in first_out[2:]:
            stage(k)
            exchange(k).start()
    pairs = ((mix_b, mix_o), (up_b, up_o), (down_b, down_o))
    def write(k, r):
        l, j = divmod(k, 3)
        b, o = pairs[j]
        n = b.shape[1] // depth
        at = pl.ds(al(me.planes[r] * n, n), n)
        return pltpu.make_async_copy(b.at[l, at], o.at[l, at], lsem.at[k, r])
    totals, count, sent = [1, 2, 3, 4], 0, 0
    for item in weave(order, fwd.steps()):
        if not isinstance(item, tuple):
            item()
            continue
        k, what, r = item
        if what == "o":
            if settle and k in first_out[2:]:
                settle()
                settle = None
            ready(k)
        gather.event(k, what, r)
        if what == "o" and settle:
            if k % 3 < 2: sent += 1
            if sent == 2:
                settle()
                settle = None
        if what == "d": write(k, r).start()
        count += 1
        if totals and not settle and count % 5 == 0: total.step(totals.pop(0))
    for k in range(6):
        gather.drain(k)
        if k % 3 < 2: exchange(k).wait_send()
    for k in range(6):
        for r in range(depth): write(k, r).wait()
    fwd.finish()

def fwd_call(mesh, order, kinds, w_qkv, w_out, w_up, w_down, gains, h, history, cotangent, rope, lengths, first, second):
    depth = mesh.shape["wide"] // 2
    rows = w_qkv.shape[1]
    D, FF = rows * mesh.size, w_down.shape[1] * mesh.size
    T = h.shape[0]
    n = mesh.size // 2
    M = 4 * D
    body = functools.partial(fwd_kernel, depth, order, kinds)
    vm = pl.BlockSpec(memory_space=pltpu.VMEM); an = pl.BlockSpec(memory_space=pl.ANY); sm = pl.BlockSpec(memory_space=pltpu.SMEM)
    shapes = [((2, D, M), BF), ((2, D, FF), BF), ((2, n, 2, FF // n // 2, D), BF)]
    saved = list(saved_shapes(T, D, FF).values())
    got = pl.pallas_call(body,
        out_shape=[jax.ShapeDtypeStruct(s, d) for s, d in shapes + saved],
        in_specs=[vm] * 5 + [an] * 4 + [sm] * 3, out_specs=[an] * (3 + len(saved)),
        scratch_shapes=[pltpu.VMEM(s, d) for s, d in shapes] + [
            pltpu.VMEM((2, 2 * rows, M // 2), F32), pltpu.VMEM((2, 2 * rows, FF // 2), F32),
            pltpu.VMEM((2, rows, M // 2), F32), pltpu.VMEM((2, rows, FF // 2), F32),
            pltpu.SemaphoreType.DMA((6, 5)), pltpu.SemaphoreType.DMA((6, 4 * depth)),
            pltpu.SemaphoreType.DMA((2, 6)), pltpu.SemaphoreType.DMA((6, depth)), pltpu.SemaphoreType.DMA((24,)),
            pltpu.SemaphoreType.DMA((4,)), pltpu.VMEM((T, T), F32), pltpu.VMEM((5, 8, D), F32), pltpu.VMEM((2 + depth, 8, D), F32),
            pltpu.VMEM(h.shape, F32), pltpu.VMEM(history.shape, BF), pltpu.VMEM(cotangent.shape, F32), pltpu.VMEM(rope.shape, F32), pltpu.SemaphoreType.DMA((2 + depth,)), pltpu.SemaphoreType.DMA((2 + depth,))] + [pltpu.VMEM(s, d) for s, d in saved],
        compiler_params=pltpu.CompilerParams(collective_id=0, has_side_effects=True, vmem_limit_bytes=62 * 2**20),
        cost_estimate=pl.CostEstimate(flops=16 * T * D * FF, bytes_accessed=2**26, transcendentals=2**21),
    )(w_qkv, w_out, w_up, w_down, gains, h, history, cotangent, rope, lengths, first, second)
    return got[:3], SimpleNamespace(**dict(zip(SAVED, got[3:])))


def norm_back(e, h, gain):
    unit, inverse = normalized(h)
    scaled = e * gain
    grad = inverse * (scaled - jnp.mean(scaled, axis=-1, keepdims=True) - unit * jnp.mean(scaled * unit, axis=-1, keepdims=True))
    return grad, jnp.sum(e * unit, axis=0, keepdims=True)


class Backward:
    def __init__(self, io, s, g, planes, first, second):
        self.planes = planes
        self.io, self.s, self.g = io, s, g
        self.first, self.second = first, second
        self.T, self.D = s.gy.shape
        self.width = self.D // HEADS
        self.q, self.o = 3 * self.D // 2, self.D // 2
        self.half = g.mix.shape[1] // 2
        self.tiles = s.act.shape[0]
        self.hist = io.history.shape[0]
        self.writes = []

    SLOTS = ("act", "slope", "n2", "n1", "att", "after", "h", "probs", "qkv", "mix", "history", "gout", "sums", "gain", "rope")

    def load(self, name, src, dst=None):
        i = self.SLOTS.index(name)
        return pltpu.make_async_copy(src, getattr(self.s, name) if dst is None else dst, self.io.load_sem.at[i])

    def source(self, name, l):
        return getattr(self.io, name).at[l]

    def fetch(self, l, names):
        for name in names:
            src = (self.io.inputs if l == 0 else self.io.carried) if name == "h" else getattr(self.io, name).at[l]
            self.load(name, src).start()

    def here(self, l, *names):
        for name in names:
            src = (self.io.inputs if l == 0 else self.io.carried) if name == "h" else getattr(self.io, name).at[l]
            self.load(name, src).wait()

    def tile_copy(self, l, t, up):
        src = self.io.up.at[l, :, pl.ds(t * self.D, self.D)] if up else self.io.down.at[l, t]
        return pltpu.make_async_copy(src, self.s.tile.at[t], self.io.tile_sem.at[t])

    def send(self, src, dst):
        n = len(self.writes)
        self.writes.append((src, dst, n))
        pltpu.make_async_copy(src, dst, self.io.write_sem.at[n]).start()

    def finish(self):
        for src, dst, n in self.writes:
            pltpu.make_async_copy(src, dst, self.io.write_sem.at[n]).wait()

    WHOLE = ("sums", "gain", "rope")

    def begin(self):
        self.load("gout", self.io.gout).start()
        self.fetch(1, ("act",))
        for t in range(self.tiles): self.tile_copy(1, t, False).start()
        self.fetch(1, ("slope", "n2"))
        for name in self.WHOLE: self.load(name, getattr(self.io, name)).start()
        s = self.s
        self.load("gout", self.io.gout).wait()
        s.gy[...] = self.second[self.hist + 1] * s.gout[...]

    def down_weight(self, l, r):
        s = self.s
        if r == len(self.planes) - 1:
            s.gm[...] = s.gy[...].astype(BF)
            self.here(l, "act")
        z = self.planes[r]
        chips = self.g.down.shape[0] // len(self.planes)
        grad = dot_tn(s.act[z], s.gm[...])
        self.g.down[pl.ds(z * chips, chips)] = grad.astype(BF).reshape((chips,) + self.g.down.shape[1:])

    def act_grad(self, l, t):
        s = self.s
        if t == 0: self.here(l, "slope")
        if l == 1 and t == 1:
            self.fetch(1, ("after", "mix", "probs", "qkv"))
            for name in self.WHOLE: self.load(name, getattr(self.io, name)).wait()
        self.tile_copy(l, t, False).wait()
        grad = dot_nt(s.gm[...], s.tile[t])
        s.slope[t] = (grad * s.slope[t].astype(F32)).astype(BF)
        self.tile_copy(l, t, True).start()

    def turned(self, l, name):
        self.here(l, name)
        self.s.turned[...] = getattr(self.s, name)[...].T

    def up_weight(self, l, t):
        s = self.s
        tile, at = divmod(t * self.o, self.D)
        self.g.up[:, t * self.o:(t + 1) * self.o] = dot(s.turned[...], s.slope[tile, :, at:at + self.o]).astype(BF)

    def norm_two_grad(self, l, t):
        s = self.s
        self.tile_copy(l, t, True).wait()
        part = dot_nt(s.slope[t], s.tile[t])
        if l == 1 and t == 1:
            self.fetch(1, ("att", "n1", "h"))
            self.load("history", self.io.history).start()
        if t == 0: s.gn[...] = part
        else: s.gn[...] = s.gn[...] + part
        if l == 1: self.tile_copy(0, t, False).start()

    def after_grad(self, l):
        s = self.s
        self.here(l, "after")
        grad, gain = norm_back(s.gn[...], s.after[...], s.gain[2 * l + 1:2 * l + 2, :])
        s.sums[3 + 2 * l:4 + 2 * l, :] = gain
        s.gy[...] = s.gy[...] + grad
        s.gm[...] = s.gy[...].astype(BF)
        if l == 1:
            self.fetch(0, ("slope", "n2", "act"))
            self.load("after", self.io.stored.at[0]).start()

    def out_weight(self, l, h):
        s = self.s
        if h == 0: self.turned(l, "att")
        at = h * self.half + self.q
        self.g.mix[:, at:at + self.o] = dot(s.turned[...], s.gm[:, h * self.o:(h + 1) * self.o]).astype(BF)

    def att_grad(self, l):
        s = self.s
        self.here(l, "mix")
        a, b = self.q, self.half + self.q
        grad = dot_nt(s.gm[:, :self.o], s.mix[:, a:a + self.o]) + dot_nt(s.gm[:, self.o:], s.mix[:, b:b + self.o])
        s.ga[...] = grad.astype(BF)

    def attend(self, l, a):
        s, D = self.s, self.D
        if a == 0: self.here(l, "probs", "qkv")
        q, k, v = (s.qkv[:, i * D + a * 128:i * D + a * 128 + 128] for i in range(3))
        ga = s.ga[:, a * 128:a * 128 + 128]
        lanes = lax.broadcasted_iota(jnp.int32, q.shape, 1)
        got = []
        for e in range(2):
            mine = (lanes < self.width) if e == 0 else (lanes >= self.width)
            probs = s.probs[2 * a + e]
            wide = probs.astype(F32)
            gp = wide * dot_nt(jnp.where(mine, ga, jnp.zeros_like(ga)), v)
            gs = (gp - wide * jnp.sum(gp, axis=-1, keepdims=True)).astype(BF)
            got.append((dot(gs, k), dot_tn(gs, q), dot_tn(probs, ga)))
        gq, gk, gv = (jnp.where(lanes < self.width, x, y) for x, y in zip(*got))
        back = lambda g: g * s.cos[...] - swap_halves(g, self.width // 2) * s.sin[...]
        for i, g in enumerate((back(gq) * self.width ** -0.5, back(gk), gv)):
            s.gj[:, i * D + a * 128:i * D + a * 128 + 128] = g.astype(BF)

    def qkv_weight(self, l, t):
        s = self.s
        if t == 0:
            self.turned(l, "n1")
            if l == 1: self.fetch(0, ("probs", "qkv", "n1", "att"))
        h, i = divmod(t, 3)
        W = self.q // 3
        at = h * self.half + i * W
        self.g.mix[:, at:at + W] = dot(s.turned[...], s.gj[:, t * W:(t + 1) * W]).astype(BF)

    def norm_one_grad(self, l, t):
        s = self.s
        W = self.D // 3
        rows = slice(t * W, (t + 1) * W)
        b = self.half
        s.gn[:, rows] = dot_nt(s.gj[:, :self.q], s.mix[rows, :self.q]) + dot_nt(s.gj[:, self.q:], s.mix[rows, b:b + self.q])

    def layer_grad(self, l):
        s = self.s
        self.here(l, "h")
        grad, gain = norm_back(s.gn[...], s.h[...], s.gain[2 * l:2 * l + 1, :])
        s.sums[2 + 2 * l:3 + 2 * l, :] = gain
        s.gy[...] = s.gy[...] + grad
        if l == 1: self.fetch(0, ("mix", "h"))
        if l == 1:
            s.kept[...] = s.gy[...]
            self.send(s.kept, self.io.grad_carried)
        else: self.send(s.gy, self.io.grad_inputs)

    def between(self):
        s, n = self.s, self.hist
        self.load("history", self.io.history).wait()
        self.load("after", self.io.stored.at[0]).wait()
        grad = s.gy[...]
        for j in range(n): add_sum(s.sums, 0, j, s.history[j].astype(F32) * grad)
        add_sum(s.sums, 0, n, s.after[...] * grad)
        s.gy[...] = self.first[n] * grad + self.second[n] * s.gout[...]
        self.fetch(0, ("after",))

    def steps(self):
        P = functools.partial
        out = [("do", -1, self.begin)]
        for l in (1, 0):
            k = 3 * l
            tiles = range(self.tiles)
            if l == 0: out.append(("do", -1, self.between))
            out += [("make", (k + 2, r), P(self.down_weight, l, r)) for r in reversed(range(len(self.planes)))]
            out += [("do", -1, P(self.act_grad, l, t)) for t in tiles]
            out.append(("do", -1, P(self.turned, l, "n2")))
            out += [("make", (k + 1, -1), P(self.up_weight, l, t)) for t in range(2 * self.tiles)]
            out += [("do", -1, P(self.norm_two_grad, l, t)) for t in tiles]
            out.append(("do", -1, P(self.after_grad, l)))
            out.append(("do", -1, P(self.att_grad, l)))
            out += [("do", -1, P(self.attend, l, a)) for a in range(self.D // 128)]
            out += [("make", (k, -1), P(self.out_weight, l, h)) for h in range(2)]
            out += [("make", (k, -1), P(self.qkv_weight, l, t)) for t in range(6)]
            out += [("do", -1, P(self.norm_one_grad, l, t)) for t in range(3)]
            out.append(("sums" if l == 0 else "do", -1, P(self.layer_grad, l)))
        return out


def weave_back(order, work):
    to_make, over, drained, done, queue = {}, set(), set(), [], list(work)
    for name, k, _ in work:
        if name == "make": to_make[k] = to_make.get(k, 0) + 1
    for v in order:
        if v == NEXT:
            name, k, act = queue.pop(0)
            if name == "make":
                before = k[0] + 3
                if k[0] < 3 and before not in drained:
                    assert before in over
                    drained.add(before)
                    done.append(("drain", before))
                to_make[k] -= 1
            done.append(act)
            if name == "sums": done.append(("sums", 0))
            continue
        k, what, r = v
        if what == "d": assert not to_make.get((k, r), 0) and not to_make.get((k, -1), 0)
        if what == "o": over.add(k)
        done.append(v)
    assert not queue
    return done


class Total:
    def __init__(self, me, value, land, ssem, rsem):
        self.me, self.value, self.land, self.ssem, self.rsem = me, value, land, ssem, rsem
    def copy(self, i, src, target):
        return pltpu.make_async_remote_copy(src_ref=src, dst_ref=self.land.at[i], send_sem=self.ssem.at[i], recv_sem=self.rsem.at[i],
            device_id=target, device_id_type=MESH)
    def step(self, n):
        me, v = self.me, self.value
        targets = (me.sib, me.xn, me.yn)
        if 0 < n <= 3:
            self.copy(n - 1, v.at[n - 1], targets[n - 1]).wait()
            v[n] = v[n - 1] + self.land[n - 1]
        if n < 3: self.copy(n, v.at[n], targets[n]).start()
        elif n == 3:
            for i, t in enumerate(me.line): self.copy(3 + i, v.at[3], t).start()
        else:
            total = v[3]
            for i, t in enumerate(me.line):
                self.copy(3 + i, v.at[3], t).wait()
                total = total + self.land[3 + i]
            v[4] = total


def bwd_kernel(depth, order, kinds, first, second, *rest):
    io = SimpleNamespace()
    (io.gout, io.sums, io.gain, io.rope, io.mix, io.up, io.down, io.n1, io.qkv, io.probs, io.att, io.after, io.n2, io.act, io.slope, io.stored, io.carried, io.inputs,
        io.history), rest = rest[:19], rest[19:]
    (mix_o, up_o, down_o, io.grad_carried, io.grad_inputs, sums_o), rest = rest[:6], rest[6:]
    (mix_g, up_g, down_g, mix_d, up_d, down_d, mix_l, up_l, down_l, mix_f, up_f, down_f,
        ssem, rsem, esem, credit, io.load_sem, io.tile_sem, io.write_sem, tsend, trecv, fsem), rest = rest[:22], rest[22:]
    s = SimpleNamespace()
    (s.tile, s.mix, s.act, s.slope, s.n2, s.n1, s.att, s.after, s.h, s.probs, s.qkv, s.gy, s.gn, s.gm, s.ga, s.gj, s.turned, s.history,
        s.kept, s.value, s.land, s.gout, s.gain, s.rope) = rest
    s.cos, s.sin = s.rope.at[0], s.rope.at[1]
    scratch = s
    scratch.sums = scratch.value.at[0]
    me = Place(depth)
    c = me.c
    bar = greet(me, True)
    rows = mix_o.shape[1]
    mine = lambda w: pl.ds(al(c * w, 128), w)
    other = lambda w: pl.ds(al((1 - c) * w, 128), w)
    bwd = Backward(io, scratch, SimpleNamespace(mix=mix_g, up=up_g, down=down_g), me.planes, first, second)
    chunks = {}
    for k in range(6):
        l, j = divmod(k, 3)
        if j == 2:
            R = down_g.shape[2]
            def plane_add(z):
                for i in range(4): add_into(down_g.at[z * 4 + i, c], [down_d.at[z * 4 + i]], R)
            chunks[k] = SimpleNamespace(kind=kinds[k], rows=R, share=lambda chip: down_g.at[chip, c],
                plane=lambda z, own: down_g.at[pl.ds(z * 4, 4), c if own else 1 - c], plane_land=lambda z: down_d.at[pl.ds(z * 4, 4)],
                plane_add=plane_add, land=lambda s: down_l.at[s], result=down_f.at[l])
        else:
            g, d, land, f = ((mix_g, mix_d, mix_l, mix_f), (up_g, up_d, up_l, up_f))[j]
            half = g.shape[1] // 2
            def plane_add(z, g=g, d=d, half=half):
                at = pl.ds(al(z * 8 * rows, 16), 8 * rows)
                add_into(g.at[at, mine(half)], [d.at[at, :]], 8 * rows)
            chunks[k] = SimpleNamespace(kind=kinds[k], rows=2 * rows, share=lambda chip, g=g, half=half: g.at[pl.ds(al(chip * 2 * rows, 16), 2 * rows), mine(half)],
                plane=lambda z, own, g=g, half=half: g.at[pl.ds(al(z * 8 * rows, 16), 8 * rows), mine(half) if own else other(half)],
                plane_land=lambda z, d=d: d.at[pl.ds(al(z * 8 * rows, 16), 8 * rows), :],
                plane_add=plane_add, land=lambda s, land=land: land.at[s], result=f.at[l])
    sc = Scatter(me, chunks, ssem, rsem)
    total = Total(me, scratch.value, scratch.land, tsend, trecv)
    def result(k):
        l, j = divmod(k, 3)
        if j == 2: return [pltpu.make_async_copy(down_f.at[l], down_o.at[l], fsem.at[k])]
        f, o = ((mix_f, mix_o), (up_f, up_o))[j]
        half = f.shape[2]
        return [pltpu.make_async_copy(f.at[l, pl.ds(al(c * rows, 8), rows), :], o.at[l, :, mine(half)], fsem.at[k]),
            pltpu.make_async_remote_copy(src_ref=f.at[l, pl.ds(al((1 - c) * rows, 8), rows), :], dst_ref=o.at[l, :, mine(half)],
                send_sem=esem.at[0, k], recv_sem=esem.at[1, k], device_id=me.sib, device_id_type=MESH)]
    def tell(j):
        for d in (me.xn, me.yn): pl.semaphore_signal(credit.at[1, j], inc=1, device_id=d, device_id_type=MESH)
        when(me.has_up, lambda: pl.semaphore_signal(credit.at[2, j], inc=1, device_id=me.up, device_id_type=MESH))
        when(me.has_down, lambda: pl.semaphore_signal(credit.at[2, j], inc=1, device_id=me.down, device_id_type=MESH))
    planes_left, told, totals = {k: depth for k in range(6)}, {}, []
    greeted_yet = []
    for n, item in enumerate(weave_back(order, bwd.steps())):
        if not isinstance(item, tuple):
            item()
            continue
        if not greeted_yet:
            greeted(me, bar, True)
            greeted_yet.append(1)
        if item[0] == "drain":
            sc.drain(item[1])
            continue
        if item[0] == "sums":
            totals = [0, 1, 2, 3, 4]
            since = 0
            continue
        k, what, r = item
        l, j = divmod(k, 3)
        if l == 0 and what == "d" and (0, j) not in told:
            told[0, j] = True
            pl.semaphore_wait(credit.at[0, j], 1)
        if l == 0 and what == "q" and (1, j) not in told:
            told[1, j] = True
            pl.semaphore_wait(credit.at[1, j], 2)
        if l == 0 and what == "l" and (2, j) not in told:
            told[2, j] = True
            pl.semaphore_wait(credit.at[2, j], me.has_up.astype(jnp.int32) + me.has_down.astype(jnp.int32))
        sc.event(k, what, r)
        if what == "q":
            planes_left[k] -= 1
            if l == 1 and planes_left[k] == 0:
                pl.semaphore_signal(credit.at[0, j], inc=1, device_id=me.sib, device_id_type=MESH)
        if what == "o":
            for cp in result(k): cp.start()
            if l == 1: tell(j)
        if totals:
            since += 1
            if since % 4 == 0: total.step(totals.pop(0))
    for i in totals: total.step(i)
    everything = pltpu.make_async_copy(s.value.at[4], sums_o, fsem.at[6])
    everything.start()
    for k in range(3): sc.drain(k)
    for k in range(6):
        for cp in result(k): cp.wait()
    everything.wait()
    bwd.finish()


def bwd_call(mesh, order, kinds, weights, saved, inputs, history, rope, first, second):
    mix, up, down = weights
    depth = mesh.shape["wide"] // 2
    D, M = mix.shape[1:]
    FF = up.shape[2]
    T = inputs.shape[0]
    n = mesh.size // 2
    rows, drows = D // mesh.size, FF // mesh.size
    down = down.reshape(2, FF // D, D, D)
    slots = 4 * depth + 3
    body = functools.partial(bwd_kernel, depth, order, kinds)
    vm = pl.BlockSpec(memory_space=pltpu.VMEM); an = pl.BlockSpec(memory_space=pl.ANY); sm = pl.BlockSpec(memory_space=pltpu.SMEM)
    V, S = pltpu.VMEM, pltpu.SemaphoreType.DMA
    return pl.pallas_call(body,
        out_shape=[jax.ShapeDtypeStruct(s, F32) for s in ((2, rows, M), (2, rows, FF), (2, drows, D), (T, D), (T, D), (8, D))],
        in_specs=[sm] * 2 + [an] * 19, out_specs=[an] * 6,
        scratch_shapes=[V((D, M), BF), V((D, FF), BF), V((n, 2, drows, D), BF),
            V((D, M // 2), BF), V((D, FF // 2), BF), V((n, drows, D), BF),
            V((slots, 2 * rows, M // 2), BF), V((slots, 2 * rows, FF // 2), BF), V((slots, drows, D), BF),
            V((2, 2 * rows, M // 2), F32), V((2, 2 * rows, FF // 2), F32), V((2, drows, D), F32),
            S((6, 5)), S((6, slots + depth)), S((2, 6)), pltpu.SemaphoreType.REGULAR((3, 3)),
            S((len(Backward.SLOTS),)), S((FF // D,)), S((2,)), S((2 + depth,)), S((2 + depth,)), S((7,)),
            V((FF // D, D, D), BF), V((D, M), BF), V((FF // D, T, D), BF), V((FF // D, T, D), BF), V((T, D), BF), V((T, D), BF), V((T, D), BF),
            V((T, D), F32), V((T, D), F32), V((HEADS, T, T), BF), V((T, 3 * D), BF), V((T, D), F32), V((T, D), F32), V((T, D), BF),
            V((T, D), BF), V((T, 3 * D), BF), V((D, T), BF), V(history.shape, BF), V((T, D), F32), V((5, 8, D), F32),
            V((2 + depth, 8, D), F32), V((T, D), F32), V((8, D), F32), V(rope.shape, F32)],
        compiler_params=pltpu.CompilerParams(collective_id=1, has_side_effects=True, vmem_limit_bytes=63 * 2**20),
        cost_estimate=pl.CostEstimate(flops=32 * T * D * FF, bytes_accessed=2**27, transcendentals=2**10),
    )(first, second, saved.gout, saved.sums, saved.gain, rope, mix, up, down, saved.n1, saved.qkv, saved.probs, saved.att,
        saved.after, saved.n2, saved.act, saved.slope, saved.stored, saved.carried, inputs, history)


def results_kernel(first, second, sums, sums_v, grad_carried, gout, blended, stored, grad_inputs, mix, up, down,
                   blended_o, stored_o, inputs_o, history_o, qkv_o, out_o, up_o, down_o, gain_o, first_o, second_o,
                   mixed, carried_b, gout_b, blended_b, stored_b, inputs_b, mix_b, up_b, down_b, sem):
    q, o = qkv_o.shape[2] // 2, out_o.shape[2] // 2
    half = mix.shape[2] // 2
    ins = [(grad_carried, carried_b), (gout, gout_b), (stored.at[0], stored_b.at[0]), (stored.at[1], stored_b.at[1]), (blended, blended_b), (grad_inputs, inputs_b), (mix, mix_b), (up, up_b), (down, down_b)]
    outs = [[], [], [(stored_b.at[0], stored_o.at[0])], [(stored_b.at[1], stored_o.at[1])], [(blended_b, blended_o)], [(inputs_b, inputs_o)], [], [(up_b, up_o)], [(down_b, down_o)]]
    for h in range(2):
        outs[6].append((mix_b.at[:, :, pl.ds(h * half, q)], qkv_o.at[:, :, pl.ds(h * q, q)]))
        outs[6].append((mix_b.at[:, :, pl.ds(h * half + q, o)], out_o.at[:, :, pl.ds(h * o, o)]))
    loads = [pltpu.make_async_copy(a, b, sem.at[i]) for i, (a, b) in enumerate(ins)]
    for cp in loads: cp.start()
    copies = []
    def leave(a, b):
        copies.append(pltpu.make_async_copy(a, b, sem.at[len(ins) + len(copies)]))
        copies[-1].start()
    hist = history_o.shape[0]
    for cp in loads[:2]: cp.wait()
    for j in range(hist):
        mixed[j] = first[j] * carried_b[...] + second[j] * gout_b[...]
        leave(mixed.at[j], history_o.at[j])
    for j in range(hist + 1): first_o[j] = sums[0, j]
    for j in range(hist + 2): second_o[j] = sums[1, j]
    for cp, pairs in list(zip(loads, outs))[2:]:
        cp.wait()
        for a, b in pairs: leave(a, b)
    rows = gain_o.shape[2]
    device = lax.axis_index("wide") * lax.axis_size("narrow") + lax.axis_index("narrow")
    own = pltpu.roll(sums_v[...], lax.rem(sums_v.shape[1] - device * rows, sums_v.shape[1]), 1)
    for l in range(2): gain_o[l] = own[2 + 2 * l:4 + 2 * l, 0:rows]
    for cp in copies: cp.wait()


def results_call(first, second, sums, grad_carried, saved, grad_inputs, mix, up, down, hist):
    T, D = grad_inputs.shape
    rows = mix.shape[1]
    vm = pl.BlockSpec(memory_space=pltpu.VMEM); an = pl.BlockSpec(memory_space=pl.ANY); sm = pl.BlockSpec(memory_space=pltpu.SMEM)
    shapes = [(T, D), (2, T, D), (T, D), (hist, T, D), (2, rows, 3 * D), (2, rows, D), up.shape, down.shape, (2, 2, rows), (hist + 1,), (hist + 2,)]
    return pl.pallas_call(results_kernel,
        out_shape=[jax.ShapeDtypeStruct(s, F32) for s in shapes],
        in_specs=[sm] * 3 + [vm] + [an] * 8, out_specs=[an] * 8 + [vm] + [sm] * 2,
        scratch_shapes=[pltpu.VMEM((hist, T, D), F32), pltpu.VMEM((T, D), F32), pltpu.VMEM((T, D), F32), pltpu.VMEM((T, D), F32), pltpu.VMEM((2, T, D), F32), pltpu.VMEM((T, D), F32),
            pltpu.VMEM(mix.shape, F32), pltpu.VMEM(up.shape, F32), pltpu.VMEM(down.shape, F32), pltpu.SemaphoreType.DMA((20 + hist,))],
        compiler_params=pltpu.CompilerParams(vmem_limit_bytes=60 * 2**20),
    )(first, second, sums, sums, grad_carried, saved.gout, saved.blended, saved.stored, grad_inputs, mix, up, down)


def fast_body(mesh, inputs, history, lengths, cotangent, w_qkv, w_out, w_up, w_down, gains, alpha_first, alpha_second):
    rope = jnp.asarray(rotary_lanes(inputs.shape[0], inputs.shape[1] // HEADS, 128))
    weights, saved = fwd_call(mesh, steps(GATHER_ORDER), GATHER_KINDS, w_qkv, w_out, w_up, w_down, gains,
        inputs, history, cotangent, rope, lengths, alpha_first, alpha_second)
    mix, up, down, grad_carried, grad_inputs, sums = bwd_call(mesh, steps(SCATTER_ORDER), SCATTER_KINDS, weights, saved,
        inputs, history, rope, alpha_first, alpha_second)
    return results_call(alpha_first, alpha_second, sums, grad_carried, saved, grad_inputs, mix, up, down, history.shape[0])


def solution(mesh):
    axes = ("wide", "narrow")
    split, row_split = P(None, axes, None), P(axes, None)
    placed = (row_split, split, P(axes), row_split, split, split, split, split, P(None, None, axes), P(), P())
    results = (row_split, split, row_split, split, split, split, split, split, P(None, None, axes), P(), P())

    def body(*args):
        rows, hist = args[4].shape[1], args[1].shape[0]
        fits = mesh.shape["narrow"] == 4 and mesh.shape["wide"] == 8 and rows % 8 == 0
        fits = fits and hist * args[4].shape[1] == args[7].shape[1]
        return fast_body(mesh, *args) if fits else plain_body(*args)

    return jax.shard_map(body, mesh=mesh, in_specs=placed, out_specs=results, check_vma=False)
```

```python
import functools
import math
from types import SimpleNamespace

import jax
import jax.numpy as jnp
import numpy as np
from jax import lax
from jax.experimental import pallas as pl
from jax.experimental.pallas import tpu as pltpu
from jax.sharding import PartitionSpec as P

MESH = pl.DeviceIdType.MESH
BF = jnp.bfloat16
F32 = jnp.float32


HEADS = 12


norm_eps = 1e-05
gelu_coef = 0.044715
gelu_scale = math.sqrt(2.0 / math.pi)
masked_score = -1e30


def product(left, right):
    return jnp.dot(left, right, preferred_element_type=jnp.float32)


def layer_norm(hidden, gain_row):
    center = hidden - jnp.mean(hidden, axis=-1, keepdims=True)
    inverse = lax.rsqrt(jnp.mean(center * center, axis=-1, keepdims=True) + norm_eps)
    standard = center * inverse
    return (standard * gain_row, standard, inverse)


def plain_norm_back(grad_rows, standard, inverse, gain_row):
    scaled = grad_rows * gain_row
    grad_gain = jnp.sum(grad_rows * standard, axis=0)
    grad_in = inverse * (
        scaled
        - jnp.mean(scaled, axis=-1, keepdims=True)
        - standard * jnp.mean(scaled * standard, axis=-1, keepdims=True)
    )
    return (grad_in, grad_gain)


def gelu(values):
    return (
        0.5
        * values
        * (1.0 + jnp.tanh(gelu_scale * (values + gelu_coef * values * values * values)))
    )


def gelu_slope(values):
    tangent = jnp.tanh(gelu_scale * (values + gelu_coef * values * values * values))
    return 0.5 * (1.0 + tangent) + 0.5 * values * (1.0 - tangent * tangent) * gelu_scale * (
        1.0 + 3.0 * gelu_coef * values * values
    )


def rotary_tables(seq_length, head_width):
    half_width = head_width // 2
    frequency = 10000.0 ** (-jnp.arange(half_width, dtype=jnp.float32) / half_width)
    angles = jnp.arange(seq_length, dtype=jnp.float32)[:, None] * frequency[None, :]
    return (jnp.cos(angles)[:, None, :], jnp.sin(angles)[:, None, :])


def rotate(values, cos_table, sin_table):
    half_width = values.shape[-1] // 2
    left_half = values[..., :half_width]
    right_half = values[..., half_width:]
    return jnp.concatenate(
        [
            left_half * cos_table - right_half * sin_table,
            right_half * cos_table + left_half * sin_table,
        ],
        axis=-1,
    )


def rotate_back(grad_rows, cos_table, sin_table):
    half_width = grad_rows.shape[-1] // 2
    left_grad = grad_rows[..., :half_width]
    right_grad = grad_rows[..., half_width:]
    return jnp.concatenate(
        [
            left_grad * cos_table + right_grad * sin_table,
            right_grad * cos_table - left_grad * sin_table,
        ],
        axis=-1,
    )


def allowed_mask(block_rows, key_count, length):
    row_place = jnp.arange(block_rows)
    col_place = jnp.arange(key_count)
    return (col_place[None, :] <= row_place[:, None]) & (col_place[None, :] < length)


def attention_forward(queries, key_rows, value_rows, length):
    seq_length, head_count, head_width = queries.shape
    score_scale = head_width ** (-0.5)
    block_rows = min(512, seq_length)
    scores = (
        jnp.einsum("qhe,khe->hqk", queries, key_rows, preferred_element_type=jnp.float32)
        * score_scale
    )
    allowed = allowed_mask(block_rows, block_rows, length)
    scores = jnp.where(allowed[None], scores, masked_score)
    row_top = jnp.max(scores, axis=-1, keepdims=True)
    exp_scores = jnp.exp(scores - row_top)
    row_total = jnp.sum(exp_scores, axis=-1, keepdims=True)
    prob_rows = (exp_scores / row_total).astype(jnp.bfloat16)
    pieces = jnp.einsum("hqk,khe->qhe", prob_rows, value_rows, preferred_element_type=jnp.float32)
    log_sums = row_top + jnp.log(row_total)
    return (pieces, log_sums)


def attention_backward(queries, key_rows, value_rows, log_sums, grad_attended, length):
    seq_length, head_count, head_width = queries.shape
    score_scale = head_width ** (-0.5)
    grad_keys = jnp.zeros(queries.shape, jnp.float32)
    grad_values = jnp.zeros(queries.shape, jnp.float32)
    block_rows = min(512, seq_length)
    scores = (
        jnp.einsum("qhe,khe->hqk", queries, key_rows, preferred_element_type=jnp.float32)
        * score_scale
    )
    allowed = allowed_mask(block_rows, block_rows, length)
    prob_rows = jnp.where(allowed[None], jnp.exp(scores - log_sums), 0.0)
    grad_prob = jnp.einsum(
        "qhe,khe->hqk", grad_attended, value_rows, preferred_element_type=jnp.float32
    )
    inner_sum = jnp.sum(prob_rows * grad_prob, axis=-1, keepdims=True)
    grad_score = (prob_rows * (grad_prob - inner_sum)).astype(jnp.bfloat16)
    grad_pieces = (
        jnp.einsum("hqk,khe->qhe", grad_score, key_rows, preferred_element_type=jnp.float32)
        * score_scale
    )
    grad_keys = grad_keys.at[:block_rows].add(
        jnp.einsum("hqk,qhe->khe", grad_score, queries, preferred_element_type=jnp.float32)
        * score_scale
    )
    grad_values = grad_values.at[:block_rows].add(
        jnp.einsum(
            "hqk,qhe->khe",
            prob_rows.astype(jnp.bfloat16),
            grad_attended,
            preferred_element_type=jnp.float32,
        )
    )
    return (grad_pieces, grad_keys, grad_values)


def layer_forward(hidden, weights, length):
    layer_qkv, layer_out, layer_up, layer_down, layer_gains = weights
    seq_length = hidden.shape[0]
    head_width = layer_out.shape[0] // HEADS
    normed, unit_one, inverse_one = layer_norm(hidden, layer_gains[0])
    normed = normed.astype(jnp.bfloat16)
    joined = product(normed, layer_qkv).reshape(seq_length, 3, HEADS, head_width)
    cos_table, sin_table = rotary_tables(seq_length, head_width)
    queries = rotate(joined[:, 0], cos_table, sin_table).astype(jnp.bfloat16)
    key_rows = rotate(joined[:, 1], cos_table, sin_table).astype(jnp.bfloat16)
    value_rows = joined[:, 2].astype(jnp.bfloat16)
    attended, log_sums = attention_forward(queries, key_rows, value_rows, length)
    attended = attended.reshape(seq_length, HEADS * head_width).astype(jnp.bfloat16)
    after_attn = hidden + product(attended, layer_out)
    normed_two, unit_two, inverse_two = layer_norm(after_attn, layer_gains[1])
    normed_two = normed_two.astype(jnp.bfloat16)
    up_vals = product(normed_two, layer_up)
    result = after_attn + product(gelu(up_vals).astype(jnp.bfloat16), layer_down)
    kept_state = (
        normed,
        unit_one,
        inverse_one,
        queries,
        key_rows,
        value_rows,
        log_sums,
        attended,
        unit_two,
        inverse_two,
        normed_two,
        up_vals,
    )
    return (result, kept_state)


def layer_backward(grad_rows, weights, kept_state, length):
    layer_qkv, layer_out, layer_up, layer_down, layer_gains = weights
    (
        normed,
        unit_one,
        inverse_one,
        queries,
        key_rows,
        value_rows,
        log_sums,
        attended,
        unit_two,
        inverse_two,
        normed_two,
        up_vals,
    ) = kept_state
    seq_length, head_count, head_width = queries.shape
    grad_low = grad_rows.astype(jnp.bfloat16)
    active = gelu(up_vals).astype(jnp.bfloat16)
    grad_down = jnp.einsum("tf,td->fd", active, grad_low, preferred_element_type=jnp.float32)
    grad_active = jnp.einsum("td,fd->tf", grad_low, layer_down, preferred_element_type=jnp.float32)
    grad_upv = (grad_active * gelu_slope(up_vals)).astype(jnp.bfloat16)
    grad_up = jnp.einsum("td,tf->df", normed_two, grad_upv, preferred_element_type=jnp.float32)
    grad_norm_two = jnp.einsum("tf,df->td", grad_upv, layer_up, preferred_element_type=jnp.float32)
    grad_after, gain_two = plain_norm_back(grad_norm_two, unit_two, inverse_two, layer_gains[1])
    grad_after = grad_rows + grad_after
    grad_branch = grad_after.astype(jnp.bfloat16)
    grad_wout = jnp.einsum("ta,td->ad", attended, grad_branch, preferred_element_type=jnp.float32)
    grad_attended = jnp.einsum(
        "td,ad->ta", grad_branch, layer_out, preferred_element_type=jnp.float32
    )
    grad_attended = grad_attended.astype(jnp.bfloat16).reshape(seq_length, head_count, head_width)
    grad_query, grad_keys, grad_values = attention_backward(
        queries, key_rows, value_rows, log_sums, grad_attended, length
    )
    cos_table, sin_table = rotary_tables(seq_length, head_width)
    grad_joined = jnp.stack(
        [
            rotate_back(grad_query, cos_table, sin_table),
            rotate_back(grad_keys, cos_table, sin_table),
            grad_values,
        ],
        axis=1,
    )
    grad_joined = grad_joined.reshape(seq_length, 3 * head_count * head_width).astype(jnp.bfloat16)
    grad_qkv = jnp.einsum("td,tj->dj", normed, grad_joined, preferred_element_type=jnp.float32)
    grad_norm_one = jnp.einsum(
        "tj,dj->td", grad_joined, layer_qkv, preferred_element_type=jnp.float32
    )
    grad_in, gain_one = plain_norm_back(grad_norm_one, unit_one, inverse_one, layer_gains[0])
    return (
        grad_after + grad_in,
        (grad_qkv, grad_wout, grad_up, grad_down, jnp.stack([gain_one, gain_two])),
    )


def mix_history(alphas, history):
    blended = alphas[0] * history[0].astype(jnp.float32)
    for entry in range(1, history.shape[0]):
        blended = blended + alphas[entry] * history[entry].astype(jnp.float32)
    return blended


def plain_body(
    inputs,
    history,
    lengths,
    cotangent,
    w_qkv,
    w_out,
    w_up,
    w_down,
    gains,
    alpha_first,
    alpha_second,
):
    token_total = lax.psum(jnp.sum(lengths.astype(jnp.float32)), ("wide", "narrow"))
    length = lengths[0]
    hist_count = history.shape[0]

    def fetch_layer(layer_no):
        return (
            lax.all_gather(w_qkv[layer_no], ("wide", "narrow"), axis=0, tiled=True),
            lax.all_gather(w_out[layer_no], ("wide", "narrow"), axis=0, tiled=True),
            lax.all_gather(w_up[layer_no], ("wide", "narrow"), axis=0, tiled=True),
            lax.all_gather(w_down[layer_no], ("wide", "narrow"), axis=0, tiled=True),
            lax.all_gather(gains[layer_no], ("wide", "narrow"), axis=1, tiled=True),
        )

    def fetch_again(layer_no):
        return (
            lax.all_gather(w_qkv[layer_no], ("wide", "narrow"), axis=0, tiled=True),
            lax.all_gather(w_out[layer_no], ("wide", "narrow"), axis=0, tiled=True),
            lax.all_gather(w_up[layer_no], ("wide", "narrow"), axis=0, tiled=True),
            lax.all_gather(w_down[layer_no], ("wide", "narrow"), axis=0, tiled=True),
            lax.all_gather(gains[layer_no], ("wide", "narrow"), axis=1, tiled=True),
        )

    def reduce_grads(grad_set):
        return (
            lax.psum_scatter(grad_set[0], ("wide", "narrow"), scatter_dimension=0, tiled=True),
            lax.psum_scatter(grad_set[1], ("wide", "narrow"), scatter_dimension=0, tiled=True),
            lax.psum_scatter(grad_set[2], ("wide", "narrow"), scatter_dimension=0, tiled=True),
            lax.psum_scatter(grad_set[3], ("wide", "narrow"), scatter_dimension=0, tiled=True),
            lax.psum_scatter(grad_set[4], ("wide", "narrow"), scatter_dimension=1, tiled=True),
        )

    weights_one = fetch_layer(0)
    kept_one, state_one = layer_forward(inputs, weights_one, length)
    carried = mix_history(alpha_first, history) + alpha_first[hist_count] * kept_one
    weights_two = fetch_layer(1)
    kept_two, state_two = layer_forward(carried, weights_two, length)
    blended = (
        mix_history(alpha_second, history)
        + alpha_second[hist_count] * kept_one
        + alpha_second[hist_count + 1] * kept_two
    )
    seq_length = inputs.shape[0]
    live_mask = (jnp.arange(seq_length) < length).astype(jnp.float32)[:, None]
    grad_blend = cotangent * live_mask / token_total
    back_two = fetch_again(1)
    grad_carried, grads_two = layer_backward(
        alpha_second[hist_count + 1] * grad_blend, back_two, state_two, length
    )
    shard_two = reduce_grads(grads_two)
    grad_first = alpha_first[hist_count] * grad_carried + alpha_second[hist_count] * grad_blend
    back_one = fetch_again(0)
    grad_inputs, grads_one = layer_backward(grad_first, back_one, state_one, length)
    shard_one = reduce_grads(grads_one)
    grad_history = jnp.stack(
        [
            alpha_first[entry] * grad_carried + alpha_second[entry] * grad_blend
            for entry in range(hist_count)
        ]
    )
    first_terms = []
    second_terms = []
    for entry in range(hist_count):
        past_row = history[entry].astype(jnp.float32)
        first_terms.append(jnp.sum(past_row * grad_carried))
        second_terms.append(jnp.sum(past_row * grad_blend))
    first_terms.append(jnp.sum(kept_one * grad_carried))
    second_terms.append(jnp.sum(kept_one * grad_blend))
    second_terms.append(jnp.sum(kept_two * grad_blend))
    grad_alpha_first, grad_alpha_second = lax.psum(
        (jnp.stack(first_terms), jnp.stack(second_terms)), ("wide", "narrow")
    )
    return (
        blended,
        jnp.stack([kept_one, kept_two]),
        grad_inputs,
        grad_history,
        jnp.stack([shard_one[0], shard_two[0]]),
        jnp.stack([shard_one[1], shard_two[1]]),
        jnp.stack([shard_one[2], shard_two[2]]),
        jnp.stack([shard_one[3], shard_two[3]]),
        jnp.stack([shard_one[4], shard_two[4]]),
        grad_alpha_first,
        grad_alpha_second,
    )


GATHER_KINDS = "accacc"
GATHER_ORDER = (
    200, 400, 100, 0, 110, 21, 22, 500, -1, 30, 210, 23, 300, 121, 31, 32, 33, 122, 123, 40, 41, 51, 510, 321,
    140, 410, 42, 52, 50, 150, 330, 240, 250, 43, 53, -1, 322, 323, 141, 142, 221, 143, 153, 222, -1, -1, -1,
    -1, -1, -1, -1, -1, -1, -1, 440, 223, -1, -1, -1, -1, -1, 331, 332, 333, 151, 540, 152, -1, -1, -1, 340,
    350, 521, 421, 422, 241, 251, 242, -1, -1, -1, -1, -1, -1, -1, 522, -1, -1, -1, 252, -1, 341, 351, 342,
    343, 243, 353, 423, 352, 253, -1, -1, -1, -1, -1, -1, -1, -1, -1, -1, -1, -1, 441, 523, 442, 443, 550,
    541, 542, -1, -1, -1, -1, -1, -1, -1, 451, 452, 453, 450, -1, -1, -1, 543, -1, -1, -1, -1, -1, -1, -1,
    552, 553, 551, -1, -1, -1, -1,
)
SCATTER_KINDS = "acacac"
SCATTER_ORDER = (
    -1, -1, -1, 553, -1, 551, 552, 543, -1, -1, 550, -1, -1, -1, -1, 542, 541, 540, -1, -1, -1, 523, -1, -1,
    -1, -1, -1, 453, 452, 450, -1, -1, -1, -1, -1, -1, 451, 443, 442, 441, 522, 521, -1, -1, -1, -1, -1, 433,
    -1, 432, 440, -1, -1, -1, -1, -1, -1, -1, -1, 353, 431, 350, 423, 422, 343, -1, -1, -1, -1, 352, 351, 510,
    421, 430, -1, 342, 341, 340, 323, 500, -1, 253, -1, 252, -1, 251, -1, 250, -1, -1, -1, -1, 243, -1, 242,
    241, 322, 321, 400, -1, -1, -1, -1, -1, -1, -1, -1, 150, -1, 151, 152, 153, 143, -1, 142, -1, 141, -1,
    140, -1, -1, 123, -1, 310, 240, -1, -1, -1, -1, 122, -1, 121, 233, 232, 231, 300, -1, -1, -1, -1, -1, -1,
    -1, -1, 53, 43, -1, 52, -1, 42, -1, 50, -1, 223, 51, 33, 41, 40, 222, 221, 32, 31, 23, 230, 30, 22, 110,
    21, 200, 100, 0,
)
NEXT = -1


def steps(codes):
    return [v if v == NEXT else (v // 100, "oplaqd"[v // 10 % 10], v % 10) for v in codes]


def al(v, m): return pl.multiple_of(v, m)
def when(cond, fn): pl.when(cond)(fn)

class Place:
    def __init__(self, depth):
        self.depth = depth
        w = lax.axis_index("wide"); n = lax.axis_index("narrow")
        self.w, self.n = w, n
        self.z, self.x = w // 2, lax.rem(w, 2)
        self.y, self.c = n // 2, lax.rem(n, 2)
        first = self.c == 0
        p = jnp.where(first, self.x, self.y)
        q = jnp.where(first, self.y, self.x)
        self.sib = (w, self.y * 2 + 1 - self.c)
        self.xn = (self.z * 2 + 1 - self.x, n)
        self.yn = (w, (1 - self.y) * 2 + self.c)
        self.pn = tuple(jnp.where(first, a, b) for a, b in zip(self.xn, self.yn))
        self.qn = tuple(jnp.where(first, b, a) for a, b in zip(self.xn, self.yn))
        self.has_up = self.z < depth - 1
        self.has_down = self.z > 0
        self.up = (w + 2, n)
        self.down = (w - 2, n)
        self.line = [(lax.rem(w + 2 * i, 2 * depth), n) for i in range(1, depth)]
        self.chip = self.z * 4 + self.x * 2 + self.y
        self.planes = [self.plane(r) for r in range(depth)]
        self.chips = [[[z * 4 + jnp.where(first, 2, 1) * (1 - p if a else p) + jnp.where(first, 1, 2) * (1 - q if b else q)
                        for z in self.planes] for b in (0, 1)] for a in (0, 1)]
        self.onward_up = [(z < self.z) & self.has_up for z in self.planes]
        self.onward_down = [(z > self.z) & self.has_down for z in self.planes]
    def plane(self, r):
        if r == 0: return self.z
        z, last = self.z, self.depth - 1
        short = jnp.minimum(z, last - z)
        low = z * 2 < self.depth
        dist = jnp.where(r <= 2 * short, (r + 1) // 2, r - short)
        below = jnp.where((r <= 2 * short) & (r % 2 == 1), low, ~low)
        return jnp.where(below, z - dist, z + dist)

class Gather:
    def __init__(self, me, chunks, ssem, rsem):
        self.me, self.chunks, self.ssem, self.rsem = me, chunks, ssem, rsem
    def copy(self, k, chip, way, target, sem):
        ref = self.chunks[k][1](chip, 1)
        return pltpu.make_async_remote_copy(src_ref=ref, dst_ref=ref, send_sem=self.ssem.at[k, way],
            recv_sem=self.rsem.at[k, sem], device_id=target, device_id_type=MESH)
    def plane_copy(self, k, r):
        ref = self.chunks[k][2](self.me.planes[r])
        return pltpu.make_async_remote_copy(src_ref=ref, dst_ref=ref, send_sem=self.ssem.at[k, 4],
            recv_sem=self.rsem.at[k, 3 * self.me.depth + self.me.planes[r]], device_id=self.me.sib, device_id_type=MESH)
    def p(self, k, chip, r): self.copy(k, chip, 0, self.me.pn, 2 * self.me.depth + self.me.planes[r]).start()
    def q(self, k, chip, r): self.copy(k, chip, 1, self.me.qn, self.me.planes[r]).start()
    def up(self, k, chip, r): self.copy(k, chip, 2, self.me.up, self.me.depth + self.me.planes[r]).start()
    def down(self, k, chip, r): self.copy(k, chip, 3, self.me.down, self.me.depth + self.me.planes[r]).start()
    def wait(self, k, n, sem):
        ref = self.chunks[k][1](0, n)
        pltpu.make_async_remote_copy(src_ref=ref, dst_ref=ref, send_sem=self.ssem.at[k, 0], recv_sem=self.rsem.at[k, sem],
            device_id=self.me.pn, device_id_type=MESH).wait_recv()
    def event(self, k, what, r):
        me, Z = self.me, self.me.depth
        kind = self.chunks[k][0]
        own, flip = me.chips[0][0][r], me.chips[1][0][r]
        if what == "o":
            when(me.has_up, lambda: self.up(k, own, 0))
            when(me.has_down, lambda: self.down(k, own, 0))
            self.p(k, own, 0)
            self.q(k, own, 0)
        elif what == "p":
            self.wait(k, 1, 2 * Z + me.planes[0])
            when(me.has_up, lambda: self.up(k, flip, 0))
            when(me.has_down, lambda: self.down(k, flip, 0))
            self.q(k, flip, 0)
        elif what == "l":
            both = (own, flip) if kind == "c" else (own,)
            self.wait(k, len(both), Z + me.planes[r])
            def fwd(send):
                for chip in both: send(k, chip, r)
            when(me.onward_up[r], lambda: fwd(self.up))
            when(me.onward_down[r], lambda: fwd(self.down))
            if kind == "a": self.p(k, own, r)
            for chip in both: self.q(k, chip, r)
        elif what == "a":
            self.wait(k, 1, 2 * Z + me.planes[r])
            self.q(k, flip, r)
        elif what == "q":
            self.wait(k, 2, me.planes[r])
            self.plane_copy(k, r).start()
        elif what == "d":
            self.plane_copy(k, r).wait_recv()
    def drain(self, k):
        me, Z = self.me, self.me.depth
        per = 2 if self.chunks[k][0] == "c" else 1
        counts = [1 if per == 2 else Z, 2 * Z, jnp.where(me.has_up, per * (me.z + 1), 0), jnp.where(me.has_down, per * (Z - me.z), 0)]
        for way, count in enumerate(counts):
            def one(_, carry):
                self.copy(k, 0, way, me.pn, 0).wait_send()
                return carry
            lax.fori_loop(0, count, one, 0)
        def one(_, carry):
            self.plane_copy(k, 0).wait_send()
            return carry
        lax.fori_loop(0, Z, one, 0)

def greet(me, whole_line=False):
    bar = pltpu.get_barrier_semaphore()
    def signal(d): pl.semaphore_signal(bar, inc=1, device_id=d, device_id_type=MESH)
    for d in (me.sib, me.xn, me.yn): signal(d)
    if whole_line:
        for d in me.line: signal(d)
    else:
        when(me.has_up, lambda: signal(me.up))
        when(me.has_down, lambda: signal(me.down))
    return bar


def greeted(me, bar, whole_line=False):
    line = len(me.line) if whole_line else me.has_up.astype(jnp.int32) + me.has_down.astype(jnp.int32)
    pl.semaphore_wait(bar, 3 + line)


def add_into(dst, sources, rows, out=None):
    step = 48 if rows % 48 == 0 else 16
    @pl.loop(0, rows // step)
    def _(i):
        at = pl.ds(al(i * step, 16), step)
        if out is None and len(sources) == 1:
            dst[at, :] = dst[at, :] + sources[0][at, :]
            return
        total = dst[at, :].astype(F32)
        for s in sources: total = total + s[at, :].astype(F32)
        if out is None: dst[at, :] = total.astype(dst.dtype)
        else: out[at, :] = total


class Scatter:
    def __init__(self, me, chunks, ssem, rsem):
        self.me, self.chunks, self.ssem, self.rsem = me, chunks, ssem, rsem
        Z = me.depth
        self.Z = Z
        self.q_slot = lambda flip, z: (Z if flip else 0) + z
        self.line_slot = lambda flip, z: 2 * Z + (Z if flip else 0) + z
        self.late_slot = lambda flip: 4 * Z + (1 if flip else 0)
        self.p_slot = lambda kind, z: 3 * Z + z if kind == "a" else 4 * Z + 2
        self.slots = 4 * Z + 3
    def land(self, k, slot): return self.chunks[k].land(slot)
    def copy(self, k, chip, way, target, slot):
        ch = self.chunks[k]
        return pltpu.make_async_remote_copy(src_ref=ch.share(chip), dst_ref=ch.land(slot), send_sem=self.ssem.at[k, way],
            recv_sem=self.rsem.at[k, slot], device_id=target, device_id_type=MESH)
    def plane_copy(self, k, r):
        ch, me = self.chunks[k], self.me
        z = me.planes[r]
        return pltpu.make_async_remote_copy(src_ref=ch.plane(z, False), dst_ref=ch.plane_land(z), send_sem=self.ssem.at[k, 4],
            recv_sem=self.rsem.at[k, self.slots + z], device_id=me.sib, device_id_type=MESH)
    def wait(self, k, slot):
        self.copy(k, 0, 0, self.me.pn, slot).wait_recv()
    def take(self, k, chip, slots, out=None):
        ch = self.chunks[k]
        for s in slots: self.wait(k, s)
        add_into(ch.share(chip), [ch.land(s) for s in slots], ch.rows, out)
    def event(self, k, what, r):
        me, Z = self.me, self.Z
        ch = self.chunks[k]
        kind = ch.kind
        own, flip = me.chips[0][0][r], me.chips[1][0][r]
        z = me.planes[r]
        if what == "d":
            self.plane_copy(k, r).start()
        elif what == "q":
            self.plane_copy(k, r).wait_recv()
            ch.plane_add(z)
            self.copy(k, me.chips[0][1][r], 1, me.qn, self.q_slot(False, z)).start()
            self.copy(k, me.chips[1][1][r], 1, me.qn, self.q_slot(True, z)).start()
        elif what == "a":
            self.take(k, flip, [self.q_slot(True, z)])
            self.copy(k, flip, 0, me.pn, self.p_slot(kind, z)).start()
        elif what == "l":
            first = [self.q_slot(False, z)] + ([self.p_slot(kind, z)] if kind == "a" else [])
            self.take(k, own, first)
            if kind == "c": self.take(k, flip, [self.q_slot(True, z)])
            flips = (False, True) if kind == "c" else (False,)
            def behind():
                for f in flips: self.take(k, flip if f else own, [self.line_slot(f, z)])
            when((z < me.z) & me.has_up, behind)
            when((z > me.z) & me.has_down, behind)
            def send(way, target, late):
                for f in flips:
                    self.copy(k, flip if f else own, way, target, self.late_slot(f) if late else self.line_slot(f, z)).start()
            when((z > me.z) & (z == me.z + 1), lambda: send(2, me.up, False))
            when((z > me.z) & (z != me.z + 1), lambda: send(2, me.up, False))
            when((z < me.z) & (z == me.z - 1), lambda: send(3, me.down, True))
            when((z < me.z) & (z != me.z - 1), lambda: send(3, me.down, False))
        elif what in "po":
            f = what == "p"
            chip = flip if f else own
            slots = [self.q_slot(f, z)]
            if not f: slots.append(self.p_slot(kind, z))
            when(me.has_down, lambda: self.take(k, chip, [self.line_slot(f, z)]))
            when(me.has_up, lambda: self.take(k, chip, [self.late_slot(f)]))
            self.take(k, chip, slots, None if f else ch.result)
            if f: self.copy(k, chip, 0, me.pn, self.p_slot(kind, z)).start()
    def drain(self, k):
        me, Z = self.me, self.Z
        per = 2 if self.chunks[k].kind == "c" else 1
        counts = [1 if per == 2 else Z, 2 * Z, jnp.where(me.has_up, per * (Z - 1 - me.z), 0), jnp.where(me.has_down, per * me.z, 0)]
        for way, count in enumerate(counts):
            def one(_, carry):
                self.copy(k, 0, way, me.pn, 0).wait_send()
                return carry
            lax.fori_loop(0, count, one, 0)
        def one(_, carry):
            self.plane_copy(k, 0).wait_send()
            return carry
        lax.fori_loop(0, Z, one, 0)


def dot(a, b):
    return jnp.dot(a, b, preferred_element_type=F32)


def dot_nt(a, b):
    return lax.dot_general(a, b, (((1,), (1,)), ((), ())), preferred_element_type=F32)


def dot_tn(a, b):
    return lax.dot_general(a, b, (((0,), (0,)), ((), ())), preferred_element_type=F32)


def normalized(h):
    center = h - jnp.mean(h, axis=-1, keepdims=True)
    inverse = lax.rsqrt(jnp.mean(center * center, axis=-1, keepdims=True) + norm_eps)
    return center * inverse, inverse


def swap_halves(v, half):
    lanes = lax.broadcasted_iota(jnp.int32, v.shape, 1)
    width = v.shape[1]
    return jnp.where(lanes % (2 * half) < half, pltpu.roll(v, width - half, 1), pltpu.roll(v, half, 1))


def rotary_lanes(seq_length, head_width, lanes):
    half = head_width // 2
    frequency = (10000.0 ** (-np.arange(half, dtype=np.float32) / half)).astype(np.float32)
    angles = np.arange(seq_length, dtype=np.float32)[:, None] * frequency[None, :]
    cos, sin = np.cos(angles), np.sin(angles)
    both = np.stack([np.concatenate([cos, cos], 1), np.concatenate([-sin, sin], 1)])
    return np.tile(both, (1, 1, lanes // head_width)).astype(np.float32)


def add_sum(ref, row, lane, product):
    rows = lax.broadcasted_iota(jnp.int32, ref.shape, 0)
    lanes = lax.broadcasted_iota(jnp.int32, ref.shape, 1)
    total = jnp.sum(jnp.sum(product, axis=0, keepdims=True), axis=1, keepdims=True)
    ref[...] = ref[...] + jnp.where((rows == row) & (lanes == lane), total, 0.0)


class Forward:
    def __init__(self, w, io, s, planes, length, first, second):
        self.planes = planes
        self.w, self.io, self.s = w, io, s
        self.length, self.first, self.second = length, first, second
        self.T, self.D = s.h.shape
        self.width = self.D // HEADS
        self.q, self.o = 3 * self.D // 2, self.D // 2
        self.half = w.mix.shape[2] // 2
        self.writes = []

    def send(self, name, l=None):
        src, dst = getattr(self.s, name), getattr(self.io, name)
        if l is not None: src, dst = src.at[l], dst.at[l]
        n = len(self.writes)
        self.writes.append((src, dst, n))
        pltpu.make_async_copy(src, dst, self.io.wsem.at[n]).start()

    def finish(self):
        for src, dst, n in self.writes:
            pltpu.make_async_copy(src, dst, self.io.wsem.at[n]).wait()

    def load(self, i):
        s, io = self.s, self.io
        src, dst = ((io.h, s.h), (io.rope, s.rope), (io.cotangent, s.cotangent), (io.history, s.history))[i]
        return pltpu.make_async_copy(src, dst, io.isem.at[i])

    def setup(self):
        s, T = self.s, self.T
        row = lax.broadcasted_iota(jnp.int32, (T, T), 0)
        col = lax.broadcasted_iota(jnp.int32, (T, T), 1)
        s.bias[...] = jnp.where((col <= row) & (col < self.length), 0.0, masked_score)
        s.sums[...] = jnp.zeros_like(s.sums)

    def loss_grad(self):
        s, io = self.s, self.io
        count = jnp.sum(s.gain[4:5, :])
        row = lax.broadcasted_iota(jnp.int32, (self.T, 1), 0)
        grad = jnp.where(row < self.length, s.cotangent[...], 0.0) / count
        s.gout[...] = grad
        self.send("gout")
        n = s.history.shape[0]
        for j in range(n): add_sum(s.sums, 1, j, s.history[j].astype(F32) * grad)

    def layer_in(self, l):
        return self.s.h if l == 0 else self.s.carried

    def norm_one(self, l):
        s, w = self.s, self.w
        if l == 0:
            s.gain[...] = s.total[...]
            self.send("gain")
            for i in range(4): self.load(i).wait()
        x, _ = normalized(self.layer_in(l)[...])
        s.n1[l] = (x * s.gain[2 * l:2 * l + 1, :]).astype(BF)
        self.send("n1", l)

    def project(self, l, t):
        s, w = self.s, self.w
        h, i = divmod(t, 3)
        W = self.q // 3
        at = h * self.half + i * W
        joined = dot(s.n1[l], w.mix[l, :, at:at + W])
        for j in range(W // 128):
            col = t * W + j * 128
            part = joined[:, j * 128:(j + 1) * 128]
            if col < 2 * self.D:
                part = part * s.cos[...] + swap_halves(part, self.width // 2) * s.sin[...]
                if col < self.D: part = part * self.width ** -0.5
            s.qkv[l, :, col:col + 128] = part.astype(BF)

    def attend(self, l, a):
        s, D = self.s, self.D
        q, k, v = (s.qkv[l, :, i * D + a * 128:i * D + a * 128 + 128] for i in range(3))
        lanes = lax.broadcasted_iota(jnp.int32, q.shape, 1)
        outs = []
        for e in range(2):
            mine = (lanes < self.width) if e == 0 else (lanes >= self.width)
            scores = dot_nt(jnp.where(mine, q, jnp.zeros_like(q)), k) + s.bias[...]
            top = jnp.max(scores, axis=-1, keepdims=True)
            weights = jnp.exp(scores - top)
            probs = (weights * (1.0 / jnp.sum(weights, axis=-1, keepdims=True))).astype(BF)
            s.probs[l, 2 * a + e] = probs
            outs.append(dot(probs, v))
        s.att[l, :, a * 128:a * 128 + 128] = jnp.where(lanes < self.width, outs[0], outs[1]).astype(BF)

    def attend_done(self, l):
        for name in ("qkv", "probs", "att"): self.send(name, l)

    def out(self, l, h):
        s, w = self.s, self.w
        cols = slice(h * self.o, (h + 1) * self.o)
        at = h * self.half + self.q
        s.after[l, :, cols] = self.layer_in(l)[:, cols] + dot(s.att[l], w.mix[l, :, at:at + self.o])

    def norm_two(self, l):
        s = self.s
        x, _ = normalized(s.after[l])
        s.n2[l] = (x * s.gain[2 * l + 1:2 * l + 2, :]).astype(BF)
        self.send("n2", l)
        self.send("after", l)

    def raise_(self, l, t, W):
        s, w = self.s, self.w
        u = dot(s.n2[l], w.up[l, :, t * W:(t + 1) * W])
        tile, at = divmod(t * W, self.D)
        cols = slice(at, at + W)
        square = u * u
        tangent = jnp.tanh(gelu_scale * u * (1.0 + gelu_coef * square))
        s.act[l, tile, :, cols] = (0.5 * u * (1.0 + tangent)).astype(BF)
        s.slope[l, tile, :, cols] = (
            0.5 * (1.0 + tangent) + 0.5 * u * (1.0 - tangent * tangent) * gelu_scale * (1.0 + 3.0 * gelu_coef * square)
        ).astype(BF)

    def raise_done(self, l):
        for name in ("act", "slope"): self.send(name, l)

    def lower(self, l, r):
        s, w = self.s, self.w
        z = self.planes[r]
        chips = w.down.shape[1] // len(self.planes)
        part = dot(s.act[l, z], w.down[l, pl.ds(z * chips, chips)].reshape(-1, self.D))
        s.stored[l] = (s.after[l] if r == 0 else s.stored[l]) + part

    def mixed(self, l):
        s, io = self.s, self.io
        n = s.history.shape[0]
        if l == 0:
            s.carried[...] = mix_history([self.first[j] for j in range(n)], s.history) + self.first[n] * s.stored[0]
            self.send("carried")
            s.blended[...] = mix_history([self.second[j] for j in range(n)], s.history) + self.second[n] * s.stored[0]
        else:
            s.blended[...] = s.blended[...] + self.second[n + 1] * s.stored[1]
            self.send("blended")
        self.send("stored", l)
        add_sum(s.sums, 1, n + l, s.stored[l] * s.gout[...])
        if l == 1: self.send("sums")

    def steps(self):
        out = [(-1, self.setup)]
        P = functools.partial
        for l in range(2):
            k = 3 * l
            out.append((k, P(self.norm_one, l)))
            out += [(k, P(self.project, l, t)) for t in range(6)]
            if l == 0: out.append((k, self.loss_grad))
            out += [(k, P(self.attend, l, a)) for a in range(self.D // 128)]
            out.append((k, P(self.attend_done, l)))
            out += [(k, P(self.out, l, h)) for h in range(2)]
            out.append((k, P(self.norm_two, l)))
            W = self.D // 2
            out += [(k + 1, P(self.raise_, l, t, W)) for t in range(4 * self.D // W)]
            out.append((k + 1, P(self.raise_done, l)))
            out += [((k + 2, r), P(self.lower, l, r)) for r in range(len(self.planes))]
            out.append((k + 2, P(self.mixed, l)))
        return out


def weave(order, work):
    left, whole, done, queue = {}, set([-1]), [], list(work)
    for v in order:
        if v != NEXT and v[1] == "d": left[v[0]] = left.get(v[0], 0) + 1
    for v in order:
        if v == NEXT:
            need, act = queue.pop(0)
            assert need in whole
            done.append(act)
            continue
        done.append(v)
        k, what, r = v
        if what == "d":
            whole.add((k, r))
            left[k] -= 1
            if not left[k]: whole.add(k)
    assert not queue
    return done


def saved_shapes(T, D, FF):
    return dict(n1=((2, T, D), BF), qkv=((2, T, 3 * D), BF), probs=((2, HEADS, T, T), BF), att=((2, T, D), BF), after=((2, T, D), F32),
        n2=((2, T, D), BF), act=((2, FF // D, T, D), BF), slope=((2, FF // D, T, D), BF), stored=((2, T, D), F32), carried=((T, D), F32),
        blended=((T, D), F32), gout=((T, D), F32), sums=((8, D), F32), gain=((8, D), F32))


SAVED = tuple(saved_shapes(1, 1, 1))


def fwd_kernel(depth, order, kinds, qkv_in, out_in, up_in, down_in, gain_in, h_in, history_in, cotangent_in, rope_in, length, first, second,
              mix_o, up_o, down_o, *rest):
    n = len(SAVED)
    saved_o, rest = rest[:n], rest[n:]
    (mix_b, up_b, down_b, mix_s, up_s, mix_t, up_t, ssem, rsem, esem, lsem, wsem, isem, bias, value, land, h_b, history_b, cotangent_b,
        rope_b, tsend, trecv), saved_b = rest[:22], rest[22:]
    me = Place(depth)
    bar = greet(me, True)
    rows = qkv_in.shape[1]
    c = me.c
    wq, wo, wu = qkv_in.shape[2] // 2, out_in.shape[2] // 2, up_in.shape[2] // 2
    mine = lambda w: pl.ds(al(c * w, 128), w)
    other = lambda w: pl.ds(al((1 - c) * w, 128), w)
    my_rows = pl.ds(al(c * rows, 8), rows)
    def stage(k):
        l, j = divmod(k, 3)
        if j == 0:
            for ref, at, pick in ((mix_s, (l, my_rows), mine), (mix_t, (l, slice(None)), other)):
                ref[at[0], at[1], 0:wq] = qkv_in[l, :, pick(wq)].astype(F32)
                ref[at[0], at[1], wq:wq + wo] = out_in[l, :, pick(wo)].astype(F32)
        elif j == 1:
            up_s[l, my_rows, :] = up_in[l, :, mine(wu)].astype(F32)
            up_t[l] = up_in[l, :, other(wu)].astype(F32)
    def place_gains():
        small = value.at[2]
        small[...] = jnp.zeros_like(small)
        for l in range(2): small[2 * l:2 * l + 2, 0:rows] = gain_in[l].astype(F32)
        n = value.shape[2]
        at = rows * (me.w * 4 + me.n)
        one = lax.broadcasted_iota(jnp.int32, (128, n), 1) == lax.broadcasted_iota(jnp.int32, (128, n), 0) + at
        own = dot(small[:, 0:128].astype(BF), one.astype(BF))
        row = lax.broadcasted_iota(jnp.int32, own.shape, 0)
        col = lax.broadcasted_iota(jnp.int32, own.shape, 1)
        value[0] = own + jnp.where((row == 4) & (col == 0), length[0].astype(F32), 0.0)
    def exchange(k):
        l, j = divmod(k, 3)
        if j == 2: return None
        s, t = ((mix_s, mix_t), (up_s, up_t))[j]
        return pltpu.make_async_remote_copy(src_ref=t.at[l], dst_ref=s.at[l, my_rows, :], send_sem=esem.at[0, k],
            recv_sem=esem.at[1, k], device_id=me.sib, device_id_type=MESH)
    def ready(k):
        l, j = divmod(k, 3)
        if j == 2:
            down_b[l, me.chip, c] = down_in[l]
            return
        exchange(k).wait_recv()
        s, b = ((mix_s, mix_b), (up_s, up_b))[j]
        b[l, pl.ds(al(me.chip * 2 * rows, 16), 2 * rows), mine(s.shape[2])] = s[l].astype(BF)
    chunks = []
    for k in range(6):
        l, j = divmod(k, 3)
        if j == 2:
            chunks.append((kinds[k], lambda chip, n, l=l: down_b.at[l, pl.ds(chip, n), c], lambda z, l=l: down_b.at[l, pl.ds(z * 4, 4), c]))
        else:
            b = (mix_b, up_b)[j]
            half = b.shape[2] // 2
            chunks.append((kinds[k],
                lambda chip, n, b=b, l=l, half=half: b.at[l, pl.ds(al(chip * 2 * rows, 16), n * 2 * rows), mine(half)],
                lambda z, b=b, l=l, half=half: b.at[l, pl.ds(al(z * 8 * rows, 16), 8 * rows), mine(half)]))
    gather = Gather(me, chunks, ssem, rsem)
    io = SimpleNamespace(**dict(zip(SAVED, saved_o)), h=h_in, history=history_in, cotangent=cotangent_in, rope=rope_in,
        wsem=wsem, isem=isem)
    scratch = SimpleNamespace(**dict(zip(SAVED, saved_b)), bias=bias, total=value.at[4], h=h_b, history=history_b,
        cotangent=cotangent_b, rope=rope_b, cos=rope_b.at[0], sin=rope_b.at[1])
    fwd = Forward(SimpleNamespace(mix=mix_b, up=up_b, down=down_b), io, scratch, me.planes, length[0], first, second)
    first_out = []
    for v in order:
        if v != NEXT and v[1] == "o" and v[0] % 3 < 2: first_out.append(v[0])
    for k in first_out[:2]: stage(k)
    greeted(me, bar, True)
    for k in first_out[:2]: exchange(k).start()
    total = Total(me, value, land, tsend, trecv)
    def settle():
        place_gains()
        total.step(0)
        for i in range(4): fwd.load(i).start()
        for k in first_out[2:]:
            stage(k)
            exchange(k).start()
    pairs = ((mix_b, mix_o), (up_b, up_o), (down_b, down_o))
    def write(k, r):
        l, j = divmod(k, 3)
        b, o = pairs[j]
        n = b.shape[1] // depth
        at = pl.ds(al(me.planes[r] * n, n), n)
        return pltpu.make_async_copy(b.at[l, at], o.at[l, at], lsem.at[k, r])
    totals, count, sent = [1, 2, 3, 4], 0, 0
    for item in weave(order, fwd.steps()):
        if not isinstance(item, tuple):
            item()
            continue
        k, what, r = item
        if what == "o":
            if settle and k in first_out[2:]:
                settle()
                settle = None
            ready(k)
        gather.event(k, what, r)
        if what == "o" and settle:
            if k % 3 < 2: sent += 1
            if sent == 2:
                settle()
                settle = None
        if what == "d": write(k, r).start()
        count += 1
        if totals and not settle and count % 5 == 0: total.step(totals.pop(0))
    for k in range(6):
        gather.drain(k)
        if k % 3 < 2: exchange(k).wait_send()
    for k in range(6):
        for r in range(depth): write(k, r).wait()
    fwd.finish()

def fwd_call(mesh, order, kinds, w_qkv, w_out, w_up, w_down, gains, h, history, cotangent, rope, lengths, first, second):
    depth = mesh.shape["wide"] // 2
    rows = w_qkv.shape[1]
    D, FF = rows * mesh.size, w_down.shape[1] * mesh.size
    T = h.shape[0]
    n = mesh.size // 2
    M = 4 * D
    body = functools.partial(fwd_kernel, depth, order, kinds)
    vm = pl.BlockSpec(memory_space=pltpu.VMEM); an = pl.BlockSpec(memory_space=pl.ANY); sm = pl.BlockSpec(memory_space=pltpu.SMEM)
    shapes = [((2, D, M), BF), ((2, D, FF), BF), ((2, n, 2, FF // n // 2, D), BF)]
    saved = list(saved_shapes(T, D, FF).values())
    got = pl.pallas_call(body,
        out_shape=[jax.ShapeDtypeStruct(s, d) for s, d in shapes + saved],
        in_specs=[vm] * 5 + [an] * 4 + [sm] * 3, out_specs=[an] * (3 + len(saved)),
        scratch_shapes=[pltpu.VMEM(s, d) for s, d in shapes] + [
            pltpu.VMEM((2, 2 * rows, M // 2), F32), pltpu.VMEM((2, 2 * rows, FF // 2), F32),
            pltpu.VMEM((2, rows, M // 2), F32), pltpu.VMEM((2, rows, FF // 2), F32),
            pltpu.SemaphoreType.DMA((6, 5)), pltpu.SemaphoreType.DMA((6, 4 * depth)),
            pltpu.SemaphoreType.DMA((2, 6)), pltpu.SemaphoreType.DMA((6, depth)), pltpu.SemaphoreType.DMA((24,)),
            pltpu.SemaphoreType.DMA((4,)), pltpu.VMEM((T, T), F32), pltpu.VMEM((5, 8, D), F32), pltpu.VMEM((2 + depth, 8, D), F32),
            pltpu.VMEM(h.shape, F32), pltpu.VMEM(history.shape, BF), pltpu.VMEM(cotangent.shape, F32), pltpu.VMEM(rope.shape, F32), pltpu.SemaphoreType.DMA((2 + depth,)), pltpu.SemaphoreType.DMA((2 + depth,))] + [pltpu.VMEM(s, d) for s, d in saved],
        compiler_params=pltpu.CompilerParams(collective_id=0, has_side_effects=True, vmem_limit_bytes=62 * 2**20),
        cost_estimate=pl.CostEstimate(flops=16 * T * D * FF, bytes_accessed=2**26, transcendentals=2**21),
    )(w_qkv, w_out, w_up, w_down, gains, h, history, cotangent, rope, lengths, first, second)
    return got[:3], SimpleNamespace(**dict(zip(SAVED, got[3:])))


def norm_back(e, h, gain):
    unit, inverse = normalized(h)
    scaled = e * gain
    grad = inverse * (scaled - jnp.mean(scaled, axis=-1, keepdims=True) - unit * jnp.mean(scaled * unit, axis=-1, keepdims=True))
    return grad, jnp.sum(e * unit, axis=0, keepdims=True)


class Backward:
    def __init__(self, io, s, g, planes, first, second):
        self.planes = planes
        self.io, self.s, self.g = io, s, g
        self.first, self.second = first, second
        self.T, self.D = s.gy.shape
        self.width = self.D // HEADS
        self.q, self.o = 3 * self.D // 2, self.D // 2
        self.half = g.mix.shape[1] // 2
        self.tiles = s.act.shape[0]
        self.hist = io.history.shape[0]
        self.writes = []

    SLOTS = ("act", "slope", "n2", "n1", "att", "after", "h", "probs", "qkv", "mix", "history", "gout", "sums", "gain", "rope")

    def load(self, name, src, dst=None):
        i = self.SLOTS.index(name)
        return pltpu.make_async_copy(src, getattr(self.s, name) if dst is None else dst, self.io.load_sem.at[i])

    def source(self, name, l):
        return getattr(self.io, name).at[l]

    def fetch(self, l, names):
        for name in names:
            src = (self.io.inputs if l == 0 else self.io.carried) if name == "h" else getattr(self.io, name).at[l]
            self.load(name, src).start()

    def here(self, l, *names):
        for name in names:
            src = (self.io.inputs if l == 0 else self.io.carried) if name == "h" else getattr(self.io, name).at[l]
            self.load(name, src).wait()

    def tile_copy(self, l, t, up):
        src = self.io.up.at[l, :, pl.ds(t * self.D, self.D)] if up else self.io.down.at[l, t]
        return pltpu.make_async_copy(src, self.s.tile.at[t], self.io.tile_sem.at[t])

    def send(self, src, dst):
        n = len(self.writes)
        self.writes.append((src, dst, n))
        pltpu.make_async_copy(src, dst, self.io.write_sem.at[n]).start()

    def finish(self):
        for src, dst, n in self.writes:
            pltpu.make_async_copy(src, dst, self.io.write_sem.at[n]).wait()

    WHOLE = ("sums", "gain", "rope")

    def begin(self):
        self.load("gout", self.io.gout).start()
        self.fetch(1, ("act",))
        for t in range(self.tiles): self.tile_copy(1, t, False).start()
        self.fetch(1, ("slope", "n2"))
        for name in self.WHOLE: self.load(name, getattr(self.io, name)).start()
        s = self.s
        self.load("gout", self.io.gout).wait()
        s.gy[...] = self.second[self.hist + 1] * s.gout[...]

    def down_weight(self, l, r):
        s = self.s
        if r == len(self.planes) - 1:
            s.gm[...] = s.gy[...].astype(BF)
            self.here(l, "act")
        z = self.planes[r]
        chips = self.g.down.shape[0] // len(self.planes)
        grad = dot_tn(s.act[z], s.gm[...])
        self.g.down[pl.ds(z * chips, chips)] = grad.astype(BF).reshape((chips,) + self.g.down.shape[1:])

    def act_grad(self, l, t):
        s = self.s
        if t == 0: self.here(l, "slope")
        if l == 1 and t == 1:
            self.fetch(1, ("after", "mix", "probs", "qkv"))
            for name in self.WHOLE: self.load(name, getattr(self.io, name)).wait()
        self.tile_copy(l, t, False).wait()
        grad = dot_nt(s.gm[...], s.tile[t])
        s.slope[t] = (grad * s.slope[t].astype(F32)).astype(BF)
        self.tile_copy(l, t, True).start()

    def turned(self, l, name):
        self.here(l, name)
        self.s.turned[...] = getattr(self.s, name)[...].T

    def up_weight(self, l, t):
        s = self.s
        tile, at = divmod(t * self.o, self.D)
        self.g.up[:, t * self.o:(t + 1) * self.o] = dot(s.turned[...], s.slope[tile, :, at:at + self.o]).astype(BF)

    def norm_two_grad(self, l, t):
        s = self.s
        self.tile_copy(l, t, True).wait()
        part = dot_nt(s.slope[t], s.tile[t])
        if l == 1 and t == 1:
            self.fetch(1, ("att", "n1", "h"))
            self.load("history", self.io.history).start()
        if t == 0: s.gn[...] = part
        else: s.gn[...] = s.gn[...] + part
        if l == 1: self.tile_copy(0, t, False).start()

    def after_grad(self, l):
        s = self.s
        self.here(l, "after")
        grad, gain = norm_back(s.gn[...], s.after[...], s.gain[2 * l + 1:2 * l + 2, :])
        s.sums[3 + 2 * l:4 + 2 * l, :] = gain
        s.gy[...] = s.gy[...] + grad
        s.gm[...] = s.gy[...].astype(BF)
        if l == 1:
            self.fetch(0, ("slope", "n2", "act"))
            self.load("after", self.io.stored.at[0]).start()

    def out_weight(self, l, h):
        s = self.s
        if h == 0: self.turned(l, "att")
        at = h * self.half + self.q
        self.g.mix[:, at:at + self.o] = dot(s.turned[...], s.gm[:, h * self.o:(h + 1) * self.o]).astype(BF)

    def att_grad(self, l):
        s = self.s
        self.here(l, "mix")
        a, b = self.q, self.half + self.q
        grad = dot_nt(s.gm[:, :self.o], s.mix[:, a:a + self.o]) + dot_nt(s.gm[:, self.o:], s.mix[:, b:b + self.o])
        s.ga[...] = grad.astype(BF)

    def attend(self, l, a):
        s, D = self.s, self.D
        if a == 0: self.here(l, "probs", "qkv")
        q, k, v = (s.qkv[:, i * D + a * 128:i * D + a * 128 + 128] for i in range(3))
        ga = s.ga[:, a * 128:a * 128 + 128]
        lanes = lax.broadcasted_iota(jnp.int32, q.shape, 1)
        got = []
        for e in range(2):
            mine = (lanes < self.width) if e == 0 else (lanes >= self.width)
            probs = s.probs[2 * a + e]
            wide = probs.astype(F32)
            gp = wide * dot_nt(jnp.where(mine, ga, jnp.zeros_like(ga)), v)
            gs = (gp - wide * jnp.sum(gp, axis=-1, keepdims=True)).astype(BF)
            got.append((dot(gs, k), dot_tn(gs, q), dot_tn(probs, ga)))
        gq, gk, gv = (jnp.where(lanes < self.width, x, y) for x, y in zip(*got))
        back = lambda g: g * s.cos[...] - swap_halves(g, self.width // 2) * s.sin[...]
        for i, g in enumerate((back(gq) * self.width ** -0.5, back(gk), gv)):
            s.gj[:, i * D + a * 128:i * D + a * 128 + 128] = g.astype(BF)

    def qkv_weight(self, l, t):
        s = self.s
        if t == 0:
            self.turned(l, "n1")
            if l == 1: self.fetch(0, ("probs", "qkv", "n1", "att"))
        h, i = divmod(t, 3)
        W = self.q // 3
        at = h * self.half + i * W
        self.g.mix[:, at:at + W] = dot(s.turned[...], s.gj[:, t * W:(t + 1) * W]).astype(BF)

    def norm_one_grad(self, l, t):
        s = self.s
        W = self.D // 3
        rows = slice(t * W, (t + 1) * W)
        b = self.half
        s.gn[:, rows] = dot_nt(s.gj[:, :self.q], s.mix[rows, :self.q]) + dot_nt(s.gj[:, self.q:], s.mix[rows, b:b + self.q])

    def layer_grad(self, l):
        s = self.s
        self.here(l, "h")
        grad, gain = norm_back(s.gn[...], s.h[...], s.gain[2 * l:2 * l + 1, :])
        s.sums[2 + 2 * l:3 + 2 * l, :] = gain
        s.gy[...] = s.gy[...] + grad
        if l == 1: self.fetch(0, ("mix", "h"))
        if l == 1:
            s.kept[...] = s.gy[...]
            self.send(s.kept, self.io.grad_carried)
        else: self.send(s.gy, self.io.grad_inputs)

    def between(self):
        s, n = self.s, self.hist
        self.load("history", self.io.history).wait()
        self.load("after", self.io.stored.at[0]).wait()
        grad = s.gy[...]
        for j in range(n): add_sum(s.sums, 0, j, s.history[j].astype(F32) * grad)
        add_sum(s.sums, 0, n, s.after[...] * grad)
        s.gy[...] = self.first[n] * grad + self.second[n] * s.gout[...]
        self.fetch(0, ("after",))

    def steps(self):
        P = functools.partial
        out = [("do", -1, self.begin)]
        for l in (1, 0):
            k = 3 * l
            tiles = range(self.tiles)
            if l == 0: out.append(("do", -1, self.between))
            out += [("make", (k + 2, r), P(self.down_weight, l, r)) for r in reversed(range(len(self.planes)))]
            out += [("do", -1, P(self.act_grad, l, t)) for t in tiles]
            out.append(("do", -1, P(self.turned, l, "n2")))
            out += [("make", (k + 1, -1), P(self.up_weight, l, t)) for t in range(2 * self.tiles)]
            out += [("do", -1, P(self.norm_two_grad, l, t)) for t in tiles]
            out.append(("do", -1, P(self.after_grad, l)))
            out.append(("do", -1, P(self.att_grad, l)))
            out += [("do", -1, P(self.attend, l, a)) for a in range(self.D // 128)]
            out += [("make", (k, -1), P(self.out_weight, l, h)) for h in range(2)]
            out += [("make", (k, -1), P(self.qkv_weight, l, t)) for t in range(6)]
            out += [("do", -1, P(self.norm_one_grad, l, t)) for t in range(3)]
            out.append(("sums" if l == 0 else "do", -1, P(self.layer_grad, l)))
        return out


def weave_back(order, work):
    to_make, over, drained, done, queue = {}, set(), set(), [], list(work)
    for name, k, _ in work:
        if name == "make": to_make[k] = to_make.get(k, 0) + 1
    for v in order:
        if v == NEXT:
            name, k, act = queue.pop(0)
            if name == "make":
                before = k[0] + 3
                if k[0] < 3 and before not in drained:
                    assert before in over
                    drained.add(before)
                    done.append(("drain", before))
                to_make[k] -= 1
            done.append(act)
            if name == "sums": done.append(("sums", 0))
            continue
        k, what, r = v
        if what == "d": assert not to_make.get((k, r), 0) and not to_make.get((k, -1), 0)
        if what == "o": over.add(k)
        done.append(v)
    assert not queue
    return done


class Total:
    def __init__(self, me, value, land, ssem, rsem):
        self.me, self.value, self.land, self.ssem, self.rsem = me, value, land, ssem, rsem
    def copy(self, i, src, target):
        return pltpu.make_async_remote_copy(src_ref=src, dst_ref=self.land.at[i], send_sem=self.ssem.at[i], recv_sem=self.rsem.at[i],
            device_id=target, device_id_type=MESH)
    def step(self, n):
        me, v = self.me, self.value
        targets = (me.sib, me.xn, me.yn)
        if 0 < n <= 3:
            self.copy(n - 1, v.at[n - 1], targets[n - 1]).wait()
            v[n] = v[n - 1] + self.land[n - 1]
        if n < 3: self.copy(n, v.at[n], targets[n]).start()
        elif n == 3:
            for i, t in enumerate(me.line): self.copy(3 + i, v.at[3], t).start()
        else:
            total = v[3]
            for i, t in enumerate(me.line):
                self.copy(3 + i, v.at[3], t).wait()
                total = total + self.land[3 + i]
            v[4] = total


def bwd_kernel(depth, order, kinds, first, second, *rest):
    io = SimpleNamespace()
    (io.gout, io.sums, io.gain, io.rope, io.mix, io.up, io.down, io.n1, io.qkv, io.probs, io.att, io.after, io.n2, io.act, io.slope, io.stored, io.carried, io.inputs,
        io.history), rest = rest[:19], rest[19:]
    (mix_o, up_o, down_o, io.grad_carried, io.grad_inputs, sums_o), rest = rest[:6], rest[6:]
    (mix_g, up_g, down_g, mix_d, up_d, down_d, mix_l, up_l, down_l, mix_f, up_f, down_f,
        ssem, rsem, esem, credit, io.load_sem, io.tile_sem, io.write_sem, tsend, trecv, fsem), rest = rest[:22], rest[22:]
    s = SimpleNamespace()
    (s.tile, s.mix, s.act, s.slope, s.n2, s.n1, s.att, s.after, s.h, s.probs, s.qkv, s.gy, s.gn, s.gm, s.ga, s.gj, s.turned, s.history,
        s.kept, s.value, s.land, s.gout, s.gain, s.rope) = rest
    s.cos, s.sin = s.rope.at[0], s.rope.at[1]
    scratch = s
    scratch.sums = scratch.value.at[0]
    me = Place(depth)
    c = me.c
    bar = greet(me, True)
    rows = mix_o.shape[1]
    mine = lambda w: pl.ds(al(c * w, 128), w)
    other = lambda w: pl.ds(al((1 - c) * w, 128), w)
    bwd = Backward(io, scratch, SimpleNamespace(mix=mix_g, up=up_g, down=down_g), me.planes, first, second)
    chunks = {}
    for k in range(6):
        l, j = divmod(k, 3)
        if j == 2:
            R = down_g.shape[2]
            def plane_add(z):
                for i in range(4): add_into(down_g.at[z * 4 + i, c], [down_d.at[z * 4 + i]], R)
            chunks[k] = SimpleNamespace(kind=kinds[k], rows=R, share=lambda chip: down_g.at[chip, c],
                plane=lambda z, own: down_g.at[pl.ds(z * 4, 4), c if own else 1 - c], plane_land=lambda z: down_d.at[pl.ds(z * 4, 4)],
                plane_add=plane_add, land=lambda s: down_l.at[s], result=down_f.at[l])
        else:
            g, d, land, f = ((mix_g, mix_d, mix_l, mix_f), (up_g, up_d, up_l, up_f))[j]
            half = g.shape[1] // 2
            def plane_add(z, g=g, d=d, half=half):
                at = pl.ds(al(z * 8 * rows, 16), 8 * rows)
                add_into(g.at[at, mine(half)], [d.at[at, :]], 8 * rows)
            chunks[k] = SimpleNamespace(kind=kinds[k], rows=2 * rows, share=lambda chip, g=g, half=half: g.at[pl.ds(al(chip * 2 * rows, 16), 2 * rows), mine(half)],
                plane=lambda z, own, g=g, half=half: g.at[pl.ds(al(z * 8 * rows, 16), 8 * rows), mine(half) if own else other(half)],
                plane_land=lambda z, d=d: d.at[pl.ds(al(z * 8 * rows, 16), 8 * rows), :],
                plane_add=plane_add, land=lambda s, land=land: land.at[s], result=f.at[l])
    sc = Scatter(me, chunks, ssem, rsem)
    total = Total(me, scratch.value, scratch.land, tsend, trecv)
    def result(k):
        l, j = divmod(k, 3)
        if j == 2: return [pltpu.make_async_copy(down_f.at[l], down_o.at[l], fsem.at[k])]
        f, o = ((mix_f, mix_o), (up_f, up_o))[j]
        half = f.shape[2]
        return [pltpu.make_async_copy(f.at[l, pl.ds(al(c * rows, 8), rows), :], o.at[l, :, mine(half)], fsem.at[k]),
            pltpu.make_async_remote_copy(src_ref=f.at[l, pl.ds(al((1 - c) * rows, 8), rows), :], dst_ref=o.at[l, :, mine(half)],
                send_sem=esem.at[0, k], recv_sem=esem.at[1, k], device_id=me.sib, device_id_type=MESH)]
    def tell(j):
        for d in (me.xn, me.yn): pl.semaphore_signal(credit.at[1, j], inc=1, device_id=d, device_id_type=MESH)
        when(me.has_up, lambda: pl.semaphore_signal(credit.at[2, j], inc=1, device_id=me.up, device_id_type=MESH))
        when(me.has_down, lambda: pl.semaphore_signal(credit.at[2, j], inc=1, device_id=me.down, device_id_type=MESH))
    planes_left, told, totals = {k: depth for k in range(6)}, {}, []
    greeted_yet = []
    for n, item in enumerate(weave_back(order, bwd.steps())):
        if not isinstance(item, tuple):
            item()
            continue
        if not greeted_yet:
            greeted(me, bar, True)
            greeted_yet.append(1)
        if item[0] == "drain":
            sc.drain(item[1])
            continue
        if item[0] == "sums":
            totals = [0, 1, 2, 3, 4]
            since = 0
            continue
        k, what, r = item
        l, j = divmod(k, 3)
        if l == 0 and what == "d" and (0, j) not in told:
            told[0, j] = True
            pl.semaphore_wait(credit.at[0, j], 1)
        if l == 0 and what == "q" and (1, j) not in told:
            told[1, j] = True
            pl.semaphore_wait(credit.at[1, j], 2)
        if l == 0 and what == "l" and (2, j) not in told:
            told[2, j] = True
            pl.semaphore_wait(credit.at[2, j], me.has_up.astype(jnp.int32) + me.has_down.astype(jnp.int32))
        sc.event(k, what, r)
        if what == "q":
            planes_left[k] -= 1
            if l == 1 and planes_left[k] == 0:
                pl.semaphore_signal(credit.at[0, j], inc=1, device_id=me.sib, device_id_type=MESH)
        if what == "o":
            for cp in result(k): cp.start()
            if l == 1: tell(j)
        if totals:
            since += 1
            if since % 4 == 0: total.step(totals.pop(0))
    for i in totals: total.step(i)
    everything = pltpu.make_async_copy(s.value.at[4], sums_o, fsem.at[6])
    everything.start()
    for k in range(3): sc.drain(k)
    for k in range(6):
        for cp in result(k): cp.wait()
    everything.wait()
    bwd.finish()


def bwd_call(mesh, order, kinds, weights, saved, inputs, history, rope, first, second):
    mix, up, down = weights
    depth = mesh.shape["wide"] // 2
    D, M = mix.shape[1:]
    FF = up.shape[2]
    T = inputs.shape[0]
    n = mesh.size // 2
    rows, drows = D // mesh.size, FF // mesh.size
    down = down.reshape(2, FF // D, D, D)
    slots = 4 * depth + 3
    body = functools.partial(bwd_kernel, depth, order, kinds)
    vm = pl.BlockSpec(memory_space=pltpu.VMEM); an = pl.BlockSpec(memory_space=pl.ANY); sm = pl.BlockSpec(memory_space=pltpu.SMEM)
    V, S = pltpu.VMEM, pltpu.SemaphoreType.DMA
    return pl.pallas_call(body,
        out_shape=[jax.ShapeDtypeStruct(s, F32) for s in ((2, rows, M), (2, rows, FF), (2, drows, D), (T, D), (T, D), (8, D))],
        in_specs=[sm] * 2 + [an] * 19, out_specs=[an] * 6,
        scratch_shapes=[V((D, M), BF), V((D, FF), BF), V((n, 2, drows, D), BF),
            V((D, M // 2), BF), V((D, FF // 2), BF), V((n, drows, D), BF),
            V((slots, 2 * rows, M // 2), BF), V((slots, 2 * rows, FF // 2), BF), V((slots, drows, D), BF),
            V((2, 2 * rows, M // 2), F32), V((2, 2 * rows, FF // 2), F32), V((2, drows, D), F32),
            S((6, 5)), S((6, slots + depth)), S((2, 6)), pltpu.SemaphoreType.REGULAR((3, 3)),
            S((len(Backward.SLOTS),)), S((FF // D,)), S((2,)), S((2 + depth,)), S((2 + depth,)), S((7,)),
            V((FF // D, D, D), BF), V((D, M), BF), V((FF // D, T, D), BF), V((FF // D, T, D), BF), V((T, D), BF), V((T, D), BF), V((T, D), BF),
            V((T, D), F32), V((T, D), F32), V((HEADS, T, T), BF), V((T, 3 * D), BF), V((T, D), F32), V((T, D), F32), V((T, D), BF),
            V((T, D), BF), V((T, 3 * D), BF), V((D, T), BF), V(history.shape, BF), V((T, D), F32), V((5, 8, D), F32),
            V((2 + depth, 8, D), F32), V((T, D), F32), V((8, D), F32), V(rope.shape, F32)],
        compiler_params=pltpu.CompilerParams(collective_id=1, has_side_effects=True, vmem_limit_bytes=63 * 2**20),
        cost_estimate=pl.CostEstimate(flops=32 * T * D * FF, bytes_accessed=2**27, transcendentals=2**10),
    )(first, second, saved.gout, saved.sums, saved.gain, rope, mix, up, down, saved.n1, saved.qkv, saved.probs, saved.att,
        saved.after, saved.n2, saved.act, saved.slope, saved.stored, saved.carried, inputs, history)


def results_kernel(first, second, sums, sums_v, grad_carried, gout, blended, stored, grad_inputs, mix, up, down,
                   blended_o, stored_o, inputs_o, history_o, qkv_o, out_o, up_o, down_o, gain_o, first_o, second_o,
                   mixed, carried_b, gout_b, blended_b, stored_b, inputs_b, mix_b, up_b, down_b, sem):
    q, o = qkv_o.shape[2] // 2, out_o.shape[2] // 2
    half = mix.shape[2] // 2
    ins = [(grad_carried, carried_b), (gout, gout_b), (stored.at[0], stored_b.at[0]), (stored.at[1], stored_b.at[1]), (blended, blended_b), (grad_inputs, inputs_b), (mix, mix_b), (up, up_b), (down, down_b)]
    outs = [[], [], [(stored_b.at[0], stored_o.at[0])], [(stored_b.at[1], stored_o.at[1])], [(blended_b, blended_o)], [(inputs_b, inputs_o)], [], [(up_b, up_o)], [(down_b, down_o)]]
    for h in range(2):
        outs[6].append((mix_b.at[:, :, pl.ds(h * half, q)], qkv_o.at[:, :, pl.ds(h * q, q)]))
        outs[6].append((mix_b.at[:, :, pl.ds(h * half + q, o)], out_o.at[:, :, pl.ds(h * o, o)]))
    loads = [pltpu.make_async_copy(a, b, sem.at[i]) for i, (a, b) in enumerate(ins)]
    for cp in loads: cp.start()
    copies = []
    def leave(a, b):
        copies.append(pltpu.make_async_copy(a, b, sem.at[len(ins) + len(copies)]))
        copies[-1].start()
    hist = history_o.shape[0]
    for j in range(hist + 1): first_o[j] = sums[0, j]
    for j in range(hist + 2): second_o[j] = sums[1, j]
    for cp, pairs in list(zip(loads, outs))[2:]:
        cp.wait()
        for a, b in pairs: leave(a, b)
    for cp in loads[:2]: cp.wait()
    for j in range(hist):
        mixed[j] = first[j] * carried_b[...] + second[j] * gout_b[...]
        leave(mixed.at[j], history_o.at[j])
    rows = gain_o.shape[2]
    device = lax.axis_index("wide") * lax.axis_size("narrow") + lax.axis_index("narrow")
    own = pltpu.roll(sums_v[...], lax.rem(sums_v.shape[1] - device * rows, sums_v.shape[1]), 1)
    for l in range(2): gain_o[l] = own[2 + 2 * l:4 + 2 * l, 0:rows]
    for cp in copies: cp.wait()


def results_call(first, second, sums, grad_carried, saved, grad_inputs, mix, up, down, hist):
    T, D = grad_inputs.shape
    rows = mix.shape[1]
    vm = pl.BlockSpec(memory_space=pltpu.VMEM); an = pl.BlockSpec(memory_space=pl.ANY); sm = pl.BlockSpec(memory_space=pltpu.SMEM)
    shapes = [(T, D), (2, T, D), (T, D), (hist, T, D), (2, rows, 3 * D), (2, rows, D), up.shape, down.shape, (2, 2, rows), (hist + 1,), (hist + 2,)]
    return pl.pallas_call(results_kernel,
        out_shape=[jax.ShapeDtypeStruct(s, F32) for s in shapes],
        in_specs=[sm] * 3 + [vm] + [an] * 8, out_specs=[an] * 8 + [vm] + [sm] * 2,
        scratch_shapes=[pltpu.VMEM((hist, T, D), F32), pltpu.VMEM((T, D), F32), pltpu.VMEM((T, D), F32), pltpu.VMEM((T, D), F32), pltpu.VMEM((2, T, D), F32), pltpu.VMEM((T, D), F32),
            pltpu.VMEM(mix.shape, F32), pltpu.VMEM(up.shape, F32), pltpu.VMEM(down.shape, F32), pltpu.SemaphoreType.DMA((20 + hist,))],
        compiler_params=pltpu.CompilerParams(vmem_limit_bytes=60 * 2**20),
    )(first, second, sums, sums, grad_carried, saved.gout, saved.blended, saved.stored, grad_inputs, mix, up, down)


def fast_body(mesh, inputs, history, lengths, cotangent, w_qkv, w_out, w_up, w_down, gains, alpha_first, alpha_second):
    rope = jnp.asarray(rotary_lanes(inputs.shape[0], inputs.shape[1] // HEADS, 128))
    weights, saved = fwd_call(mesh, steps(GATHER_ORDER), GATHER_KINDS, w_qkv, w_out, w_up, w_down, gains,
        inputs, history, cotangent, rope, lengths, alpha_first, alpha_second)
    mix, up, down, grad_carried, grad_inputs, sums = bwd_call(mesh, steps(SCATTER_ORDER), SCATTER_KINDS, weights, saved,
        inputs, history, rope, alpha_first, alpha_second)
    return results_call(alpha_first, alpha_second, sums, grad_carried, saved, grad_inputs, mix, up, down, history.shape[0])


def solution(mesh):
    axes = ("wide", "narrow")
    split, row_split = P(None, axes, None), P(axes, None)
    placed = (row_split, split, P(axes), row_split, split, split, split, split, P(None, None, axes), P(), P())
    results = (row_split, split, row_split, split, split, split, split, split, P(None, None, axes), P(), P())

    def body(*args):
        rows, hist = args[4].shape[1], args[1].shape[0]
        fits = mesh.shape["narrow"] == 4 and mesh.shape["wide"] == 8 and rows % 8 == 0
        fits = fits and hist * args[4].shape[1] == args[7].shape[1]
        return fast_body(mesh, *args) if fits else plain_body(*args)

    return jax.shard_map(body, mesh=mesh, in_specs=placed, out_specs=results, check_vma=False)
```
